32 devices in a mesh: shard: 4 (over z), rep: 8 (over y, x, core).
Axes of the slice: x: 2, y: 2, z: 4, core: 2. Of those that a mesh axis runs over, the one named last changes fastest.
Arguments:
- tokens: bfloat16 [128, 256, 384], P(('shard', 'rep')), may hold values from -6 to 6
- condition: bfloat16 [128, 384], P(('shard', 'rep')), may hold values from -6 to 6
- cotangent: bfloat16 [128, 256, 384], P(('shard', 'rep')), may hold values from -6 to 6
- attend_weight: float32 [384, 1152], P(None, 'shard'), may hold values from -0.3125 to 0.3125
- project_weight: float32 [384, 384], P(None, 'shard'), may hold values from -1.75 to 1.75
- expand_weight: float32 [384, 1536], P(None, 'shard'), may hold values from -0.3125 to 0.3125
- contract_weight: float32 [384, 1536], P(None, 'shard'), may hold values from -0.15625 to 0.15625
- modulate_weight: float32 [384, 2304], P(None, 'shard'), may hold values from -0.3125 to 0.3125
- biases: float32 [4224], P('shard'), may hold values from -1.2 to 1.2
- attend_moment: float32 [384, 1152], P(None, 'shard'), may hold values from -2606.6784 to 2606.6784
- project_moment: float32 [384, 384], P(None, 'shard'), may hold values from -488.7522 to 488.7522
- expand_moment: float32 [384, 1536], P(None, 'shard'), may hold values from -814.58701 to 814.58701
- contract_moment: float32 [384, 1536], P(None, 'shard'), may hold values from -1629.17402 to 1629.17402
- modulate_moment: float32 [384, 2304], P(None, 'shard'), may hold values from -1955.0088 to 1955.0088
- bias_first: float32 [4224], P('shard'), may hold values from -121.282955 to 121.282955
- bias_second: float32 [4224], P('shard'), may hold values from 0.65536 to 262.144, as said below
Outputs:
- block_output: bfloat16 [128, 256, 384], P(('shard', 'rep'))
- tokens_grad: float32 [128, 256, 384], P(('shard', 'rep'))
- condition_grad: float32 [128, 384], P(('shard', 'rep'))
- attend_grad: float32 [384, 1152], P(None, 'shard')
- project_grad: float32 [384, 384], P(None, 'shard')
- expand_grad: float32 [384, 1536], P(None, 'shard')
- contract_grad: float32 [384, 1536], P(None, 'shard')
- modulate_grad: float32 [384, 2304], P(None, 'shard')
- attend_momentum: float32 [384, 1152], P(None, 'shard')
- project_momentum: float32 [384, 384], P(None, 'shard')
- expand_momentum: float32 [384, 1536], P(None, 'shard')
- contract_momentum: float32 [384, 1536], P(None, 'shard')
- modulate_momentum: float32 [384, 2304], P(None, 'shard')
- attend_updated: float32 [384, 1152], P(None, 'shard')
- project_updated: float32 [384, 384], P(None, 'shard')
- expand_updated: float32 [384, 1536], P(None, 'shard')
- contract_updated: float32 [384, 1536], P(None, 'shard')
- modulate_updated: float32 [384, 2304], P(None, 'shard')
- bias_gradient: float32 [4224], P('shard')
- bias_momentum: float32 [4224], P('shard')
- bias_variance: float32 [4224], P('shard')
- bias_updated: float32 [4224], P('shard')
The draws below stay inside these ranges and needn't reach their ends.
Inputs may be any that keep to these rules, and one draw needn't show every extreme that they name: `bias_second`: second moment of the biases, positive.
All inputs are finite; a program needn't handle non-finite values.
Results may differ from the reference program's by a relative error of at most 0.013.
The reference program's roundings to bfloat16 on the way count: a program that leaves them out, or rounds other values in their place, can miss the bound.
Values may be sent and summed in bfloat16 or wider, within the bound.
No kernel may reach another device: no remote copies, remote signals or barrier semaphores. Data moves between devices by JAX's collectives and lax.ppermute only.
A program may use at most 128 MiB of HBM per device.

```python
import math
import jax
import jax.numpy as jnp
from jax import lax

D = 384
HEADS = 6
HEAD = 64
FF = 1536
LEN = 256
NS_ITERS = 5
STEP = 10
SEQS = 128
BIAS_LEN = 4224


def moment_matrix(key, columns, factor, column_rise, spread):
    row_key, column_key, entry_key = jax.random.split(key, 3)
    unit_scale = factor * math.sqrt(SEQS * LEN) / 3.0
    row_scale = jnp.exp(jax.random.uniform(row_key, (D, 1), jnp.float32, math.log(0.5), math.log(2.0)))
    position = jnp.arange(columns, dtype=jnp.float32)[None, :] / max(columns - 1, 1)
    column_scale = jnp.exp(position * math.log(column_rise) + jax.random.uniform(column_key, (1, columns), jnp.float32, 0.0, math.log(spread)))
    entries = jax.random.truncated_normal(entry_key, -3.0, 3.0, (D, columns), jnp.float32)
    return entries * row_scale * column_scale * unit_scale


def draw_attend_moment(key, part):
    key = jax.random.fold_in(key, 11)
    return moment_matrix(key, 3 * D, 0.8, 3.0, 3.0)


def draw_project_moment(key, part):
    key = jax.random.fold_in(key, 12)
    return moment_matrix(key, D, 0.15, 3.0, 3.0)


def draw_expand_moment(key, part):
    key = jax.random.fold_in(key, 13)
    return moment_matrix(key, FF, 0.25, 3.0, 3.0)


def draw_contract_moment(key, part):
    key = jax.random.fold_in(key, 14)
    return moment_matrix(key, FF, 0.5, 3.0, 3.0)


def draw_modulate_moment(key, part):
    key = jax.random.fold_in(key, 15)
    return moment_matrix(key, 6 * D, 0.6, 3.0, 3.0)


def segment_scale():
    position = jnp.arange(BIAS_LEN)
    return jnp.where(position < 6 * D, 1.0, jnp.where(position < 6 * D + FF, 0.2, 0.7)).astype(jnp.float32)


def draw_bias_first(key, part):
    key = jax.random.fold_in(key, 21)
    entry_key, size_key = jax.random.split(key)
    entries = jax.random.truncated_normal(entry_key, -3.0, 3.0, (BIAS_LEN,), jnp.float32)
    factors = jnp.exp(jax.random.uniform(size_key, (BIAS_LEN,), jnp.float32, math.log(0.5), math.log(2.0)))
    return entries * factors * segment_scale() * math.sqrt(SEQS * LEN) / 9.0


def draw_bias_second(key, part):
    key = jax.random.fold_in(key, 22)
    factors = jnp.exp(jax.random.uniform(key, (BIAS_LEN,), jnp.float32, math.log(0.5), math.log(8.0)))
    segment = segment_scale()
    return 0.001 * segment * segment * float(SEQS * LEN) * factors


def level_of(key, shape, shards, low, top_value):
    level, own = 1.0, jax.random.fold_in(key, 6)
    for dim, shards_of in shards:
        steps = jnp.exp(jax.random.uniform(jax.random.fold_in(own, dim), (shards_of,), jnp.float32, low / len(shards), top_value / len(shards)))
        level = level * jnp.repeat(steps, shape[dim] // shards_of).reshape([-1 if axis == dim else 1 for axis in range(len(shape))])
    return level


def normal_values(own_key, extent, scale, limit, cuts=(), held_as=jnp.bfloat16):
    values = jax.random.normal(own_key, extent, jnp.float32) * scale
    if len(cuts) > 0:
        values = level_of(own_key, extent, cuts, -0.22, 0.18) * values
    return jnp.clip(values, min=-limit, max=limit).astype(held_as)


def setup_inputs(seed: int = 0) -> dict:
    arg_keys = jax.random.split(jax.random.key(seed), 17)
    tokens = normal_values(arg_keys[0], (SEQS, LEN, D), 1.0, 6.0, ((0, 32),))
    condition = normal_values(arg_keys[1], (SEQS, D), 1.0, 6.0, ((0, 32),))
    cotangent = normal_values(arg_keys[2], (SEQS, LEN, D), 1.0, 6.0, ((0, 32),))
    attend_weight = normal_values(arg_keys[3], (D, 3 * D), D ** -0.5, 0.3125, ((1, 4),), jnp.float32)
    project_weight = normal_values(arg_keys[4], (D, D), (D // 32) ** -0.5, 1.75, ((1, 4),), jnp.float32)
    expand_weight = normal_values(arg_keys[5], (D, FF), D ** -0.5, 0.3125, ((1, 4),), jnp.float32)
    contract_weight = normal_values(arg_keys[6], (D, FF), FF ** -0.5, 0.15625, ((1, 4),), jnp.float32)
    modulate_weight = normal_values(arg_keys[7], (D, 6 * D), D ** -0.5, 0.3125, ((1, 4),), jnp.float32)
    biases = normal_values(arg_keys[8], (BIAS_LEN,), 0.2, 1.2, ((0, 4),), jnp.float32)
    attend_moment = draw_attend_moment(jax.random.fold_in(arg_keys[16], 71), 0)
    project_moment = draw_project_moment(jax.random.fold_in(arg_keys[16], 71), 0)
    expand_moment = draw_expand_moment(jax.random.fold_in(arg_keys[16], 71), 0)
    contract_moment = draw_contract_moment(jax.random.fold_in(arg_keys[16], 71), 0)
    modulate_moment = draw_modulate_moment(jax.random.fold_in(arg_keys[16], 71), 0)
    bias_first = draw_bias_first(jax.random.fold_in(arg_keys[16], 71), 0)
    bias_second = draw_bias_second(jax.random.fold_in(arg_keys[16], 71), 0)
    return {"tokens": tokens, "condition": condition, "cotangent": cotangent, "attend_weight": attend_weight, "project_weight": project_weight, "expand_weight": expand_weight, "contract_weight": contract_weight, "modulate_weight": modulate_weight, "biases": biases, "attend_moment": attend_moment, "project_moment": project_moment, "expand_moment": expand_moment, "contract_moment": contract_moment, "modulate_moment": modulate_moment, "bias_first": bias_first, "bias_second": bias_second}


EXACT_PRECISION = lax.Precision.HIGHEST
POLY_LINEAR = 3.4445
POLY_CUBIC = -4.775
POLY_QUINTIC = 2.0315
MOMENTUM = 0.95
MUON_RATE = 0.4
WEIGHT_DECAY = 0.01
ADAM_RATE = 0.1
BETA_ONE = 0.9
BETA_TWO = 0.999
ADAM_EPSILON = 1e-08

@jax.custom_vjp
def reduced_value(v):
    return lax.optimization_barrier(v.astype(jnp.bfloat16)).astype(jnp.float32)

@jax.custom_vjp
def reduced_backward(v):
    return v

def low_keep(v):
    return (reduced_value(v), None)

def low_pass(kept, grad):
    return (grad,)

def back_keep(v):
    return (v, None)

def back_low(kept, grad):
    return (reduced_value(grad),)
reduced_value.defvjp(low_keep, low_pass)
reduced_backward.defvjp(back_keep, back_low)

def layer_norm(values):
    centered = values - lax.optimization_barrier(jnp.mean(values, -1, keepdims=True))
    return centered * lax.rsqrt(lax.optimization_barrier(jnp.mean(centered * centered, -1, keepdims=True)) + 1e-06)

def sequence_group(inputs, modulation, attention_weight_matrix, projection_weight_matrix, widening_weight_matrix, narrowing_weight_matrix, widening_bias, narrowing_bias):
    shift_one, scale_one, gate_one, shift_two, scale_two, gate_two = jnp.split(modulation[:, None, :], 6, axis=2)
    group_size = inputs.shape[0]
    residual_first = reduced_value(layer_norm(inputs) * (1.0 + scale_one) + shift_one)
    projection_output = reduced_value(reduced_backward(jnp.einsum('rvx,xf->rvf', residual_first, attention_weight_matrix, precision=EXACT_PRECISION)))
    heads_view = projection_output.reshape(group_size, LEN, 3, HEADS, HEAD)
    queries = heads_view[:, :, 0]
    key_heads = heads_view[:, :, 1]
    value_heads = heads_view[:, :, 2]
    scores = reduced_backward(jnp.einsum('sqhe,skhe->shqk', queries, key_heads, precision=EXACT_PRECISION) * HEAD ** (-0.5))
    attention = jnp.exp(scores - jax.nn.logsumexp(scores, axis=-1, keepdims=True))
    attention_output = jnp.einsum('shqk,skhe->sqhe', reduced_value(attention), value_heads, precision=EXACT_PRECISION).reshape(group_size, LEN, D)
    attention_output = reduced_value(reduced_backward(attention_output))
    attention_branch = reduced_backward(jnp.einsum('rvx,xf->rvf', attention_output, projection_weight_matrix, precision=EXACT_PRECISION))
    mixed = inputs + gate_one * attention_branch
    residual_second = reduced_value(layer_norm(mixed) * (1.0 + scale_two) + shift_two)
    preactivation_value = reduced_backward(jnp.einsum('pvk,km->pvm', residual_second, widening_weight_matrix, precision=EXACT_PRECISION) + widening_bias)
    activation_output = reduced_value(jax.nn.gelu(preactivation_value, approximate=True))
    perceptron_branch = reduced_backward(jnp.einsum('mgr,ir->mgi', activation_output, narrowing_weight_matrix, precision=EXACT_PRECISION) + narrowing_bias)
    return mixed + gate_two * perceptron_branch

def forward(inputs, cond_float, attention_weight_matrix, projection_weight_matrix, widening_weight_matrix, narrowing_weight_matrix, modulate_matrix, bias_all):
    attention_weight_matrix = reduced_value(attention_weight_matrix)
    projection_weight_matrix = reduced_value(projection_weight_matrix)
    widening_weight_matrix = reduced_value(widening_weight_matrix)
    narrowing_weight_matrix = reduced_value(narrowing_weight_matrix)
    modulate_matrix = reduced_value(modulate_matrix)
    bias_all = reduced_value(bias_all)
    cond_low = reduced_value(jax.nn.silu(cond_float))
    modulation = reduced_backward(jnp.dot(cond_low, modulate_matrix, precision=EXACT_PRECISION) + bias_all[:6 * D])
    widening_bias = bias_all[6 * D:6 * D + FF]
    narrowing_bias = bias_all[6 * D + FF:]
    group_size = math.gcd(SEQS, 16)
    groups = SEQS // group_size
    stacked = inputs.reshape(groups, group_size, LEN, D)
    grouped_mods = modulation.reshape(groups, group_size, 6 * D)
    checked_group = jax.checkpoint(sequence_group)

    def scan_body(carried, slices):
        return (carried, checked_group(slices[0], slices[1], attention_weight_matrix, projection_weight_matrix, widening_weight_matrix, narrowing_weight_matrix, widening_bias, narrowing_bias))
    carried, results = lax.scan(scan_body, jnp.zeros((), jnp.float32), (stacked, grouped_mods))
    return results.reshape(SEQS, LEN, D)

def newton_schulz(matrix):
    current = matrix / (jnp.sqrt(jnp.sum(matrix * matrix)) + 1e-07)
    for iteration in range(NS_ITERS):
        gram = jnp.dot(current, current.T, precision=EXACT_PRECISION)
        mixing = POLY_CUBIC * gram + POLY_QUINTIC * jnp.dot(gram, gram, precision=EXACT_PRECISION)
        current = POLY_LINEAR * current + jnp.dot(mixing, current, precision=EXACT_PRECISION)
    return current

def muon_update(master, moment, gradient):
    momentum_new = MOMENTUM * moment + gradient
    nesterov = gradient + MOMENTUM * momentum_new
    ortho = newton_schulz(nesterov)
    updated = master * (1.0 - MUON_RATE * WEIGHT_DECAY) - MUON_RATE * 0.2 * math.sqrt(master.shape[1]) * ortho
    return (momentum_new, updated)

def reference(tokens, condition, cotangent, attend_weight, project_weight, expand_weight, contract_weight, modulate_weight, biases, attend_moment, project_moment, expand_moment, contract_moment, modulate_moment, bias_first, bias_second):
    result, pullback = jax.vjp(forward, tokens.astype(jnp.float32), condition.astype(jnp.float32), attend_weight, project_weight, expand_weight, contract_weight, modulate_weight, biases)
    grads = pullback(cotangent.astype(jnp.float32))
    tokens_grad, condition_grad, attend_grad, project_grad, expand_grad, contract_grad, modulate_grad, bias_gradient = grads
    attend_momentum, attend_updated = muon_update(attend_weight, attend_moment, attend_grad)
    project_momentum, project_updated = muon_update(project_weight, project_moment, project_grad)
    expand_momentum, expand_updated = muon_update(expand_weight, expand_moment, expand_grad)
    contract_momentum, contract_updated = muon_update(contract_weight, contract_moment, contract_grad)
    modulate_momentum, modulate_updated = muon_update(modulate_weight, modulate_moment, modulate_grad)
    bias_momentum = BETA_ONE * bias_first + (1.0 - BETA_ONE) * bias_gradient
    bias_variance = BETA_TWO * bias_second + (1.0 - BETA_TWO) * bias_gradient * bias_gradient
    corrected_first = bias_momentum / (1.0 - BETA_ONE ** STEP)
    corrected_second = bias_variance / (1.0 - BETA_TWO ** STEP)
    bias_updated = biases * (1.0 - ADAM_RATE * WEIGHT_DECAY) - ADAM_RATE * corrected_first / (jnp.sqrt(corrected_second) + ADAM_EPSILON)
    return (result.astype(jnp.bfloat16), tokens_grad, condition_grad, attend_grad, project_grad, expand_grad, contract_grad, modulate_grad, attend_momentum, project_momentum, expand_momentum, contract_momentum, modulate_momentum, attend_updated, project_updated, expand_updated, contract_updated, modulate_updated, bias_gradient, bias_momentum, bias_variance, bias_updated)
```

```python
from functools import partial
import math

import jax
import jax.numpy as jnp
from jax import lax
from jax.sharding import PartitionSpec as P

D = 384
HEADS = 6
HEAD = 64
FF = 1536
LEN = 256
NS_ITERS = 5
STEP = 10


EXACT_PRECISION = lax.Precision.HIGHEST
POLY_LINEAR = 3.4445
POLY_CUBIC = -4.775
POLY_QUINTIC = 2.0315
MOMENTUM = 0.95
MUON_RATE = 0.4
WEIGHT_DECAY = 0.01
ADAM_RATE = 0.1
BETA_ONE = 0.9
BETA_TWO = 0.999
ADAM_EPSILON = 1e-08


def normalize(values):
    centered = values - jnp.mean(values, -1, keepdims=True)
    inverse_spread = lax.rsqrt(jnp.mean(centered * centered, -1, keepdims=True) + 1e-06)
    return (centered * inverse_spread, inverse_spread)


def normalize_back(upstream, normed, inverse_spread):
    return inverse_spread * (
        upstream
        - jnp.mean(upstream, -1, keepdims=True)
        - normed * jnp.mean(upstream * normed, -1, keepdims=True)
    )


def pad_columns(blocks, width, rows):
    filled = sum((block.shape[1] for block in blocks))
    if filled < width:
        blocks = blocks + [jnp.zeros((rows, width - filled), jnp.float32)]
    return jnp.concatenate(blocks, axis=1)


def shift(value, distance):
    size = lax.axis_size("shard")
    return lax.ppermute(value, "shard", [(i, (i + distance) % size) for i in range(size)])


def flip(value, bit):
    size = lax.axis_size("rep")
    return lax.ppermute(value, "rep", [(i, i ^ (1 << bit)) for i in range(size)])


def bit_orders():
    count = lax.axis_size("rep").bit_length() - 1
    outer = list(range(1, count))
    return (outer + [0], outer[::-1] + [0])


def relative_order(bits):
    order = [0]
    for bit in bits:
        order = order + [j ^ (1 << bit) for j in order]
    return order


def gather_rep(value, bits):
    value = value[None]
    for bit in bits:
        value = jnp.concatenate([value, flip(value, bit)], axis=0)
    return value


def reduce_rep(value, bits):
    for bit in reversed(bits):
        half = value.shape[0] // 2
        received = flip(value[half:].astype(jnp.bfloat16), bit)
        value = value[:half] + received.astype(jnp.float32)
    return value[0]


def gather_weights(blocks):
    shards, reps = lax.axis_size("shard"), lax.axis_size("rep")
    shard, rep = lax.axis_index("shard"), lax.axis_index("rep")
    rows = D // reps
    packed = jnp.concatenate(
        [lax.dynamic_slice_in_dim(block, rep * rows, rows, 0).astype(jnp.bfloat16) for block in blocks],
        axis=1,
    )
    pieces = jnp.stack([packed] + [shift(packed, d) for d in range(1, shards)])
    middle = (shards + 1) // 2
    full = []
    for part, bits in zip((pieces[:middle], pieces[middle:]), bit_orders()):
        gathered = gather_rep(part, bits)
        order = jnp.array(relative_order(bits))
        inverse = jnp.argsort(order)
        full.append(jnp.take(gathered, jnp.take(inverse, rep ^ jnp.arange(reps)), axis=0))
    full = jnp.concatenate(full, axis=1)
    full = jnp.take(full, (shard - jnp.arange(shards)) % shards, axis=1)
    full = full.transpose(0, 2, 1, 3).reshape(D, shards, packed.shape[1])
    results, start = [], 0
    for block in blocks:
        width = block.shape[1]
        results.append(full[:, :, start : start + width].reshape(D, shards * width))
        start = start + width
    return results


def reduce_gradients(matrices):
    shards, reps = lax.axis_size("shard"), lax.axis_size("rep")
    shard, rep = lax.axis_index("shard"), lax.axis_index("rep")
    rows = D // reps
    packed = jnp.concatenate(
        [m.reshape(reps, rows, shards, m.shape[1] // shards) for m in matrices], axis=3
    ).transpose(0, 2, 1, 3)
    packed = jnp.take(packed, (shard + jnp.arange(shards)) % shards, axis=1)
    middle = (shards + 1) // 2
    mine = []
    for part, bits in zip((packed[:, :middle], packed[:, middle:]), bit_orders()):
        order = jnp.array(relative_order(bits))
        mine.append(reduce_rep(jnp.take(part, rep ^ order, axis=0), bits))
    mine = jnp.concatenate(mine, axis=0)
    total = mine[0]
    for d in range(1, shards):
        total = total + shift(mine[d].astype(jnp.bfloat16), d).astype(jnp.float32)
    bits = bit_orders()[0]
    gathered = gather_rep(total.astype(jnp.bfloat16), bits)
    inverse = jnp.argsort(jnp.array(relative_order(bits)))
    whole = jnp.take(gathered, jnp.take(inverse, rep ^ jnp.arange(reps)), axis=0)
    whole = whole.reshape(D, -1).astype(jnp.float32)
    results, start = [], 0
    for m in matrices:
        width = m.shape[1] // shards
        results.append(whole[:, start : start + width])
        start = start + width
    return results


def exact(left, right):
    return jnp.dot(left, right, precision=EXACT_PRECISION)


SLOTS = ((4, 0, 2), (4, 1, 2), (0, 0, 1), (2, 0, 2), (2, 1, 2), (3, 0, 2), (3, 1, 2), (1, 0, 1))


def polynomial(gram):
    scale = 1.0 / (jnp.sqrt(jnp.trace(gram)) + 1e-07)
    gram = gram * (scale * scale)
    product = None
    for step in range(NS_ITERS):
        mixing = POLY_CUBIC * gram + POLY_QUINTIC * exact(gram, gram)
        if step + 1 < NS_ITERS:
            half = POLY_LINEAR * gram + exact(mixing, gram)
            gram = POLY_LINEAR * half + exact(mixing, half)
        if product is None:
            product = POLY_LINEAR * jnp.eye(D, dtype=jnp.float32) + mixing
        else:
            product = POLY_LINEAR * product + exact(mixing, product)
    return product * scale


def orthogonalize(shares):
    shards, reps = lax.axis_size("shard"), lax.axis_size("rep")
    shard, rep = lax.axis_index("shard"), lax.axis_index("rep")
    slot = rep % len(SLOTS)
    widest = max(share.shape[1] for share in shares)
    slot_widest = max(shares[m].shape[1] // parts for m, _, parts in SLOTS)
    padded = jnp.stack([pad_columns([share], widest, D) for share in shares])
    matrix = lax.dynamic_index_in_dim(
        padded, jnp.array([m for m, _, _ in SLOTS])[slot], 0, keepdims=False
    )
    slots = jnp.stack(
        [
            pad_columns(
                [shares[m][:, p * (shares[m].shape[1] // parts) : (p + 1) * (shares[m].shape[1] // parts)]],
                slot_widest,
                D,
            )
            for m, p, parts in SLOTS
        ]
    )
    columns = lax.dynamic_index_in_dim(slots, slot, 0, keepdims=False)
    partial_gram = exact(matrix, matrix.T).reshape(shards, D // shards, D)
    partial_gram = jnp.take(partial_gram, (shard + jnp.arange(shards)) % shards, axis=0)
    piece = partial_gram[0]
    for d in range(1, shards):
        piece = piece + shift(partial_gram[d], d)
    gram = jnp.stack([piece] + [shift(piece, d) for d in range(1, shards)])
    gram = jnp.take(gram, (shard - jnp.arange(shards)) % shards, axis=0).reshape(D, D)
    answer = exact(polynomial(gram), columns).astype(jnp.bfloat16)
    bits = [b for b in bit_orders()[0] if (1 << b) < len(SLOTS)]
    gathered = gather_rep(answer, bits)
    order = relative_order(bits)
    inverse = jnp.argsort(jnp.array(order))
    whole = jnp.take(gathered, jnp.take(inverse, slot ^ jnp.arange(len(SLOTS))), axis=0)
    results = []
    for number, share in enumerate(shares):
        results.append(
            jnp.concatenate(
                [
                    whole[k][:, : share.shape[1] // parts]
                    for k, (m, p, parts) in enumerate(SLOTS)
                    if m == number
                ],
                axis=1,
            ).astype(jnp.float32)
        )
    return results


def per_device(
    tokens,
    condition,
    cotangent,
    attend_weight,
    project_weight,
    expand_weight,
    contract_weight,
    modulate_weight,
    biases,
    attend_moment,
    project_moment,
    expand_moment,
    contract_moment,
    modulate_moment,
    bias_first,
    bias_second,
):
    bfloat = jnp.bfloat16
    single_layer_input = jnp.float32
    latents = tokens.shape[0]
    shards, reps = lax.axis_size("shard"), lax.axis_size("rep")
    shard, rep = lax.axis_index("shard"), lax.axis_index("rep")
    attention_weight_whole, projection_weight_whole = gather_weights([attend_weight, project_weight])
    widening_weight_whole, narrowing_weight_whole = gather_weights([expand_weight, contract_weight])
    modulate_low = modulate_weight.astype(bfloat)
    bias_low = biases.astype(bfloat)
    bias_pieces = jnp.stack([bias_low] + [shift(bias_low, d) for d in range(1, shards)])
    source_order = (shard - jnp.arange(shards)) % shards
    bias_full = jnp.take(bias_pieces, source_order, axis=0).reshape(-1)
    ada_bias = bias_full[: 6 * D].astype(single_layer_input)
    widening_bias = bias_full[6 * D : 6 * D + FF].astype(single_layer_input)
    narrowing_bias = bias_full[6 * D + FF :].astype(single_layer_input)
    inputs = tokens.astype(single_layer_input)
    silu_value, silu_back = jax.vjp(jax.nn.silu, condition.astype(single_layer_input))
    cond_low = silu_value.astype(bfloat)
    cond_pieces = jnp.stack([cond_low] + [shift(cond_low, d) for d in range(1, shards)])
    share = jnp.dot(
        cond_pieces.reshape(shards * latents, D), modulate_low, preferred_element_type=single_layer_input
    ).reshape(shards, latents, -1)
    answers = jnp.stack([share[0]] + [shift(share[d], shards - d) for d in range(1, shards)])
    answers = jnp.take(answers, (jnp.arange(shards) - shard) % shards, axis=0)
    modulation = answers.transpose(1, 0, 2).reshape(latents, 6 * D) + ada_bias
    shift_one, scale_one, gate_one, shift_two, scale_two, gate_two = jnp.split(
        modulation[:, None, :], 6, axis=2
    )
    normed_one, spread_one = normalize(inputs)
    residual_first = (normed_one * (1.0 + scale_one) + shift_one).astype(bfloat)
    projection_output = jnp.einsum(
        "rvx,xf->rvf",
        residual_first,
        attention_weight_whole,
        preferred_element_type=single_layer_input,
    ).astype(bfloat)
    heads_view = projection_output.reshape(latents, LEN, 3, HEADS, HEAD)
    queries = heads_view[:, :, 0]
    key_heads = heads_view[:, :, 1]
    value_heads = heads_view[:, :, 2]
    score_scale = HEAD ** (-0.5)
    scores = (
        jnp.einsum("sqhe,skhe->shqk", queries, key_heads, preferred_element_type=single_layer_input)
        * score_scale
    )
    log_total = jax.nn.logsumexp(scores, axis=-1, keepdims=True)
    attention_low = jnp.exp(scores - log_total).astype(bfloat)
    attention_output = (
        jnp.einsum(
            "shqk,skhe->sqhe", attention_low, value_heads, preferred_element_type=single_layer_input
        )
        .reshape(latents, LEN, D)
        .astype(bfloat)
    )
    attention_branch = jnp.einsum(
        "rvx,xf->rvf",
        attention_output,
        projection_weight_whole,
        preferred_element_type=single_layer_input,
    )
    mixed = inputs + gate_one * attention_branch
    normed_two, spread_two = normalize(mixed)
    residual_second = (normed_two * (1.0 + scale_two) + shift_two).astype(bfloat)
    preactivation_value = (
        jnp.einsum(
            "pvk,km->pvm",
            residual_second,
            widening_weight_whole,
            preferred_element_type=single_layer_input,
        )
        + widening_bias
    )
    act_value, act_back = jax.vjp(partial(jax.nn.gelu, approximate=True), preactivation_value)
    activation_reduced = act_value.astype(bfloat)
    perceptron_branch = (
        jnp.einsum(
            "mgr,ir->mgi",
            activation_reduced,
            narrowing_weight_whole,
            preferred_element_type=single_layer_input,
        )
        + narrowing_bias
    )
    block_output = (mixed + gate_two * perceptron_branch).astype(bfloat)
    grad_out = cotangent.astype(single_layer_input)
    grad_gate_two = jnp.sum(grad_out * perceptron_branch, axis=1, keepdims=True)
    branch_gradient = (gate_two * grad_out).astype(bfloat)
    narrowing_gradient = jnp.einsum(
        "gpr,gpw->rw",
        branch_gradient,
        activation_reduced,
        preferred_element_type=single_layer_input,
    )
    activation_gradient = jnp.einsum(
        "pvk,km->pvm",
        branch_gradient,
        narrowing_weight_whole,
        preferred_element_type=single_layer_input,
    )
    preactivation_gradient = act_back(activation_gradient)[0].astype(bfloat)
    widening_gradient = jnp.einsum(
        "gpr,gpw->rw",
        residual_second,
        preactivation_gradient,
        preferred_element_type=single_layer_input,
    )
    grad_hidden_two = jnp.einsum(
        "mgr,ir->mgi",
        preactivation_gradient,
        widening_weight_whole,
        preferred_element_type=single_layer_input,
    )
    grad_shift_two = jnp.sum(grad_hidden_two, axis=1, keepdims=True)
    grad_scale_two = jnp.sum(grad_hidden_two * normed_two, axis=1, keepdims=True)
    grad_mixed = grad_out + normalize_back(
        grad_hidden_two * (1.0 + scale_two), normed_two, spread_two
    )
    grad_gate_one = jnp.sum(grad_mixed * attention_branch, axis=1, keepdims=True)
    attention_branch_gradient = (gate_one * grad_mixed).astype(bfloat)
    grad_project = jnp.einsum(
        "ztm,ztg->mg",
        attention_output,
        attention_branch_gradient,
        preferred_element_type=single_layer_input,
    )
    grad_attended = (
        jnp.einsum(
            "hfc,zc->hfz",
            attention_branch_gradient,
            projection_weight_whole,
            preferred_element_type=single_layer_input,
        )
        .astype(bfloat)
        .reshape(latents, LEN, HEADS, HEAD)
    )
    scores_again = (
        jnp.einsum("sqhe,skhe->shqk", queries, key_heads, preferred_element_type=single_layer_input)
        * score_scale
    )
    attention = jnp.exp(scores_again - log_total)
    grad_attention = jnp.einsum(
        "sqhe,skhe->shqk", grad_attended, value_heads, preferred_element_type=single_layer_input
    )
    grad_scores = (
        attention * (grad_attention - jnp.sum(attention * grad_attention, axis=-1, keepdims=True))
    ).astype(bfloat)
    grad_queries = (
        jnp.einsum(
            "shqk,skhe->sqhe", grad_scores, key_heads, preferred_element_type=single_layer_input
        )
        * score_scale
    )
    grad_keys = (
        jnp.einsum(
            "shqk,sqhe->skhe", grad_scores, queries, preferred_element_type=single_layer_input
        )
        * score_scale
    )
    grad_values = jnp.einsum(
        "shqk,sqhe->skhe", attention_low, grad_attended, preferred_element_type=single_layer_input
    )
    projection_output_gradient = (
        jnp.stack([grad_queries, grad_keys, grad_values], axis=2)
        .reshape(latents, LEN, 3 * D)
        .astype(bfloat)
    )
    grad_attend = jnp.einsum(
        "ztm,ztg->mg",
        residual_first,
        projection_output_gradient,
        preferred_element_type=single_layer_input,
    )
    grad_hidden_one = jnp.einsum(
        "hfc,zc->hfz",
        projection_output_gradient,
        attention_weight_whole,
        preferred_element_type=single_layer_input,
    )
    grad_shift_one = jnp.sum(grad_hidden_one, axis=1, keepdims=True)
    grad_scale_one = jnp.sum(grad_hidden_one * normed_one, axis=1, keepdims=True)
    tokens_grad = grad_mixed + normalize_back(
        grad_hidden_one * (1.0 + scale_one), normed_one, spread_one
    )
    grad_modulation = jnp.concatenate(
        [
            grad_shift_one,
            grad_scale_one,
            grad_gate_one,
            grad_shift_two,
            grad_scale_two,
            grad_gate_two,
        ],
        axis=2,
    )[:, 0, :].astype(bfloat)
    outgoing = grad_modulation.reshape(latents, shards, -1).transpose(1, 0, 2)
    outgoing = jnp.take(outgoing, (shard + jnp.arange(shards)) % shards, axis=0)
    received = jnp.stack([outgoing[0]] + [shift(outgoing[d], d) for d in range(1, shards)])
    bits = bit_orders()[0]
    grad_columns = gather_rep(received.reshape(shards * latents, -1), bits)
    cond_all = gather_rep(cond_pieces.reshape(shards * latents, D), bits)
    grad_modulate = jnp.einsum(
        "rsd,rse->de", cond_all, grad_columns, preferred_element_type=single_layer_input
    )
    grad_cond_share = jnp.einsum(
        "se,de->sd",
        received.reshape(shards * latents, -1),
        modulate_low,
        preferred_element_type=single_layer_input,
    ).reshape(shards, latents, D)
    grad_cond_low = grad_cond_share[0]
    for d in range(1, shards):
        grad_cond_low = grad_cond_low + shift(grad_cond_share[d], shards - d)
    condition_grad = silu_back(grad_cond_low)[0]
    grad_bias = jnp.concatenate(
        [
            jnp.sum(grad_modulation, axis=0, dtype=single_layer_input),
            jnp.sum(preactivation_gradient, axis=(0, 1), dtype=single_layer_input),
            jnp.sum(branch_gradient, axis=(0, 1), dtype=single_layer_input),
        ]
    )
    grad_expand, grad_contract = reduce_gradients([widening_gradient, narrowing_gradient])
    grad_attend, grad_project = reduce_gradients([grad_attend, grad_project])
    gradients = [grad_attend, grad_project, grad_expand, grad_contract, grad_modulate]
    bias_parts = jnp.take(
        grad_bias.reshape(shards, -1), (shard + jnp.arange(shards)) % shards, axis=0
    )
    bias_gradient = bias_parts[0]
    for d in range(1, shards):
        bias_gradient = bias_gradient + shift(bias_parts[d], d)
    for bit in bits:
        bias_gradient = bias_gradient + flip(bias_gradient, bit)
    masters = [attend_weight, project_weight, expand_weight, contract_weight, modulate_weight]
    moments = [attend_moment, project_moment, expand_moment, contract_moment, modulate_moment]
    momenta = [MOMENTUM * moment_old + gradient for moment_old, gradient in zip(moments, gradients)]
    nesterov = [
        gradient + MOMENTUM * moment_new for gradient, moment_new in zip(gradients, momenta)
    ]
    ortho = orthogonalize(nesterov)
    updated = []
    for master, direction in zip(masters, ortho):
        full_columns = master.shape[1] * lax.axis_size("shard")
        updated.append(
            master * (1.0 - MUON_RATE * WEIGHT_DECAY)
            - MUON_RATE * 0.2 * math.sqrt(full_columns) * direction
        )
    bias_momentum = BETA_ONE * bias_first + (1.0 - BETA_ONE) * bias_gradient
    bias_variance = BETA_TWO * bias_second + (1.0 - BETA_TWO) * bias_gradient * bias_gradient
    corrected_first = bias_momentum / (1.0 - BETA_ONE**STEP)
    corrected_second = bias_variance / (1.0 - BETA_TWO**STEP)
    bias_updated = biases * (1.0 - ADAM_RATE * WEIGHT_DECAY) - ADAM_RATE * corrected_first / (
        jnp.sqrt(corrected_second) + ADAM_EPSILON
    )
    return (
        block_output,
        tokens_grad,
        condition_grad,
        gradients[0],
        gradients[1],
        gradients[2],
        gradients[3],
        gradients[4],
        momenta[0],
        momenta[1],
        momenta[2],
        momenta[3],
        momenta[4],
        updated[0],
        updated[1],
        updated[2],
        updated[3],
        updated[4],
        bias_gradient,
        bias_momentum,
        bias_variance,
        bias_updated,
    )


def solution(mesh):
    placed = (
        P(("shard", "rep"), None, None),
        P(("shard", "rep"), None),
        P(("shard", "rep"), None, None),
        P(None, "shard"),
        P(None, "shard"),
        P(None, "shard"),
        P(None, "shard"),
        P(None, "shard"),
        P("shard"),
        P(None, "shard"),
        P(None, "shard"),
        P(None, "shard"),
        P(None, "shard"),
        P(None, "shard"),
        P("shard"),
        P("shard"),
    )
    return jax.shard_map(
        per_device,
        mesh=mesh,
        in_specs=placed,
        out_specs=(
            P(("shard", "rep"), None, None),
            P(("shard", "rep"), None, None),
            P(("shard", "rep"), None),
            P(None, "shard"),
            P(None, "shard"),
            P(None, "shard"),
            P(None, "shard"),
            P(None, "shard"),
            P(None, "shard"),
            P(None, "shard"),
            P(None, "shard"),
            P(None, "shard"),
            P(None, "shard"),
            P(None, "shard"),
            P(None, "shard"),
            P(None, "shard"),
            P(None, "shard"),
            P(None, "shard"),
            P("shard"),
            P("shard"),
            P("shard"),
            P("shard"),
        ),
        check_vma=False,
    )
```

```python
from functools import partial
import math

import jax
import jax.numpy as jnp
from jax import lax
from jax.experimental import pallas as pl
from jax.experimental.pallas import tpu as pltpu
from jax.sharding import PartitionSpec as P

D = 384
HEADS = 6
HEAD = 64
FF = 1536
LEN = 256
NS_ITERS = 5
STEP = 10
PAIR = 2 * HEAD
CHUNK = 512
GROUP = 8
BLOCK = 2

POLY_LINEAR = 3.4445
POLY_CUBIC = -4.775
POLY_QUINTIC = 2.0315
MOMENTUM = 0.95
MUON_RATE = 0.4
WEIGHT_DECAY = 0.01
ADAM_RATE = 0.1
BETA_ONE = 0.9
BETA_TWO = 0.999
ADAM_EPSILON = 1e-08
GELU_SLOPE = math.sqrt(2.0 / math.pi)
GELU_CUBIC = 0.044715

LOW = jnp.bfloat16
FULL = jnp.float32

SLOTS = ((4, 0), (4, 1), (0, 0), (2, 0), (2, 1), (3, 0), (3, 1), (1, 0))


def shift(value, distance):
    size = lax.axis_size("shard")
    return lax.ppermute(value, "shard", [(i, (i + distance) % size) for i in range(size)])


def flip(value, bit):
    size = lax.axis_size("rep")
    return lax.ppermute(value, "rep", [(i, i ^ (1 << bit)) for i in range(size)])


def rotate(value, start):
    doubled = jnp.concatenate([value, value], axis=0)
    return lax.dynamic_slice_in_dim(doubled, start, value.shape[0], 0)


def bit_orders():
    return ((1, 2, 0), (2, 1, 0))


def position(j, bits):
    total = 0
    for place, bit in enumerate(bits):
        total = total | (((j >> bit) & 1) << place)
    return total


def gather_rep(value, bits):
    value = value[None]
    for bit in bits:
        value = jnp.concatenate([value, flip(value, bit)], axis=0)
    return value


def gather_weights(blocks, low):
    shards = lax.axis_size("shard")
    rows = D // GROUP
    packed = jnp.concatenate(
        [lax.dynamic_slice_in_dim(block, low * rows, rows, 0).astype(LOW) for block in blocks],
        axis=1,
    )
    pieces = [packed] + [shift(packed, d) for d in range(1, shards)]
    middle = (shards + 1) // 2
    return [
        gather_rep(jnp.stack(part), bits)
        for part, bits in zip((pieces[:middle], pieces[middle:]), bit_orders())
    ]


def reduce_pieces(keep, send):
    shards = lax.axis_size("shard")
    middle = (shards + 1) // 2
    total = keep + flip(send, 0).astype(FULL)
    first = total[:, :, :middle]
    first = first[0] + flip(first[1].astype(LOW), 2).astype(FULL)
    first = first[0] + flip(first[1].astype(LOW), 1).astype(FULL)
    second = total[:, :, middle:]
    second = second[:, 0] + flip(second[:, 1].astype(LOW), 1).astype(FULL)
    second = second[0] + flip(second[1].astype(LOW), 2).astype(FULL)
    mine = first[0]
    for d in range(1, shards):
        piece = first[d] if d < middle else second[d - middle]
        mine = mine + shift(piece.astype(LOW), d).astype(FULL)
    mine = mine.astype(LOW)
    for bit in range(3, lax.axis_size("rep").bit_length() - 1):
        mine = (mine.astype(FULL) + flip(mine, bit).astype(FULL)).astype(LOW)
    return mine


def dot(left, right):
    return lax.dot_general(left, right, (((1,), (0,)), ((), ())), preferred_element_type=FULL)


def dot_nt(left, right):
    return lax.dot_general(left, right, (((1,), (1,)), ((), ())), preferred_element_type=FULL)


def dot_tn(left, right):
    return lax.dot_general(left, right, (((0,), (0,)), ((), ())), preferred_element_type=FULL)


def split_low(value):
    high = value.astype(LOW)
    return high, (value - high.astype(FULL)).astype(LOW)


def dot_split(left, right, product=dot):
    return product(left[0], right[0]) + (product(left[0], right[1]) + product(left[1], right[0]))


def normalize(values):
    centered = values - jnp.mean(values, -1, keepdims=True)
    inverse_spread = lax.rsqrt(jnp.mean(centered * centered, -1, keepdims=True) + 1e-06)
    return centered * inverse_spread, inverse_spread


def normalize_back(upstream, normed, inverse_spread):
    return inverse_spread * (
        upstream
        - jnp.mean(upstream, -1, keepdims=True)
        - normed * jnp.mean(upstream * normed, -1, keepdims=True)
    )


def local_call(kernel, ids, inputs, outputs, scratch, steps, flops, name):
    def spec(shape, blocked):
        zeros = (0,) * (len(shape) - 1)
        if blocked:
            block = (shape[0] // steps,) + tuple(shape[1:])
            return pl.BlockSpec(block, lambda i, _: (i,) + zeros)
        return pl.BlockSpec(tuple(shape), lambda i, _: (0,) + zeros)

    moved = sum(v.size * v.dtype.itemsize for v, _ in inputs)
    moved += sum(math.prod(shape) * jnp.dtype(kind).itemsize for shape, kind, _ in outputs)
    return pl.pallas_call(
        kernel,
        grid_spec=pltpu.PrefetchScalarGridSpec(
            num_scalar_prefetch=1,
            grid=(steps,),
            in_specs=[spec(v.shape, blocked) for v, blocked in inputs],
            out_specs=[spec(shape, blocked) for shape, _, blocked in outputs],
            scratch_shapes=scratch,
        ),
        out_shape=[jax.ShapeDtypeStruct(shape, kind) for shape, kind, _ in outputs],
        compiler_params=pltpu.CompilerParams(
            dimension_semantics=("arbitrary",), vmem_limit_bytes=48 * 1024 * 1024
        ),
        cost_estimate=pl.CostEstimate(flops=flops, bytes_accessed=moved, transcendentals=0),
        name=name,
    )(ids, *[v for v, _ in inputs])


def arrange(ids, first, second, ordered):
    shards = ordered.shape[1]
    middle = first.shape[1]
    shard, low = ids[0], ids[1]
    bits_first, bits_second = bit_orders()
    for i in range(GROUP):
        j = low ^ i
        for d in range(shards):
            source = lax.rem(shard - d + shards, shards)
            if d < middle:
                ordered[i, source] = first[position(j, bits_first), d]
            else:
                ordered[i, source] = second[position(j, bits_second), d - middle]


def join(pieces):
    return jnp.concatenate([piece.astype(FULL) for piece in pieces], axis=1).astype(LOW)


def lane_mask(rows):
    return lax.broadcasted_iota(jnp.int32, (rows, PAIR), 1) < HEAD


def head_masks(values):
    lane = lax.broadcasted_iota(jnp.int32, values.shape, 1) % PAIR
    zero = jnp.zeros_like(values)
    return (
        jnp.where(lane < HEAD, values, zero).astype(LOW),
        jnp.where(lane < HEAD, zero, values).astype(LOW),
    )


def attention_forward(
    ids, tokens, mod, first, second,
    qkv, probs, attended, branch, wq, wo,
    ordered, query_a, query_b,
):
    shards = ordered.shape[1]
    rows = D // GROUP
    width = 3 * D // shards

    @pl.when(pl.program_id(0) == 0)
    def _():
        arrange(ids, first, second, ordered)
        for i in range(GROUP):
            pieces = [ordered[i, s].astype(FULL) for s in range(shards)]
            wq[i * rows : (i + 1) * rows, :] = join([p[:, :width] for p in pieces])
            wo[i * rows : (i + 1) * rows, :] = join([p[:, width:] for p in pieces])

    count = tokens.shape[0]
    normed, _ = normalize(tokens[...].astype(FULL))
    hidden = normed * (1.0 + mod[:, 1:2, :]) + mod[:, 0:1, :]
    hidden = hidden.reshape(count * LEN, D).astype(LOW)
    queries = dot(hidden, wq[:, :D])
    masked_a, masked_b = head_masks(queries)
    query_a[...] = masked_a
    query_b[...] = masked_b
    qkv[:, :, :D] = queries.astype(LOW).reshape(count, LEN, D)
    qkv[:, :, D:] = dot(hidden, wq[:, D:]).astype(LOW).reshape(count, LEN, 2 * D)
    mask = lane_mask(LEN)
    for latent in range(count):
        span = slice(latent * LEN, (latent + 1) * LEN)
        for pair in range(HEADS // 2):
            lanes = slice(pair * PAIR, (pair + 1) * PAIR)
            keys = qkv[latent, :, D + pair * PAIR : D + (pair + 1) * PAIR]
            values = qkv[latent, :, 2 * D + pair * PAIR : 2 * D + (pair + 1) * PAIR]
            results = []
            for member, masked in enumerate((query_a, query_b)):
                scores = dot_nt(masked[span, lanes], keys) * (HEAD ** (-0.5))
                top = jnp.max(scores, -1, keepdims=True)
                raised = jnp.exp(scores - top)
                share = (raised * (1.0 / jnp.sum(raised, -1, keepdims=True))).astype(LOW)
                probs[latent, 2 * pair + member] = share
                results.append(dot(share, values))
            attended[latent, :, lanes] = jnp.where(mask, results[0], results[1]).astype(LOW)
    branch[...] = dot(attended[...].reshape(count * LEN, D), wo[...]).reshape(count, LEN, D)


def perceptron(
    ids, tokens, branch, mod, cotangent, first, second, bias_up, bias_down,
    out, grad_mixed, grad_mod, keep, send, sum_up, sum_down,
    ordered, wu, wd, act, slope, total_up, total_down,
):
    shards = ordered.shape[1]
    rows = D // GROUP
    width = FF // shards
    step = pl.program_id(0)

    @pl.when(step == 0)
    def _():
        arrange(ids, first, second, ordered)
        for i in range(GROUP):
            pieces = [ordered[i, s] for s in range(shards)]
            span = slice(i * rows, (i + 1) * rows)
            wu[span, :] = jnp.concatenate([p[:, :width] for p in pieces], axis=1)
            wd[span, :] = jnp.concatenate([p[:, width:] for p in pieces], axis=1)
        total_up[...] = jnp.zeros_like(total_up)
        total_down[...] = jnp.zeros_like(total_down)
        sum_up[...] = jnp.zeros_like(sum_up)
        sum_down[...] = jnp.zeros_like(sum_down)

    count = tokens.shape[0]
    flat = count * LEN
    branch_out = branch[...]
    mixed = tokens[...].astype(FULL) + mod[:, 2:3, :] * branch_out
    normed, inverse_spread = normalize(mixed)
    hidden = (normed * (1.0 + mod[:, 4:5, :]) + mod[:, 3:4, :]).reshape(flat, D).astype(LOW)
    result = jnp.zeros((flat, D), FULL)
    for start in range(0, FF, CHUNK):
        span = slice(start, start + CHUNK)
        u = dot(hidden, wu[:, span]) + bias_up[:, span]
        square = u * u
        bent = jnp.tanh(GELU_SLOPE * u * (1.0 + GELU_CUBIC * square))
        half = 0.5 * (1.0 + bent)
        act_low = (u * half).astype(LOW)
        act[:, span] = act_low
        slope[:, span] = half + (0.5 * GELU_SLOPE) * u * (1.0 - bent * bent) * (
            1.0 + 3.0 * GELU_CUBIC * square
        )
        result = result + dot_nt(act_low, wd[:, span])
    result = (result + bias_down[...]).reshape(count, LEN, D)
    gate = mod[:, 5:6, :]
    out[...] = (mixed + gate * result).astype(LOW)
    upstream = cotangent[...].astype(FULL)
    grad_mod[:, 3:4, :] = jnp.sum(upstream * result, axis=1, keepdims=True)
    grad_result = (gate * upstream).reshape(flat, D).astype(LOW)
    sum_down[...] += jnp.sum(grad_result.astype(FULL), axis=0, keepdims=True)
    grad_hidden = jnp.zeros((flat, D), FULL)
    for start in range(0, FF, CHUNK):
        span = slice(start, start + CHUNK)
        grad_u = (dot(grad_result, wd[:, span]) * slope[:, span]).astype(LOW)
        sum_up[:, span] += jnp.sum(grad_u.astype(FULL), axis=0, keepdims=True)
        total_down[:, span] += dot_tn(grad_result, act[:, span])
        total_up[:, span] += dot_tn(hidden, grad_u)
        grad_hidden = grad_hidden + dot_nt(grad_u, wu[:, span])
    grad_hidden = grad_hidden.reshape(count, LEN, D)
    grad_mod[:, 1:2, :] = jnp.sum(grad_hidden, axis=1, keepdims=True)
    grad_mod[:, 2:3, :] = jnp.sum(grad_hidden * normed, axis=1, keepdims=True)
    back = upstream + normalize_back(
        grad_hidden * (1.0 + mod[:, 4:5, :]), normed, inverse_spread
    )
    grad_mixed[...] = back
    grad_mod[:, 0:1, :] = jnp.sum(back * branch_out, axis=1, keepdims=True)

    @pl.when(step == pl.num_programs(0) - 1)
    def _():
        shard, low = ids[0], ids[1]
        for j in range(GROUP):
            span = pl.ds(pl.multiple_of((low ^ j) * rows, rows), rows)
            for s in range(shards):
                d = lax.rem(s - shard + shards, shards)
                lanes = slice(s * width, (s + 1) * width)
                piece = jnp.concatenate([total_up[span, lanes], total_down[span, lanes]], axis=1)
                if j & 1:
                    send[j >> 2, (j >> 1) & 1, d] = piece.astype(LOW)
                else:
                    keep[j >> 2, (j >> 1) & 1, d] = piece


def attention_backward(
    ids, tokens, mod, qkv, probs, attended, grad_mixed, wq, wo,
    grad_tokens, grad_mod, keep, send,
    grad_qkv, total_attend, total_project,
):
    rows = D // GROUP
    shards = keep.shape[2]
    step = pl.program_id(0)

    @pl.when(step == 0)
    def _():
        total_attend[...] = jnp.zeros_like(total_attend)
        total_project[...] = jnp.zeros_like(total_project)

    count = tokens.shape[0]
    flat = count * LEN
    upstream = grad_mixed[...]
    grad_branch = (mod[:, 2:3, :] * upstream).reshape(flat, D).astype(LOW)
    total_project[...] += dot_tn(attended[...].reshape(flat, D), grad_branch)
    grad_attended = dot_nt(grad_branch, wo[...])
    masked = head_masks(grad_attended)
    grad_attended = grad_attended.astype(LOW)
    mask = lane_mask(LEN)
    scale = HEAD ** (-0.5)
    for latent in range(count):
        span = slice(latent * LEN, (latent + 1) * LEN)
        for pair in range(HEADS // 2):
            lanes = slice(pair * PAIR, (pair + 1) * PAIR)
            queries = qkv[latent, :, lanes]
            keys = qkv[latent, :, D + pair * PAIR : D + (pair + 1) * PAIR]
            values = qkv[latent, :, 2 * D + pair * PAIR : 2 * D + (pair + 1) * PAIR]
            upper = grad_attended[span, lanes]
            by_query, by_key, by_value = [], [], []
            for member in range(2):
                share = probs[latent, 2 * pair + member]
                weight = share.astype(FULL)
                grad_share = dot_nt(masked[member][span, lanes], values)
                product = weight * grad_share
                grad_scores = (
                    product - weight * jnp.sum(product, -1, keepdims=True)
                ).astype(LOW)
                by_query.append(dot(grad_scores, keys))
                by_key.append(dot_tn(grad_scores, queries))
                by_value.append(dot_tn(share, upper))
            for block, (members, factor) in enumerate(
                ((by_query, scale), (by_key, scale), (by_value, 1.0))
            ):
                merged = jnp.where(mask, members[0], members[1]) * factor
                grad_qkv[span, block * D + pair * PAIR : block * D + (pair + 1) * PAIR] = (
                    merged.astype(LOW)
                )
    normed, inverse_spread = normalize(tokens[...].astype(FULL))
    hidden = (normed * (1.0 + mod[:, 1:2, :]) + mod[:, 0:1, :]).reshape(flat, D).astype(LOW)
    grad_low = grad_qkv[...]
    total_attend[...] += dot_tn(hidden, grad_low)
    grad_hidden = dot_nt(grad_low, wq[...]).reshape(count, LEN, D)
    grad_mod[:, 0:1, :] = jnp.sum(grad_hidden, axis=1, keepdims=True)
    grad_mod[:, 1:2, :] = jnp.sum(grad_hidden * normed, axis=1, keepdims=True)
    grad_tokens[...] = upstream + normalize_back(
        grad_hidden * (1.0 + mod[:, 1:2, :]), normed, inverse_spread
    )

    @pl.when(step == pl.num_programs(0) - 1)
    def _():
        shard, low = ids[0], ids[1]
        wide, narrow = 3 * D // shards, D // shards
        for j in range(GROUP):
            span = pl.ds(pl.multiple_of((low ^ j) * rows, rows), rows)
            whole_attend, whole_project = total_attend[span, :], total_project[span, :]
            for s in range(shards):
                d = lax.rem(s - shard + shards, shards)
                piece = jnp.concatenate(
                    [
                        whole_attend[:, s * wide : (s + 1) * wide],
                        whole_project[:, s * narrow : (s + 1) * narrow],
                    ],
                    axis=1,
                )
                if j & 1:
                    send[j >> 2, (j >> 1) & 1, d] = piece.astype(LOW)
                else:
                    keep[j >> 2, (j >> 1) & 1, d] = piece


def slot_span(width, part):
    cut = max(width // 2 // 128, 1) * 128
    return (0, cut) if part == 0 else (cut, width)


def slot_spans(widths):
    counts = [sum(1 for m, _ in SLOTS if m == number) for number in range(len(widths))]
    return [
        slot_span(widths[m], part) if counts[m] > 1 else (0, widths[m]) for m, part in SLOTS
    ]


def momenta_kernel(ids, late, early, cond, *refs):
    moments, grads, momenta = refs[0:5], refs[5:10], refs[10:15]
    gram, columns, bias = refs[15:18]
    mixed = refs[18:23]
    low = ids[1]
    rows = D // GROUP
    widths = [m.shape[1] for m in moments]
    shards = gram.shape[0]
    bits = bit_orders()[0]
    blocks = -(-widths[4] // D)
    latents = cond.shape[0] // GROUP
    for i in range(GROUP):
        place = position(low ^ i, bits)
        span = slice(i * rows, (i + 1) * rows)
        piece = late[place, :rows, :].astype(FULL)
        grads[0][span, :] = piece[:, : widths[0]]
        grads[1][span, :] = piece[:, widths[0] : widths[0] + widths[1]]
        piece = early[place].astype(FULL)
        grads[2][span, :] = piece[:, : widths[2]]
        grads[3][span, :] = piece[:, widths[2] :]
    for block in range(blocks):
        start = rows + block * latents
        rising = jnp.concatenate([late[g, start : start + latents, :] for g in range(GROUP)], axis=0)
        filled = min(D, widths[4] - block * D)
        grads[4][:, block * D : block * D + filled] = dot_tn(cond[...], rising)[:, :filled]
    total = jnp.zeros((16, D), FULL)
    for i in range(GROUP):
        total = total + late[position(low ^ i, bits), rows + blocks * latents :, :].astype(FULL)
    bias[...] = total[:8] + total[8:]
    for number in range(5):
        grad = grads[number][...]
        moment = MOMENTUM * moments[number][...] + grad
        momenta[number][...] = moment
        mixed[number][...] = grad + MOMENTUM * moment
    for number in range(5):
        owners = [k for k, (m, _) in enumerate(SLOTS) if m == number]
        condition = low == owners[0]
        for owner in owners[1:]:
            condition = condition | (low == owner)

        @pl.when(condition)
        def _(number=number):
            parts = split_low(mixed[number][...])
            partial_gram = dot_split(parts, parts, dot_nt)
            for s in range(shards):
                d = lax.rem(s - ids[0] + shards, shards)
                gram[d] = partial_gram[s * (D // shards) : (s + 1) * (D // shards), :]

    spans = slot_spans(widths)
    for k, ((number, _), (start, stop)) in enumerate(zip(SLOTS, spans)):

        @pl.when(low == k)
        def _(number=number, start=start, stop=stop):
            filled = stop - start
            columns[:, :filled] = mixed[number][:, start:stop]
            if filled < columns.shape[1]:
                columns[:, filled:] = jnp.zeros((D, columns.shape[1] - filled), FULL)


def polynomial_kernel(ids, *refs):
    shards = len(refs) - 4
    pieces, columns, first, second, gram_ref = refs[:shards], *refs[shards:]
    size = D // shards
    for d in range(shards):
        source = lax.rem(ids[0] - d + shards, shards)
        gram_ref[pl.ds(pl.multiple_of(source * size, size), size), :] = pieces[d][...]
    gram = gram_ref[...]
    diagonal = lax.broadcasted_iota(jnp.int32, (D, D), 0) == lax.broadcasted_iota(
        jnp.int32, (D, D), 1
    )
    trace = jnp.sum(jnp.where(diagonal, gram, 0.0))
    scale = 1.0 / (jnp.sqrt(jnp.full((1, 1), trace)) + 1e-07)
    gram = (gram * scale) * scale
    product = None
    for step in range(NS_ITERS):
        parts = split_low(gram)
        mixing = POLY_CUBIC * gram + POLY_QUINTIC * dot_split(parts, parts)
        mixing_parts = split_low(mixing)
        if step + 1 < NS_ITERS:
            half = POLY_LINEAR * gram + dot_split(mixing_parts, parts)
            gram = POLY_LINEAR * half + dot_split(mixing_parts, split_low(half))
        if product is None:
            product = jnp.where(diagonal, POLY_LINEAR, 0.0) + mixing
        else:
            product = POLY_LINEAR * product + dot_split(mixing_parts, split_low(product))
    answer = dot_split(split_low(product), split_low(columns[...] * scale)).astype(LOW)
    first[...] = answer[: D // 2, :]
    second[...] = answer[D // 2 :, :]


def update_kernel(ids, first, second, *refs):
    masters, updated = refs[:5], refs[5:]
    low = ids[1]
    widths = [m.shape[1] for m in masters]
    spans = slot_spans(widths)
    for half, (gathered, bits) in enumerate(zip((first, second), bit_orders())):
        rows = slice(half * (D // 2), (half + 1) * (D // 2))
        for k, ((number, _), (start, stop)) in enumerate(zip(SLOTS, spans)):
            direction = gathered[position(low ^ k, bits)][:, : stop - start].astype(FULL)
            full_columns = COLUMNS[number]
            updated[number][rows, start:stop] = (
                masters[number][rows, start:stop] * (1.0 - MUON_RATE * WEIGHT_DECAY)
                - (MUON_RATE * 0.2 * math.sqrt(full_columns)) * direction
            )


COLUMNS = (3 * D, D, FF, FF, 6 * D)


def whole_rows(vector):
    rows = -(-vector.shape[-1] // D)
    padded = jnp.pad(vector, [(0, 0)] * (vector.ndim - 1) + [(0, rows * D - vector.shape[-1])])
    return padded.reshape(vector.shape[:-1] + (rows, D))


def per_device(
    tokens,
    condition,
    cotangent,
    attend_weight,
    project_weight,
    expand_weight,
    contract_weight,
    modulate_weight,
    biases,
    attend_moment,
    project_moment,
    expand_moment,
    contract_moment,
    modulate_moment,
    bias_first,
    bias_second,
):
    latents = tokens.shape[0]
    steps = latents // BLOCK
    shards = lax.axis_size("shard")
    shard = lax.axis_index("shard")
    low = lax.axis_index("rep") % GROUP
    middle = (shards + 1) // 2
    ids = jnp.stack([shard, low]).astype(jnp.int32)
    rows = D // GROUP
    bias_share = biases.shape[0]
    mod_share = modulate_weight.shape[1]

    silu_value, silu_back = jax.vjp(jax.nn.silu, condition.astype(FULL))
    bias_rows = whole_rows(biases.astype(LOW))
    note = jnp.concatenate([silu_value.astype(LOW), bias_rows], axis=0)
    notes = jnp.stack([note] + [shift(note, d) for d in range(1, shards)])
    late_first, late_second = gather_weights([attend_weight, project_weight], low)
    cond_rows = notes[:, :latents].reshape(shards * latents, D)
    modulate_low = modulate_weight.astype(LOW)
    share = jnp.dot(cond_rows, modulate_low, preferred_element_type=FULL)
    share = share.reshape(shards, latents, mod_share)
    answers = [share[0]] + [shift(share[d], shards - d) for d in range(1, shards)]
    answers = rotate(jnp.stack(answers), (shards - shard) % shards)
    bias_all = rotate(notes[:, latents:].reshape(shards, -1)[::-1], (shards - 1 - shard) % shards)
    bias_all = bias_all[:, :bias_share].reshape(-1).astype(FULL)
    mod = answers.transpose(1, 0, 2).reshape(latents, 6 * D) + bias_all[: 6 * D]
    mod = mod.reshape(latents, 6, D)
    bias_up = bias_all[6 * D : 6 * D + FF].reshape(1, FF)
    bias_down = bias_all[6 * D + FF :].reshape(1, D)
    early_first, early_second = gather_weights([expand_weight, contract_weight], low)

    tokens_shape = (latents, LEN, D)
    qkv, probs, attended, branch, wq, wo = local_call(
        attention_forward,
        ids,
        [(tokens, True), (mod, True), (late_first, False), (late_second, False)],
        [
            ((latents, LEN, 3 * D), LOW, True),
            ((latents, HEADS, LEN, LEN), LOW, True),
            (tokens_shape, LOW, True),
            (tokens_shape, FULL, True),
            ((D, 3 * D), LOW, False),
            ((D, D), LOW, False),
        ],
        [
            pltpu.VMEM((GROUP, shards, rows, 4 * D // shards), LOW),
            pltpu.VMEM((BLOCK * LEN, D), LOW),
            pltpu.VMEM((BLOCK * LEN, D), LOW),
        ],
        steps,
        latents * (2 * LEN * D * 4 * D + 4 * HEADS * LEN * LEN * PAIR) * 2,
        "attention_forward",
    )
    early_shape = (2, 2, shards, rows, 2 * FF // shards)
    block_output, grad_mixed, grad_mod_late, keep, send, sum_up, sum_down = local_call(
        perceptron,
        ids,
        [
            (tokens, True),
            (branch, True),
            (mod, True),
            (cotangent, True),
            (early_first, False),
            (early_second, False),
            (bias_up, False),
            (bias_down, False),
        ],
        [
            (tokens_shape, LOW, True),
            (tokens_shape, FULL, True),
            ((latents, 4, D), FULL, True),
            (early_shape, FULL, False),
            (early_shape, LOW, False),
            ((1, FF), FULL, False),
            ((1, D), FULL, False),
        ],
        [
            pltpu.VMEM((GROUP, shards, rows, 2 * FF // shards), LOW),
            pltpu.VMEM((D, FF), LOW),
            pltpu.VMEM((D, FF), LOW),
            pltpu.VMEM((BLOCK * LEN, FF), LOW),
            pltpu.VMEM((BLOCK * LEN, FF), FULL),
            pltpu.VMEM((D, FF), FULL),
            pltpu.VMEM((D, FF), FULL),
        ],
        steps,
        latents * 2 * LEN * D * FF * 6 * 2,
        "perceptron",
    )
    early = reduce_pieces(keep, send)
    late_shape = (2, 2, shards, rows, 4 * D // shards)
    tokens_grad, grad_mod_first, keep, send = local_call(
        attention_backward,
        ids,
        [
            (tokens, True),
            (mod, True),
            (qkv, True),
            (probs, True),
            (attended, True),
            (grad_mixed, True),
            (wq, False),
            (wo, False),
        ],
        [
            (tokens_shape, FULL, True),
            ((latents, 2, D), FULL, True),
            (late_shape, FULL, False),
            (late_shape, LOW, False),
        ],
        [
            pltpu.VMEM((BLOCK * LEN, 3 * D), LOW),
            pltpu.VMEM((D, 3 * D), FULL),
            pltpu.VMEM((D, D), FULL),
        ],
        steps,
        latents * (2 * LEN * D * 8 * D + 10 * HEADS * LEN * LEN * PAIR) * 2,
        "attention_backward",
    )
    late = reduce_pieces(keep, send)

    grad_modulation = jnp.concatenate([grad_mod_first, grad_mod_late], axis=1)
    grad_modulation = grad_modulation.astype(LOW).astype(FULL).reshape(latents, 6 * D)
    grad_bias = jnp.concatenate(
        [jnp.sum(grad_modulation, axis=0), sum_up.reshape(-1), sum_down.reshape(-1)]
    )
    outgoing = jnp.concatenate(
        [
            grad_modulation.reshape(latents, shards, mod_share)
            .transpose(1, 0, 2)
            .reshape(shards, latents * mod_share),
            grad_bias.reshape(shards, bias_share),
        ],
        axis=1,
    )
    outgoing = rotate(outgoing, shard)
    incoming = jnp.stack([outgoing[0]] + [shift(outgoing[d], d) for d in range(1, shards)])
    grad_rows = incoming[:, : latents * mod_share].reshape(shards * latents, mod_share).astype(LOW)
    bias_sum = jnp.sum(incoming[:, latents * mod_share :], axis=0)
    bias_high = bias_sum.astype(LOW)
    bias_rest = (bias_sum - bias_high.astype(FULL)).astype(LOW)
    blocks = -(-mod_share // D)
    grad_blocks = jnp.pad(grad_rows, ((0, 0), (0, blocks * D - mod_share)))
    payload = jnp.concatenate(
        [jnp.pad(late, ((0, 0), (0, D - late.shape[1])))]
        + [grad_blocks[:, b * D : (b + 1) * D] for b in range(blocks)]
        + [
            jnp.pad(whole_rows(part), ((0, 8 - -(-bias_share // D)), (0, 0)))
            for part in (bias_high, bias_rest)
        ],
        axis=0,
    )
    bits = bit_orders()[0]
    cond_all = gather_rep(cond_rows, bits).reshape(GROUP * shards * latents, D)
    early_all = gather_rep(early, bits)
    late_all = gather_rep(payload, bits)

    masters = [attend_weight, project_weight, expand_weight, contract_weight, modulate_weight]
    moments = [attend_moment, project_moment, expand_moment, contract_moment, modulate_moment]
    widths = [m.shape[1] for m in masters]
    slot_width = max(stop - start for start, stop in slot_spans(widths))
    results = local_call(
        momenta_kernel,
        ids,
        [(late_all, False), (early_all, False), (cond_all, False)] + [(m, False) for m in moments],
        [((D, w), FULL, False) for w in widths] * 2
        + [
            ((shards, D // shards, D), FULL, False),
            ((D, slot_width), FULL, False),
            ((8, D), FULL, False),
        ],
        [pltpu.VMEM((D, w), FULL) for w in widths],
        1,
        6 * D * D * D,
        "momenta",
    )
    gradients, momenta = results[0:5], results[5:10]
    gram, columns, bias_block = results[10:13]
    piece = gram[0]
    for d in range(1, shards):
        piece = piece + shift(gram[d], d)
    pieces = [piece] + [shift(piece, d) for d in range(1, shards)]
    answer_first, answer_second = local_call(
        polynomial_kernel,
        ids,
        [(p, False) for p in pieces] + [(columns, False)],
        [((D // 2, slot_width), LOW, False)] * 2,
        [pltpu.VMEM((D, D), FULL)],
        1,
        2 * 3 * 18 * D * D * D,
        "polynomial",
    )
    orders = bit_orders()
    updated = local_call(
        update_kernel,
        ids,
        [(gather_rep(answer_first, orders[0]), False), (gather_rep(answer_second, orders[1]), False)]
        + [(m, False) for m in masters],
        [((D, w), FULL, False) for w in widths],
        [],
        1,
        2 * D * sum(widths),
        "update",
    )

    grad_cond_share = lax.dot_general(
        grad_rows, modulate_low, (((1,), (1,)), ((), ())), preferred_element_type=FULL
    ).reshape(shards, latents, D)
    grad_cond_low = grad_cond_share[0]
    for d in range(1, shards):
        grad_cond_low = grad_cond_low + shift(grad_cond_share[d], shards - d)
    condition_grad = silu_back(grad_cond_low)[0]

    bias_gradient = bias_block.reshape(-1)[:bias_share]
    bias_momentum = BETA_ONE * bias_first + (1.0 - BETA_ONE) * bias_gradient
    bias_variance = BETA_TWO * bias_second + (1.0 - BETA_TWO) * bias_gradient * bias_gradient
    corrected_first = bias_momentum / (1.0 - BETA_ONE**STEP)
    corrected_second = bias_variance / (1.0 - BETA_TWO**STEP)
    bias_updated = biases * (1.0 - ADAM_RATE * WEIGHT_DECAY) - ADAM_RATE * corrected_first / (
        jnp.sqrt(corrected_second) + ADAM_EPSILON
    )
    return (
        block_output,
        tokens_grad,
        condition_grad,
        *gradients,
        *momenta,
        *updated,
        bias_gradient,
        bias_momentum,
        bias_variance,
        bias_updated,
    )


def solution(mesh):
    rows = P(("shard", "rep"), None, None)
    vectors = P(("shard", "rep"), None)
    columns = P(None, "shard")
    flat = P("shard")
    return jax.shard_map(
        per_device,
        mesh=mesh,
        in_specs=(rows, vectors, rows) + (columns,) * 5 + (flat,) + (columns,) * 5 + (flat,) * 2,
        out_specs=(rows, rows, vectors) + (columns,) * 15 + (flat,) * 4,
        check_vma=False,
    )
```

```python
from functools import partial
import math

import jax
import jax.numpy as jnp
from jax import lax
from jax.experimental import pallas as pl
from jax.experimental.pallas import tpu as pltpu
from jax.sharding import PartitionSpec as P

D = 384
HEADS = 6
HEAD = 64
FF = 1536
LEN = 256
NS_ITERS = 5
STEP = 10
PAIR = 2 * HEAD
CHUNK = 512
GROUP = 8
BLOCK = 2

POLY_LINEAR = 3.4445
POLY_CUBIC = -4.775
POLY_QUINTIC = 2.0315
MOMENTUM = 0.95
MUON_RATE = 0.4
WEIGHT_DECAY = 0.01
ADAM_RATE = 0.1
BETA_ONE = 0.9
BETA_TWO = 0.999
ADAM_EPSILON = 1e-08
GELU_SLOPE = math.sqrt(2.0 / math.pi)
GELU_CUBIC = 0.044715

LOW = jnp.bfloat16
FULL = jnp.float32

SLOTS = ((4, 0), (4, 1), (0, 0), (2, 0), (2, 1), (3, 0), (3, 1), (1, 0))


def shift(value, distance):
    size = lax.axis_size("shard")
    return lax.ppermute(value, "shard", [(i, (i + distance) % size) for i in range(size)])


def flip(value, mask):
    size = lax.axis_size("rep")
    return lax.ppermute(value, "rep", [(i, i ^ mask) for i in range(size)])


def rotate(value, start):
    doubled = jnp.concatenate([value, value], axis=0)
    return lax.dynamic_slice_in_dim(doubled, start, value.shape[0], 0)


def exchange(pieces):
    return [pieces[0]] + [shift(pieces[d], d) for d in range(1, len(pieces))]


def gather_group(value):
    stacked = jnp.stack([value] + [flip(value, 2 * t) for t in range(1, GROUP // 2)])
    return stacked, flip(stacked, 1)


def sum_cores(keep, send):
    return keep + flip(send, 1).astype(FULL)


def sum_chips(total):
    mine = total[0]
    for t in range(1, GROUP // 2):
        mine = mine + flip(total[t].astype(LOW), 2 * t).astype(FULL)
    return mine


def sum_rest(value):
    for bit in range(3, lax.axis_size("rep").bit_length() - 1):
        value = (value.astype(FULL) + flip(value, 1 << bit).astype(FULL)).astype(LOW)
    return value


def dot(left, right):
    return lax.dot_general(left, right, (((1,), (0,)), ((), ())), preferred_element_type=FULL)


def dot_nt(left, right):
    return lax.dot_general(left, right, (((1,), (1,)), ((), ())), preferred_element_type=FULL)


def dot_tn(left, right):
    return lax.dot_general(left, right, (((0,), (0,)), ((), ())), preferred_element_type=FULL)


def split_low(value):
    high = value.astype(LOW)
    return high, (value - high.astype(FULL)).astype(LOW)


def dot_split(left, right, product=dot):
    return product(left[0], right[0]) + (product(left[0], right[1]) + product(left[1], right[0]))


def normalize(values):
    centered = values - jnp.mean(values, -1, keepdims=True)
    inverse_spread = lax.rsqrt(jnp.mean(centered * centered, -1, keepdims=True) + 1e-06)
    return centered * inverse_spread, inverse_spread


def normalize_back(upstream, normed, inverse_spread):
    return inverse_spread * (
        upstream
        - jnp.mean(upstream, -1, keepdims=True)
        - normed * jnp.mean(upstream * normed, -1, keepdims=True)
    )


def local_call(kernel, ids, inputs, outputs, scratch, steps, flops, name, after=()):
    def run(*refs):
        kernel(*refs[: 1 + len(inputs)], *refs[1 + len(inputs) + len(after) :])

    def spec(shape, blocked):
        zeros = (0,) * (len(shape) - 1)
        if blocked:
            block = (shape[0] // steps,) + tuple(shape[1:])
            return pl.BlockSpec(block, lambda i, _: (i,) + zeros)
        return pl.BlockSpec(tuple(shape), lambda i, _: (0,) + zeros)

    moved = sum(v.size * v.dtype.itemsize for v, _ in inputs)
    moved += sum(math.prod(shape) * jnp.dtype(kind).itemsize for shape, kind, _ in outputs)
    return pl.pallas_call(
        run,
        grid_spec=pltpu.PrefetchScalarGridSpec(
            num_scalar_prefetch=1,
            grid=(steps,),
            in_specs=[spec(v.shape, blocked) for v, blocked in inputs]
            + [pl.BlockSpec(memory_space=pl.ANY) for _ in after],
            out_specs=[spec(shape, blocked) for shape, _, blocked in outputs],
            scratch_shapes=scratch,
        ),
        out_shape=[jax.ShapeDtypeStruct(shape, kind) for shape, kind, _ in outputs],
        compiler_params=pltpu.CompilerParams(
            dimension_semantics=("arbitrary",), vmem_limit_bytes=48 * 1024 * 1024
        ),
        cost_estimate=pl.CostEstimate(flops=flops, bytes_accessed=moved, transcendentals=0),
        name=name,
    )(ids, *[v for v, _ in inputs], *after)


def pieces_of(ids, stacked, flipped):
    for t in range(GROUP // 2):
        for bit, blocks in enumerate((stacked, flipped)):
            yield ids[1] ^ (2 * t + bit), blocks.at[t]


def rows_at(place, rows):
    return pl.ds(pl.multiple_of(place * rows, rows), rows)


def turn(value):
    filled = value.shape[1]
    extra = -filled % 128
    if extra:
        value = jnp.concatenate([value, jnp.zeros((value.shape[0], extra), value.dtype)], axis=1)
    return value.T[:filled]


def head_masks(values):
    lane = lax.broadcasted_iota(jnp.int32, values.shape, 1) % PAIR
    zero = jnp.zeros_like(values)
    return (
        jnp.where(lane < HEAD, values, zero).astype(LOW),
        jnp.where(lane < HEAD, zero, values).astype(LOW),
    )


def attention_forward(
    ids, tokens, mod, stacked, flipped,
    qkv, probs, attended, branch, wq, wo,
    ordered, query_a, query_b,
):
    shards = ordered.shape[0]
    rows = ordered.shape[1] // GROUP
    wide, narrow = 3 * D // shards, D // shards

    @pl.when(pl.program_id(0) == 0)
    def _():
        for place, block in pieces_of(ids, stacked, flipped):
            for d in range(shards):
                source = lax.rem(ids[0] - d + shards, shards)
                ordered[source, rows_at(place, rows), :] = block[d].astype(FULL)
        for s in range(shards):
            wq[s * wide : (s + 1) * wide, :] = ordered[s, :wide, :].astype(LOW)
            wo[s * narrow : (s + 1) * narrow, :] = ordered[s, wide:, :].astype(LOW)

    count = tokens.shape[0]
    normed, _ = normalize(tokens[...].astype(FULL))
    hidden = normed * (1.0 + mod[:, 1:2, :]) + mod[:, 0:1, :]
    hidden = hidden.reshape(count * LEN, D).astype(LOW)
    queries = dot_nt(hidden, wq[:D, :])
    masked_a, masked_b = head_masks(queries)
    query_a[...] = masked_a
    query_b[...] = masked_b
    qkv[:, :, :D] = queries.astype(LOW).reshape(count, LEN, D)
    qkv[:, :, D:] = dot_nt(hidden, wq[D:, :]).astype(LOW).reshape(count, LEN, 2 * D)
    for latent in range(count):
        span = slice(latent * LEN, (latent + 1) * LEN)
        for pair in range(HEADS // 2):
            lanes = slice(pair * PAIR, (pair + 1) * PAIR)
            keys = qkv[latent, :, D + pair * PAIR : D + (pair + 1) * PAIR]
            values = qkv[latent, :, 2 * D + pair * PAIR : 2 * D + (pair + 1) * PAIR].T
            results = []
            for member, masked in enumerate((query_a, query_b)):
                scores = dot_nt(keys, masked[span, lanes]) * (HEAD ** (-0.5))
                top = jnp.max(scores, 0, keepdims=True)
                raised = jnp.exp(scores - top)
                share = (raised * (1.0 / jnp.sum(raised, 0, keepdims=True))).astype(LOW)
                probs[latent, 2 * pair + member] = share
                results.append(dot(values[member * HEAD : (member + 1) * HEAD], share))
            attended[latent, :, lanes] = jnp.concatenate(results, axis=0).T.astype(LOW)
    branch[...] = dot_nt(attended[...].reshape(count * LEN, D), wo[...]).reshape(count, LEN, D)


def perceptron(
    ids, tokens, branch, mod, cotangent, weights, bias_up, bias_down,
    out, grad_mixed, grad_mod, keep, send, sum_up, sum_down,
    wu, wd, act, slope, total_up, total_down,
):
    shards = weights.shape[0]
    rows = D // GROUP
    width = FF // shards
    step = pl.program_id(0)

    @pl.when(step == 0)
    def _():
        for i in range(GROUP):
            span = slice(i * rows, (i + 1) * rows)
            pieces = [weights[s, span, :] for s in range(shards)]
            wu[span, :] = jnp.concatenate([p[:, :width] for p in pieces], axis=1)
            wd[span, :] = jnp.concatenate([p[:, width:] for p in pieces], axis=1)
        total_up[...] = jnp.zeros_like(total_up)
        total_down[...] = jnp.zeros_like(total_down)
        sum_up[...] = jnp.zeros_like(sum_up)
        sum_down[...] = jnp.zeros_like(sum_down)

    count = tokens.shape[0]
    flat = count * LEN
    branch_out = branch[...]
    mixed = tokens[...].astype(FULL) + mod[:, 2:3, :] * branch_out
    normed, inverse_spread = normalize(mixed)
    hidden = (normed * (1.0 + mod[:, 4:5, :]) + mod[:, 3:4, :]).reshape(flat, D).astype(LOW)
    result = jnp.zeros((flat, D), FULL)
    for start in range(0, FF, CHUNK):
        span = slice(start, start + CHUNK)
        u = dot(hidden, wu[:, span]) + bias_up[:, span]
        square = u * u
        bent = jnp.tanh(GELU_SLOPE * u * (1.0 + GELU_CUBIC * square))
        half = 0.5 * (1.0 + bent)
        act_low = (u * half).astype(LOW)
        act[:, span] = act_low
        slope[:, span] = half + (0.5 * GELU_SLOPE) * u * (1.0 - bent * bent) * (
            1.0 + 3.0 * GELU_CUBIC * square
        )
        result = result + dot_nt(act_low, wd[:, span])
    result = (result + bias_down[...]).reshape(count, LEN, D)
    gate = mod[:, 5:6, :]
    out[...] = (mixed + gate * result).astype(LOW)
    upstream = cotangent[...].astype(FULL)
    grad_mod[:, 3:4, :] = jnp.sum(upstream * result, axis=1, keepdims=True)
    grad_result = (gate * upstream).reshape(flat, D).astype(LOW)
    sum_down[...] += jnp.sum(grad_result.astype(FULL), axis=0, keepdims=True)
    grad_hidden = jnp.zeros((flat, D), FULL)
    for start in range(0, FF, CHUNK):
        span = slice(start, start + CHUNK)
        grad_u = (dot(grad_result, wd[:, span]) * slope[:, span]).astype(LOW)
        sum_up[:, span] += jnp.sum(grad_u.astype(FULL), axis=0, keepdims=True)
        total_down[:, span] += dot_tn(grad_result, act[:, span])
        total_up[:, span] += dot_tn(hidden, grad_u)
        grad_hidden = grad_hidden + dot_nt(grad_u, wu[:, span])
    grad_hidden = grad_hidden.reshape(count, LEN, D)
    grad_mod[:, 1:2, :] = jnp.sum(grad_hidden, axis=1, keepdims=True)
    grad_mod[:, 2:3, :] = jnp.sum(grad_hidden * normed, axis=1, keepdims=True)
    back = upstream + normalize_back(
        grad_hidden * (1.0 + mod[:, 4:5, :]), normed, inverse_spread
    )
    grad_mixed[...] = back
    grad_mod[:, 0:1, :] = jnp.sum(back * branch_out, axis=1, keepdims=True)

    @pl.when(step == pl.num_programs(0) - 1)
    def _():
        shard, low = ids[0], ids[1]
        for j in range(GROUP):
            span = pl.ds(pl.multiple_of((low ^ j) * rows, rows), rows)
            for s in range(shards):
                d = lax.rem(s - shard + shards, shards)
                lanes = slice(s * width, (s + 1) * width)
                piece = jnp.concatenate([total_up[span, lanes], total_down[span, lanes]], axis=1)
                if j & 1:
                    send[j // 2, d] = piece.astype(LOW)
                else:
                    keep[j // 2, d] = piece


def project_backward(
    ids, mod, attended, grad_mixed, wo,
    grad_attended, total_project,
):
    @pl.when(pl.program_id(0) == 0)
    def _():
        total_project[...] = jnp.zeros_like(total_project)

    count = attended.shape[0]
    flat = count * LEN
    grad_branch = (mod[:, 2:3, :] * grad_mixed[...]).reshape(flat, D).astype(LOW)
    total_project[...] += dot_tn(attended[...].reshape(flat, D), grad_branch)
    grad_attended[...] = dot(grad_branch, wo[...]).astype(LOW).reshape(count, LEN, D)


def attention_backward(ids, qkv, probs, grad_attended, grad_qkv):
    mask = lax.broadcasted_iota(jnp.int32, (LEN, PAIR), 1) < HEAD
    scale = HEAD ** (-0.5)
    for latent in range(qkv.shape[0]):
        for pair in range(HEADS // 2):
            lanes = slice(pair * PAIR, (pair + 1) * PAIR)
            key_lanes = slice(D + pair * PAIR, D + (pair + 1) * PAIR)
            value_lanes = slice(2 * D + pair * PAIR, 2 * D + (pair + 1) * PAIR)
            queries = qkv[latent, :, lanes]
            keys = qkv[latent, :, key_lanes].T
            values = qkv[latent, :, value_lanes]
            upper = grad_attended[latent, :, lanes]
            masked = head_masks(upper.astype(FULL))
            by_query, by_key, by_value = [], [], []
            for member in range(2):
                share = probs[latent, 2 * pair + member]
                weight = share.astype(FULL)
                grad_share = dot_nt(values, masked[member])
                product = weight * grad_share
                grad_scores = (
                    product - weight * jnp.sum(product, 0, keepdims=True)
                ).astype(LOW)
                by_query.append(dot(keys[member * HEAD : (member + 1) * HEAD], grad_scores))
                by_key.append(dot(grad_scores, queries))
                by_value.append(dot(share, upper))
            merged = jnp.concatenate(by_query, axis=0).T * scale
            grad_qkv[latent, :, lanes] = merged.astype(LOW)
            merged = jnp.where(mask, by_key[0], by_key[1]) * scale
            grad_qkv[latent, :, key_lanes] = merged.astype(LOW)
            merged = jnp.where(mask, by_value[0], by_value[1])
            grad_qkv[latent, :, value_lanes] = merged.astype(LOW)


def attend_backward(
    ids, tokens, mod, grad_mixed, grad_qkv, wq, total_project,
    grad_tokens, grad_mod, keep, send,
    total_attend,
):
    rows = D // GROUP
    shards = keep.shape[1]
    step = pl.program_id(0)

    @pl.when(step == 0)
    def _():
        total_attend[...] = jnp.zeros_like(total_attend)

    count = tokens.shape[0]
    flat = count * LEN
    normed, inverse_spread = normalize(tokens[...].astype(FULL))
    hidden = (normed * (1.0 + mod[:, 1:2, :]) + mod[:, 0:1, :]).reshape(flat, D).astype(LOW)
    grad_low = grad_qkv[...].reshape(flat, 3 * D)
    total_attend[...] += dot_tn(hidden, grad_low)
    grad_hidden = dot(grad_low, wq[...]).reshape(count, LEN, D)
    grad_mod[:, 0:1, :] = jnp.sum(grad_hidden, axis=1, keepdims=True)
    grad_mod[:, 1:2, :] = jnp.sum(grad_hidden * normed, axis=1, keepdims=True)
    grad_tokens[...] = grad_mixed[...] + normalize_back(
        grad_hidden * (1.0 + mod[:, 1:2, :]), normed, inverse_spread
    )

    @pl.when(step == pl.num_programs(0) - 1)
    def _():
        shard, low = ids[0], ids[1]
        wide, narrow = 3 * D // shards, D // shards
        for j in range(GROUP):
            span = rows_at(low ^ j, rows)
            whole_attend, whole_project = total_attend[span, :], total_project[span, :]
            for s in range(shards):
                d = lax.rem(s - shard + shards, shards)
                piece = jnp.concatenate(
                    [
                        whole_attend[:, s * wide : (s + 1) * wide],
                        whole_project[:, s * narrow : (s + 1) * narrow],
                    ],
                    axis=1,
                )
                if j & 1:
                    send[j // 2, d] = piece.astype(LOW)
                else:
                    keep[j // 2, d] = piece


COLUMNS = (3 * D, D, FF, FF, 6 * D)
TURNED = (True, True, False, False, True)
TRIANGLE = ((0, 0), (0, 1), (0, 2), (1, 1), (1, 2), (2, 2))


def slot_spans(widths):
    counts = [sum(1 for m, _ in SLOTS if m == number) for number in range(len(widths))]
    return [
        (part * (widths[m] // counts[m]), (part + 1) * (widths[m] // counts[m]))
        for m, part in SLOTS
    ]


def momenta_kernel(ids, late, late_flipped, early, early_flipped, *refs):
    moments, grads, momenta = refs[0:5], refs[5:10], refs[10:15]
    gram, columns, bias = refs[15:18]
    mixed = refs[18:23]
    late_whole, flat_gram = refs[23:25]
    low = ids[1]
    rows = D // GROUP
    shards = gram.shape[0]
    widths = [whole // shards for whole in COLUMNS]
    blocks = -(-widths[4] // D)
    latents = late.shape[1] - rows - 16
    latents = latents // (blocks + 1)
    late_width = widths[0] + widths[1]
    for place, block in pieces_of(ids, late, late_flipped):
        late_whole[rows_at(place, rows), :] = block[:rows, :].astype(FULL)
    for place, block in pieces_of(ids, early, early_flipped):
        piece = block[...].astype(FULL)
        grads[2][rows_at(place, rows), :] = piece[:, : widths[2]]
        grads[3][rows_at(place, rows), :] = piece[:, widths[2] :]
    turned = turn(late_whole[...])
    grads[0][...] = turned[: widths[0]]
    grads[1][...] = turned[widths[0] : late_width]
    parts = [ref.at[t] for ref in (late, late_flipped) for t in range(GROUP // 2)]
    start = rows + blocks * latents + 16
    cond = jnp.concatenate([part[start : start + latents, :] for part in parts], axis=0)
    for block in range(blocks):
        start = rows + block * latents
        rising = jnp.concatenate([part[start : start + latents, :] for part in parts], axis=0)
        filled = min(D, widths[4] - block * D)
        grads[4][block * D : block * D + filled, :] = dot_tn(rising, cond)[:filled]
    start = rows + blocks * latents
    total = jnp.zeros((16, D), FULL)
    for part in parts:
        total = total + part[start : start + 16, :].astype(FULL)
    bias[...] = total[:8] + total[8:]
    for number in range(5):
        grad = grads[number][...]
        moment = MOMENTUM * moments[number][...] + grad
        momenta[number][...] = moment
        mixed[number][...] = grad + MOMENTUM * moment
    for number in range(5):
        owners = [k for k, (m, _) in enumerate(SLOTS) if m == number]
        condition = low == owners[0]
        for owner in owners[1:]:
            condition = condition | (low == owner)

        @pl.when(condition)
        def _(number=number):
            parts = split_low(mixed[number][...])
            whole = dot_split(parts, parts, dot_tn if TURNED[number] else dot_nt)
            for place, (a, b) in enumerate(TRIANGLE):
                flat_gram[place * 128 : (place + 1) * 128, :] = whole[
                    a * 128 : (a + 1) * 128, b * 128 : (b + 1) * 128
                ]

    size = gram.shape[1]
    for s in range(shards):
        gram[lax.rem(s - ids[0] + shards, shards)] = flat_gram[s * size : (s + 1) * size, :]
    spans = slot_spans(widths)
    for k, ((number, _), (start, stop)) in enumerate(zip(SLOTS, spans)):

        @pl.when(low == k)
        def _(number=number, start=start, stop=stop):
            filled = stop - start
            if TURNED[number]:
                columns[:filled, :] = mixed[number][start:stop, :]
            else:
                columns[:filled, :] = turn(mixed[number][...])[start:stop]
            if filled < columns.shape[0]:
                columns[filled:, :] = jnp.zeros((columns.shape[0] - filled, D), FULL)


def polynomial_kernel(ids, *refs):
    shards = len(refs) - 4
    pieces, columns, answer, flat_gram, gram_ref = refs[:shards], *refs[shards:]
    size = pieces[0].shape[0]
    for d in range(shards):
        source = lax.rem(ids[0] - d + shards, shards)
        flat_gram[rows_at(source, size), :] = pieces[d][...]
    for place, (a, b) in enumerate(TRIANGLE):
        block = flat_gram[place * 128 : (place + 1) * 128, :]
        gram_ref[a * 128 : (a + 1) * 128, b * 128 : (b + 1) * 128] = block
        if a != b:
            gram_ref[b * 128 : (b + 1) * 128, a * 128 : (a + 1) * 128] = block.T
    gram = gram_ref[...]
    diagonal = lax.broadcasted_iota(jnp.int32, (D, D), 0) == lax.broadcasted_iota(
        jnp.int32, (D, D), 1
    )
    trace = jnp.sum(jnp.where(diagonal, gram, 0.0))
    scale = 1.0 / (jnp.sqrt(jnp.full((1, 1), trace)) + 1e-07)
    gram = (gram * scale) * scale
    product = None
    for step in range(NS_ITERS):
        parts = split_low(gram)
        mixing = POLY_CUBIC * gram + POLY_QUINTIC * dot_split(parts, parts)
        mixing_parts = split_low(mixing)
        if step + 1 < NS_ITERS:
            half = POLY_LINEAR * gram + dot_split(mixing_parts, parts)
            gram = POLY_LINEAR * half + dot_split(mixing_parts, split_low(half))
        if product is None:
            product = jnp.where(diagonal, POLY_LINEAR, 0.0) + mixing
        else:
            product = POLY_LINEAR * product + dot_split(mixing_parts, split_low(product))
    answer[...] = dot_split(split_low(columns[...] * scale), split_low(product)).astype(LOW)


def update_kernel(ids, answers, answers_flipped, *refs):
    masters, updated, ordered = refs[:5], refs[5:10], refs[10]
    for place, block in pieces_of(ids, answers, answers_flipped):
        ordered[place] = block[...]
    widths = [m.shape[0 if turned else 1] for m, turned in zip(masters, TURNED)]
    spans = slot_spans(widths)
    for number in range(5):
        factor = MUON_RATE * 0.2 * math.sqrt(COLUMNS[number])
        mine = [k for k, (m, _) in enumerate(SLOTS) if m == number]
        if TURNED[number]:
            for k in mine:
                start, stop = spans[k]
                updated[number][start:stop, :] = masters[number][start:stop, :] * (
                    1.0 - MUON_RATE * WEIGHT_DECAY
                ) - factor * ordered[k, : stop - start, :].astype(FULL)
        else:
            direction = jnp.concatenate(
                [ordered[k, : spans[k][1] - spans[k][0], :].astype(FULL) for k in mine], axis=0
            )
            updated[number][...] = masters[number][...] * (
                1.0 - MUON_RATE * WEIGHT_DECAY
            ) - factor * direction.T


def whole_rows(vector):
    rows = -(-vector.shape[-1] // D)
    padded = jnp.pad(vector, [(0, 0)] * (vector.ndim - 1) + [(0, rows * D - vector.shape[-1])])
    return padded.reshape(vector.shape[:-1] + (rows, D))


def per_device(
    tokens,
    condition,
    cotangent,
    attend_weight,
    project_weight,
    expand_weight,
    contract_weight,
    modulate_weight,
    biases,
    attend_moment,
    project_moment,
    expand_moment,
    contract_moment,
    modulate_moment,
    bias_first,
    bias_second,
):
    latents = tokens.shape[0]
    steps = latents // BLOCK
    shards = lax.axis_size("shard")
    shard = lax.axis_index("shard")
    reps = lax.axis_size("rep")
    rep = lax.axis_index("rep")
    low = rep % GROUP
    ids = jnp.stack([shard, low]).astype(jnp.int32)
    rows = D // GROUP
    bias_share = biases.shape[0]
    mod_share = modulate_weight.shape[1]
    late_width = 4 * D // shards
    late_rows = late_width // GROUP

    early_weights = jnp.concatenate(
        [
            lax.dynamic_slice_in_dim(w, rep * (D // reps), D // reps, 0).astype(LOW)
            for w in (expand_weight, contract_weight)
        ],
        axis=1,
    )
    early_weights = lax.all_gather(early_weights, ("shard", "rep"), axis=0)
    early_weights = early_weights.reshape(shards, D, 2 * FF // shards)

    silu_value, silu_back = jax.vjp(jax.nn.silu, condition.astype(FULL))
    bias_rows = whole_rows(biases.astype(LOW))
    late_weights = jnp.concatenate([attend_weight.T, project_weight.T], axis=0).astype(LOW)
    late_weights = lax.dynamic_slice_in_dim(late_weights, low * late_rows, late_rows, 0)
    note = jnp.concatenate([late_weights, silu_value.astype(LOW), bias_rows], axis=0)
    note = jnp.pad(note, ((0, -note.shape[0] % 16), (0, 0)))
    notes = jnp.stack(exchange([note] * shards))
    late_stacked, late_flipped = gather_group(notes[:, :late_rows])

    cond_rows = notes[:, late_rows : late_rows + latents].reshape(shards * latents, D)
    modulate_low = modulate_weight.astype(LOW)
    share = jnp.dot(cond_rows, modulate_low, preferred_element_type=FULL)
    share = share.reshape(shards, latents, mod_share)
    answers = [share[0]] + [shift(share[d], shards - d) for d in range(1, shards)]
    answers = rotate(jnp.stack(answers), (shards - shard) % shards)
    start = late_rows + latents
    bias_all = notes[:, start : start + bias_rows.shape[0]].reshape(shards, -1)
    bias_all = rotate(bias_all[::-1], (shards - 1 - shard) % shards)
    bias_all = bias_all[:, :bias_share].reshape(-1).astype(FULL)
    mod = answers.transpose(1, 0, 2).reshape(latents, 6 * D) + bias_all[: 6 * D]
    mod = mod.reshape(latents, 6, D)
    bias_up = bias_all[6 * D : 6 * D + FF].reshape(1, FF)
    bias_down = bias_all[6 * D + FF :].reshape(1, D)

    tokens_shape = (latents, LEN, D)
    qkv, probs, attended, branch, wq, wo = local_call(
        attention_forward,
        ids,
        [(tokens, True), (mod, True), (late_stacked, False), (late_flipped, False)],
        [
            ((latents, LEN, 3 * D), LOW, True),
            ((latents, HEADS, LEN, LEN), LOW, True),
            (tokens_shape, LOW, True),
            (tokens_shape, FULL, True),
            ((3 * D, D), LOW, False),
            ((D, D), LOW, False),
        ],
        [
            pltpu.VMEM((shards, late_width, D), FULL),
            pltpu.VMEM((BLOCK * LEN, D), LOW),
            pltpu.VMEM((BLOCK * LEN, D), LOW),
        ],
        steps,
        latents * (2 * LEN * D * 4 * D + 4 * HEADS * LEN * LEN * PAIR) * 2,
        "attention_forward",
    )
    early_shape = (GROUP // 2, shards, rows, 2 * FF // shards)
    block_output, grad_mixed, grad_mod_late, keep, send, sum_up, sum_down = local_call(
        perceptron,
        ids,
        [
            (tokens, True),
            (branch, True),
            (mod, True),
            (cotangent, True),
            (early_weights, False),
            (bias_up, False),
            (bias_down, False),
        ],
        [
            (tokens_shape, LOW, True),
            (tokens_shape, FULL, True),
            ((latents, 4, D), FULL, True),
            (early_shape, FULL, False),
            (early_shape, LOW, False),
            ((1, FF), FULL, False),
            ((1, D), FULL, False),
        ],
        [
            pltpu.VMEM((D, FF), LOW),
            pltpu.VMEM((D, FF), LOW),
            pltpu.VMEM((BLOCK * LEN, FF), LOW),
            pltpu.VMEM((BLOCK * LEN, FF), FULL),
            pltpu.VMEM((D, FF), FULL),
            pltpu.VMEM((D, FF), FULL),
        ],
        steps,
        latents * 2 * LEN * D * FF * 6 * 2,
        "perceptron",
    )

    early_cores = sum_cores(keep, send)
    grad_attended, total_project = local_call(
        project_backward,
        ids,
        [(mod, True), (attended, True), (grad_mixed, True), (wo, False)],
        [(tokens_shape, LOW, True), ((D, D), FULL, False)],
        [],
        steps,
        latents * 2 * LEN * D * D * 2,
        "project_backward",
    )
    early_chips = sum_chips(early_cores)
    (grad_qkv,) = local_call(
        attention_backward,
        ids,
        [(qkv, True), (probs, True), (grad_attended, True)],
        [((latents, LEN, 3 * D), LOW, True)],
        [],
        steps,
        latents * 10 * HEADS * LEN * LEN * PAIR,
        "attention_backward",
        after=(early_cores,),
    )
    early = exchange([early_chips[d].astype(LOW) for d in range(shards)])
    early = sum(piece.astype(FULL) for piece in early[1:]) + early_chips[0]
    early = sum_rest(early.astype(LOW))
    late_shape = (GROUP // 2, shards, rows, late_width)
    tokens_grad, grad_mod_first, keep, send = local_call(
        attend_backward,
        ids,
        [
            (tokens, True),
            (mod, True),
            (grad_mixed, True),
            (grad_qkv, True),
            (wq, False),
            (total_project, False),
        ],
        [
            (tokens_shape, FULL, True),
            ((latents, 2, D), FULL, True),
            (late_shape, FULL, False),
            (late_shape, LOW, False),
        ],
        [pltpu.VMEM((D, 3 * D), FULL)],
        steps,
        latents * 2 * LEN * D * 6 * D * 2,
        "attend_backward",
        after=(early_chips,),
    )
    early_stacked, early_flipped = gather_group(early)
    late_chips = sum_chips(sum_cores(keep, send))

    grad_modulation = jnp.concatenate([grad_mod_first, grad_mod_late], axis=1)
    grad_modulation = grad_modulation.astype(LOW).reshape(latents, 6 * D)
    grad_bias = jnp.concatenate(
        [
            jnp.sum(grad_modulation.astype(FULL), axis=0),
            sum_up.reshape(-1),
            sum_down.reshape(-1),
        ]
    ).reshape(shards, bias_share)
    blocks = -(-mod_share // D)
    mod_rows = whole_rows(grad_modulation.reshape(latents, shards, mod_share))
    mod_rows = mod_rows.transpose(1, 2, 0, 3).reshape(shards, blocks * latents, D)
    bias_rows = whole_rows(grad_bias)
    bias_high = bias_rows.astype(LOW)
    bias_rest = (bias_rows - bias_high.astype(FULL)).astype(LOW)
    count = bias_rows.shape[1]
    extra = jnp.concatenate([mod_rows, bias_high, bias_rest], axis=1)
    extra = rotate(jnp.pad(extra, ((0, 0), (0, -extra.shape[1] % 16), (0, 0))), shard)
    outgoing = jnp.pad(late_chips.astype(LOW), ((0, 0), (0, 0), (0, D - late_width)))
    outgoing = jnp.concatenate([outgoing, extra], axis=1)
    incoming = jnp.stack(exchange([outgoing[d] for d in range(shards)]))
    late = sum_rest(jnp.sum(incoming[:, :rows].astype(FULL), axis=0).astype(LOW))
    grad_blocks = incoming[:, rows : rows + blocks * latents].reshape(shards, blocks, latents, D)
    grad_blocks = grad_blocks.transpose(1, 0, 2, 3).reshape(blocks, shards * latents, D)
    start = rows + blocks * latents
    bias_sum = jnp.sum(incoming[:, start : start + 2 * count].astype(FULL), axis=0)
    bias_sum = bias_sum[:count] + bias_sum[count:]
    bias_sum = jnp.pad(bias_sum, ((0, 8 - count), (0, 0)))
    bias_high = bias_sum.astype(LOW)
    bias_rest = (bias_sum - bias_high.astype(FULL)).astype(LOW)
    payload = jnp.concatenate(
        [late, grad_blocks.reshape(-1, D), bias_high, bias_rest, cond_rows], axis=0
    )
    late_stacked, late_flipped = gather_group(payload)

    grad_rows = jnp.concatenate([grad_blocks[b] for b in range(blocks)], axis=1)[:, :mod_share]
    grad_cond_share = lax.dot_general(
        grad_rows, modulate_low, (((1,), (1,)), ((), ())), preferred_element_type=FULL
    ).reshape(shards, latents, D)
    grad_cond_low = grad_cond_share[0]
    for d in range(1, shards):
        grad_cond_low = grad_cond_low + shift(grad_cond_share[d], shards - d)
    condition_grad = silu_back(grad_cond_low)[0]

    def as_held(values):
        return [v.T if turned else v for v, turned in zip(values, TURNED)]

    masters = as_held(
        [attend_weight, project_weight, expand_weight, contract_weight, modulate_weight]
    )
    moments = as_held(
        [attend_moment, project_moment, expand_moment, contract_moment, modulate_moment]
    )
    shapes = [m.shape for m in masters]
    widths = [whole // shards for whole in COLUMNS]
    slot_width = max(stop - start for start, stop in slot_spans(widths))
    piece_rows = 128 * len(TRIANGLE) // shards
    results = local_call(
        momenta_kernel,
        ids,
        [(v, False) for v in (late_stacked, late_flipped, early_stacked, early_flipped, *moments)],
        [(shape, FULL, False) for shape in shapes * 2]
        + [
            ((shards, piece_rows, 128), FULL, False),
            ((slot_width, D), FULL, False),
            ((8, D), FULL, False),
        ],
        [pltpu.VMEM(shape, FULL) for shape in shapes]
        + [pltpu.VMEM((D, D), FULL), pltpu.VMEM((128 * len(TRIANGLE), 128), FULL)],
        1,
        6 * D * D * D,
        "momenta",
    )
    gradients, momenta = as_held(results[0:5]), as_held(results[5:10])
    gram, columns, bias_block = results[10:13]
    piece = sum(exchange([gram[d] for d in range(shards)]))
    (answer,) = local_call(
        polynomial_kernel,
        ids,
        [(p, False) for p in exchange([piece] * shards)] + [(columns, False)],
        [((slot_width, D), LOW, False)],
        [pltpu.VMEM((128 * len(TRIANGLE), 128), FULL), pltpu.VMEM((D, D), FULL)],
        1,
        2 * 3 * 18 * D * D * D,
        "polynomial",
        after=(condition_grad,),
    )
    updated = local_call(
        update_kernel,
        ids,
        [(v, False) for v in (*gather_group(answer), *masters)],
        [(shape, FULL, False) for shape in shapes],
        [pltpu.VMEM((GROUP, slot_width, D), LOW)],
        1,
        2 * D * sum(widths),
        "update",
    )
    updated = as_held(updated)

    bias_gradient = bias_block.reshape(-1)[:bias_share]
    bias_momentum = BETA_ONE * bias_first + (1.0 - BETA_ONE) * bias_gradient
    bias_variance = BETA_TWO * bias_second + (1.0 - BETA_TWO) * bias_gradient * bias_gradient
    corrected_first = bias_momentum / (1.0 - BETA_ONE**STEP)
    corrected_second = bias_variance / (1.0 - BETA_TWO**STEP)
    bias_updated = biases * (1.0 - ADAM_RATE * WEIGHT_DECAY) - ADAM_RATE * corrected_first / (
        jnp.sqrt(corrected_second) + ADAM_EPSILON
    )
    return (
        block_output,
        tokens_grad,
        condition_grad,
        *gradients,
        *momenta,
        *updated,
        bias_gradient,
        bias_momentum,
        bias_variance,
        bias_updated,
    )


def solution(mesh):
    rows = P(("shard", "rep"), None, None)
    vectors = P(("shard", "rep"), None)
    columns = P(None, "shard")
    flat = P("shard")
    return jax.shard_map(
        per_device,
        mesh=mesh,
        in_specs=(rows, vectors, rows) + (columns,) * 5 + (flat,) + (columns,) * 5 + (flat,) * 2,
        out_specs=(rows, rows, vectors) + (columns,) * 15 + (flat,) * 4,
        check_vma=False,
    )
```

```python
from functools import partial
import math

import jax
import jax.numpy as jnp
from jax import lax
from jax.experimental import pallas as pl
from jax.experimental.pallas import tpu as pltpu
from jax.sharding import PartitionSpec as P

D = 384
HEADS = 6
HEAD = 64
FF = 1536
LEN = 256
NS_ITERS = 5
STEP = 10
PAIR = 2 * HEAD
CHUNK = 512
GROUP = 8
BLOCK = 2
BIAS_LEN = 6 * D + FF + D
NOTE = 16

POLY_LINEAR = 3.4445
POLY_CUBIC = -4.775
POLY_QUINTIC = 2.0315
MOMENTUM = 0.95
MUON_RATE = 0.4
WEIGHT_DECAY = 0.01
ADAM_RATE = 0.1
BETA_ONE = 0.9
BETA_TWO = 0.999
ADAM_EPSILON = 1e-08
GELU_SLOPE = math.sqrt(2.0 / math.pi)
GELU_CUBIC = 0.044715

LOW = jnp.bfloat16
FULL = jnp.float32

SLOTS = ((4, 0), (4, 1), (0, 0), (2, 0), (2, 1), (3, 0), (3, 1), (1, 0))


def shift(value, distance):
    size = lax.axis_size("shard")
    return lax.ppermute(value, "shard", [(i, (i + distance) % size) for i in range(size)])


def flip(value, mask):
    size = lax.axis_size("rep")
    return lax.ppermute(value, "rep", [(i, i ^ mask) for i in range(size)])


def exchange(pieces):
    return [pieces[0]] + [shift(pieces[d], d) for d in range(1, len(pieces))]


def gather_group(value):
    stacked = jnp.stack([value] + [flip(value, 2 * t) for t in range(1, GROUP // 2)])
    return stacked, flip(stacked, 1)


def sum_cores(keep, send, ids, name):
    received = flip(send, 1)
    shape = keep.shape[1:]
    return local_call(
        split_sum,
        ids,
        [(keep, False), (received, False)],
        [(shape, FULL, False)] + [(shape, LOW, False)] * (keep.shape[0] - 1),
        [],
        1,
        keep.size,
        name,
    )


def exchange_chips(totals):
    return [totals[0]] + [flip(totals[t], 2 * t) for t in range(1, GROUP // 2)]


def sum_rest(value):
    for bit in range(3, lax.axis_size("rep").bit_length() - 1):
        value = (value.astype(FULL) + flip(value, 1 << bit).astype(FULL)).astype(LOW)
    return value


def dot(left, right):
    return lax.dot_general(left, right, (((1,), (0,)), ((), ())), preferred_element_type=FULL)


def dot_nt(left, right):
    return lax.dot_general(left, right, (((1,), (1,)), ((), ())), preferred_element_type=FULL)


def dot_tn(left, right):
    return lax.dot_general(left, right, (((0,), (0,)), ((), ())), preferred_element_type=FULL)


def split_low(value):
    high = value.astype(LOW)
    return high, (value - high.astype(FULL)).astype(LOW)


def dot_split(left, right, product=dot):
    return product(left[0], right[0]) + (product(left[0], right[1]) + product(left[1], right[0]))


def normalize(values):
    centered = values - jnp.mean(values, -1, keepdims=True)
    inverse_spread = lax.rsqrt(jnp.mean(centered * centered, -1, keepdims=True) + 1e-06)
    return centered * inverse_spread, inverse_spread


def normalize_back(upstream, normed, inverse_spread):
    return inverse_spread * (
        upstream
        - jnp.mean(upstream, -1, keepdims=True)
        - normed * jnp.mean(upstream * normed, -1, keepdims=True)
    )


def local_call(kernel, ids, inputs, outputs, scratch, steps, flops, name, after=()):
    def run(*refs):
        kernel(*refs[: 1 + len(inputs)], *refs[1 + len(inputs) + len(after) :])

    def spec(shape, blocked):
        zeros = (0,) * (len(shape) - 1)
        if blocked:
            block = (shape[0] // steps,) + tuple(shape[1:])
            return pl.BlockSpec(block, lambda i, _: (i,) + zeros)
        return pl.BlockSpec(tuple(shape), lambda i, _: (0,) + zeros)

    moved = sum(v.size * v.dtype.itemsize for v, _ in inputs)
    moved += sum(math.prod(shape) * jnp.dtype(kind).itemsize for shape, kind, _ in outputs)
    return pl.pallas_call(
        run,
        grid_spec=pltpu.PrefetchScalarGridSpec(
            num_scalar_prefetch=1,
            grid=(steps,),
            in_specs=[spec(v.shape, blocked) for v, blocked in inputs]
            + [pl.BlockSpec(memory_space=pl.ANY) for _ in after],
            out_specs=[spec(shape, blocked) for shape, _, blocked in outputs],
            scratch_shapes=scratch,
        ),
        out_shape=[jax.ShapeDtypeStruct(shape, kind) for shape, kind, _ in outputs],
        compiler_params=pltpu.CompilerParams(
            dimension_semantics=("arbitrary",), vmem_limit_bytes=48 * 1024 * 1024
        ),
        cost_estimate=pl.CostEstimate(flops=flops, bytes_accessed=moved, transcendentals=0),
        name=name,
    )(ids, *[v for v, _ in inputs], *after)


def pieces_of(ids, stacked, flipped):
    for t in range(GROUP // 2):
        for bit, blocks in enumerate((stacked, flipped)):
            yield ids[1] ^ (2 * t + bit), blocks.at[t]


def rows_at(place, rows):
    return pl.ds(pl.multiple_of(place * rows, rows), rows)


def turn(value):
    filled = value.shape[1]
    extra = -filled % 128
    if extra:
        value = jnp.concatenate([value, jnp.zeros((value.shape[0], extra), value.dtype)], axis=1)
    return value.T[:filled]


def head_masks(values):
    lane = lax.broadcasted_iota(jnp.int32, values.shape, 1) % PAIR
    zero = jnp.zeros_like(values)
    return (
        jnp.where(lane < HEAD, values, zero).astype(LOW),
        jnp.where(lane < HEAD, zero, values).astype(LOW),
    )


def split_sum(ids, keep, received, own, *others):
    own[...] = keep[0] + received[0].astype(FULL)
    for t, other in enumerate(others):
        other[...] = (keep[t + 1] + received[t + 1].astype(FULL)).astype(LOW)


def modulation_kernel(ids, *refs):
    shards = (len(refs) - 2) // 2
    notes, weight, answers, weight_low = (
        refs[:shards], refs[shards], refs[shards + 1 : -1], refs[-1],
    )
    low = weight[...].astype(LOW)
    weight_low[...] = low
    for note, answer in zip(notes, answers):
        answer[...] = dot_nt(note[:NOTE, :], low)[: answer.shape[0]]


def attention_forward(
    ids, tokens, stacked, flipped, *refs,
):
    shards = (len(refs) - 14) // 2
    answers, notes = refs[:shards], refs[shards : 2 * shards]
    (
        qkv, probs, attended, branch, wq, wo, mod_all, bias_up, bias_down,
        ordered, query_a, query_b, mod_parts, bias_parts,
    ) = refs[2 * shards :]
    rows = ordered.shape[1] // GROUP
    wide, narrow = 3 * D // shards, D // shards

    @pl.when(pl.program_id(0) == 0)
    def _():
        for place, block in pieces_of(ids, stacked, flipped):
            for d in range(shards):
                source = lax.rem(ids[0] - d + shards, shards)
                ordered[source, rows_at(place, rows), :] = block[d].astype(FULL)
        for s in range(shards):
            wq[s * wide : (s + 1) * wide, :] = ordered[s, :wide, :].astype(LOW)
            wo[s * narrow : (s + 1) * narrow, :] = ordered[s, wide:, :].astype(LOW)
        for d in range(shards):
            mod_parts[lax.rem(ids[0] + d, shards)] = answers[d][...]
            bias_parts[lax.rem(ids[0] - d + shards, shards)] = notes[d][:NOTE, :].astype(FULL)
        latents = mod_all.shape[0]
        share = BIAS_LEN // shards
        pieces = []
        for s in range(shards):
            for b in range(-(-share // D)):
                row = bias_parts[s, latents + b : latents + b + 1, :]
                pieces.append(row[:, : min(D, share - b * D)])
        bias = jnp.concatenate(pieces, axis=1)
        whole = jnp.concatenate([mod_parts[s] for s in range(shards)], axis=1) + bias[:, : 6 * D]
        for latent in range(latents):
            for b in range(6):
                mod_all[latent, b : b + 1, :] = whole[latent : latent + 1, b * D : (b + 1) * D]
        bias_up[...] = bias[:, 6 * D : 6 * D + FF]
        bias_down[...] = bias[:, 6 * D + FF :]

    count = tokens.shape[0]
    mod = mod_all[pl.ds(pl.program_id(0) * count, count)]
    normed, _ = normalize(tokens[...].astype(FULL))
    hidden = normed * (1.0 + mod[:, 1:2, :]) + mod[:, 0:1, :]
    hidden = hidden.reshape(count * LEN, D).astype(LOW)
    queries = dot_nt(hidden, wq[:D, :])
    masked_a, masked_b = head_masks(queries)
    query_a[...] = masked_a
    query_b[...] = masked_b
    qkv[:, :, :D] = queries.astype(LOW).reshape(count, LEN, D)
    qkv[:, :, D:] = dot_nt(hidden, wq[D:, :]).astype(LOW).reshape(count, LEN, 2 * D)
    for latent in range(count):
        span = slice(latent * LEN, (latent + 1) * LEN)
        for pair in range(HEADS // 2):
            lanes = slice(pair * PAIR, (pair + 1) * PAIR)
            keys = qkv[latent, :, D + pair * PAIR : D + (pair + 1) * PAIR]
            values = qkv[latent, :, 2 * D + pair * PAIR : 2 * D + (pair + 1) * PAIR].T
            results = []
            for member, masked in enumerate((query_a, query_b)):
                scores = dot_nt(keys, masked[span, lanes]) * (HEAD ** (-0.5))
                top = jnp.max(scores, 0, keepdims=True)
                raised = jnp.exp(scores - top)
                share = (raised * (1.0 / jnp.sum(raised, 0, keepdims=True))).astype(LOW)
                probs[latent, 2 * pair + member] = share
                results.append(dot(values[member * HEAD : (member + 1) * HEAD], share))
            attended[latent, :, lanes] = jnp.concatenate(results, axis=0).T.astype(LOW)
    branch[...] = dot_nt(attended[...].reshape(count * LEN, D), wo[...]).reshape(count, LEN, D)


def perceptron(
    ids, tokens, branch, mod, cotangent, stacked, flipped, bias_up, bias_down,
    out, grad_mixed, grad_mod, keep, send, sum_up, sum_down,
    ordered, wu, wd, act, slope, total_up, total_down,
):
    shards = ordered.shape[0]
    rows = D // GROUP
    width = FF // shards
    step = pl.program_id(0)

    @pl.when(step == 0)
    def _():
        for place, block in pieces_of(ids, stacked, flipped):
            for d in range(shards):
                source = lax.rem(ids[0] - d + shards, shards)
                ordered[source, rows_at(place, rows), :] = block[d]
        for i in range(GROUP):
            span = slice(i * rows, (i + 1) * rows)
            pieces = [ordered[s, span, :] for s in range(shards)]
            wu[span, :] = jnp.concatenate([p[:, :width] for p in pieces], axis=1)
            wd[span, :] = jnp.concatenate([p[:, width:] for p in pieces], axis=1)
        total_up[...] = jnp.zeros_like(total_up)
        total_down[...] = jnp.zeros_like(total_down)
        sum_up[...] = jnp.zeros_like(sum_up)
        sum_down[...] = jnp.zeros_like(sum_down)

    count = tokens.shape[0]
    flat = count * LEN
    branch_out = branch[...]
    mixed = tokens[...].astype(FULL) + mod[:, 2:3, :] * branch_out
    normed, inverse_spread = normalize(mixed)
    hidden = (normed * (1.0 + mod[:, 4:5, :]) + mod[:, 3:4, :]).reshape(flat, D).astype(LOW)
    result = jnp.zeros((flat, D), FULL)
    for start in range(0, FF, CHUNK):
        span = slice(start, start + CHUNK)
        u = dot(hidden, wu[:, span]) + bias_up[:, span]
        square = u * u
        bent = jnp.tanh(GELU_SLOPE * u * (1.0 + GELU_CUBIC * square))
        half = 0.5 * (1.0 + bent)
        act_low = (u * half).astype(LOW)
        act[:, span] = act_low
        slope[:, span] = half + (0.5 * GELU_SLOPE) * u * (1.0 - bent * bent) * (
            1.0 + 3.0 * GELU_CUBIC * square
        )
        result = result + dot_nt(act_low, wd[:, span])
    result = (result + bias_down[...]).reshape(count, LEN, D)
    gate = mod[:, 5:6, :]
    out[...] = (mixed + gate * result).astype(LOW)
    upstream = cotangent[...].astype(FULL)
    grad_mod[:, 3:4, :] = jnp.sum(upstream * result, axis=1, keepdims=True)
    grad_result = (gate * upstream).reshape(flat, D).astype(LOW)
    sum_down[...] += jnp.sum(grad_result.astype(FULL), axis=0, keepdims=True)
    grad_hidden = jnp.zeros((flat, D), FULL)
    for start in range(0, FF, CHUNK):
        span = slice(start, start + CHUNK)
        grad_u = (dot(grad_result, wd[:, span]) * slope[:, span]).astype(LOW)
        sum_up[:, span] += jnp.sum(grad_u.astype(FULL), axis=0, keepdims=True)
        total_down[:, span] += dot_tn(grad_result, act[:, span])
        total_up[:, span] += dot_tn(hidden, grad_u)
        grad_hidden = grad_hidden + dot_nt(grad_u, wu[:, span])
    grad_hidden = grad_hidden.reshape(count, LEN, D)
    grad_mod[:, 1:2, :] = jnp.sum(grad_hidden, axis=1, keepdims=True)
    grad_mod[:, 2:3, :] = jnp.sum(grad_hidden * normed, axis=1, keepdims=True)
    back = upstream + normalize_back(
        grad_hidden * (1.0 + mod[:, 4:5, :]), normed, inverse_spread
    )
    grad_mixed[...] = back
    grad_mod[:, 0:1, :] = jnp.sum(back * branch_out, axis=1, keepdims=True)

    @pl.when(step == pl.num_programs(0) - 1)
    def _():
        shard, low = ids[0], ids[1]
        for j in range(GROUP):
            span = pl.ds(pl.multiple_of((low ^ j) * rows, rows), rows)
            for s in range(shards):
                d = lax.rem(s - shard + shards, shards)
                lanes = slice(s * width, (s + 1) * width)
                piece = jnp.concatenate([total_up[span, lanes], total_down[span, lanes]], axis=1)
                if j & 1:
                    send[j // 2, d] = piece.astype(LOW)
                else:
                    keep[j // 2, d] = piece


def project_backward(
    ids, mod, attended, grad_mixed, wo,
    grad_attended, total_project,
):
    @pl.when(pl.program_id(0) == 0)
    def _():
        total_project[...] = jnp.zeros_like(total_project)

    count = attended.shape[0]
    flat = count * LEN
    grad_branch = (mod[:, 2:3, :] * grad_mixed[...]).reshape(flat, D).astype(LOW)
    total_project[...] += dot_tn(attended[...].reshape(flat, D), grad_branch)
    grad_attended[...] = dot(grad_branch, wo[...]).astype(LOW).reshape(count, LEN, D)


def attention_backward(ids, qkv, probs, grad_attended, grad_qkv):
    mask = lax.broadcasted_iota(jnp.int32, (LEN, PAIR), 1) < HEAD
    scale = HEAD ** (-0.5)
    for latent in range(qkv.shape[0]):
        for pair in range(HEADS // 2):
            lanes = slice(pair * PAIR, (pair + 1) * PAIR)
            key_lanes = slice(D + pair * PAIR, D + (pair + 1) * PAIR)
            value_lanes = slice(2 * D + pair * PAIR, 2 * D + (pair + 1) * PAIR)
            queries = qkv[latent, :, lanes]
            keys = qkv[latent, :, key_lanes].T
            values = qkv[latent, :, value_lanes]
            upper = grad_attended[latent, :, lanes]
            masked = head_masks(upper.astype(FULL))
            by_query, by_key, by_value = [], [], []
            for member in range(2):
                share = probs[latent, 2 * pair + member]
                weight = share.astype(FULL)
                grad_share = dot_nt(values, masked[member])
                product = weight * grad_share
                grad_scores = (
                    product - weight * jnp.sum(product, 0, keepdims=True)
                ).astype(LOW)
                by_query.append(dot(keys[member * HEAD : (member + 1) * HEAD], grad_scores))
                by_key.append(dot(grad_scores, queries))
                by_value.append(dot(share, upper))
            merged = jnp.concatenate(by_query, axis=0).T * scale
            grad_qkv[latent, :, lanes] = merged.astype(LOW)
            merged = jnp.where(mask, by_key[0], by_key[1]) * scale
            grad_qkv[latent, :, key_lanes] = merged.astype(LOW)
            merged = jnp.where(mask, by_value[0], by_value[1])
            grad_qkv[latent, :, value_lanes] = merged.astype(LOW)


def attend_backward(
    ids, tokens, mod, grad_mixed, grad_qkv, wq, total_project, grad_mod_late, sum_up, sum_down,
    grad_tokens, keep, send, extra,
    total_attend, grad_mod, extra_rows,
):
    rows = D // GROUP
    shards = keep.shape[1]
    step = pl.program_id(0)

    @pl.when(step == 0)
    def _():
        total_attend[...] = jnp.zeros_like(total_attend)

    count = tokens.shape[0]
    flat = count * LEN
    normed, inverse_spread = normalize(tokens[...].astype(FULL))
    hidden = (normed * (1.0 + mod[:, 1:2, :]) + mod[:, 0:1, :]).reshape(flat, D).astype(LOW)
    grad_low = grad_qkv[...].reshape(flat, 3 * D)
    total_attend[...] += dot_tn(hidden, grad_low)
    grad_hidden = dot(grad_low, wq[...]).reshape(count, LEN, D)
    mine = pl.ds(step * count, count)
    grad_mod[mine, 0:1, :] = jnp.sum(grad_hidden, axis=1, keepdims=True)
    grad_mod[mine, 1:2, :] = jnp.sum(grad_hidden * normed, axis=1, keepdims=True)
    grad_tokens[...] = grad_mixed[...] + normalize_back(
        grad_hidden * (1.0 + mod[:, 1:2, :]), normed, inverse_spread
    )

    @pl.when(step == pl.num_programs(0) - 1)
    def _():
        shard, low = ids[0], ids[1]
        wide, narrow = 3 * D // shards, D // shards
        for j in range(GROUP):
            span = rows_at(low ^ j, rows)
            whole_attend, whole_project = total_attend[span, :], total_project[span, :]
            for s in range(shards):
                d = lax.rem(s - shard + shards, shards)
                piece = jnp.concatenate(
                    [
                        whole_attend[:, s * wide : (s + 1) * wide],
                        whole_project[:, s * narrow : (s + 1) * narrow],
                    ],
                    axis=1,
                )
                if j & 1:
                    send[j // 2, d] = piece.astype(LOW)
                else:
                    keep[j // 2, d] = piece
        latents = grad_mod.shape[0]
        columns = [grad_mod[:, b, :] for b in range(2)] + [grad_mod_late[:, b, :] for b in range(4)]
        whole = jnp.concatenate(columns, axis=1).astype(LOW).astype(FULL)
        sums = jnp.sum(whole, axis=0, keepdims=True)
        sums = jnp.concatenate([sums, sum_up[...], sum_down[...]], axis=1)
        mod_share, bias_share = 6 * D // shards, BIAS_LEN // shards
        blocks, lines = -(-mod_share // D), -(-bias_share // D)

        def padded(values, start, stop):
            part = values[:, start : min(start + D, stop)]
            if part.shape[1] < D:
                rest = jnp.zeros((part.shape[0], D - part.shape[1]), FULL)
                part = jnp.concatenate([part, rest], axis=1)
            return part

        extra_rows[...] = jnp.zeros_like(extra_rows)
        for s in range(shards):
            for b in range(blocks):
                extra_rows[b * latents : (b + 1) * latents, :] = padded(
                    whole, s * mod_share + b * D, (s + 1) * mod_share
                )
            for b in range(lines):
                row = padded(sums, s * bias_share + b * D, (s + 1) * bias_share)
                high = row.astype(LOW).astype(FULL)
                place = blocks * latents + b
                extra_rows[place : place + 1, :] = high
                extra_rows[place + lines : place + lines + 1, :] = row - high
            extra[lax.rem(s - shard + shards, shards)] = extra_rows[...].astype(LOW)


def late_pieces(ids, own, first, second, third, extra, *pieces):
    total = own[...]
    for received in (first, second, third):
        total = total + received[...].astype(FULL)
    for d, piece in enumerate(pieces):
        piece[:NOTE, :] = extra[d]
        if total.shape[2] < D:
            piece[NOTE:, :] = jnp.zeros((total.shape[1], D), LOW)
        piece[NOTE:, : total.shape[2]] = total[d].astype(LOW)


def combine(shards, latents, ids, *refs):
    incoming, notes, weight, payload = (
        refs[:shards], refs[shards : 2 * shards], refs[2 * shards], refs[2 * shards + 1],
    )
    answers, rows_ref = refs[2 * shards + 2 : -1], refs[-1]
    rows = D // GROUP
    mod_share, bias_share = 6 * D // shards, BIAS_LEN // shards
    blocks, lines = -(-mod_share // D), -(-bias_share // D)
    total = jnp.zeros((rows, D), FULL)
    bias = jnp.zeros((NOTE, D), FULL)
    for d in range(shards):
        total = total + incoming[d][NOTE:, :].astype(FULL)
        extra = incoming[d][:NOTE, :].astype(FULL)
        bias = bias + extra
        for b in range(blocks):
            start = (b * shards + d) * latents
            rows_ref[start : start + latents, :] = extra[b * latents : (b + 1) * latents]
        start = (blocks * shards + d) * latents
        rows_ref[start : start + latents, :] = notes[d][:NOTE, :].astype(FULL)[:latents]
    payload[:rows, :] = total.astype(LOW)
    count = (blocks + 1) * shards * latents
    start = blocks * latents
    bias = bias[start : start + lines] + bias[start + lines : start + 2 * lines]
    high = bias.astype(LOW).astype(FULL)
    rows_ref[count:, :] = jnp.zeros((16, D), FULL)
    rows_ref[count : count + lines, :] = high
    rows_ref[count + 8 : count + 8 + lines, :] = bias - high
    payload[rows:, :] = rows_ref[...].astype(LOW)
    for d, answer in enumerate(answers):
        result = jnp.zeros((NOTE, D), FULL)
        for b in range(blocks):
            filled = min(D, mod_share - b * D)
            product = dot(incoming[d][:NOTE, :filled], weight[b * D : b * D + filled, :])
            result = result + shifted(product, b * latents)
        answer[...] = result[:latents]


def shifted(values, count):
    if count == 0:
        return values
    return jnp.concatenate([values[count:], values[:count]], axis=0)


COLUMNS = (3 * D, D, FF, FF, 6 * D)
TURNED = (True, True, False, False, True)
TRIANGLE = ((0, 0), (0, 1), (0, 2), (1, 1), (1, 2), (2, 2))


def slot_spans(widths):
    counts = [sum(1 for m, _ in SLOTS if m == number) for number in range(len(widths))]
    return [
        (part * (widths[m] // counts[m]), (part + 1) * (widths[m] // counts[m]))
        for m, part in SLOTS
    ]


def momenta_kernel(latents, ids, late, late_flipped, early, early_flipped, *refs):
    moments, grads, momenta = refs[0:5], refs[5:10], refs[10:15]
    gram, columns, bias = refs[15:18]
    mixed = refs[18:23]
    late_whole, flat_gram = refs[23:25]
    low = ids[1]
    rows = D // GROUP
    shards = gram.shape[0]
    widths = [whole // shards for whole in COLUMNS]
    blocks = -(-widths[4] // D)
    unit = (blocks + 1) * latents + 16
    starts = range(rows, late.shape[1], unit)
    late_width = widths[0] + widths[1]
    for place, block in pieces_of(ids, late, late_flipped):
        late_whole[rows_at(place, rows), :] = block[:rows, :].astype(FULL)
    for place, block in pieces_of(ids, early, early_flipped):
        piece = block[...].astype(FULL)
        grads[2][rows_at(place, rows), :] = piece[:, : widths[2]]
        grads[3][rows_at(place, rows), :] = piece[:, widths[2] :]
    turned = turn(late_whole[...])
    grads[0][...] = turned[: widths[0]]
    grads[1][...] = turned[widths[0] : late_width]
    parts = [
        ref[t, start : start + unit, :]
        for ref in (late, late_flipped)
        for t in range(GROUP // 2)
        for start in starts
    ]
    cond = jnp.concatenate([p[blocks * latents : (blocks + 1) * latents] for p in parts], axis=0)
    for block in range(blocks):
        rising = jnp.concatenate(
            [p[block * latents : (block + 1) * latents] for p in parts], axis=0
        )
        filled = min(D, widths[4] - block * D)
        grads[4][block * D : block * D + filled, :] = dot_tn(rising, cond)[:filled]
    total = jnp.zeros((16, D), FULL)
    for part in parts:
        total = total + part[(blocks + 1) * latents :].astype(FULL)
    bias[...] = total[:8] + total[8:]
    for number in range(5):
        grad = grads[number][...]
        moment = MOMENTUM * moments[number][...] + grad
        momenta[number][...] = moment
        mixed[number][...] = grad + MOMENTUM * moment
    for number in range(5):
        owners = [k for k, (m, _) in enumerate(SLOTS) if m == number]
        condition = low == owners[0]
        for owner in owners[1:]:
            condition = condition | (low == owner)

        @pl.when(condition)
        def _(number=number):
            parts = split_low(mixed[number][...])
            whole = dot_split(parts, parts, dot_tn if TURNED[number] else dot_nt)
            for place, (a, b) in enumerate(TRIANGLE):
                flat_gram[place * 128 : (place + 1) * 128, :] = whole[
                    a * 128 : (a + 1) * 128, b * 128 : (b + 1) * 128
                ]

    size = gram.shape[1]
    for s in range(shards):
        gram[lax.rem(s - ids[0] + shards, shards)] = flat_gram[s * size : (s + 1) * size, :]
    spans = slot_spans(widths)
    for k, ((number, _), (start, stop)) in enumerate(zip(SLOTS, spans)):

        @pl.when(low == k)
        def _(number=number, start=start, stop=stop):
            filled = stop - start
            if TURNED[number]:
                columns[:filled, :] = mixed[number][start:stop, :]
            else:
                columns[:filled, :] = turn(mixed[number][...])[start:stop]
            if filled < columns.shape[0]:
                columns[filled:, :] = jnp.zeros((columns.shape[0] - filled, D), FULL)


def polynomial_kernel(ids, *refs):
    shards = len(refs) - 4
    pieces, columns, answer, flat_gram, gram_ref = refs[:shards], *refs[shards:]
    size = pieces[0].shape[0]
    for d in range(shards):
        source = lax.rem(ids[0] - d + shards, shards)
        flat_gram[rows_at(source, size), :] = pieces[d][...]
    for place, (a, b) in enumerate(TRIANGLE):
        block = flat_gram[place * 128 : (place + 1) * 128, :]
        gram_ref[a * 128 : (a + 1) * 128, b * 128 : (b + 1) * 128] = block
        if a != b:
            gram_ref[b * 128 : (b + 1) * 128, a * 128 : (a + 1) * 128] = block.T
    gram = gram_ref[...]
    diagonal = lax.broadcasted_iota(jnp.int32, (D, D), 0) == lax.broadcasted_iota(
        jnp.int32, (D, D), 1
    )
    trace = jnp.sum(jnp.where(diagonal, gram, 0.0))
    scale = 1.0 / (jnp.sqrt(jnp.full((1, 1), trace)) + 1e-07)
    gram = (gram * scale) * scale
    product = jnp.where(diagonal, 1.0, 0.0)
    for step in range(NS_ITERS):
        mixing = POLY_CUBIC * gram + POLY_QUINTIC * dot_deep(left_deep(gram), right_deep(gram))
        mixing_deep = left_deep(mixing)
        if step == 0:
            half = POLY_LINEAR * gram + dot_deep(mixing_deep, right_deep(gram))
            product = POLY_LINEAR * product + mixing
        elif step + 1 < NS_ITERS:
            both = jnp.concatenate([gram, product], axis=1)
            both = POLY_LINEAR * both + dot_deep(mixing_deep, right_deep(both))
            half, product = both[:, :D], both[:, D:]
        else:
            product = POLY_LINEAR * product + dot_deep(mixing_deep, right_deep(product))
        if step + 1 < NS_ITERS:
            gram = POLY_LINEAR * half + dot_deep(mixing_deep, right_deep(half))
    answer[...] = dot_deep(left_deep(columns[...] * scale), right_deep(product)).astype(LOW)


def left_deep(value):
    high, rest = split_low(value)
    return jnp.concatenate([high, rest, high], axis=1)


def right_deep(value):
    high, rest = split_low(value)
    return jnp.concatenate([high, high, rest], axis=0)


def dot_deep(left, right):
    return dot(left, right)


def update_kernel(ids, answers, answers_flipped, *refs):
    masters, updated, ordered = refs[:5], refs[5:10], refs[10]
    for place, block in pieces_of(ids, answers, answers_flipped):
        ordered[place] = block[...]
    widths = [m.shape[0 if turned else 1] for m, turned in zip(masters, TURNED)]
    spans = slot_spans(widths)
    for number in range(5):
        factor = MUON_RATE * 0.2 * math.sqrt(COLUMNS[number])
        mine = [k for k, (m, _) in enumerate(SLOTS) if m == number]
        if TURNED[number]:
            for k in mine:
                start, stop = spans[k]
                updated[number][start:stop, :] = masters[number][start:stop, :] * (
                    1.0 - MUON_RATE * WEIGHT_DECAY
                ) - factor * ordered[k, : stop - start, :].astype(FULL)
        else:
            direction = jnp.concatenate(
                [ordered[k, : spans[k][1] - spans[k][0], :].astype(FULL) for k in mine], axis=0
            )
            updated[number][...] = masters[number][...] * (
                1.0 - MUON_RATE * WEIGHT_DECAY
            ) - factor * direction.T


def whole_rows(vector):
    rows = -(-vector.shape[-1] // D)
    padded = jnp.pad(vector, [(0, 0)] * (vector.ndim - 1) + [(0, rows * D - vector.shape[-1])])
    return padded.reshape(vector.shape[:-1] + (rows, D))


def per_device(
    tokens,
    condition,
    cotangent,
    attend_weight,
    project_weight,
    expand_weight,
    contract_weight,
    modulate_weight,
    biases,
    attend_moment,
    project_moment,
    expand_moment,
    contract_moment,
    modulate_moment,
    bias_first,
    bias_second,
):
    latents = tokens.shape[0]
    steps = latents // BLOCK
    shards = lax.axis_size("shard")
    shard = lax.axis_index("shard")
    low = lax.axis_index("rep") % GROUP
    ids = jnp.stack([shard, low]).astype(jnp.int32)
    rows = D // GROUP
    bias_share = biases.shape[0]
    mod_share = modulate_weight.shape[1]
    late_width = 4 * D // shards
    late_rows = late_width // GROUP

    silu_value, silu_back = jax.vjp(jax.nn.silu, condition.astype(FULL))
    note = jnp.concatenate([silu_value.astype(LOW), whole_rows(biases.astype(LOW))], axis=0)
    note = jnp.pad(note, ((0, NOTE - note.shape[0]), (0, 0)))
    late_weights = jnp.concatenate([attend_weight.T, project_weight.T], axis=0).astype(LOW)
    late_weights = lax.dynamic_slice_in_dim(late_weights, low * late_rows, late_rows, 0)
    note = jnp.concatenate([note, late_weights], axis=0)
    notes = exchange([note] * shards)
    early_weights = jnp.concatenate(
        [
            lax.dynamic_slice_in_dim(w, low * rows, rows, 0).astype(LOW)
            for w in (expand_weight, contract_weight)
        ],
        axis=1,
    )
    early_weights = jnp.stack(exchange([early_weights] * shards))
    late_stacked, late_flipped = gather_group(jnp.stack([piece[NOTE:] for piece in notes]))

    *shares, modulate_low = local_call(
        modulation_kernel,
        ids,
        [(piece, False) for piece in notes] + [(modulate_weight.T, False)],
        [((latents, mod_share), FULL, False)] * shards + [((mod_share, D), LOW, False)],
        [],
        1,
        2 * shards * NOTE * D * mod_share,
        "modulation",
    )
    answers = [shares[0]] + [shift(shares[d], shards - d) for d in range(1, shards)]
    early_weights_stacked, early_weights_flipped = gather_group(early_weights)

    tokens_shape = (latents, LEN, D)
    qkv, probs, attended, branch, wq, wo, mod, bias_up, bias_down = local_call(
        attention_forward,
        ids,
        [(tokens, True), (late_stacked, False), (late_flipped, False)]
        + [(v, False) for v in (*answers, *notes)],
        [
            ((latents, LEN, 3 * D), LOW, True),
            ((latents, HEADS, LEN, LEN), LOW, True),
            (tokens_shape, LOW, True),
            (tokens_shape, FULL, True),
            ((3 * D, D), LOW, False),
            ((D, D), LOW, False),
            ((latents, 6, D), FULL, False),
            ((1, FF), FULL, False),
            ((1, D), FULL, False),
        ],
        [
            pltpu.VMEM((shards, late_width, D), FULL),
            pltpu.VMEM((BLOCK * LEN, D), LOW),
            pltpu.VMEM((BLOCK * LEN, D), LOW),
            pltpu.VMEM((shards, latents, mod_share), FULL),
            pltpu.VMEM((shards, NOTE, D), FULL),
        ],
        steps,
        latents * (2 * LEN * D * 4 * D + 4 * HEADS * LEN * LEN * PAIR) * 2,
        "attention_forward",
        after=(early_weights,),
    )
    early_shape = (GROUP // 2, shards, rows, 2 * FF // shards)
    block_output, grad_mixed, grad_mod_late, keep, send, sum_up, sum_down = local_call(
        perceptron,
        ids,
        [
            (tokens, True),
            (branch, True),
            (mod, True),
            (cotangent, True),
            (early_weights_stacked, False),
            (early_weights_flipped, False),
            (bias_up, False),
            (bias_down, False),
        ],
        [
            (tokens_shape, LOW, True),
            (tokens_shape, FULL, True),
            ((latents, 4, D), FULL, True),
            (early_shape, FULL, False),
            (early_shape, LOW, False),
            ((1, FF), FULL, False),
            ((1, D), FULL, False),
        ],
        [
            pltpu.VMEM((shards, D, 2 * FF // shards), LOW),
            pltpu.VMEM((D, FF), LOW),
            pltpu.VMEM((D, FF), LOW),
            pltpu.VMEM((BLOCK * LEN, FF), LOW),
            pltpu.VMEM((BLOCK * LEN, FF), FULL),
            pltpu.VMEM((D, FF), FULL),
            pltpu.VMEM((D, FF), FULL),
        ],
        steps,
        latents * 2 * LEN * D * FF * 6 * 2,
        "perceptron",
    )

    early_totals = sum_cores(keep, send, ids, "early_sum")
    grad_attended, total_project = local_call(
        project_backward,
        ids,
        [(mod, True), (attended, True), (grad_mixed, True), (wo, False)],
        [(tokens_shape, LOW, True), ((D, D), FULL, False)],
        [],
        steps,
        latents * 2 * LEN * D * D * 2,
        "project_backward",
    )
    arrived = exchange_chips(early_totals)
    early_chips = sum(piece.astype(FULL) for piece in arrived[1:]) + arrived[0]
    (grad_qkv,) = local_call(
        attention_backward,
        ids,
        [(qkv, True), (probs, True), (grad_attended, True)],
        [((latents, LEN, 3 * D), LOW, True)],
        [],
        steps,
        latents * 10 * HEADS * LEN * LEN * PAIR,
        "attention_backward",
        after=tuple(early_totals[1:]),
    )
    early = exchange([early_chips[d].astype(LOW) for d in range(shards)])
    early = sum(piece.astype(FULL) for piece in early[1:]) + early_chips[0]
    early = sum_rest(early.astype(LOW))
    late_shape = (GROUP // 2, shards, rows, late_width)
    tokens_grad, keep, send, extra = local_call(
        attend_backward,
        ids,
        [
            (tokens, True),
            (mod, True),
            (grad_mixed, True),
            (grad_qkv, True),
            (wq, False),
            (total_project, False),
            (grad_mod_late, False),
            (sum_up, False),
            (sum_down, False),
        ],
        [
            (tokens_shape, FULL, True),
            (late_shape, FULL, False),
            (late_shape, LOW, False),
            ((shards, NOTE, D), LOW, False),
        ],
        [
            pltpu.VMEM((D, 3 * D), FULL),
            pltpu.VMEM((latents, 2, D), FULL),
            pltpu.VMEM((NOTE, D), FULL),
        ],
        steps,
        latents * 2 * LEN * D * 6 * D * 2,
        "attend_backward",
        after=(early_chips,),
    )
    early_stacked, early_flipped = gather_group(early)

    arrived = exchange_chips(sum_cores(keep, send, ids, "late_sum"))
    outgoing = local_call(
        late_pieces,
        ids,
        [(v, False) for v in (*arrived, extra)],
        [((NOTE + rows, D), LOW, False)] * shards,
        [],
        1,
        4 * shards * rows * late_width,
        "late_pieces",
    )
    group_latents = shards * latents
    unit = (-(-mod_share // D) + 1) * group_latents + 16
    payload, *shares = local_call(
        partial(combine, shards, latents),
        ids,
        [(v, False) for v in (*exchange(outgoing), *notes, modulate_low)],
        [((rows + unit, D), LOW, False)] + [((latents, D), FULL, False)] * shards,
        [pltpu.VMEM((unit, D), FULL)],
        1,
        2 * shards * NOTE * D * mod_share,
        "combine",
    )
    if lax.axis_size("rep") > GROUP:
        late, others = sum_rest(payload[:rows]), payload[rows:]
        for bit in range(3, lax.axis_size("rep").bit_length() - 1):
            others = jnp.concatenate([others, flip(others, 1 << bit)], axis=0)
        payload = jnp.concatenate([late, others], axis=0)
    late_stacked, late_flipped = gather_group(payload)

    grad_cond_low = shares[0]
    for d in range(1, shards):
        grad_cond_low = grad_cond_low + shift(shares[d], shards - d)
    condition_grad = silu_back(grad_cond_low)[0]

    def as_held(values):
        return [v.T if turned else v for v, turned in zip(values, TURNED)]

    masters = as_held(
        [attend_weight, project_weight, expand_weight, contract_weight, modulate_weight]
    )
    moments = as_held(
        [attend_moment, project_moment, expand_moment, contract_moment, modulate_moment]
    )
    shapes = [m.shape for m in masters]
    widths = [whole // shards for whole in COLUMNS]
    slot_width = max(stop - start for start, stop in slot_spans(widths))
    piece_rows = 128 * len(TRIANGLE) // shards
    results = local_call(
        partial(momenta_kernel, group_latents),
        ids,
        [(v, False) for v in (late_stacked, late_flipped, early_stacked, early_flipped, *moments)],
        [(shape, FULL, False) for shape in shapes * 2]
        + [
            ((shards, piece_rows, 128), FULL, False),
            ((slot_width, D), FULL, False),
            ((8, D), FULL, False),
        ],
        [pltpu.VMEM(shape, FULL) for shape in shapes]
        + [pltpu.VMEM((D, D), FULL), pltpu.VMEM((128 * len(TRIANGLE), 128), FULL)],
        1,
        6 * D * D * D,
        "momenta",
    )
    gradients, momenta = as_held(results[0:5]), as_held(results[5:10])
    gram, columns, bias_block = results[10:13]
    piece = sum(exchange([gram[d] for d in range(shards)]))
    (answer,) = local_call(
        polynomial_kernel,
        ids,
        [(p, False) for p in exchange([piece] * shards)] + [(columns, False)],
        [((slot_width, D), LOW, False)],
        [pltpu.VMEM((128 * len(TRIANGLE), 128), FULL), pltpu.VMEM((D, D), FULL)],
        1,
        2 * 3 * 18 * D * D * D,
        "polynomial",
        after=(condition_grad,),
    )
    updated = local_call(
        update_kernel,
        ids,
        [(v, False) for v in (*gather_group(answer), *masters)],
        [(shape, FULL, False) for shape in shapes],
        [pltpu.VMEM((GROUP, slot_width, D), LOW)],
        1,
        2 * D * sum(widths),
        "update",
    )
    updated = as_held(updated)

    bias_gradient = bias_block.reshape(-1)[:bias_share]
    bias_momentum = BETA_ONE * bias_first + (1.0 - BETA_ONE) * bias_gradient
    bias_variance = BETA_TWO * bias_second + (1.0 - BETA_TWO) * bias_gradient * bias_gradient
    corrected_first = bias_momentum / (1.0 - BETA_ONE**STEP)
    corrected_second = bias_variance / (1.0 - BETA_TWO**STEP)
    bias_updated = biases * (1.0 - ADAM_RATE * WEIGHT_DECAY) - ADAM_RATE * corrected_first / (
        jnp.sqrt(corrected_second) + ADAM_EPSILON
    )
    return (
        block_output,
        tokens_grad,
        condition_grad,
        *gradients,
        *momenta,
        *updated,
        bias_gradient,
        bias_momentum,
        bias_variance,
        bias_updated,
    )


def solution(mesh):
    rows = P(("shard", "rep"), None, None)
    vectors = P(("shard", "rep"), None)
    columns = P(None, "shard")
    flat = P("shard")
    return jax.shard_map(
        per_device,
        mesh=mesh,
        in_specs=(rows, vectors, rows) + (columns,) * 5 + (flat,) + (columns,) * 5 + (flat,) * 2,
        out_specs=(rows, rows, vectors) + (columns,) * 15 + (flat,) * 4,
        check_vma=False,
    )
```

```python
from functools import partial
import math

import jax
import jax.numpy as jnp
from jax import lax
from jax.experimental import pallas as pl
from jax.experimental.pallas import tpu as pltpu
from jax.sharding import PartitionSpec as P

D = 384
HEADS = 6
HEAD = 64
FF = 1536
LEN = 256
NS_ITERS = 5
STEP = 10
PAIR = 2 * HEAD
CHUNK = 512
GROUP = 8
BLOCK = 2
BIAS_LEN = 6 * D + FF + D
NOTE = 16
GRANTS = {
    "attention_forward": 40,
    "perceptron": 48,
    "project_backward": 24,
    "attention_backward": 32,
    "attend_backward": 40,
    "momenta": 32,
    "polynomial": 20,
    "update": 24,
}

POLY_LINEAR = 3.4445
POLY_CUBIC = -4.775
POLY_QUINTIC = 2.0315
MOMENTUM = 0.95
MUON_RATE = 0.4
WEIGHT_DECAY = 0.01
ADAM_RATE = 0.1
BETA_ONE = 0.9
BETA_TWO = 0.999
ADAM_EPSILON = 1e-08
GELU_SLOPE = math.sqrt(2.0 / math.pi)
GELU_CUBIC = 0.044715

LOW = jnp.bfloat16
FULL = jnp.float32

SLOTS = ((4, 0), (4, 1), (0, 0), (2, 0), (2, 1), (3, 0), (3, 1), (1, 0))


def shift(value, distance):
    size = lax.axis_size("shard")
    return lax.ppermute(value, "shard", [(i, (i + distance) % size) for i in range(size)])


def flip(value, mask):
    size = lax.axis_size("rep")
    return lax.ppermute(value, "rep", [(i, i ^ mask) for i in range(size)])


def exchange(pieces):
    return [pieces[0]] + [shift(pieces[d], d) for d in range(1, len(pieces))]


def gather_chips(value):
    return [value] + [flip(value, 2 * t) for t in range(1, GROUP // 2)]


def gather_group(value):
    stacked = jnp.stack(gather_chips(value))
    return stacked, flip(stacked, 1)


def sum_cores(keep, send, ids, name, after):
    received = flip(send, 1)
    shape = keep.shape[1:]
    return local_call(
        split_sum,
        ids,
        [(keep, False), (received, False)],
        [(shape, FULL, False)] + [(shape, LOW, False)] * (keep.shape[0] - 1),
        [],
        1,
        keep.size,
        name,
        after=after,
    )


def exchange_chips(totals):
    return [totals[0]] + [flip(totals[t], 2 * t) for t in range(1, GROUP // 2)]


def sum_rest(value):
    for bit in range(3, lax.axis_size("rep").bit_length() - 1):
        value = (value.astype(FULL) + flip(value, 1 << bit).astype(FULL)).astype(LOW)
    return value


def dot(left, right):
    return lax.dot_general(left, right, (((1,), (0,)), ((), ())), preferred_element_type=FULL)


def dot_nt(left, right):
    return lax.dot_general(left, right, (((1,), (1,)), ((), ())), preferred_element_type=FULL)


def dot_tn(left, right):
    return lax.dot_general(left, right, (((0,), (0,)), ((), ())), preferred_element_type=FULL)


def split_low(value):
    high = value.astype(LOW)
    return high, (value - high.astype(FULL)).astype(LOW)


def dot_split(left, right, product=dot):
    return product(left[0], right[0]) + (product(left[0], right[1]) + product(left[1], right[0]))


def normalize(values):
    centered = values - jnp.mean(values, -1, keepdims=True)
    inverse_spread = lax.rsqrt(jnp.mean(centered * centered, -1, keepdims=True) + 1e-06)
    return centered * inverse_spread, inverse_spread


def normalize_back(upstream, normed, inverse_spread):
    return inverse_spread * (
        upstream
        - jnp.mean(upstream, -1, keepdims=True)
        - normed * jnp.mean(upstream * normed, -1, keepdims=True)
    )


def local_call(kernel, ids, inputs, outputs, scratch, steps, flops, name, after=()):
    def run(*refs):
        kernel(*refs[: 1 + len(inputs)], *refs[1 + len(inputs) + len(after) :])

    def spec(shape, blocked):
        zeros = (0,) * (len(shape) - 1)
        if blocked == "low":
            return pl.BlockSpec((shape[0] // GROUP,) + tuple(shape[1:]), lambda i, ids: (ids[1],) + zeros)
        if blocked:
            block = (shape[0] // steps,) + tuple(shape[1:])
            return pl.BlockSpec(block, lambda i, _: (i,) + zeros)
        return pl.BlockSpec(tuple(shape), lambda i, _: (0,) + zeros)

    moved = sum(v.size * v.dtype.itemsize for v, _ in inputs)
    moved += sum(math.prod(shape) * jnp.dtype(kind).itemsize for shape, kind, _ in outputs)
    return pl.pallas_call(
        run,
        grid_spec=pltpu.PrefetchScalarGridSpec(
            num_scalar_prefetch=1,
            grid=(steps,),
            in_specs=[spec(v.shape, blocked) for v, blocked in inputs]
            + [pl.BlockSpec(memory_space=pl.ANY) for _ in after],
            out_specs=[spec(shape, blocked) for shape, _, blocked in outputs],
            scratch_shapes=scratch,
        ),
        out_shape=[jax.ShapeDtypeStruct(shape, kind) for shape, kind, _ in outputs],
        compiler_params=pltpu.CompilerParams(
            dimension_semantics=("arbitrary",), vmem_limit_bytes=GRANTS.get(name, 16) * 1024 * 1024
        ),
        cost_estimate=pl.CostEstimate(flops=flops, bytes_accessed=moved, transcendentals=0),
        name=name,
    )(ids, *[v for v, _ in inputs], *after)


def pieces_of(ids, stacked, flipped):
    for t in range(GROUP // 2):
        for bit, blocks in enumerate((stacked, flipped)):
            yield ids[1] ^ (2 * t + bit), blocks.at[t]


def rows_at(place, rows):
    return pl.ds(pl.multiple_of(place * rows, rows), rows)


def turn(value):
    filled = value.shape[1]
    extra = -filled % 128
    if extra:
        value = jnp.concatenate([value, jnp.zeros((value.shape[0], extra), value.dtype)], axis=1)
    return value.T[:filled]


def head_masks(values):
    lane = lax.broadcasted_iota(jnp.int32, values.shape, 1) % PAIR
    zero = jnp.zeros_like(values)
    return (
        jnp.where(lane < HEAD, values, zero).astype(LOW),
        jnp.where(lane < HEAD, zero, values).astype(LOW),
    )


def split_sum(ids, keep, received, own, *others):
    own[...] = keep[0] + received[0].astype(FULL)
    for t, other in enumerate(others):
        other[...] = (keep[t + 1] + received[t + 1].astype(FULL)).astype(LOW)


def modulation_kernel(ids, *refs):
    shards = refs[-1].shape[0]
    notes, weight, answers, weight_low, stacked = (
        refs[:shards], refs[shards], refs[shards + 1 : -2], refs[-2], refs[-1],
    )
    low = weight[...].astype(LOW)
    weight_low[...] = low
    for d, (note, answer) in enumerate(zip(notes, answers)):
        answer[...] = dot_nt(note[:NOTE, :], low)[: answer.shape[0]]
        stacked[d] = note[NOTE:, :]


def pack(ids, *refs):
    start = 0
    for weight in refs[:-1]:
        width = weight.shape[1]
        refs[-1][:, start : start + width] = weight[...].astype(LOW)
        start = start + width


def stack(ids, *refs):
    for t, block in enumerate(refs[:-1]):
        refs[-1][t] = block[...]


def attention_forward(
    ids, tokens, stacked, flipped, *refs,
):
    shards = (len(refs) - 16) // 2
    answers, notes = refs[:shards], refs[shards : 2 * shards]
    (
        qkv, probs, attended, branch, wq, wo, mod_all, bias_up, bias_down,
        ordered, query_a, query_b, mod_parts, bias_parts, wq_plain, wo_plain,
    ) = refs[2 * shards :]
    rows = ordered.shape[1] // GROUP
    wide, narrow = 3 * D // shards, D // shards

    @pl.when(pl.program_id(0) == 0)
    def _():
        for place, block in pieces_of(ids, stacked, flipped):
            for d in range(shards):
                source = lax.rem(ids[0] - d + shards, shards)
                ordered[source, rows_at(place, rows), :] = block[d].astype(ordered.dtype)
        for s in range(shards):
            wq[s * wide : (s + 1) * wide, :] = ordered[s, :wide, :].astype(LOW)
            wo[s * narrow : (s + 1) * narrow, :] = ordered[s, wide:, :].astype(LOW)
        wq_plain[...] = wq[...].T
        wo_plain[...] = wo[...].T
        for d in range(shards):
            mod_parts[lax.rem(ids[0] + d, shards)] = answers[d][...]
            bias_parts[lax.rem(ids[0] - d + shards, shards)] = notes[d][:NOTE, :].astype(FULL)
        latents = mod_all.shape[0]
        share = BIAS_LEN // shards
        pieces = []
        for s in range(shards):
            for b in range(-(-share // D)):
                row = bias_parts[s, latents + b : latents + b + 1, :]
                pieces.append(row[:, : min(D, share - b * D)])
        bias = jnp.concatenate(pieces, axis=1)
        whole = jnp.concatenate([mod_parts[s] for s in range(shards)], axis=1) + bias[:, : 6 * D]
        for latent in range(latents):
            for b in range(6):
                mod_all[latent, b : b + 1, :] = whole[latent : latent + 1, b * D : (b + 1) * D]
        bias_up[...] = bias[:, 6 * D : 6 * D + FF]
        bias_down[...] = bias[:, 6 * D + FF :]

    count = tokens.shape[0]
    mod = mod_all[pl.ds(pl.program_id(0) * count, count)]
    normed, _ = normalize(tokens[...].astype(FULL))
    hidden = normed * (1.0 + mod[:, 1:2, :]) + mod[:, 0:1, :]
    hidden = hidden.reshape(count * LEN, D).astype(LOW)
    queries = dot(hidden, wq_plain[:, :D])
    masked_a, masked_b = head_masks(queries)
    query_a[...] = masked_a
    query_b[...] = masked_b
    qkv[:, :, :D] = queries.astype(LOW).reshape(count, LEN, D)
    qkv[:, :, D:] = dot(hidden, wq_plain[:, D:]).astype(LOW).reshape(count, LEN, 2 * D)
    for latent in range(count):
        span = slice(latent * LEN, (latent + 1) * LEN)
        for pair in range(HEADS // 2):
            lanes = slice(pair * PAIR, (pair + 1) * PAIR)
            keys = qkv[latent, :, D + pair * PAIR : D + (pair + 1) * PAIR]
            values = qkv[latent, :, 2 * D + pair * PAIR : 2 * D + (pair + 1) * PAIR].T
            results = []
            for member, masked in enumerate((query_a, query_b)):
                scores = dot_nt(keys, masked[span, lanes]) * (HEAD ** (-0.5) / math.log(2.0))
                top = jnp.max(scores, 0, keepdims=True)
                raised = jnp.exp2(scores - top)
                share = (raised * (1.0 / jnp.sum(raised, 0, keepdims=True))).astype(LOW)
                probs[latent, 2 * pair + member] = share
                results.append(dot(values[member * HEAD : (member + 1) * HEAD], share))
            attended[latent, :, lanes] = jnp.concatenate(results, axis=0).T.astype(LOW)
    branch[...] = dot(attended[...].reshape(count * LEN, D), wo_plain[...]).reshape(count, LEN, D)


def perceptron(
    ids, tokens, branch, mod, cotangent, stacked, flipped, bias_up, bias_down,
    out, grad_mixed, grad_mod, keep, send, sum_up, sum_down,
    ordered, wu, wd, wu_turned, wd_turned, act, slope, total_up, total_down,
):
    shards = ordered.shape[0]
    rows = D // GROUP
    width = FF // shards
    step = pl.program_id(0)

    @pl.when(step == 0)
    def _():
        for place, block in pieces_of(ids, stacked, flipped):
            for d in range(shards):
                source = lax.rem(ids[0] - d + shards, shards)
                ordered[source, rows_at(place, rows), :] = block[d]
        for i in range(GROUP):
            span = slice(i * rows, (i + 1) * rows)
            pieces = [ordered[s, span, :] for s in range(shards)]
            wu[span, :] = jnp.concatenate([p[:, :width] for p in pieces], axis=1)
            wd[span, :] = jnp.concatenate([p[:, width:] for p in pieces], axis=1)
        wu_turned[...] = wu[...].T
        wd_turned[...] = wd[...].T
        total_up[...] = jnp.zeros_like(total_up)
        total_down[...] = jnp.zeros_like(total_down)
        sum_up[...] = jnp.zeros_like(sum_up)
        sum_down[...] = jnp.zeros_like(sum_down)

    count = tokens.shape[0]
    flat = count * LEN
    branch_out = branch[...]
    mixed = tokens[...].astype(FULL) + mod[:, 2:3, :] * branch_out
    normed, inverse_spread = normalize(mixed)
    hidden = (normed * (1.0 + mod[:, 4:5, :]) + mod[:, 3:4, :]).reshape(flat, D).astype(LOW)
    result = jnp.zeros((flat, D), FULL)
    for start in range(0, FF, CHUNK):
        span = slice(start, start + CHUNK)
        u = dot(hidden, wu[:, span]) + bias_up[:, span]
        square = u * u
        bent = jnp.tanh(GELU_SLOPE * u * (1.0 + GELU_CUBIC * square))
        half = 0.5 * (1.0 + bent)
        act_low = (u * half).astype(LOW)
        act[:, span] = act_low
        slope[:, span] = half + (0.5 * GELU_SLOPE) * u * (1.0 - bent * bent) * (
            1.0 + 3.0 * GELU_CUBIC * square
        )
        result = result + dot(act_low, wd_turned[span, :])
    result = (result + bias_down[...]).reshape(count, LEN, D)
    gate = mod[:, 5:6, :]
    out[...] = (mixed + gate * result).astype(LOW)
    upstream = cotangent[...].astype(FULL)
    grad_mod[:, 3:4, :] = jnp.sum(upstream * result, axis=1, keepdims=True)
    grad_result = (gate * upstream).reshape(flat, D).astype(LOW)
    sum_down[...] += jnp.sum(grad_result.astype(FULL), axis=0, keepdims=True)
    grad_hidden = jnp.zeros((flat, D), FULL)
    for start in range(0, FF, CHUNK):
        span = slice(start, start + CHUNK)
        grad_u = (dot(grad_result, wd[:, span]) * slope[:, span]).astype(LOW)
        sum_up[:, span] += jnp.sum(grad_u.astype(FULL), axis=0, keepdims=True)
        total_down[:, span] += dot_tn(grad_result, act[:, span])
        total_up[:, span] += dot_tn(hidden, grad_u)
        grad_hidden = grad_hidden + dot(grad_u, wu_turned[span, :])
    grad_hidden = grad_hidden.reshape(count, LEN, D)
    grad_mod[:, 1:2, :] = jnp.sum(grad_hidden, axis=1, keepdims=True)
    grad_mod[:, 2:3, :] = jnp.sum(grad_hidden * normed, axis=1, keepdims=True)
    back = upstream + normalize_back(
        grad_hidden * (1.0 + mod[:, 4:5, :]), normed, inverse_spread
    )
    grad_mixed[...] = back
    grad_mod[:, 0:1, :] = jnp.sum(back * branch_out, axis=1, keepdims=True)

    @pl.when(step == pl.num_programs(0) - 1)
    def _():
        shard, low = ids[0], ids[1]
        for j in range(GROUP):
            span = pl.ds(pl.multiple_of((low ^ j) * rows, rows), rows)
            for s in range(shards):
                d = lax.rem(s - shard + shards, shards)
                lanes = slice(s * width, (s + 1) * width)
                piece = jnp.concatenate([total_up[span, lanes], total_down[span, lanes]], axis=1)
                if j & 1:
                    send[j // 2, d] = piece.astype(LOW)
                else:
                    keep[j // 2, d] = piece


def project_backward(
    ids, mod, attended, grad_mixed, wo,
    grad_attended, total_project,
):
    @pl.when(pl.program_id(0) == 0)
    def _():
        total_project[...] = jnp.zeros_like(total_project)

    count = attended.shape[0]
    flat = count * LEN
    grad_branch = (mod[:, 2:3, :] * grad_mixed[...]).reshape(flat, D).astype(LOW)
    total_project[...] += dot_tn(attended[...].reshape(flat, D), grad_branch)
    grad_attended[...] = dot(grad_branch, wo[...]).astype(LOW).reshape(count, LEN, D)


def attention_backward(ids, qkv, probs, grad_attended, grad_qkv):
    mask = lax.broadcasted_iota(jnp.int32, (LEN, PAIR), 1) < HEAD
    scale = HEAD ** (-0.5)
    for latent in range(qkv.shape[0]):
        for pair in range(HEADS // 2):
            lanes = slice(pair * PAIR, (pair + 1) * PAIR)
            key_lanes = slice(D + pair * PAIR, D + (pair + 1) * PAIR)
            value_lanes = slice(2 * D + pair * PAIR, 2 * D + (pair + 1) * PAIR)
            queries = qkv[latent, :, lanes]
            keys = qkv[latent, :, key_lanes].T
            values = qkv[latent, :, value_lanes]
            upper = grad_attended[latent, :, lanes]
            masked = head_masks(upper.astype(FULL))
            by_query, by_key, by_value = [], [], []
            for member in range(2):
                share = probs[latent, 2 * pair + member]
                weight = share.astype(FULL)
                grad_share = dot_nt(values, masked[member])
                product = weight * grad_share
                grad_scores = (
                    product - weight * jnp.sum(product, 0, keepdims=True)
                ).astype(LOW)
                by_query.append(dot(keys[member * HEAD : (member + 1) * HEAD], grad_scores))
                by_key.append(dot(grad_scores, queries))
                by_value.append(dot(share, upper))
            merged = jnp.concatenate(by_query, axis=0).T * scale
            grad_qkv[latent, :, lanes] = merged.astype(LOW)
            merged = jnp.where(mask, by_key[0], by_key[1]) * scale
            grad_qkv[latent, :, key_lanes] = merged.astype(LOW)
            merged = jnp.where(mask, by_value[0], by_value[1])
            grad_qkv[latent, :, value_lanes] = merged.astype(LOW)


def attend_backward(
    ids, tokens, mod, grad_mixed, grad_qkv, wq, total_project, grad_mod_late, sum_up, sum_down,
    grad_tokens, keep, send, extra,
    total_attend, grad_mod, extra_rows,
):
    rows = D // GROUP
    shards = keep.shape[1]
    step = pl.program_id(0)

    @pl.when(step == 0)
    def _():
        total_attend[...] = jnp.zeros_like(total_attend)

    count = tokens.shape[0]
    flat = count * LEN
    normed, inverse_spread = normalize(tokens[...].astype(FULL))
    hidden = (normed * (1.0 + mod[:, 1:2, :]) + mod[:, 0:1, :]).reshape(flat, D).astype(LOW)
    grad_low = grad_qkv[...].reshape(flat, 3 * D)
    total_attend[...] += dot_tn(hidden, grad_low)
    grad_hidden = dot(grad_low, wq[...]).reshape(count, LEN, D)
    mine = pl.ds(step * count, count)
    grad_mod[mine, 0:1, :] = jnp.sum(grad_hidden, axis=1, keepdims=True)
    grad_mod[mine, 1:2, :] = jnp.sum(grad_hidden * normed, axis=1, keepdims=True)
    grad_tokens[...] = grad_mixed[...] + normalize_back(
        grad_hidden * (1.0 + mod[:, 1:2, :]), normed, inverse_spread
    )

    @pl.when(step == pl.num_programs(0) - 1)
    def _():
        shard, low = ids[0], ids[1]
        wide, narrow = 3 * D // shards, D // shards
        for j in range(GROUP):
            span = rows_at(low ^ j, rows)
            whole_attend, whole_project = total_attend[span, :], total_project[span, :]
            for s in range(shards):
                d = lax.rem(s - shard + shards, shards)
                piece = jnp.concatenate(
                    [
                        whole_attend[:, s * wide : (s + 1) * wide],
                        whole_project[:, s * narrow : (s + 1) * narrow],
                    ],
                    axis=1,
                )
                if j & 1:
                    send[j // 2, d] = piece.astype(LOW)
                else:
                    keep[j // 2, d] = piece
        latents = grad_mod.shape[0]
        columns = [grad_mod[:, b, :] for b in range(2)] + [grad_mod_late[:, b, :] for b in range(4)]
        whole = jnp.concatenate(columns, axis=1).astype(LOW).astype(FULL)
        sums = jnp.sum(whole, axis=0, keepdims=True)
        sums = jnp.concatenate([sums, sum_up[...], sum_down[...]], axis=1)
        mod_share, bias_share = 6 * D // shards, BIAS_LEN // shards
        blocks, lines = -(-mod_share // D), -(-bias_share // D)

        def padded(values, start, stop):
            part = values[:, start : min(start + D, stop)]
            if part.shape[1] < D:
                rest = jnp.zeros((part.shape[0], D - part.shape[1]), FULL)
                part = jnp.concatenate([part, rest], axis=1)
            return part

        extra_rows[...] = jnp.zeros_like(extra_rows)
        for s in range(shards):
            for b in range(blocks):
                extra_rows[b * latents : (b + 1) * latents, :] = padded(
                    whole, s * mod_share + b * D, (s + 1) * mod_share
                )
            for b in range(lines):
                row = padded(sums, s * bias_share + b * D, (s + 1) * bias_share)
                high = row.astype(LOW).astype(FULL)
                place = blocks * latents + b
                extra_rows[place : place + 1, :] = high
                extra_rows[place + lines : place + lines + 1, :] = row - high
            extra[lax.rem(s - shard + shards, shards)] = extra_rows[...].astype(LOW)


def late_pieces(ids, own, first, second, third, extra, *pieces):
    total = own[...]
    for received in (first, second, third):
        total = total + received[...].astype(FULL)
    for d, piece in enumerate(pieces):
        piece[:NOTE, :] = extra[d]
        if total.shape[2] < D:
            piece[NOTE:, :] = jnp.zeros((total.shape[1], D), LOW)
        piece[NOTE:, : total.shape[2]] = total[d].astype(LOW)


def combine(shards, latents, ids, *refs):
    incoming, notes, weight, payload = (
        refs[:shards], refs[shards : 2 * shards], refs[2 * shards], refs[2 * shards + 1],
    )
    answers, rows_ref = refs[2 * shards + 2 : -1], refs[-1]
    rows = D // GROUP
    mod_share, bias_share = 6 * D // shards, BIAS_LEN // shards
    blocks, lines = -(-mod_share // D), -(-bias_share // D)
    total = jnp.zeros((rows, D), FULL)
    bias = jnp.zeros((NOTE, D), FULL)
    for d in range(shards):
        total = total + incoming[d][NOTE:, :].astype(FULL)
        extra = incoming[d][:NOTE, :].astype(FULL)
        bias = bias + extra
        for b in range(blocks):
            start = (b * shards + d) * latents
            rows_ref[start : start + latents, :] = extra[b * latents : (b + 1) * latents]
        start = (blocks * shards + d) * latents
        rows_ref[start : start + latents, :] = notes[d][:NOTE, :].astype(FULL)[:latents]
    payload[:rows, :] = total.astype(LOW)
    count = (blocks + 1) * shards * latents
    start = blocks * latents
    bias = bias[start : start + lines] + bias[start + lines : start + 2 * lines]
    high = bias.astype(LOW).astype(FULL)
    rows_ref[count:, :] = jnp.zeros((16, D), FULL)
    rows_ref[count : count + lines, :] = high
    rows_ref[count + 8 : count + 8 + lines, :] = bias - high
    payload[rows:, :] = rows_ref[...].astype(LOW)
    for d, answer in enumerate(answers):
        result = jnp.zeros((NOTE, D), FULL)
        for b in range(blocks):
            filled = min(D, mod_share - b * D)
            product = dot(incoming[d][:NOTE, :filled], weight[b * D : b * D + filled, :])
            result = result + shifted(product, b * latents)
        answer[...] = result[:latents]


def shifted(values, count):
    if count == 0:
        return values
    return jnp.concatenate([values[count:], values[:count]], axis=0)


COLUMNS = (3 * D, D, FF, FF, 6 * D)
TURNED = (True, True, False, False, True)
TRIANGLE = ((0, 0), (0, 1), (0, 2), (1, 1), (1, 2), (2, 2))


def slot_spans(widths):
    counts = [sum(1 for m, _ in SLOTS if m == number) for number in range(len(widths))]
    return [
        (part * (widths[m] // counts[m]), (part + 1) * (widths[m] // counts[m]))
        for m, part in SLOTS
    ]


def momenta_kernel(latents, ids, late, late_flipped, early, early_flipped, *refs):
    moments, grads, momenta = refs[0:5], refs[5:10], refs[10:15]
    gram, columns, bias = refs[15:18]
    mixed = refs[18:23]
    late_whole, flat_gram = refs[23:25]
    low = ids[1]
    rows = D // GROUP
    shards = gram.shape[0]
    widths = [whole // shards for whole in COLUMNS]
    blocks = -(-widths[4] // D)
    unit = (blocks + 1) * latents + 16
    starts = range(rows, late.shape[1], unit)
    late_width = widths[0] + widths[1]
    for place, block in pieces_of(ids, late, late_flipped):
        late_whole[rows_at(place, rows), :] = block[:rows, :].astype(FULL)
    for place, block in pieces_of(ids, early, early_flipped):
        piece = block[...].astype(FULL)
        grads[2][rows_at(place, rows), :] = piece[:, : widths[2]]
        grads[3][rows_at(place, rows), :] = piece[:, widths[2] :]
    turned = turn(late_whole[...])
    grads[0][...] = turned[: widths[0]]
    grads[1][...] = turned[widths[0] : late_width]
    parts = [
        ref[t, start : start + unit, :]
        for ref in (late, late_flipped)
        for t in range(GROUP // 2)
        for start in starts
    ]
    cond = jnp.concatenate([p[blocks * latents : (blocks + 1) * latents] for p in parts], axis=0)
    for block in range(blocks):
        rising = jnp.concatenate(
            [p[block * latents : (block + 1) * latents] for p in parts], axis=0
        )
        filled = min(D, widths[4] - block * D)
        grads[4][block * D : block * D + filled, :] = dot_tn(rising, cond)[:filled]
    total = jnp.zeros((16, D), FULL)
    for part in parts:
        total = total + part[(blocks + 1) * latents :].astype(FULL)
    bias[...] = total[:8] + total[8:]
    for number in range(5):
        grad = grads[number][...]
        moment = MOMENTUM * moments[number][...] + grad
        momenta[number][...] = moment
        mixed[number][...] = grad + MOMENTUM * moment
    for number in range(5):
        owners = [k for k, (m, _) in enumerate(SLOTS) if m == number]
        condition = low == owners[0]
        for owner in owners[1:]:
            condition = condition | (low == owner)

        @pl.when(condition)
        def _(number=number):
            parts = split_low(mixed[number][...])
            whole = dot_split(parts, parts, dot_tn if TURNED[number] else dot_nt)
            for place, (a, b) in enumerate(TRIANGLE):
                flat_gram[place * 128 : (place + 1) * 128, :] = whole[
                    a * 128 : (a + 1) * 128, b * 128 : (b + 1) * 128
                ]

    size = gram.shape[1]
    for s in range(shards):
        gram[lax.rem(s - ids[0] + shards, shards)] = flat_gram[s * size : (s + 1) * size, :]
    spans = slot_spans(widths)
    for k, ((number, _), (start, stop)) in enumerate(zip(SLOTS, spans)):

        @pl.when(low == k)
        def _(number=number, start=start, stop=stop):
            filled = stop - start
            if TURNED[number]:
                columns[:filled, :] = mixed[number][start:stop, :]
            else:
                columns[:filled, :] = turn(mixed[number][...])[start:stop]
            if filled < columns.shape[0]:
                columns[filled:, :] = jnp.zeros((columns.shape[0] - filled, D), FULL)


def polynomial_kernel(ids, *refs):
    shards = len(refs) - 4
    pieces, columns, answer, flat_gram, gram_ref = refs[:shards], *refs[shards:]
    size = pieces[0].shape[0]
    for d in range(shards):
        source = lax.rem(ids[0] - d + shards, shards)
        flat_gram[rows_at(source, size), :] = pieces[d][...]
    for place, (a, b) in enumerate(TRIANGLE):
        block = flat_gram[place * 128 : (place + 1) * 128, :]
        gram_ref[a * 128 : (a + 1) * 128, b * 128 : (b + 1) * 128] = block
        if a != b:
            gram_ref[b * 128 : (b + 1) * 128, a * 128 : (a + 1) * 128] = block.T
    gram = gram_ref[...]
    diagonal = lax.broadcasted_iota(jnp.int32, (D, D), 0) == lax.broadcasted_iota(
        jnp.int32, (D, D), 1
    )
    trace = jnp.sum(jnp.where(diagonal, gram, 0.0))
    scale = 1.0 / (jnp.sqrt(jnp.full((1, 1), trace)) + 1e-07)
    gram = (gram * scale) * scale
    product = jnp.where(diagonal, 1.0, 0.0)
    for step in range(NS_ITERS):
        mixing = POLY_CUBIC * gram + POLY_QUINTIC * dot_deep(left_deep(gram), right_deep(gram))
        mixing_deep = left_deep(mixing)
        if step == 0:
            half = POLY_LINEAR * gram + dot_deep(mixing_deep, right_deep(gram))
            product = POLY_LINEAR * product + mixing
        elif step + 1 < NS_ITERS:
            both = jnp.concatenate([gram, product], axis=1)
            both = POLY_LINEAR * both + dot_deep(mixing_deep, right_deep(both))
            half, product = both[:, :D], both[:, D:]
        else:
            product = POLY_LINEAR * product + dot_deep(mixing_deep, right_deep(product))
        if step + 1 < NS_ITERS:
            gram = POLY_LINEAR * half + dot_deep(mixing_deep, right_deep(half))
    answer[...] = dot_deep(left_deep(columns[...] * scale), right_deep(product)).astype(LOW)


def left_deep(value):
    high, rest = split_low(value)
    return jnp.concatenate([high, rest, high], axis=1)


def right_deep(value):
    high, rest = split_low(value)
    return jnp.concatenate([high, high, rest], axis=0)


def dot_deep(left, right):
    return dot(left, right)


def update_kernel(ids, answers, answers_flipped, *refs):
    masters, updated, ordered = refs[:5], refs[5:10], refs[10]
    for place, block in pieces_of(ids, answers, answers_flipped):
        ordered[place] = block[...]
    widths = [m.shape[0 if turned else 1] for m, turned in zip(masters, TURNED)]
    spans = slot_spans(widths)
    for number in range(5):
        factor = MUON_RATE * 0.2 * math.sqrt(COLUMNS[number])
        mine = [k for k, (m, _) in enumerate(SLOTS) if m == number]
        if TURNED[number]:
            for k in mine:
                start, stop = spans[k]
                updated[number][start:stop, :] = masters[number][start:stop, :] * (
                    1.0 - MUON_RATE * WEIGHT_DECAY
                ) - factor * ordered[k, : stop - start, :].astype(FULL)
        else:
            direction = jnp.concatenate(
                [ordered[k, : spans[k][1] - spans[k][0], :].astype(FULL) for k in mine], axis=0
            )
            updated[number][...] = masters[number][...] * (
                1.0 - MUON_RATE * WEIGHT_DECAY
            ) - factor * direction.T


def whole_rows(vector):
    rows = -(-vector.shape[-1] // D)
    padded = jnp.pad(vector, [(0, 0)] * (vector.ndim - 1) + [(0, rows * D - vector.shape[-1])])
    return padded.reshape(vector.shape[:-1] + (rows, D))


def per_device(
    tokens,
    condition,
    cotangent,
    attend_weight,
    project_weight,
    expand_weight,
    contract_weight,
    modulate_weight,
    biases,
    attend_moment,
    project_moment,
    expand_moment,
    contract_moment,
    modulate_moment,
    bias_first,
    bias_second,
):
    latents = tokens.shape[0]
    steps = latents // BLOCK
    shards = lax.axis_size("shard")
    shard = lax.axis_index("shard")
    low = lax.axis_index("rep") % GROUP
    ids = jnp.stack([shard, low]).astype(jnp.int32)
    rows = D // GROUP
    bias_share = biases.shape[0]
    mod_share = modulate_weight.shape[1]
    late_width = 4 * D // shards
    late_rows = late_width // GROUP

    silu_value, silu_back = jax.vjp(jax.nn.silu, condition.astype(FULL))
    note = jnp.concatenate([silu_value.astype(LOW), whole_rows(biases.astype(LOW))], axis=0)
    note = jnp.pad(note, ((0, NOTE - note.shape[0]), (0, 0)))
    late_weights = jnp.concatenate([attend_weight.T, project_weight.T], axis=0).astype(LOW)
    late_weights = lax.dynamic_slice_in_dim(late_weights, low * late_rows, late_rows, 0)
    note = jnp.concatenate([note, late_weights], axis=0)
    notes = exchange([note] * shards)

    *shares, modulate_low, late_weights = local_call(
        modulation_kernel,
        ids,
        [(piece, False) for piece in notes] + [(modulate_weight.T, False)],
        [((latents, mod_share), FULL, False)] * shards
        + [((mod_share, D), LOW, False), ((shards, late_rows, D), LOW, False)],
        [],
        1,
        2 * shards * NOTE * D * mod_share,
        "modulation",
    )
    answers = [shares[0]] + [shift(shares[d], shards - d) for d in range(1, shards)]
    late_stacked, late_flipped = gather_group(late_weights)
    (early_weights,) = local_call(
        pack,
        ids,
        [(expand_weight, "low"), (contract_weight, "low")],
        [((rows, 2 * FF // shards), LOW, False)],
        [],
        1,
        D * D,
        "pack",
        after=tuple(notes[1:]),
    )
    early_weights = jnp.stack(exchange([early_weights] * shards))
    early_weights_chips = gather_chips(early_weights)

    tokens_shape = (latents, LEN, D)
    qkv, probs, attended, branch, wq, wo, mod, bias_up, bias_down = local_call(
        attention_forward,
        ids,
        [(tokens, True), (late_stacked, False), (late_flipped, False)]
        + [(v, False) for v in (*answers, *notes)],
        [
            ((latents, LEN, 3 * D), LOW, True),
            ((latents, HEADS, LEN, LEN), LOW, True),
            (tokens_shape, LOW, True),
            (tokens_shape, FULL, True),
            ((3 * D, D), LOW, False),
            ((D, D), LOW, False),
            ((latents, 6, D), FULL, False),
            ((1, FF), FULL, False),
            ((1, D), FULL, False),
        ],
        [
            pltpu.VMEM((shards, late_width, D), LOW if late_rows % 16 == 0 else FULL),
            pltpu.VMEM((BLOCK * LEN, D), LOW),
            pltpu.VMEM((BLOCK * LEN, D), LOW),
            pltpu.VMEM((shards, latents, mod_share), FULL),
            pltpu.VMEM((shards, NOTE, D), FULL),
            pltpu.VMEM((D, 3 * D), LOW),
            pltpu.VMEM((D, D), LOW),
        ],
        steps,
        latents * (2 * LEN * D * 4 * D + 4 * HEADS * LEN * LEN * PAIR) * 2,
        "attention_forward",
        after=(early_weights,),
    )
    early_shape = (GROUP // 2, shards, rows, 2 * FF // shards)
    (early_weights_stacked,) = local_call(
        stack,
        ids,
        [(v, False) for v in early_weights_chips],
        [(early_shape, LOW, False)],
        [],
        1,
        D * D,
        "stack",
        after=(branch,),
    )
    early_weights_flipped = flip(early_weights_stacked, 1)
    block_output, grad_mixed, grad_mod_late, keep, send, sum_up, sum_down = local_call(
        perceptron,
        ids,
        [
            (tokens, True),
            (branch, True),
            (mod, True),
            (cotangent, True),
            (early_weights_stacked, False),
            (early_weights_flipped, False),
            (bias_up, False),
            (bias_down, False),
        ],
        [
            (tokens_shape, LOW, True),
            (tokens_shape, FULL, True),
            ((latents, 4, D), FULL, True),
            (early_shape, FULL, False),
            (early_shape, LOW, False),
            ((1, FF), FULL, False),
            ((1, D), FULL, False),
        ],
        [
            pltpu.VMEM((shards, D, 2 * FF // shards), LOW),
            pltpu.VMEM((D, FF), LOW),
            pltpu.VMEM((D, FF), LOW),
            pltpu.VMEM((FF, D), LOW),
            pltpu.VMEM((FF, D), LOW),
            pltpu.VMEM((BLOCK * LEN, FF), LOW),
            pltpu.VMEM((BLOCK * LEN, FF), FULL),
            pltpu.VMEM((D, FF), FULL),
            pltpu.VMEM((D, FF), FULL),
        ],
        steps,
        latents * 2 * LEN * D * FF * 6 * 2,
        "perceptron",
    )

    grad_attended, total_project = local_call(
        project_backward,
        ids,
        [(mod, True), (attended, True), (grad_mixed, True), (wo, False)],
        [(tokens_shape, LOW, True), ((D, D), FULL, False)],
        [],
        steps,
        latents * 2 * LEN * D * D * 2,
        "project_backward",
    )
    early_totals = sum_cores(keep, send, ids, "early_sum", (total_project,))
    arrived = exchange_chips(early_totals)
    early_chips = sum(piece.astype(FULL) for piece in arrived[1:]) + arrived[0]
    (grad_qkv,) = local_call(
        attention_backward,
        ids,
        [(qkv, True), (probs, True), (grad_attended, True)],
        [((latents, LEN, 3 * D), LOW, True)],
        [],
        steps,
        latents * 10 * HEADS * LEN * LEN * PAIR,
        "attention_backward",
        after=tuple(early_totals[1:]),
    )
    early_pieces = exchange([early_chips[d].astype(LOW) for d in range(shards)])
    early = sum(piece.astype(FULL) for piece in early_pieces[1:]) + early_chips[0]
    early = sum_rest(early.astype(LOW))
    late_shape = (GROUP // 2, shards, rows, late_width)
    tokens_grad, keep, send, extra = local_call(
        attend_backward,
        ids,
        [
            (tokens, True),
            (mod, True),
            (grad_mixed, True),
            (grad_qkv, True),
            (wq, False),
            (total_project, False),
            (grad_mod_late, False),
            (sum_up, False),
            (sum_down, False),
        ],
        [
            (tokens_shape, FULL, True),
            (late_shape, FULL, False),
            (late_shape, LOW, False),
            ((shards, NOTE, D), LOW, False),
        ],
        [
            pltpu.VMEM((D, 3 * D), FULL),
            pltpu.VMEM((latents, 2, D), FULL),
            pltpu.VMEM((NOTE, D), FULL),
        ],
        steps,
        latents * 2 * LEN * D * 6 * D * 2,
        "attend_backward",
        after=(early_chips,),
    )
    early_stacked, early_flipped = gather_group(early)

    arrived = exchange_chips(sum_cores(keep, send, ids, "late_sum", tuple(early_pieces[1:])))
    outgoing = local_call(
        late_pieces,
        ids,
        [(v, False) for v in (*arrived, extra)],
        [((NOTE + rows, D), LOW, False)] * shards,
        [],
        1,
        4 * shards * rows * late_width,
        "late_pieces",
        after=(early_stacked,),
    )
    group_latents = shards * latents
    unit = (-(-mod_share // D) + 1) * group_latents + 16
    payload, *shares = local_call(
        partial(combine, shards, latents),
        ids,
        [(v, False) for v in (*exchange(outgoing), *notes, modulate_low)],
        [((rows + unit, D), LOW, False)] + [((latents, D), FULL, False)] * shards,
        [pltpu.VMEM((unit, D), FULL)],
        1,
        2 * shards * NOTE * D * mod_share,
        "combine",
        after=(early_flipped,),
    )
    if lax.axis_size("rep") > GROUP:
        late, others = sum_rest(payload[:rows]), payload[rows:]
        for bit in range(3, lax.axis_size("rep").bit_length() - 1):
            others = jnp.concatenate([others, flip(others, 1 << bit)], axis=0)
        payload = jnp.concatenate([late, others], axis=0)
    late_stacked, late_flipped = gather_group(payload)

    grad_cond_low = shares[0]
    for d in range(1, shards):
        grad_cond_low = grad_cond_low + shift(shares[d], shards - d)
    condition_grad = silu_back(grad_cond_low)[0]

    def as_held(values):
        return [v.T if turned else v for v, turned in zip(values, TURNED)]

    masters = as_held(
        [attend_weight, project_weight, expand_weight, contract_weight, modulate_weight]
    )
    moments = as_held(
        [attend_moment, project_moment, expand_moment, contract_moment, modulate_moment]
    )
    shapes = [m.shape for m in masters]
    widths = [whole // shards for whole in COLUMNS]
    slot_width = max(stop - start for start, stop in slot_spans(widths))
    piece_rows = 128 * len(TRIANGLE) // shards
    results = local_call(
        partial(momenta_kernel, group_latents),
        ids,
        [(v, False) for v in (late_stacked, late_flipped, early_stacked, early_flipped, *moments)],
        [(shape, FULL, False) for shape in shapes * 2]
        + [
            ((shards, piece_rows, 128), FULL, False),
            ((slot_width, D), FULL, False),
            ((8, D), FULL, False),
        ],
        [pltpu.VMEM(shape, FULL) for shape in shapes]
        + [pltpu.VMEM((D, D), FULL), pltpu.VMEM((128 * len(TRIANGLE), 128), FULL)],
        1,
        6 * D * D * D,
        "momenta",
    )
    gradients, momenta = as_held(results[0:5]), as_held(results[5:10])
    gram, columns, bias_block = results[10:13]
    piece = sum(exchange([gram[d] for d in range(shards)]))
    (answer,) = local_call(
        polynomial_kernel,
        ids,
        [(p, False) for p in exchange([piece] * shards)] + [(columns, False)],
        [((slot_width, D), LOW, False)],
        [pltpu.VMEM((128 * len(TRIANGLE), 128), FULL), pltpu.VMEM((D, D), FULL)],
        1,
        2 * 3 * 18 * D * D * D,
        "polynomial",
        after=(condition_grad,),
    )
    updated = local_call(
        update_kernel,
        ids,
        [(v, False) for v in (*gather_group(answer), *masters)],
        [(shape, FULL, False) for shape in shapes],
        [pltpu.VMEM((GROUP, slot_width, D), LOW)],
        1,
        2 * D * sum(widths),
        "update",
    )
    updated = as_held(updated)

    bias_gradient = bias_block.reshape(-1)[:bias_share]
    bias_momentum = BETA_ONE * bias_first + (1.0 - BETA_ONE) * bias_gradient
    bias_variance = BETA_TWO * bias_second + (1.0 - BETA_TWO) * bias_gradient * bias_gradient
    corrected_first = bias_momentum / (1.0 - BETA_ONE**STEP)
    corrected_second = bias_variance / (1.0 - BETA_TWO**STEP)
    bias_updated = biases * (1.0 - ADAM_RATE * WEIGHT_DECAY) - ADAM_RATE * corrected_first / (
        jnp.sqrt(corrected_second) + ADAM_EPSILON
    )
    return (
        block_output,
        tokens_grad,
        condition_grad,
        *gradients,
        *momenta,
        *updated,
        bias_gradient,
        bias_momentum,
        bias_variance,
        bias_updated,
    )


def solution(mesh):
    rows = P(("shard", "rep"), None, None)
    vectors = P(("shard", "rep"), None)
    columns = P(None, "shard")
    flat = P("shard")
    return jax.shard_map(
        per_device,
        mesh=mesh,
        in_specs=(rows, vectors, rows) + (columns,) * 5 + (flat,) + (columns,) * 5 + (flat,) * 2,
        out_specs=(rows, rows, vectors) + (columns,) * 15 + (flat,) * 4,
        check_vma=False,
    )
```

```python
from functools import partial
import math

import jax
import jax.numpy as jnp
from jax import lax
from jax.experimental import pallas as pl
from jax.experimental.pallas import tpu as pltpu
from jax.sharding import PartitionSpec as P

D = 384
HEADS = 6
HEAD = 64
FF = 1536
LEN = 256
NS_ITERS = 5
STEP = 10
PAIR = 2 * HEAD
CHUNK = 512
GROUP = 8
BLOCK = 2
BIAS_LEN = 6 * D + FF + D
NOTE = 16
GRANTS = {"momenta": 32, "gram": 24, "polynomial": 20, "update": 24}

POLY_LINEAR = 3.4445
POLY_CUBIC = -4.775
POLY_QUINTIC = 2.0315
MOMENTUM = 0.95
MUON_RATE = 0.4
WEIGHT_DECAY = 0.01
ADAM_RATE = 0.1
BETA_ONE = 0.9
BETA_TWO = 0.999
ADAM_EPSILON = 1e-08
GELU_SLOPE = math.sqrt(2.0 / math.pi)
GELU_CUBIC = 0.044715

LOW = jnp.bfloat16
FULL = jnp.float32

SLOTS = ((4, 0), (4, 1), (0, 0), (2, 0), (2, 1), (3, 0), (3, 1), (1, 0))


def shift(value, distance):
    size = lax.axis_size("shard")
    return lax.ppermute(value, "shard", [(i, (i + distance) % size) for i in range(size)])


def flip(value, mask):
    size = lax.axis_size("rep")
    return lax.ppermute(value, "rep", [(i, i ^ mask) for i in range(size)])


def exchange(pieces):
    return [pieces[0]] + [shift(pieces[d], d) for d in range(1, len(pieces))]


def gather_chips(value):
    return [value] + [flip(value, 2 * t) for t in range(1, GROUP // 2)]


def gather_group(value):
    stacked = jnp.stack(gather_chips(value))
    return stacked, flip(stacked, 1)


def sum_cores(keep, send, ids, name, after):
    received = flip(send, 1)
    shape = keep.shape[1:]
    return local_call(
        split_sum,
        ids,
        [(keep, False), (received, False)],
        [(shape, FULL, False)] + [(shape, LOW, False)] * (keep.shape[0] - 1),
        [],
        1,
        keep.size,
        name,
        after=after,
    )


def exchange_chips(totals):
    return [totals[0]] + [flip(totals[t], 2 * t) for t in range(1, GROUP // 2)]


def sum_rest(value):
    for bit in range(3, lax.axis_size("rep").bit_length() - 1):
        value = (value.astype(FULL) + flip(value, 1 << bit).astype(FULL)).astype(LOW)
    return value


def dot(left, right):
    return lax.dot_general(left, right, (((1,), (0,)), ((), ())), preferred_element_type=FULL)


def dot_nt(left, right):
    return lax.dot_general(left, right, (((1,), (1,)), ((), ())), preferred_element_type=FULL)


def dot_tn(left, right):
    return lax.dot_general(left, right, (((0,), (0,)), ((), ())), preferred_element_type=FULL)


def split_low(value):
    high = value.astype(LOW)
    return high, (value - high.astype(FULL)).astype(LOW)


def dot_split(left, right, product=dot):
    return product(left[0], right[0]) + (product(left[0], right[1]) + product(left[1], right[0]))


def normalize(values):
    centered = values - jnp.mean(values, -1, keepdims=True)
    inverse_spread = lax.rsqrt(jnp.mean(centered * centered, -1, keepdims=True) + 1e-06)
    return centered * inverse_spread, inverse_spread


def normalize_back(upstream, normed, inverse_spread):
    return inverse_spread * (
        upstream
        - jnp.mean(upstream, -1, keepdims=True)
        - normed * jnp.mean(upstream * normed, -1, keepdims=True)
    )


def local_call(kernel, ids, inputs, outputs, scratch, steps, flops, name, after=()):
    def run(*refs):
        kernel(*refs[: 1 + len(inputs)], *refs[1 + len(inputs) + len(after) :])

    def spec(shape, blocked):
        zeros = (0,) * (len(shape) - 1)
        if blocked == "low":
            return pl.BlockSpec((shape[0] // GROUP,) + tuple(shape[1:]), lambda i, ids: (ids[1],) + zeros)
        if blocked:
            block = (shape[0] // steps,) + tuple(shape[1:])
            return pl.BlockSpec(block, lambda i, _: (i,) + zeros)
        return pl.BlockSpec(tuple(shape), lambda i, _: (0,) + zeros)

    moved = sum(v.size * v.dtype.itemsize for v, _ in inputs)
    moved += sum(math.prod(shape) * jnp.dtype(kind).itemsize for shape, kind, _ in outputs)
    return pl.pallas_call(
        run,
        grid_spec=pltpu.PrefetchScalarGridSpec(
            num_scalar_prefetch=1,
            grid=(steps,),
            in_specs=[spec(v.shape, blocked) for v, blocked in inputs]
            + [pl.BlockSpec(memory_space=pl.ANY) for _ in after],
            out_specs=[spec(shape, blocked) for shape, _, blocked in outputs],
            scratch_shapes=scratch,
        ),
        out_shape=[jax.ShapeDtypeStruct(shape, kind) for shape, kind, _ in outputs],
        compiler_params=pltpu.CompilerParams(
            dimension_semantics=("arbitrary",), vmem_limit_bytes=GRANTS.get(name, 48) * 1024 * 1024
        ),
        cost_estimate=pl.CostEstimate(flops=flops, bytes_accessed=moved, transcendentals=0),
        name=name,
    )(ids, *[v for v, _ in inputs], *after)


def pieces_of(ids, stacked, flipped):
    for t in range(GROUP // 2):
        for bit, blocks in enumerate((stacked, flipped)):
            yield ids[1] ^ (2 * t + bit), blocks.at[t]


def rows_at(place, rows):
    return pl.ds(pl.multiple_of(place * rows, rows), rows)


def turn(value):
    filled = value.shape[1]
    extra = -filled % 128
    if extra:
        value = jnp.concatenate([value, jnp.zeros((value.shape[0], extra), value.dtype)], axis=1)
    return value.T[:filled]


def head_masks(values):
    lane = lax.broadcasted_iota(jnp.int32, values.shape, 1) % PAIR
    zero = jnp.zeros_like(values)
    return (
        jnp.where(lane < HEAD, values, zero).astype(LOW),
        jnp.where(lane < HEAD, zero, values).astype(LOW),
    )


def split_sum(ids, keep, received, own, *others):
    own[...] = keep[0] + received[0].astype(FULL)
    for t, other in enumerate(others):
        other[...] = (keep[t + 1] + received[t + 1].astype(FULL)).astype(LOW)


def modulation_kernel(ids, *refs):
    shards = refs[-1].shape[0]
    notes, weight, answers, weight_low, stacked = (
        refs[:shards], refs[shards], refs[shards + 1 : -2], refs[-2], refs[-1],
    )
    low = weight[...].astype(LOW)
    weight_low[...] = low
    for d, (note, answer) in enumerate(zip(notes, answers)):
        answer[...] = dot_nt(note[:NOTE, :], low)[: answer.shape[0]]
        stacked[d] = note[NOTE:, :]


def total_kernel(ids, own, *refs):
    total = own[...]
    for piece in refs[:-1]:
        total = total + piece[...].astype(FULL)
    refs[-1][...] = total.astype(LOW)


def pack(ids, *refs):
    start = 0
    for weight in refs[:-1]:
        width = weight.shape[1]
        refs[-1][:, start : start + width] = weight[...].astype(LOW)
        start = start + width


def stack(ids, *refs):
    for t, block in enumerate(refs[:-1]):
        refs[-1][t] = block[...]


def attention_forward(
    ids, tokens, stacked, flipped, *refs,
):
    shards = (len(refs) - 16) // 2
    answers, notes = refs[:shards], refs[shards : 2 * shards]
    (
        qkv, probs, attended, branch, wq, wo, mod_all, bias_up, bias_down,
        ordered, query_a, query_b, mod_parts, bias_parts, wq_plain, wo_plain,
    ) = refs[2 * shards :]
    rows = ordered.shape[1] // GROUP
    wide, narrow = 3 * D // shards, D // shards

    @pl.when(pl.program_id(0) == 0)
    def _():
        for place, block in pieces_of(ids, stacked, flipped):
            for d in range(shards):
                source = lax.rem(ids[0] - d + shards, shards)
                ordered[source, rows_at(place, rows), :] = block[d].astype(ordered.dtype)
        for s in range(shards):
            wq[s * wide : (s + 1) * wide, :] = ordered[s, :wide, :].astype(LOW)
            wo[s * narrow : (s + 1) * narrow, :] = ordered[s, wide:, :].astype(LOW)
        wq_plain[...] = wq[...].T
        wo_plain[...] = wo[...].T
        for d in range(shards):
            mod_parts[lax.rem(ids[0] + d, shards)] = answers[d][...]
            bias_parts[lax.rem(ids[0] - d + shards, shards)] = notes[d][:NOTE, :].astype(FULL)
        latents = mod_all.shape[0]
        share = BIAS_LEN // shards
        pieces = []
        for s in range(shards):
            for b in range(-(-share // D)):
                row = bias_parts[s, latents + b : latents + b + 1, :]
                pieces.append(row[:, : min(D, share - b * D)])
        bias = jnp.concatenate(pieces, axis=1)
        whole = jnp.concatenate([mod_parts[s] for s in range(shards)], axis=1) + bias[:, : 6 * D]
        for latent in range(latents):
            for b in range(6):
                mod_all[latent, b : b + 1, :] = whole[latent : latent + 1, b * D : (b + 1) * D]
        bias_up[...] = bias[:, 6 * D : 6 * D + FF]
        bias_down[...] = bias[:, 6 * D + FF :]

    count = tokens.shape[0]
    mod = mod_all[pl.ds(pl.program_id(0) * count, count)]
    normed, _ = normalize(tokens[...].astype(FULL))
    hidden = normed * (1.0 + mod[:, 1:2, :]) + mod[:, 0:1, :]
    hidden = hidden.reshape(count * LEN, D).astype(LOW)
    queries = dot(hidden, wq_plain[:, :D])
    masked_a, masked_b = head_masks(queries)
    query_a[...] = masked_a
    query_b[...] = masked_b
    qkv[:, :, :D] = queries.astype(LOW).reshape(count, LEN, D)
    qkv[:, :, D:] = dot(hidden, wq_plain[:, D:]).astype(LOW).reshape(count, LEN, 2 * D)
    for latent in range(count):
        span = slice(latent * LEN, (latent + 1) * LEN)
        for pair in range(HEADS // 2):
            lanes = slice(pair * PAIR, (pair + 1) * PAIR)
            keys = qkv[latent, :, D + pair * PAIR : D + (pair + 1) * PAIR]
            values = qkv[latent, :, 2 * D + pair * PAIR : 2 * D + (pair + 1) * PAIR].T
            results = []
            for member, masked in enumerate((query_a, query_b)):
                scores = dot_nt(keys, masked[span, lanes]) * (HEAD ** (-0.5) / math.log(2.0))
                top = jnp.max(scores, 0, keepdims=True)
                raised = jnp.exp2(scores - top)
                share = (raised * (1.0 / jnp.sum(raised, 0, keepdims=True))).astype(LOW)
                probs[latent, 2 * pair + member] = share
                results.append(dot(values[member * HEAD : (member + 1) * HEAD], share))
            attended[latent, :, lanes] = jnp.concatenate(results, axis=0).T.astype(LOW)
    branch[...] = dot(attended[...].reshape(count * LEN, D), wo_plain[...]).reshape(count, LEN, D)


def perceptron(
    ids, tokens, branch, mod, cotangent, stacked, flipped, bias_up, bias_down,
    out, grad_mixed, grad_mod, keep, send, sum_up, sum_down,
    ordered, wu, wd, wu_turned, wd_turned, act, slope, total_up, total_down,
):
    shards = ordered.shape[0]
    rows = D // GROUP
    width = FF // shards
    step = pl.program_id(0)

    @pl.when(step == 0)
    def _():
        for place, block in pieces_of(ids, stacked, flipped):
            for d in range(shards):
                source = lax.rem(ids[0] - d + shards, shards)
                ordered[source, rows_at(place, rows), :] = block[d]
        for i in range(GROUP):
            span = slice(i * rows, (i + 1) * rows)
            pieces = [ordered[s, span, :] for s in range(shards)]
            wu[span, :] = jnp.concatenate([p[:, :width] for p in pieces], axis=1)
            wd[span, :] = jnp.concatenate([p[:, width:] for p in pieces], axis=1)
        wu_turned[...] = wu[...].T
        wd_turned[...] = wd[...].T
        total_up[...] = jnp.zeros_like(total_up)
        total_down[...] = jnp.zeros_like(total_down)
        sum_up[...] = jnp.zeros_like(sum_up)
        sum_down[...] = jnp.zeros_like(sum_down)

    count = tokens.shape[0]
    flat = count * LEN
    branch_out = branch[...]
    mixed = tokens[...].astype(FULL) + mod[:, 2:3, :] * branch_out
    normed, inverse_spread = normalize(mixed)
    hidden = (normed * (1.0 + mod[:, 4:5, :]) + mod[:, 3:4, :]).reshape(flat, D).astype(LOW)
    result = jnp.zeros((flat, D), FULL)
    for start in range(0, FF, CHUNK):
        span = slice(start, start + CHUNK)
        u = dot(hidden, wu[:, span]) + bias_up[:, span]
        square = u * u
        half = 0.5 + 0.5 * jnp.tanh(u * (GELU_SLOPE + (GELU_SLOPE * GELU_CUBIC) * square))
        act_low = (u * half).astype(LOW)
        act[:, span] = act_low
        steep = u * (2.0 * GELU_SLOPE + (6.0 * GELU_SLOPE * GELU_CUBIC) * square)
        slope[:, span] = half + (half - half * half) * steep
        result = result + dot(act_low, wd_turned[span, :])
    result = (result + bias_down[...]).reshape(count, LEN, D)
    gate = mod[:, 5:6, :]
    out[...] = (mixed + gate * result).astype(LOW)
    upstream = cotangent[...].astype(FULL)
    grad_mod[:, 3:4, :] = jnp.sum(upstream * result, axis=1, keepdims=True)
    grad_result = (gate * upstream).reshape(flat, D).astype(LOW)
    sum_down[...] += jnp.sum(grad_result.astype(FULL), axis=0, keepdims=True)
    grad_hidden = jnp.zeros((flat, D), FULL)
    for start in range(0, FF, CHUNK):
        span = slice(start, start + CHUNK)
        grad_u = (dot(grad_result, wd[:, span]) * slope[:, span]).astype(LOW)
        sum_up[:, span] += jnp.sum(grad_u.astype(FULL), axis=0, keepdims=True)
        total_down[:, span] += dot_tn(grad_result, act[:, span])
        total_up[:, span] += dot_tn(hidden, grad_u)
        grad_hidden = grad_hidden + dot(grad_u, wu_turned[span, :])
    grad_hidden = grad_hidden.reshape(count, LEN, D)
    grad_mod[:, 1:2, :] = jnp.sum(grad_hidden, axis=1, keepdims=True)
    grad_mod[:, 2:3, :] = jnp.sum(grad_hidden * normed, axis=1, keepdims=True)
    back = upstream + normalize_back(
        grad_hidden * (1.0 + mod[:, 4:5, :]), normed, inverse_spread
    )
    grad_mixed[...] = back
    grad_mod[:, 0:1, :] = jnp.sum(back * branch_out, axis=1, keepdims=True)

    @pl.when(step == pl.num_programs(0) - 1)
    def _():
        shard, low = ids[0], ids[1]
        for j in range(GROUP):
            span = pl.ds(pl.multiple_of((low ^ j) * rows, rows), rows)
            for s in range(shards):
                d = lax.rem(s - shard + shards, shards)
                lanes = slice(s * width, (s + 1) * width)
                piece = jnp.concatenate([total_up[span, lanes], total_down[span, lanes]], axis=1)
                if j & 1:
                    send[j // 2, d] = piece.astype(LOW)
                else:
                    keep[j // 2, d] = piece


def project_backward(
    ids, mod, attended, grad_mixed, wo,
    grad_attended, total_project,
):
    @pl.when(pl.program_id(0) == 0)
    def _():
        total_project[...] = jnp.zeros_like(total_project)

    count = attended.shape[0]
    flat = count * LEN
    grad_branch = (mod[:, 2:3, :] * grad_mixed[...]).reshape(flat, D).astype(LOW)
    total_project[...] += dot_tn(attended[...].reshape(flat, D), grad_branch)
    grad_attended[...] = dot(grad_branch, wo[...]).astype(LOW).reshape(count, LEN, D)


def attention_backward(ids, qkv, probs, grad_attended, grad_qkv):
    mask = lax.broadcasted_iota(jnp.int32, (LEN, PAIR), 1) < HEAD
    scale = HEAD ** (-0.5)
    for latent in range(qkv.shape[0]):
        for pair in range(HEADS // 2):
            lanes = slice(pair * PAIR, (pair + 1) * PAIR)
            key_lanes = slice(D + pair * PAIR, D + (pair + 1) * PAIR)
            value_lanes = slice(2 * D + pair * PAIR, 2 * D + (pair + 1) * PAIR)
            queries = qkv[latent, :, lanes]
            keys = qkv[latent, :, key_lanes].T
            values = qkv[latent, :, value_lanes]
            upper = grad_attended[latent, :, lanes]
            masked = head_masks(upper.astype(FULL))
            by_query, by_key, by_value = [], [], []
            for member in range(2):
                share = probs[latent, 2 * pair + member]
                weight = share.astype(FULL)
                grad_share = dot_nt(values, masked[member])
                product = weight * grad_share
                grad_scores = (
                    product - weight * jnp.sum(product, 0, keepdims=True)
                ).astype(LOW)
                by_query.append(dot(keys[member * HEAD : (member + 1) * HEAD], grad_scores))
                by_key.append(dot(grad_scores, queries))
                by_value.append(dot(share, upper))
            merged = jnp.concatenate(by_query, axis=0).T * scale
            grad_qkv[latent, :, lanes] = merged.astype(LOW)
            merged = jnp.where(mask, by_key[0], by_key[1]) * scale
            grad_qkv[latent, :, key_lanes] = merged.astype(LOW)
            merged = jnp.where(mask, by_value[0], by_value[1])
            grad_qkv[latent, :, value_lanes] = merged.astype(LOW)


def attend_backward(
    ids, tokens, mod, grad_mixed, grad_qkv, wq, total_project, grad_mod_late, sum_up, sum_down,
    grad_tokens, keep, send, extra,
    total_attend, grad_mod, extra_rows,
):
    rows = D // GROUP
    shards = keep.shape[1]
    step = pl.program_id(0)

    @pl.when(step == 0)
    def _():
        total_attend[...] = jnp.zeros_like(total_attend)

    count = tokens.shape[0]
    flat = count * LEN
    normed, inverse_spread = normalize(tokens[...].astype(FULL))
    hidden = (normed * (1.0 + mod[:, 1:2, :]) + mod[:, 0:1, :]).reshape(flat, D).astype(LOW)
    grad_low = grad_qkv[...].reshape(flat, 3 * D)
    total_attend[...] += dot_tn(hidden, grad_low)
    grad_hidden = dot(grad_low, wq[...]).reshape(count, LEN, D)
    mine = pl.ds(step * count, count)
    grad_mod[mine, 0:1, :] = jnp.sum(grad_hidden, axis=1, keepdims=True)
    grad_mod[mine, 1:2, :] = jnp.sum(grad_hidden * normed, axis=1, keepdims=True)
    grad_tokens[...] = grad_mixed[...] + normalize_back(
        grad_hidden * (1.0 + mod[:, 1:2, :]), normed, inverse_spread
    )

    @pl.when(step == pl.num_programs(0) - 1)
    def _():
        shard, low = ids[0], ids[1]
        wide, narrow = 3 * D // shards, D // shards
        for j in range(GROUP):
            span = rows_at(low ^ j, rows)
            whole_attend, whole_project = total_attend[span, :], total_project[span, :]
            for s in range(shards):
                d = lax.rem(s - shard + shards, shards)
                piece = jnp.concatenate(
                    [
                        whole_attend[:, s * wide : (s + 1) * wide],
                        whole_project[:, s * narrow : (s + 1) * narrow],
                    ],
                    axis=1,
                )
                if j & 1:
                    send[j // 2, d] = piece.astype(LOW)
                else:
                    keep[j // 2, d] = piece
        latents = grad_mod.shape[0]
        columns = [grad_mod[:, b, :] for b in range(2)] + [grad_mod_late[:, b, :] for b in range(4)]
        whole = jnp.concatenate(columns, axis=1).astype(LOW).astype(FULL)
        sums = jnp.sum(whole, axis=0, keepdims=True)
        sums = jnp.concatenate([sums, sum_up[...], sum_down[...]], axis=1)
        mod_share, bias_share = 6 * D // shards, BIAS_LEN // shards
        blocks, lines = -(-mod_share // D), -(-bias_share // D)

        def padded(values, start, stop):
            part = values[:, start : min(start + D, stop)]
            if part.shape[1] < D:
                rest = jnp.zeros((part.shape[0], D - part.shape[1]), FULL)
                part = jnp.concatenate([part, rest], axis=1)
            return part

        extra_rows[...] = jnp.zeros_like(extra_rows)
        for s in range(shards):
            for b in range(blocks):
                extra_rows[b * latents : (b + 1) * latents, :] = padded(
                    whole, s * mod_share + b * D, (s + 1) * mod_share
                )
            for b in range(lines):
                row = padded(sums, s * bias_share + b * D, (s + 1) * bias_share)
                high = row.astype(LOW).astype(FULL)
                place = blocks * latents + b
                extra_rows[place : place + 1, :] = high
                extra_rows[place + lines : place + lines + 1, :] = row - high
            extra[lax.rem(s - shard + shards, shards)] = extra_rows[...].astype(LOW)


def late_pieces(ids, own, first, second, third, extra, *pieces):
    total = own[...]
    for received in (first, second, third):
        total = total + received[...].astype(FULL)
    for d, piece in enumerate(pieces):
        piece[:NOTE, :] = extra[d]
        if total.shape[2] < D:
            piece[NOTE:, :] = jnp.zeros((total.shape[1], D), LOW)
        piece[NOTE:, : total.shape[2]] = total[d].astype(LOW)


def combine(shards, latents, ids, *refs):
    incoming, notes, weight, payload = (
        refs[:shards], refs[shards : 2 * shards], refs[2 * shards], refs[2 * shards + 1],
    )
    answers, rows_ref = refs[2 * shards + 2 : -1], refs[-1]
    rows = D // GROUP
    mod_share, bias_share = 6 * D // shards, BIAS_LEN // shards
    blocks, lines = -(-mod_share // D), -(-bias_share // D)
    total = jnp.zeros((rows, D), FULL)
    bias = jnp.zeros((NOTE, D), FULL)
    for d in range(shards):
        total = total + incoming[d][NOTE:, :].astype(FULL)
        extra = incoming[d][:NOTE, :].astype(FULL)
        bias = bias + extra
        for b in range(blocks):
            start = (b * shards + d) * latents
            rows_ref[start : start + latents, :] = extra[b * latents : (b + 1) * latents]
        start = (blocks * shards + d) * latents
        rows_ref[start : start + latents, :] = notes[d][:NOTE, :].astype(FULL)[:latents]
    payload[:rows, :] = total.astype(LOW)
    count = (blocks + 1) * shards * latents
    start = blocks * latents
    bias = bias[start : start + lines] + bias[start + lines : start + 2 * lines]
    high = bias.astype(LOW).astype(FULL)
    rows_ref[count:, :] = jnp.zeros((16, D), FULL)
    rows_ref[count : count + lines, :] = high
    rows_ref[count + 8 : count + 8 + lines, :] = bias - high
    payload[rows:, :] = rows_ref[...].astype(LOW)
    for d, answer in enumerate(answers):
        result = jnp.zeros((NOTE, D), FULL)
        for b in range(blocks):
            filled = min(D, mod_share - b * D)
            product = dot(incoming[d][:NOTE, :filled], weight[b * D : b * D + filled, :])
            result = result + shifted(product, b * latents)
        answer[...] = result[:latents]


def shifted(values, count):
    if count == 0:
        return values
    return jnp.concatenate([values[count:], values[:count]], axis=0)


COLUMNS = (3 * D, D, FF, FF, 6 * D)
TURNED = (True, True, False, False, True)
TRIANGLE = ((0, 0), (0, 1), (0, 2), (1, 1), (1, 2), (2, 2))


def slot_spans(widths):
    counts = [sum(1 for m, _ in SLOTS if m == number) for number in range(len(widths))]
    return [
        (part * (widths[m] // counts[m]), (part + 1) * (widths[m] // counts[m]))
        for m, part in SLOTS
    ]


def late_parts(latents, widths, late, late_flipped):
    rows = D // GROUP
    blocks = -(-widths[4] // D)
    unit = (blocks + 1) * latents + 16
    parts = [
        ref.at[t, pl.ds(start, unit), :]
        for ref in (late, late_flipped)
        for t in range(GROUP // 2)
        for start in range(rows, late.shape[1], unit)
    ]

    def rows_of(start):
        return jnp.concatenate([p[start : start + latents, :] for p in parts], axis=0)

    return parts, blocks, rows_of


def modulate_gradient(latents, widths, late, late_flipped, target):
    _, blocks, rows_of = late_parts(latents, widths, late, late_flipped)
    cond = rows_of(blocks * latents)
    for block in range(blocks):
        filled = min(D, widths[4] - block * D)
        target[block * D : block * D + filled, :] = dot_tn(rows_of(block * latents), cond)[:filled]


def late_gradient(ids, late, late_flipped, late_whole):
    rows = D // GROUP
    for place, block in pieces_of(ids, late, late_flipped):
        late_whole[rows_at(place, rows), :] = block[:rows, :].astype(FULL)
    return turn(late_whole[...])


def mix(moment, grad):
    moment = MOMENTUM * moment + grad
    return moment, grad + MOMENTUM * moment


def gram_kernel(latents, ids, late, late_flipped, early, early_flipped, *refs):
    moments, gram, columns = refs[0:5], refs[5], refs[6]
    late_whole, flat_gram, early_whole, modulate_whole = refs[7:11]
    low = ids[1]
    rows = D // GROUP
    shards = gram.shape[0]
    widths = [whole // shards for whole in COLUMNS]
    spans = slot_spans(widths)
    for number in range(5):
        owners = [k for k, (m, _) in enumerate(SLOTS) if m == number]
        condition = low == owners[0]
        for owner in owners[1:]:
            condition = condition | (low == owner)

        @pl.when(condition)
        def _(number=number, owners=owners):
            if number < 2:
                start = 0 if number == 0 else widths[0]
                grad = late_gradient(ids, late, late_flipped, late_whole)
                grad = grad[start : start + widths[number]]
            elif number < 4:
                start = 0 if number == 2 else widths[2]
                for place, block in pieces_of(ids, early, early_flipped):
                    piece = block[...].astype(FULL)[:, start : start + widths[number]]
                    early_whole[rows_at(place, rows), :] = piece
                grad = early_whole[...]
            else:
                modulate_gradient(latents, widths, late, late_flipped, modulate_whole)
                grad = modulate_whole[...]
            mixed = mix(moments[number][...], grad)[1]
            parts = split_low(mixed)
            whole = dot_split(parts, parts, dot_tn if TURNED[number] else dot_nt)
            for place, (a, b) in enumerate(TRIANGLE):
                flat_gram[place * 128 : (place + 1) * 128, :] = whole[
                    a * 128 : (a + 1) * 128, b * 128 : (b + 1) * 128
                ]
            if not TURNED[number]:
                mixed = turn(mixed)
            for owner in owners:

                @pl.when(low == owner)
                def _(owner=owner, mixed=mixed):
                    start, stop = spans[owner]
                    filled = stop - start
                    columns[:filled, :] = mixed[start:stop]
                    if filled < columns.shape[0]:
                        columns[filled:, :] = jnp.zeros((columns.shape[0] - filled, D), FULL)

    size = gram.shape[1]
    for s in range(shards):
        gram[lax.rem(s - ids[0] + shards, shards)] = flat_gram[s * size : (s + 1) * size, :]


def momenta_kernel(latents, ids, late, late_flipped, early, early_flipped, *refs):
    moments, grads, momenta = refs[0:5], refs[5:10], refs[10:15]
    bias, late_whole = refs[15:17]
    rows = D // GROUP
    widths = [m.shape[0 if turned else 1] for m, turned in zip(moments, TURNED)]
    turned = late_gradient(ids, late, late_flipped, late_whole)
    grads[0][...] = turned[: widths[0]]
    grads[1][...] = turned[widths[0] : widths[0] + widths[1]]
    for place, block in pieces_of(ids, early, early_flipped):
        piece = block[...].astype(FULL)
        grads[2][rows_at(place, rows), :] = piece[:, : widths[2]]
        grads[3][rows_at(place, rows), :] = piece[:, widths[2] :]
    modulate_gradient(latents, widths, late, late_flipped, grads[4])
    parts, blocks, _ = late_parts(latents, widths, late, late_flipped)
    total = jnp.zeros((16, D), FULL)
    for part in parts:
        total = total + part[(blocks + 1) * latents :, :].astype(FULL)
    bias[...] = total[:8] + total[8:]
    for number in range(5):
        momenta[number][...] = mix(moments[number][...], grads[number][...])[0]


def polynomial_kernel(ids, *refs):
    shards = len(refs) - 4
    pieces, columns, answer, flat_gram, gram_ref = refs[:shards], *refs[shards:]
    size = pieces[0].shape[0]
    for d in range(shards):
        source = lax.rem(ids[0] - d + shards, shards)
        flat_gram[rows_at(source, size), :] = pieces[d][...]
    for place, (a, b) in enumerate(TRIANGLE):
        block = flat_gram[place * 128 : (place + 1) * 128, :]
        gram_ref[a * 128 : (a + 1) * 128, b * 128 : (b + 1) * 128] = block
        if a != b:
            gram_ref[b * 128 : (b + 1) * 128, a * 128 : (a + 1) * 128] = block.T
    gram = gram_ref[...]
    diagonal = lax.broadcasted_iota(jnp.int32, (D, D), 0) == lax.broadcasted_iota(
        jnp.int32, (D, D), 1
    )
    trace = jnp.sum(jnp.where(diagonal, gram, 0.0))
    scale = 1.0 / (jnp.sqrt(jnp.full((1, 1), trace)) + 1e-07)
    gram = (gram * scale) * scale
    product = jnp.where(diagonal, 1.0, 0.0)
    for step in range(NS_ITERS):
        mixing = POLY_CUBIC * gram + POLY_QUINTIC * dot_deep(left_deep(gram), right_deep(gram))
        mixing_deep = left_deep(mixing)
        if step == 0:
            half = POLY_LINEAR * gram + dot_deep(mixing_deep, right_deep(gram))
            product = POLY_LINEAR * product + mixing
        elif step + 1 < NS_ITERS:
            both = jnp.concatenate([gram, product], axis=1)
            both = POLY_LINEAR * both + dot_deep(mixing_deep, right_deep(both))
            half, product = both[:, :D], both[:, D:]
        else:
            product = POLY_LINEAR * product + dot_deep(mixing_deep, right_deep(product))
        if step + 1 < NS_ITERS:
            gram = POLY_LINEAR * half + dot_deep(mixing_deep, right_deep(half))
    answer[...] = dot_deep(left_deep(columns[...] * scale), right_deep(product)).astype(LOW)


def left_deep(value):
    high, rest = split_low(value)
    return jnp.concatenate([high, rest, high], axis=1)


def right_deep(value):
    high, rest = split_low(value)
    return jnp.concatenate([high, high, rest], axis=0)


def dot_deep(left, right):
    return dot(left, right)


def update_kernel(ids, answers, answers_flipped, *refs):
    masters, updated, ordered = refs[:5], refs[5:10], refs[10]
    for place, block in pieces_of(ids, answers, answers_flipped):
        ordered[place] = block[...]
    widths = [m.shape[0 if turned else 1] for m, turned in zip(masters, TURNED)]
    spans = slot_spans(widths)
    for number in range(5):
        factor = MUON_RATE * 0.2 * math.sqrt(COLUMNS[number])
        mine = [k for k, (m, _) in enumerate(SLOTS) if m == number]
        if TURNED[number]:
            for k in mine:
                start, stop = spans[k]
                updated[number][start:stop, :] = masters[number][start:stop, :] * (
                    1.0 - MUON_RATE * WEIGHT_DECAY
                ) - factor * ordered[k, : stop - start, :].astype(FULL)
        else:
            direction = jnp.concatenate(
                [ordered[k, : spans[k][1] - spans[k][0], :].astype(FULL) for k in mine], axis=0
            )
            updated[number][...] = masters[number][...] * (
                1.0 - MUON_RATE * WEIGHT_DECAY
            ) - factor * direction.T


def whole_rows(vector):
    rows = -(-vector.shape[-1] // D)
    padded = jnp.pad(vector, [(0, 0)] * (vector.ndim - 1) + [(0, rows * D - vector.shape[-1])])
    return padded.reshape(vector.shape[:-1] + (rows, D))


def per_device(
    tokens,
    condition,
    cotangent,
    attend_weight,
    project_weight,
    expand_weight,
    contract_weight,
    modulate_weight,
    biases,
    attend_moment,
    project_moment,
    expand_moment,
    contract_moment,
    modulate_moment,
    bias_first,
    bias_second,
):
    latents = tokens.shape[0]
    steps = latents // BLOCK
    shards = lax.axis_size("shard")
    shard = lax.axis_index("shard")
    low = lax.axis_index("rep") % GROUP
    ids = jnp.stack([shard, low]).astype(jnp.int32)
    rows = D // GROUP
    bias_share = biases.shape[0]
    mod_share = modulate_weight.shape[1]
    late_width = 4 * D // shards
    late_rows = late_width // GROUP

    silu_value, silu_back = jax.vjp(jax.nn.silu, condition.astype(FULL))
    note = jnp.concatenate([silu_value.astype(LOW), whole_rows(biases.astype(LOW))], axis=0)
    note = jnp.pad(note, ((0, NOTE - note.shape[0]), (0, 0)))
    late_weights = jnp.concatenate([attend_weight.T, project_weight.T], axis=0).astype(LOW)
    late_weights = lax.dynamic_slice_in_dim(late_weights, low * late_rows, late_rows, 0)
    note = jnp.concatenate([note, late_weights], axis=0)
    notes = exchange([note] * shards)

    *shares, modulate_low, late_weights = local_call(
        modulation_kernel,
        ids,
        [(piece, False) for piece in notes] + [(modulate_weight.T, False)],
        [((latents, mod_share), FULL, False)] * shards
        + [((mod_share, D), LOW, False), ((shards, late_rows, D), LOW, False)],
        [],
        1,
        2 * shards * NOTE * D * mod_share,
        "modulation",
    )
    answers = [shares[0]] + [shift(shares[d], shards - d) for d in range(1, shards)]
    late_weights_chips = gather_chips(late_weights)
    (early_weights,) = local_call(
        pack,
        ids,
        [(expand_weight, "low"), (contract_weight, "low")],
        [((rows, 2 * FF // shards), LOW, False)],
        [],
        1,
        D * D,
        "pack",
        after=(late_weights,),
    )
    early_weights = jnp.stack(exchange([early_weights] * shards))
    early_weights_chips = gather_chips(early_weights)
    (late_stacked,) = local_call(
        stack,
        ids,
        [(v, False) for v in late_weights_chips],
        [((GROUP // 2, shards, late_rows, D), LOW, False)],
        [],
        1,
        D * D,
        "stack_late",
        after=(early_weights,),
    )
    late_flipped = flip(late_stacked, 1)

    tokens_shape = (latents, LEN, D)
    qkv, probs, attended, branch, wq, wo, mod, bias_up, bias_down = local_call(
        attention_forward,
        ids,
        [(tokens, True), (late_stacked, False), (late_flipped, False)]
        + [(v, False) for v in (*answers, *notes)],
        [
            ((latents, LEN, 3 * D), LOW, True),
            ((latents, HEADS, LEN, LEN), LOW, True),
            (tokens_shape, LOW, True),
            (tokens_shape, FULL, True),
            ((3 * D, D), LOW, False),
            ((D, D), LOW, False),
            ((latents, 6, D), FULL, False),
            ((1, FF), FULL, False),
            ((1, D), FULL, False),
        ],
        [
            pltpu.VMEM((shards, late_width, D), LOW if late_rows % 16 == 0 else FULL),
            pltpu.VMEM((BLOCK * LEN, D), LOW),
            pltpu.VMEM((BLOCK * LEN, D), LOW),
            pltpu.VMEM((shards, latents, mod_share), FULL),
            pltpu.VMEM((shards, NOTE, D), FULL),
            pltpu.VMEM((D, 3 * D), LOW),
            pltpu.VMEM((D, D), LOW),
        ],
        steps,
        latents * (2 * LEN * D * 4 * D + 4 * HEADS * LEN * LEN * PAIR) * 2,
        "attention_forward",
        after=(early_weights,),
    )
    early_shape = (GROUP // 2, shards, rows, 2 * FF // shards)
    (early_weights_stacked,) = local_call(
        stack,
        ids,
        [(v, False) for v in early_weights_chips],
        [(early_shape, LOW, False)],
        [],
        1,
        D * D,
        "stack",
        after=(branch,),
    )
    early_weights_flipped = flip(early_weights_stacked, 1)
    block_output, grad_mixed, grad_mod_late, keep, send, sum_up, sum_down = local_call(
        perceptron,
        ids,
        [
            (tokens, True),
            (branch, True),
            (mod, True),
            (cotangent, True),
            (early_weights_stacked, False),
            (early_weights_flipped, False),
            (bias_up, False),
            (bias_down, False),
        ],
        [
            (tokens_shape, LOW, True),
            (tokens_shape, FULL, True),
            ((latents, 4, D), FULL, True),
            (early_shape, FULL, False),
            (early_shape, LOW, False),
            ((1, FF), FULL, False),
            ((1, D), FULL, False),
        ],
        [
            pltpu.VMEM((shards, D, 2 * FF // shards), LOW),
            pltpu.VMEM((D, FF), LOW),
            pltpu.VMEM((D, FF), LOW),
            pltpu.VMEM((FF, D), LOW),
            pltpu.VMEM((FF, D), LOW),
            pltpu.VMEM((BLOCK * LEN, FF), LOW),
            pltpu.VMEM((BLOCK * LEN, FF), FULL),
            pltpu.VMEM((D, FF), FULL),
            pltpu.VMEM((D, FF), FULL),
        ],
        steps,
        latents * 2 * LEN * D * FF * 6 * 2,
        "perceptron",
    )

    early_totals = sum_cores(keep, send, ids, "early_sum", ())
    grad_attended, total_project = local_call(
        project_backward,
        ids,
        [(mod, True), (attended, True), (grad_mixed, True), (wo, False)],
        [(tokens_shape, LOW, True), ((D, D), FULL, False)],
        [],
        steps,
        latents * 2 * LEN * D * D * 2,
        "project_backward",
    )
    arrived = exchange_chips(early_totals)
    early_chips = sum(piece.astype(FULL) for piece in arrived[1:]) + arrived[0]
    (grad_qkv,) = local_call(
        attention_backward,
        ids,
        [(qkv, True), (probs, True), (grad_attended, True)],
        [((latents, LEN, 3 * D), LOW, True)],
        [],
        steps,
        latents * 10 * HEADS * LEN * LEN * PAIR,
        "attention_backward",
        after=tuple(early_totals[1:]),
    )
    early_pieces = exchange([early_chips[d].astype(LOW) for d in range(shards)])
    late_shape = (GROUP // 2, shards, rows, late_width)
    tokens_grad, keep, send, extra = local_call(
        attend_backward,
        ids,
        [
            (tokens, True),
            (mod, True),
            (grad_mixed, True),
            (grad_qkv, True),
            (wq, False),
            (total_project, False),
            (grad_mod_late, False),
            (sum_up, False),
            (sum_down, False),
        ],
        [
            (tokens_shape, FULL, True),
            (late_shape, FULL, False),
            (late_shape, LOW, False),
            ((shards, NOTE, D), LOW, False),
        ],
        [
            pltpu.VMEM((D, 3 * D), FULL),
            pltpu.VMEM((latents, 2, D), FULL),
            pltpu.VMEM((NOTE, D), FULL),
        ],
        steps,
        latents * 2 * LEN * D * 6 * D * 2,
        "attend_backward",
        after=(early_chips,),
    )

    late_totals = sum_cores(keep, send, ids, "late_sum", ())
    arrived = exchange_chips(late_totals)
    (early,) = local_call(
        total_kernel,
        ids,
        [(v, False) for v in (early_chips[0], *early_pieces[1:])],
        [(early_pieces[1].shape, LOW, False)],
        [],
        1,
        D * D,
        "early_total",
        after=tuple(late_totals[1:]),
    )
    early_stacked, early_flipped = gather_group(sum_rest(early))
    outgoing = local_call(
        late_pieces,
        ids,
        [(v, False) for v in (*arrived, extra)],
        [((NOTE + rows, D), LOW, False)] * shards,
        [],
        1,
        4 * shards * rows * late_width,
        "late_pieces",
        after=(early,),
    )
    group_latents = shards * latents
    unit = (-(-mod_share // D) + 1) * group_latents + 16
    payload, *shares = local_call(
        partial(combine, shards, latents),
        ids,
        [(v, False) for v in (*exchange(outgoing), *notes, modulate_low)],
        [((rows + unit, D), LOW, False)] + [((latents, D), FULL, False)] * shards,
        [pltpu.VMEM((unit, D), FULL)],
        1,
        2 * shards * NOTE * D * mod_share,
        "combine",
        after=(early_stacked,),
    )
    if lax.axis_size("rep") > GROUP:
        late, others = sum_rest(payload[:rows]), payload[rows:]
        for bit in range(3, lax.axis_size("rep").bit_length() - 1):
            others = jnp.concatenate([others, flip(others, 1 << bit)], axis=0)
        payload = jnp.concatenate([late, others], axis=0)
    late_stacked, late_flipped = gather_group(payload)

    grad_cond_low = shares[0]
    for d in range(1, shards):
        grad_cond_low = grad_cond_low + shift(shares[d], shards - d)
    condition_grad = silu_back(grad_cond_low)[0]

    def as_held(values):
        return [v.T if turned else v for v, turned in zip(values, TURNED)]

    masters = as_held(
        [attend_weight, project_weight, expand_weight, contract_weight, modulate_weight]
    )
    moments = as_held(
        [attend_moment, project_moment, expand_moment, contract_moment, modulate_moment]
    )
    shapes = [m.shape for m in masters]
    widths = [whole // shards for whole in COLUMNS]
    slot_width = max(stop - start for start, stop in slot_spans(widths))
    piece_rows = 128 * len(TRIANGLE) // shards
    sources = [
        (v, False) for v in (late_stacked, late_flipped, early_stacked, early_flipped, *moments)
    ]
    gram, columns = local_call(
        partial(gram_kernel, group_latents),
        ids,
        sources,
        [((shards, piece_rows, 128), FULL, False), ((slot_width, D), FULL, False)],
        [
            pltpu.VMEM((D, D), FULL),
            pltpu.VMEM((128 * len(TRIANGLE), 128), FULL),
            pltpu.VMEM(shapes[2], FULL),
            pltpu.VMEM(shapes[4], FULL),
        ],
        1,
        6 * D * D * D,
        "gram",
    )
    *results, bias_block = local_call(
        partial(momenta_kernel, group_latents),
        ids,
        sources,
        [(shape, FULL, False) for shape in shapes * 2] + [((8, D), FULL, False)],
        [pltpu.VMEM((D, D), FULL)],
        1,
        D * D * D,
        "momenta",
        after=(gram,),
    )
    gradients, momenta = as_held(results[0:5]), as_held(results[5:10])
    piece = sum(exchange([gram[d] for d in range(shards)]))
    (answer,) = local_call(
        polynomial_kernel,
        ids,
        [(p, False) for p in exchange([piece] * shards)] + [(columns, False)],
        [((slot_width, D), LOW, False)],
        [pltpu.VMEM((128 * len(TRIANGLE), 128), FULL), pltpu.VMEM((D, D), FULL)],
        1,
        2 * 3 * 18 * D * D * D,
        "polynomial",
        after=(condition_grad, bias_block),
    )
    updated = local_call(
        update_kernel,
        ids,
        [(v, False) for v in (*gather_group(answer), *masters)],
        [(shape, FULL, False) for shape in shapes],
        [pltpu.VMEM((GROUP, slot_width, D), LOW)],
        1,
        2 * D * sum(widths),
        "update",
    )
    updated = as_held(updated)

    bias_gradient = bias_block.reshape(-1)[:bias_share]
    bias_momentum = BETA_ONE * bias_first + (1.0 - BETA_ONE) * bias_gradient
    bias_variance = BETA_TWO * bias_second + (1.0 - BETA_TWO) * bias_gradient * bias_gradient
    corrected_first = bias_momentum / (1.0 - BETA_ONE**STEP)
    corrected_second = bias_variance / (1.0 - BETA_TWO**STEP)
    bias_updated = biases * (1.0 - ADAM_RATE * WEIGHT_DECAY) - ADAM_RATE * corrected_first / (
        jnp.sqrt(corrected_second) + ADAM_EPSILON
    )
    return (
        block_output,
        tokens_grad,
        condition_grad,
        *gradients,
        *momenta,
        *updated,
        bias_gradient,
        bias_momentum,
        bias_variance,
        bias_updated,
    )


def solution(mesh):
    rows = P(("shard", "rep"), None, None)
    vectors = P(("shard", "rep"), None)
    columns = P(None, "shard")
    flat = P("shard")
    return jax.shard_map(
        per_device,
        mesh=mesh,
        in_specs=(rows, vectors, rows) + (columns,) * 5 + (flat,) + (columns,) * 5 + (flat,) * 2,
        out_specs=(rows, rows, vectors) + (columns,) * 15 + (flat,) * 4,
        check_vma=False,
    )
```

```python
from functools import partial
import math

import jax
import jax.numpy as jnp
from jax import lax
from jax.experimental import pallas as pl
from jax.experimental.pallas import tpu as pltpu
from jax.sharding import PartitionSpec as P

D = 384
HEADS = 6
HEAD = 64
FF = 1536
LEN = 256
NS_ITERS = 5
STEP = 10
PAIR = 2 * HEAD
CHUNK = 512
GROUP = 8
BLOCK = 2
BIAS_LEN = 6 * D + FF + D
NOTE = 16
GRANTS = {
    "attention_forward": 40,
    "perceptron": 40,
    "attention_backward": 32,
    "attend_backward": 36,
    "momenta": 32,
    "gram": 24,
    "polynomial": 20,
    "update": 24,
}

POLY_LINEAR = 3.4445
POLY_CUBIC = -4.775
POLY_QUINTIC = 2.0315
MOMENTUM = 0.95
MUON_RATE = 0.4
WEIGHT_DECAY = 0.01
ADAM_RATE = 0.1
BETA_ONE = 0.9
BETA_TWO = 0.999
ADAM_EPSILON = 1e-08
GELU_SLOPE = math.sqrt(2.0 / math.pi)
GELU_CUBIC = 0.044715

LOW = jnp.bfloat16
FULL = jnp.float32

SLOTS = ((4, 0), (4, 1), (0, 0), (2, 0), (2, 1), (3, 0), (3, 1), (1, 0))


def shift(value, distance):
    size = lax.axis_size("shard")
    return lax.ppermute(value, "shard", [(i, (i + distance) % size) for i in range(size)])


def flip(value, mask):
    size = lax.axis_size("rep")
    return lax.ppermute(value, "rep", [(i, i ^ mask) for i in range(size)])


def exchange(pieces):
    return [pieces[0]] + [shift(pieces[d], d) for d in range(1, len(pieces))]


def gather_chips(value):
    return [value] + [flip(value, 2 * t) for t in range(1, GROUP // 2)]


def gather_group(value):
    stacked = jnp.stack(gather_chips(value))
    return stacked, flip(stacked, 1)


def sum_cores(keep, send, ids, name, after):
    received = flip(send, 1)
    shape = keep.shape[1:]
    return local_call(
        split_sum,
        ids,
        [(keep, False), (received, False)],
        [(shape, FULL, False)] + [(shape, LOW, False)] * (keep.shape[0] - 1),
        [],
        1,
        keep.size,
        name,
        after=after,
    )


def exchange_chips(totals):
    return [totals[0]] + [flip(totals[t], 2 * t) for t in range(1, GROUP // 2)]


def sum_rest(value):
    for bit in range(3, lax.axis_size("rep").bit_length() - 1):
        value = (value.astype(FULL) + flip(value, 1 << bit).astype(FULL)).astype(LOW)
    return value


def dot(left, right):
    return lax.dot_general(left, right, (((1,), (0,)), ((), ())), preferred_element_type=FULL)


def dot_nt(left, right):
    return lax.dot_general(left, right, (((1,), (1,)), ((), ())), preferred_element_type=FULL)


def dot_tn(left, right):
    return lax.dot_general(left, right, (((0,), (0,)), ((), ())), preferred_element_type=FULL)


def split_low(value):
    high = value.astype(LOW)
    return high, (value - high.astype(FULL)).astype(LOW)


def dot_split(left, right, product=dot):
    return product(left[0], right[0]) + (product(left[0], right[1]) + product(left[1], right[0]))


def normalize(values):
    centered = values - jnp.mean(values, -1, keepdims=True)
    inverse_spread = lax.rsqrt(jnp.mean(centered * centered, -1, keepdims=True) + 1e-06)
    return centered * inverse_spread, inverse_spread


def normalize_back(upstream, normed, inverse_spread):
    return inverse_spread * (
        upstream
        - jnp.mean(upstream, -1, keepdims=True)
        - normed * jnp.mean(upstream * normed, -1, keepdims=True)
    )


def local_call(kernel, ids, inputs, outputs, scratch, steps, flops, name, after=()):
    def run(*refs):
        kernel(*refs[: 1 + len(inputs)], *refs[1 + len(inputs) + len(after) :])

    def spec(shape, blocked):
        zeros = (0,) * (len(shape) - 1)
        if isinstance(blocked, tuple):
            rows, place = blocked
            return pl.BlockSpec(
                (rows,) + tuple(shape[1:]), lambda i, ids: (place(ids[1]),) + zeros
            )
        if blocked:
            block = (shape[0] // steps,) + tuple(shape[1:])
            return pl.BlockSpec(block, lambda i, _: (i,) + zeros)
        return pl.BlockSpec(tuple(shape), lambda i, _: (0,) + zeros)

    moved = sum(v.size * v.dtype.itemsize for v, _ in inputs)
    moved += sum(math.prod(shape) * jnp.dtype(kind).itemsize for shape, kind, _ in outputs)
    return pl.pallas_call(
        run,
        grid_spec=pltpu.PrefetchScalarGridSpec(
            num_scalar_prefetch=1,
            grid=(steps,),
            in_specs=[spec(v.shape, blocked) for v, blocked in inputs]
            + [pl.BlockSpec(memory_space=pl.ANY) for _ in after],
            out_specs=[spec(shape, blocked) for shape, _, blocked in outputs],
            scratch_shapes=scratch,
        ),
        out_shape=[jax.ShapeDtypeStruct(shape, kind) for shape, kind, _ in outputs],
        compiler_params=pltpu.CompilerParams(
            dimension_semantics=("arbitrary",), vmem_limit_bytes=GRANTS.get(name, 16) * 1024 * 1024
        ),
        cost_estimate=pl.CostEstimate(flops=flops, bytes_accessed=moved, transcendentals=0),
        name=name,
    )(ids, *[v for v, _ in inputs], *after)


def pieces_of(ids, stacked, flipped):
    for t in range(GROUP // 2):
        for bit, blocks in enumerate((stacked, flipped)):
            yield ids[1] ^ (2 * t + bit), blocks.at[t]


def rows_at(place, rows):
    return pl.ds(pl.multiple_of(place * rows, rows), rows)


def turn(value):
    filled = value.shape[1]
    extra = -filled % 128
    if extra:
        value = jnp.concatenate([value, jnp.zeros((value.shape[0], extra), value.dtype)], axis=1)
    return value.T[:filled]


def head_masks(values):
    lane = lax.broadcasted_iota(jnp.int32, values.shape, 1) % PAIR
    zero = jnp.zeros_like(values)
    return (
        jnp.where(lane < HEAD, values, zero).astype(LOW),
        jnp.where(lane < HEAD, zero, values).astype(LOW),
    )


def split_sum(ids, keep, received, own, *others):
    own[...] = keep[0] + received[0].astype(FULL)
    for t, other in enumerate(others):
        other[...] = (keep[t + 1] + received[t + 1].astype(FULL)).astype(LOW)


def modulation_kernel(ids, *refs):
    shards = refs[-1].shape[0]
    notes, weight, answers, weight_low, stacked = (
        refs[:shards], refs[shards], refs[shards + 1 : -2], refs[-2], refs[-1],
    )
    low = weight[...].astype(LOW)
    weight_low[...] = low
    for d, (note, answer) in enumerate(zip(notes, answers)):
        answer[...] = dot_nt(note[:NOTE, :], low)[: answer.shape[0]]
        stacked[d] = note[NOTE:, :]


def total_kernel(ids, own, *refs):
    total = own[...]
    for piece in refs[:-1]:
        total = total + piece[...].astype(FULL)
    refs[-1][...] = total.astype(LOW)


def prepare(ids, condition, biases, attend, project, note, first):
    latents = condition.shape[0]
    value = condition[...].astype(FULL)
    first[...] = jnp.zeros_like(first)
    first[:latents, :] = value / (1.0 + jnp.exp(-value))
    share = biases.shape[1]
    for b in range(-(-share // D)):
        filled = min(D, share - b * D)
        first[latents + b : latents + b + 1, :filled] = biases[:, b * D : b * D + filled]
    note[:NOTE, :] = first[...].astype(LOW)

    @pl.when(ids[1] < 6)
    def _():
        note[NOTE:, :] = attend[...].astype(LOW)

    @pl.when(ids[1] >= 6)
    def _():
        note[NOTE:, :] = project[...].astype(LOW)


def pack(ids, *refs):
    start = 0
    for weight in refs[:-1]:
        width = weight.shape[1]
        refs[-1][:, start : start + width] = weight[...].astype(LOW)
        start = start + width


def stack(ids, *refs):
    for t, block in enumerate(refs[:-1]):
        refs[-1][t] = block[...]


def attention_forward(
    ids, tokens, stacked, flipped, *refs,
):
    shards = (len(refs) - 16) // 2
    answers, notes = refs[:shards], refs[shards : 2 * shards]
    (
        qkv, probs, attended, branch, wq, wo, mod_all, bias_up, bias_down,
        ordered, query_a, query_b, mod_parts, bias_parts, wq_plain, wo_plain,
    ) = refs[2 * shards :]
    rows = ordered.shape[1] // GROUP
    wide, narrow = 3 * D // shards, D // shards

    @pl.when(pl.program_id(0) == 0)
    def _():
        for place, block in pieces_of(ids, stacked, flipped):
            for d in range(shards):
                source = lax.rem(ids[0] - d + shards, shards)
                ordered[source, rows_at(place, rows), :] = block[d].astype(ordered.dtype)
        for s in range(shards):
            wq[s * wide : (s + 1) * wide, :] = ordered[s, :wide, :].astype(LOW)
            wo[s * narrow : (s + 1) * narrow, :] = ordered[s, wide:, :].astype(LOW)
        wq_plain[...] = wq[...].T
        wo_plain[...] = wo[...].T
        for d in range(shards):
            mod_parts[lax.rem(ids[0] + d, shards)] = answers[d][...]
            bias_parts[lax.rem(ids[0] - d + shards, shards)] = notes[d][:NOTE, :].astype(FULL)
        latents = mod_all.shape[0]
        share = BIAS_LEN // shards
        pieces = []
        for s in range(shards):
            for b in range(-(-share // D)):
                row = bias_parts[s, latents + b : latents + b + 1, :]
                pieces.append(row[:, : min(D, share - b * D)])
        bias = jnp.concatenate(pieces, axis=1)
        whole = jnp.concatenate([mod_parts[s] for s in range(shards)], axis=1) + bias[:, : 6 * D]
        for latent in range(latents):
            for b in range(6):
                mod_all[latent, b : b + 1, :] = whole[latent : latent + 1, b * D : (b + 1) * D]
        bias_up[...] = bias[:, 6 * D : 6 * D + FF]
        bias_down[...] = bias[:, 6 * D + FF :]

    count = tokens.shape[0]
    mod = mod_all[pl.ds(pl.program_id(0) * count, count)]
    normed, _ = normalize(tokens[...].astype(FULL))
    hidden = normed * (1.0 + mod[:, 1:2, :]) + mod[:, 0:1, :]
    hidden = hidden.reshape(count * LEN, D).astype(LOW)
    queries = dot(hidden, wq_plain[:, :D])
    masked_a, masked_b = head_masks(queries)
    query_a[...] = masked_a
    query_b[...] = masked_b
    qkv[:, :, :D] = queries.astype(LOW).reshape(count, LEN, D)
    qkv[:, :, D:] = dot(hidden, wq_plain[:, D:]).astype(LOW).reshape(count, LEN, 2 * D)
    for latent in range(count):
        span = slice(latent * LEN, (latent + 1) * LEN)
        for pair in range(HEADS // 2):
            lanes = slice(pair * PAIR, (pair + 1) * PAIR)
            keys = qkv[latent, :, D + pair * PAIR : D + (pair + 1) * PAIR]
            values = qkv[latent, :, 2 * D + pair * PAIR : 2 * D + (pair + 1) * PAIR].T
            results = []
            for member, masked in enumerate((query_a, query_b)):
                scores = dot_nt(keys, masked[span, lanes]) * (HEAD ** (-0.5) / math.log(2.0))
                top = jnp.max(scores, 0, keepdims=True)
                raised = jnp.exp2(scores - top)
                share = (raised * (1.0 / jnp.sum(raised, 0, keepdims=True))).astype(LOW)
                probs[latent, 2 * pair + member] = share
                results.append(dot(values[member * HEAD : (member + 1) * HEAD], share))
            attended[latent, :, lanes] = jnp.concatenate(results, axis=0).T.astype(LOW)
    branch[...] = dot(attended[...].reshape(count * LEN, D), wo_plain[...]).reshape(count, LEN, D)


def perceptron(
    ids, tokens, branch, mod, cotangent, stacked, flipped, bias_up, bias_down,
    out, grad_mixed, grad_mod, keep, send, sum_up, sum_down,
    ordered, wu, wd, act, slope, total_up, total_down,
):
    shards = ordered.shape[0]
    rows = D // GROUP
    width = FF // shards
    step = pl.program_id(0)

    @pl.when(step == 0)
    def _():
        for place, block in pieces_of(ids, stacked, flipped):
            for d in range(shards):
                source = lax.rem(ids[0] - d + shards, shards)
                ordered[source, rows_at(place, rows), :] = block[d]
        for i in range(GROUP):
            span = slice(i * rows, (i + 1) * rows)
            pieces = [ordered[s, span, :] for s in range(shards)]
            wu[span, :] = jnp.concatenate([p[:, :width] for p in pieces], axis=1)
            wd[span, :] = jnp.concatenate([p[:, width:] for p in pieces], axis=1)
        total_up[...] = jnp.zeros_like(total_up)
        total_down[...] = jnp.zeros_like(total_down)
        sum_up[...] = jnp.zeros_like(sum_up)
        sum_down[...] = jnp.zeros_like(sum_down)

    count = tokens.shape[0]
    flat = count * LEN
    branch_out = branch[...]
    mixed = tokens[...].astype(FULL) + mod[:, 2:3, :] * branch_out
    normed, inverse_spread = normalize(mixed)
    hidden = (normed * (1.0 + mod[:, 4:5, :]) + mod[:, 3:4, :]).reshape(flat, D).astype(LOW)
    result = jnp.zeros((flat, D), FULL)
    for start in range(0, FF, CHUNK):
        span = slice(start, start + CHUNK)
        u = dot(hidden, wu[:, span]) + bias_up[:, span]
        square = u * u
        half = 0.5 + 0.5 * jnp.tanh(u * (GELU_SLOPE + (GELU_SLOPE * GELU_CUBIC) * square))
        act_low = (u * half).astype(LOW)
        act[:, span] = act_low
        steep = u * (2.0 * GELU_SLOPE + (6.0 * GELU_SLOPE * GELU_CUBIC) * square)
        slope[:, span] = half + (half - half * half) * steep
        result = result + dot_nt(act_low, wd[:, span])
    result = (result + bias_down[...]).reshape(count, LEN, D)
    gate = mod[:, 5:6, :]
    out[...] = (mixed + gate * result).astype(LOW)
    upstream = cotangent[...].astype(FULL)
    grad_mod[:, 3:4, :] = jnp.sum(upstream * result, axis=1, keepdims=True)
    grad_result = (gate * upstream).reshape(flat, D).astype(LOW)
    sum_down[...] += jnp.sum(grad_result.astype(FULL), axis=0, keepdims=True)
    grad_hidden = jnp.zeros((flat, D), FULL)
    for start in range(0, FF, CHUNK):
        span = slice(start, start + CHUNK)
        grad_u = (dot(grad_result, wd[:, span]) * slope[:, span]).astype(LOW)
        sum_up[:, span] += jnp.sum(grad_u.astype(FULL), axis=0, keepdims=True)
        total_down[:, span] += dot_tn(grad_result, act[:, span])
        total_up[:, span] += dot_tn(hidden, grad_u)
        grad_hidden = grad_hidden + dot_nt(grad_u, wu[:, span])
    grad_hidden = grad_hidden.reshape(count, LEN, D)
    grad_mod[:, 1:2, :] = jnp.sum(grad_hidden, axis=1, keepdims=True)
    grad_mod[:, 2:3, :] = jnp.sum(grad_hidden * normed, axis=1, keepdims=True)
    back = upstream + normalize_back(
        grad_hidden * (1.0 + mod[:, 4:5, :]), normed, inverse_spread
    )
    grad_mixed[...] = back
    grad_mod[:, 0:1, :] = jnp.sum(back * branch_out, axis=1, keepdims=True)

    @pl.when(step == pl.num_programs(0) - 1)
    def _():
        shard, low = ids[0], ids[1]
        for j in range(GROUP):
            span = pl.ds(pl.multiple_of((low ^ j) * rows, rows), rows)
            for s in range(shards):
                d = lax.rem(s - shard + shards, shards)
                lanes = slice(s * width, (s + 1) * width)
                piece = jnp.concatenate([total_up[span, lanes], total_down[span, lanes]], axis=1)
                if j & 1:
                    send[j // 2, d] = piece.astype(LOW)
                else:
                    keep[j // 2, d] = piece


def attention_backward(
    ids, mod, attended, grad_mixed, qkv, probs, wo,
    grad_qkv, total_project,
    grad_attended,
):
    @pl.when(pl.program_id(0) == 0)
    def _():
        total_project[...] = jnp.zeros_like(total_project)

    count = attended.shape[0]
    flat = count * LEN
    grad_branch = (mod[:, 2:3, :] * grad_mixed[...]).reshape(flat, D).astype(LOW)
    total_project[...] += dot_tn(attended[...].reshape(flat, D), grad_branch)
    grad_attended[...] = dot(grad_branch, wo[...]).astype(LOW).reshape(count, LEN, D)
    mask = lax.broadcasted_iota(jnp.int32, (LEN, PAIR), 1) < HEAD
    scale = HEAD ** (-0.5)
    for latent in range(count):
        for pair in range(HEADS // 2):
            lanes = slice(pair * PAIR, (pair + 1) * PAIR)
            key_lanes = slice(D + pair * PAIR, D + (pair + 1) * PAIR)
            value_lanes = slice(2 * D + pair * PAIR, 2 * D + (pair + 1) * PAIR)
            queries = qkv[latent, :, lanes]
            keys = qkv[latent, :, key_lanes].T
            values = qkv[latent, :, value_lanes]
            upper = grad_attended[latent, :, lanes]
            masked = head_masks(upper.astype(FULL))
            by_query, by_key, by_value = [], [], []
            for member in range(2):
                share = probs[latent, 2 * pair + member]
                weight = share.astype(FULL)
                grad_share = dot_nt(values, masked[member])
                product = weight * grad_share
                grad_scores = (
                    product - weight * jnp.sum(product, 0, keepdims=True)
                ).astype(LOW)
                by_query.append(dot(keys[member * HEAD : (member + 1) * HEAD], grad_scores))
                by_key.append(dot(grad_scores, queries))
                by_value.append(dot(share, upper))
            merged = jnp.concatenate(by_query, axis=0).T * scale
            grad_qkv[latent, :, lanes] = merged.astype(LOW)
            merged = jnp.where(mask, by_key[0], by_key[1]) * scale
            grad_qkv[latent, :, key_lanes] = merged.astype(LOW)
            merged = jnp.where(mask, by_value[0], by_value[1])
            grad_qkv[latent, :, value_lanes] = merged.astype(LOW)


def attend_backward(
    ids, tokens, mod, grad_mixed, grad_qkv, wq, total_project, grad_mod_late, sum_up, sum_down,
    grad_tokens, keep, send, extra,
    total_attend, grad_mod, extra_rows,
):
    rows = D // GROUP
    shards = keep.shape[1]
    step = pl.program_id(0)

    @pl.when(step == 0)
    def _():
        total_attend[...] = jnp.zeros_like(total_attend)

    count = tokens.shape[0]
    flat = count * LEN
    normed, inverse_spread = normalize(tokens[...].astype(FULL))
    hidden = (normed * (1.0 + mod[:, 1:2, :]) + mod[:, 0:1, :]).reshape(flat, D).astype(LOW)
    grad_low = grad_qkv[...].reshape(flat, 3 * D)
    total_attend[...] += dot_tn(hidden, grad_low)
    grad_hidden = dot(grad_low, wq[...]).reshape(count, LEN, D)
    mine = pl.ds(step * count, count)
    grad_mod[mine, 0:1, :] = jnp.sum(grad_hidden, axis=1, keepdims=True)
    grad_mod[mine, 1:2, :] = jnp.sum(grad_hidden * normed, axis=1, keepdims=True)
    grad_tokens[...] = grad_mixed[...] + normalize_back(
        grad_hidden * (1.0 + mod[:, 1:2, :]), normed, inverse_spread
    )

    @pl.when(step == pl.num_programs(0) - 1)
    def _():
        shard, low = ids[0], ids[1]
        wide, narrow = 3 * D // shards, D // shards
        for j in range(GROUP):
            span = rows_at(low ^ j, rows)
            whole_attend, whole_project = total_attend[span, :], total_project[span, :]
            for s in range(shards):
                d = lax.rem(s - shard + shards, shards)
                piece = jnp.concatenate(
                    [
                        whole_attend[:, s * wide : (s + 1) * wide],
                        whole_project[:, s * narrow : (s + 1) * narrow],
                    ],
                    axis=1,
                )
                if j & 1:
                    send[j // 2, d] = piece.astype(LOW)
                else:
                    keep[j // 2, d] = piece
        latents = grad_mod.shape[0]
        columns = [grad_mod[:, b, :] for b in range(2)] + [grad_mod_late[:, b, :] for b in range(4)]
        whole = jnp.concatenate(columns, axis=1).astype(LOW).astype(FULL)
        sums = jnp.sum(whole, axis=0, keepdims=True)
        sums = jnp.concatenate([sums, sum_up[...], sum_down[...]], axis=1)
        mod_share, bias_share = 6 * D // shards, BIAS_LEN // shards
        blocks, lines = -(-mod_share // D), -(-bias_share // D)

        def padded(values, start, stop):
            part = values[:, start : min(start + D, stop)]
            if part.shape[1] < D:
                rest = jnp.zeros((part.shape[0], D - part.shape[1]), FULL)
                part = jnp.concatenate([part, rest], axis=1)
            return part

        extra_rows[...] = jnp.zeros_like(extra_rows)
        for s in range(shards):
            for b in range(blocks):
                extra_rows[b * latents : (b + 1) * latents, :] = padded(
                    whole, s * mod_share + b * D, (s + 1) * mod_share
                )
            for b in range(lines):
                row = padded(sums, s * bias_share + b * D, (s + 1) * bias_share)
                high = row.astype(LOW).astype(FULL)
                place = blocks * latents + b
                extra_rows[place : place + 1, :] = high
                extra_rows[place + lines : place + lines + 1, :] = row - high
            extra[lax.rem(s - shard + shards, shards)] = extra_rows[...].astype(LOW)


def late_pieces(ids, own, first, second, third, extra, *pieces):
    total = own[...]
    for received in (first, second, third):
        total = total + received[...].astype(FULL)
    for d, piece in enumerate(pieces):
        piece[:NOTE, :] = extra[d]
        if total.shape[2] < D:
            piece[NOTE:, :] = jnp.zeros((total.shape[1], D), LOW)
        piece[NOTE:, : total.shape[2]] = total[d].astype(LOW)


def combine(shards, latents, ids, *refs):
    incoming, notes, weight, payload = (
        refs[:shards], refs[shards : 2 * shards], refs[2 * shards], refs[2 * shards + 1],
    )
    answers, rows_ref = refs[2 * shards + 2 : -1], refs[-1]
    rows = D // GROUP
    mod_share, bias_share = 6 * D // shards, BIAS_LEN // shards
    blocks, lines = -(-mod_share // D), -(-bias_share // D)
    total = jnp.zeros((rows, D), FULL)
    bias = jnp.zeros((NOTE, D), FULL)
    for d in range(shards):
        total = total + incoming[d][NOTE:, :].astype(FULL)
        extra = incoming[d][:NOTE, :].astype(FULL)
        bias = bias + extra
        for b in range(blocks):
            start = (b * shards + d) * latents
            rows_ref[start : start + latents, :] = extra[b * latents : (b + 1) * latents]
        start = (blocks * shards + d) * latents
        rows_ref[start : start + latents, :] = notes[d][:NOTE, :].astype(FULL)[:latents]
    payload[:rows, :] = total.astype(LOW)
    count = (blocks + 1) * shards * latents
    start = blocks * latents
    bias = bias[start : start + lines] + bias[start + lines : start + 2 * lines]
    high = bias.astype(LOW).astype(FULL)
    rows_ref[count:, :] = jnp.zeros((16, D), FULL)
    rows_ref[count : count + lines, :] = high
    rows_ref[count + 8 : count + 8 + lines, :] = bias - high
    payload[rows:, :] = rows_ref[...].astype(LOW)
    for d, answer in enumerate(answers):
        result = jnp.zeros((NOTE, D), FULL)
        for b in range(blocks):
            filled = min(D, mod_share - b * D)
            product = dot(incoming[d][:NOTE, :filled], weight[b * D : b * D + filled, :])
            result = result + shifted(product, b * latents)
        answer[...] = result[:latents]


def shifted(values, count):
    if count == 0:
        return values
    return jnp.concatenate([values[count:], values[:count]], axis=0)


COLUMNS = (3 * D, D, FF, FF, 6 * D)
TURNED = (True, True, False, False, True)
TRIANGLE = ((0, 0), (0, 1), (0, 2), (1, 1), (1, 2), (2, 2))


def slot_spans(widths):
    counts = [sum(1 for m, _ in SLOTS if m == number) for number in range(len(widths))]
    return [
        (part * (widths[m] // counts[m]), (part + 1) * (widths[m] // counts[m]))
        for m, part in SLOTS
    ]


def late_parts(latents, widths, late, late_flipped):
    rows = D // GROUP
    blocks = -(-widths[4] // D)
    unit = (blocks + 1) * latents + 16
    parts = [
        ref.at[t, pl.ds(start, unit), :]
        for ref in (late, late_flipped)
        for t in range(GROUP // 2)
        for start in range(rows, late.shape[1], unit)
    ]

    def rows_of(start):
        return jnp.concatenate([p[start : start + latents, :] for p in parts], axis=0)

    return parts, blocks, rows_of


def modulate_gradient(latents, widths, late, late_flipped, target):
    _, blocks, rows_of = late_parts(latents, widths, late, late_flipped)
    cond = rows_of(blocks * latents)
    for block in range(blocks):
        filled = min(D, widths[4] - block * D)
        target[block * D : block * D + filled, :] = dot_tn(rows_of(block * latents), cond)[:filled]


def late_gradient(ids, late, late_flipped, late_whole):
    rows = D // GROUP
    for place, block in pieces_of(ids, late, late_flipped):
        late_whole[rows_at(place, rows), :] = block[:rows, :].astype(FULL)
    return turn(late_whole[...])


def mix(moment, grad):
    moment = MOMENTUM * moment + grad
    return moment, grad + MOMENTUM * moment


def gram_kernel(latents, ids, late, late_flipped, early, early_flipped, *refs):
    moments, gram, columns = refs[0:5], refs[5], refs[6]
    late_whole, flat_gram, early_whole, modulate_whole = refs[7:11]
    low = ids[1]
    rows = D // GROUP
    shards = gram.shape[0]
    widths = [whole // shards for whole in COLUMNS]
    spans = slot_spans(widths)
    for number in range(5):
        owners = [k for k, (m, _) in enumerate(SLOTS) if m == number]
        condition = low == owners[0]
        for owner in owners[1:]:
            condition = condition | (low == owner)

        @pl.when(condition)
        def _(number=number, owners=owners):
            if number < 2:
                start = 0 if number == 0 else widths[0]
                grad = late_gradient(ids, late, late_flipped, late_whole)
                grad = grad[start : start + widths[number]]
            elif number < 4:
                start = 0 if number == 2 else widths[2]
                for place, block in pieces_of(ids, early, early_flipped):
                    piece = block[...].astype(FULL)[:, start : start + widths[number]]
                    early_whole[rows_at(place, rows), :] = piece
                grad = early_whole[...]
            else:
                modulate_gradient(latents, widths, late, late_flipped, modulate_whole)
                grad = modulate_whole[...]
            mixed = mix(moments[number][...], grad)[1]
            parts = split_low(mixed)
            whole = dot_split(parts, parts, dot_tn if TURNED[number] else dot_nt)
            for place, (a, b) in enumerate(TRIANGLE):
                flat_gram[place * 128 : (place + 1) * 128, :] = whole[
                    a * 128 : (a + 1) * 128, b * 128 : (b + 1) * 128
                ]
            if not TURNED[number]:
                mixed = turn(mixed)
            for owner in owners:

                @pl.when(low == owner)
                def _(owner=owner, mixed=mixed):
                    start, stop = spans[owner]
                    filled = stop - start
                    columns[:filled, :] = mixed[start:stop]
                    if filled < columns.shape[0]:
                        columns[filled:, :] = jnp.zeros((columns.shape[0] - filled, D), FULL)

    size = gram.shape[1]
    for s in range(shards):
        gram[lax.rem(s - ids[0] + shards, shards)] = flat_gram[s * size : (s + 1) * size, :]


def momenta_kernel(latents, ids, late, late_flipped, early, early_flipped, *refs):
    moments, grads, momenta = refs[0:5], refs[5:10], refs[10:15]
    bias, late_whole = refs[15:17]
    rows = D // GROUP
    widths = [m.shape[0 if turned else 1] for m, turned in zip(moments, TURNED)]
    turned = late_gradient(ids, late, late_flipped, late_whole)
    grads[0][...] = turned[: widths[0]]
    grads[1][...] = turned[widths[0] : widths[0] + widths[1]]
    for place, block in pieces_of(ids, early, early_flipped):
        piece = block[...].astype(FULL)
        grads[2][rows_at(place, rows), :] = piece[:, : widths[2]]
        grads[3][rows_at(place, rows), :] = piece[:, widths[2] :]
    modulate_gradient(latents, widths, late, late_flipped, grads[4])
    parts, blocks, _ = late_parts(latents, widths, late, late_flipped)
    total = jnp.zeros((16, D), FULL)
    for part in parts:
        total = total + part[(blocks + 1) * latents :, :].astype(FULL)
    bias[...] = total[:8] + total[8:]
    for number in range(5):
        momenta[number][...] = mix(moments[number][...], grads[number][...])[0]


def polynomial_kernel(ids, *refs):
    shards = len(refs) - 4
    pieces, columns, answer, flat_gram, gram_ref = refs[:shards], *refs[shards:]
    size = pieces[0].shape[0]
    for d in range(shards):
        source = lax.rem(ids[0] - d + shards, shards)
        flat_gram[rows_at(source, size), :] = pieces[d][...]
    for place, (a, b) in enumerate(TRIANGLE):
        block = flat_gram[place * 128 : (place + 1) * 128, :]
        gram_ref[a * 128 : (a + 1) * 128, b * 128 : (b + 1) * 128] = block
        if a != b:
            gram_ref[b * 128 : (b + 1) * 128, a * 128 : (a + 1) * 128] = block.T
    gram = gram_ref[...]
    diagonal = lax.broadcasted_iota(jnp.int32, (D, D), 0) == lax.broadcasted_iota(
        jnp.int32, (D, D), 1
    )
    trace = jnp.sum(jnp.where(diagonal, gram, 0.0))
    scale = 1.0 / (jnp.sqrt(jnp.full((1, 1), trace)) + 1e-07)
    gram = (gram * scale) * scale
    product = jnp.where(diagonal, 1.0, 0.0)
    for step in range(NS_ITERS):
        mixing = POLY_CUBIC * gram + POLY_QUINTIC * dot_deep(left_deep(gram), right_deep(gram))
        mixing_deep = left_deep(mixing)
        if step == 0:
            half = POLY_LINEAR * gram + dot_deep(mixing_deep, right_deep(gram))
            product = POLY_LINEAR * product + mixing
        elif step + 1 < NS_ITERS:
            both = jnp.concatenate([gram, product], axis=1)
            both = POLY_LINEAR * both + dot_deep(mixing_deep, right_deep(both))
            half, product = both[:, :D], both[:, D:]
        else:
            product = POLY_LINEAR * product + dot_deep(mixing_deep, right_deep(product))
        if step + 1 < NS_ITERS:
            gram = POLY_LINEAR * half + dot_deep(mixing_deep, right_deep(half))
    answer[...] = dot_deep(left_deep(columns[...] * scale), right_deep(product)).astype(LOW)


def left_deep(value):
    high, rest = split_low(value)
    return jnp.concatenate([high, rest, high], axis=1)


def right_deep(value):
    high, rest = split_low(value)
    return jnp.concatenate([high, high, rest], axis=0)


def dot_deep(left, right):
    return dot(left, right)


def update_kernel(ids, answers, answers_flipped, *refs):
    masters, updated, ordered = refs[:5], refs[5:10], refs[10]
    for place, block in pieces_of(ids, answers, answers_flipped):
        ordered[place] = block[...]
    widths = [m.shape[0 if turned else 1] for m, turned in zip(masters, TURNED)]
    spans = slot_spans(widths)
    for number in range(5):
        factor = MUON_RATE * 0.2 * math.sqrt(COLUMNS[number])
        mine = [k for k, (m, _) in enumerate(SLOTS) if m == number]
        if TURNED[number]:
            for k in mine:
                start, stop = spans[k]
                updated[number][start:stop, :] = masters[number][start:stop, :] * (
                    1.0 - MUON_RATE * WEIGHT_DECAY
                ) - factor * ordered[k, : stop - start, :].astype(FULL)
        else:
            direction = jnp.concatenate(
                [ordered[k, : spans[k][1] - spans[k][0], :].astype(FULL) for k in mine], axis=0
            )
            updated[number][...] = masters[number][...] * (
                1.0 - MUON_RATE * WEIGHT_DECAY
            ) - factor * direction.T


def per_device(
    tokens,
    condition,
    cotangent,
    attend_weight,
    project_weight,
    expand_weight,
    contract_weight,
    modulate_weight,
    biases,
    attend_moment,
    project_moment,
    expand_moment,
    contract_moment,
    modulate_moment,
    bias_first,
    bias_second,
):
    latents = tokens.shape[0]
    steps = latents // BLOCK
    shards = lax.axis_size("shard")
    shard = lax.axis_index("shard")
    low = lax.axis_index("rep") % GROUP
    ids = jnp.stack([shard, low]).astype(jnp.int32)
    rows = D // GROUP
    bias_share = biases.shape[0]
    mod_share = modulate_weight.shape[1]
    late_width = 4 * D // shards
    late_rows = late_width // GROUP

    (note,) = local_call(
        prepare,
        ids,
        [
            (condition, False),
            (biases.reshape(1, -1), False),
            (attend_weight.T, (late_rows, lambda place: jnp.minimum(place, 5))),
            (project_weight.T, (late_rows, lambda place: jnp.maximum(place - 6, 0))),
        ],
        [((NOTE + late_rows, D), LOW, False)],
        [pltpu.VMEM((NOTE, D), FULL)],
        1,
        D * D,
        "prepare",
    )
    notes = exchange([note] * shards)

    *shares, modulate_low, late_weights = local_call(
        modulation_kernel,
        ids,
        [(piece, False) for piece in notes] + [(modulate_weight.T, False)],
        [((latents, mod_share), FULL, False)] * shards
        + [((mod_share, D), LOW, False), ((shards, late_rows, D), LOW, False)],
        [],
        1,
        2 * shards * NOTE * D * mod_share,
        "modulation",
    )
    answers = [shares[0]] + [shift(shares[d], shards - d) for d in range(1, shards)]
    late_weights_chips = gather_chips(late_weights)
    (early_weights,) = local_call(
        pack,
        ids,
        [(w, (rows, lambda place: place)) for w in (expand_weight, contract_weight)],
        [((rows, 2 * FF // shards), LOW, False)],
        [],
        1,
        D * D,
        "pack",
        after=(late_weights,),
    )
    early_weights = jnp.stack(exchange([early_weights] * shards))
    early_weights_chips = gather_chips(early_weights)
    (late_stacked,) = local_call(
        stack,
        ids,
        [(v, False) for v in late_weights_chips],
        [((GROUP // 2, shards, late_rows, D), LOW, False)],
        [],
        1,
        D * D,
        "stack_late",
        after=(early_weights,),
    )
    late_flipped = flip(late_stacked, 1)

    tokens_shape = (latents, LEN, D)
    qkv, probs, attended, branch, wq, wo, mod, bias_up, bias_down = local_call(
        attention_forward,
        ids,
        [(tokens, True), (late_stacked, False), (late_flipped, False)]
        + [(v, False) for v in (*answers, *notes)],
        [
            ((latents, LEN, 3 * D), LOW, True),
            ((latents, HEADS, LEN, LEN), LOW, True),
            (tokens_shape, LOW, True),
            (tokens_shape, FULL, True),
            ((3 * D, D), LOW, False),
            ((D, D), LOW, False),
            ((latents, 6, D), FULL, False),
            ((1, FF), FULL, False),
            ((1, D), FULL, False),
        ],
        [
            pltpu.VMEM((shards, late_width, D), LOW if late_rows % 16 == 0 else FULL),
            pltpu.VMEM((BLOCK * LEN, D), LOW),
            pltpu.VMEM((BLOCK * LEN, D), LOW),
            pltpu.VMEM((shards, latents, mod_share), FULL),
            pltpu.VMEM((shards, NOTE, D), FULL),
            pltpu.VMEM((D, 3 * D), LOW),
            pltpu.VMEM((D, D), LOW),
        ],
        steps,
        latents * (2 * LEN * D * 4 * D + 4 * HEADS * LEN * LEN * PAIR) * 2,
        "attention_forward",
        after=(early_weights,),
    )
    early_shape = (GROUP // 2, shards, rows, 2 * FF // shards)
    (early_weights_stacked,) = local_call(
        stack,
        ids,
        [(v, False) for v in early_weights_chips],
        [(early_shape, LOW, False)],
        [],
        1,
        D * D,
        "stack",
        after=(branch,),
    )
    early_weights_flipped = flip(early_weights_stacked, 1)
    block_output, grad_mixed, grad_mod_late, keep, send, sum_up, sum_down = local_call(
        perceptron,
        ids,
        [
            (tokens, True),
            (branch, True),
            (mod, True),
            (cotangent, True),
            (early_weights_stacked, False),
            (early_weights_flipped, False),
            (bias_up, False),
            (bias_down, False),
        ],
        [
            (tokens_shape, LOW, True),
            (tokens_shape, FULL, True),
            ((latents, 4, D), FULL, True),
            (early_shape, FULL, False),
            (early_shape, LOW, False),
            ((1, FF), FULL, False),
            ((1, D), FULL, False),
        ],
        [
            pltpu.VMEM((shards, D, 2 * FF // shards), LOW),
            pltpu.VMEM((D, FF), LOW),
            pltpu.VMEM((D, FF), LOW),
            pltpu.VMEM((BLOCK * LEN, FF), LOW),
            pltpu.VMEM((BLOCK * LEN, FF), FULL),
            pltpu.VMEM((D, FF), FULL),
            pltpu.VMEM((D, FF), FULL),
        ],
        steps,
        latents * 2 * LEN * D * FF * 6 * 2,
        "perceptron",
    )

    early_totals = sum_cores(keep, send, ids, "early_sum", ())
    arrived = exchange_chips(early_totals)
    early_chips = sum(piece.astype(FULL) for piece in arrived[1:]) + arrived[0]
    grad_qkv, total_project = local_call(
        attention_backward,
        ids,
        [
            (mod, True),
            (attended, True),
            (grad_mixed, True),
            (qkv, True),
            (probs, True),
            (wo, False),
        ],
        [((latents, LEN, 3 * D), LOW, True), ((D, D), FULL, False)],
        [pltpu.VMEM((BLOCK, LEN, D), LOW)],
        steps,
        latents * (10 * HEADS * LEN * LEN * PAIR + 4 * LEN * D * D),
        "attention_backward",
        after=tuple(early_totals[1:]),
    )
    early_pieces = exchange([early_chips[d].astype(LOW) for d in range(shards)])
    late_shape = (GROUP // 2, shards, rows, late_width)
    tokens_grad, keep, send, extra = local_call(
        attend_backward,
        ids,
        [
            (tokens, True),
            (mod, True),
            (grad_mixed, True),
            (grad_qkv, True),
            (wq, False),
            (total_project, False),
            (grad_mod_late, False),
            (sum_up, False),
            (sum_down, False),
        ],
        [
            (tokens_shape, FULL, True),
            (late_shape, FULL, False),
            (late_shape, LOW, False),
            ((shards, NOTE, D), LOW, False),
        ],
        [
            pltpu.VMEM((D, 3 * D), FULL),
            pltpu.VMEM((latents, 2, D), FULL),
            pltpu.VMEM((NOTE, D), FULL),
        ],
        steps,
        latents * 2 * LEN * D * 6 * D * 2,
        "attend_backward",
        after=(early_chips,),
    )

    late_totals = sum_cores(keep, send, ids, "late_sum", ())
    arrived = exchange_chips(late_totals)
    (early,) = local_call(
        total_kernel,
        ids,
        [(v, False) for v in (early_chips[0], *early_pieces[1:])],
        [(early_pieces[1].shape, LOW, False)],
        [],
        1,
        D * D,
        "early_total",
        after=tuple(late_totals[1:]),
    )
    early_stacked, early_flipped = gather_group(sum_rest(early))
    outgoing = local_call(
        late_pieces,
        ids,
        [(v, False) for v in (*arrived, extra)],
        [((NOTE + rows, D), LOW, False)] * shards,
        [],
        1,
        4 * shards * rows * late_width,
        "late_pieces",
        after=(early,),
    )
    group_latents = shards * latents
    unit = (-(-mod_share // D) + 1) * group_latents + 16
    payload, *shares = local_call(
        partial(combine, shards, latents),
        ids,
        [(v, False) for v in (*exchange(outgoing), *notes, modulate_low)],
        [((rows + unit, D), LOW, False)] + [((latents, D), FULL, False)] * shards,
        [pltpu.VMEM((unit, D), FULL)],
        1,
        2 * shards * NOTE * D * mod_share,
        "combine",
        after=(early_stacked,),
    )
    if lax.axis_size("rep") > GROUP:
        late, others = sum_rest(payload[:rows]), payload[rows:]
        for bit in range(3, lax.axis_size("rep").bit_length() - 1):
            others = jnp.concatenate([others, flip(others, 1 << bit)], axis=0)
        payload = jnp.concatenate([late, others], axis=0)
    late_stacked, late_flipped = gather_group(payload)

    grad_cond_low = shares[0]
    for d in range(1, shards):
        grad_cond_low = grad_cond_low + shift(shares[d], shards - d)
    _, silu_back = jax.vjp(jax.nn.silu, condition.astype(FULL))
    condition_grad = silu_back(grad_cond_low)[0]

    def as_held(values):
        return [v.T if turned else v for v, turned in zip(values, TURNED)]

    masters = as_held(
        [attend_weight, project_weight, expand_weight, contract_weight, modulate_weight]
    )
    moments = as_held(
        [attend_moment, project_moment, expand_moment, contract_moment, modulate_moment]
    )
    shapes = [m.shape for m in masters]
    widths = [whole // shards for whole in COLUMNS]
    slot_width = max(stop - start for start, stop in slot_spans(widths))
    piece_rows = 128 * len(TRIANGLE) // shards
    sources = [
        (v, False) for v in (late_stacked, late_flipped, early_stacked, early_flipped, *moments)
    ]
    gram, columns = local_call(
        partial(gram_kernel, group_latents),
        ids,
        sources,
        [((shards, piece_rows, 128), FULL, False), ((slot_width, D), FULL, False)],
        [
            pltpu.VMEM((D, D), FULL),
            pltpu.VMEM((128 * len(TRIANGLE), 128), FULL),
            pltpu.VMEM(shapes[2], FULL),
            pltpu.VMEM(shapes[4], FULL),
        ],
        1,
        6 * D * D * D,
        "gram",
    )
    *results, bias_block = local_call(
        partial(momenta_kernel, group_latents),
        ids,
        sources,
        [(shape, FULL, False) for shape in shapes * 2] + [((8, D), FULL, False)],
        [pltpu.VMEM((D, D), FULL)],
        1,
        D * D * D,
        "momenta",
        after=(gram,),
    )
    gradients, momenta = as_held(results[0:5]), as_held(results[5:10])
    piece = sum(exchange([gram[d] for d in range(shards)]))
    (answer,) = local_call(
        polynomial_kernel,
        ids,
        [(p, False) for p in exchange([piece] * shards)] + [(columns, False)],
        [((slot_width, D), LOW, False)],
        [pltpu.VMEM((128 * len(TRIANGLE), 128), FULL), pltpu.VMEM((D, D), FULL)],
        1,
        2 * 3 * 18 * D * D * D,
        "polynomial",
        after=(condition_grad, bias_block),
    )
    updated = local_call(
        update_kernel,
        ids,
        [(v, False) for v in (*gather_group(answer), *masters)],
        [(shape, FULL, False) for shape in shapes],
        [pltpu.VMEM((GROUP, slot_width, D), LOW)],
        1,
        2 * D * sum(widths),
        "update",
    )
    updated = as_held(updated)

    bias_gradient = bias_block.reshape(-1)[:bias_share]
    bias_momentum = BETA_ONE * bias_first + (1.0 - BETA_ONE) * bias_gradient
    bias_variance = BETA_TWO * bias_second + (1.0 - BETA_TWO) * bias_gradient * bias_gradient
    corrected_first = bias_momentum / (1.0 - BETA_ONE**STEP)
    corrected_second = bias_variance / (1.0 - BETA_TWO**STEP)
    bias_updated = biases * (1.0 - ADAM_RATE * WEIGHT_DECAY) - ADAM_RATE * corrected_first / (
        jnp.sqrt(corrected_second) + ADAM_EPSILON
    )
    return (
        block_output,
        tokens_grad,
        condition_grad,
        *gradients,
        *momenta,
        *updated,
        bias_gradient,
        bias_momentum,
        bias_variance,
        bias_updated,
    )


def solution(mesh):
    rows = P(("shard", "rep"), None, None)
    vectors = P(("shard", "rep"), None)
    columns = P(None, "shard")
    flat = P("shard")
    return jax.shard_map(
        per_device,
        mesh=mesh,
        in_specs=(rows, vectors, rows) + (columns,) * 5 + (flat,) + (columns,) * 5 + (flat,) * 2,
        out_specs=(rows, rows, vectors) + (columns,) * 15 + (flat,) * 4,
        check_vma=False,
    )
```

```python
from functools import partial
import math

import jax
import jax.numpy as jnp
from jax import lax
from jax.experimental import pallas as pl
from jax.experimental.pallas import tpu as pltpu
from jax.sharding import PartitionSpec as P

D = 384
HEADS = 6
HEAD = 64
FF = 1536
LEN = 256
NS_ITERS = 5
STEP = 10
PAIR = 2 * HEAD
CHUNK = 512
GROUP = 8
BLOCK = 2
BIAS_LEN = 6 * D + FF + D
NOTE = 16
GRANTS = {
    "attention_forward": 40,
    "perceptron": 42,
    "prepare": 60,
    "attention_backward": 32,
    "attend_backward": 36,
    "momenta": 32,
    "gram": 24,
    "polynomial": 20,
    "update": 24,
}

POLY_LINEAR = 3.4445
POLY_CUBIC = -4.775
POLY_QUINTIC = 2.0315
MOMENTUM = 0.95
MUON_RATE = 0.4
WEIGHT_DECAY = 0.01
ADAM_RATE = 0.1
BETA_ONE = 0.9
BETA_TWO = 0.999
ADAM_EPSILON = 1e-08
GELU_SLOPE = math.sqrt(2.0 / math.pi)
GELU_CUBIC = 0.044715

LOW = jnp.bfloat16
FULL = jnp.float32

SLOTS = ((4, 0), (4, 1), (0, 0), (2, 0), (2, 1), (3, 0), (3, 1), (1, 0))


def shift(value, distance):
    size = lax.axis_size("shard")
    return lax.ppermute(value, "shard", [(i, (i + distance) % size) for i in range(size)])


def flip(value, mask):
    size = lax.axis_size("rep")
    return lax.ppermute(value, "rep", [(i, i ^ mask) for i in range(size)])


def exchange(pieces):
    return [pieces[0]] + [shift(pieces[d], d) for d in range(1, len(pieces))]


def gather_chips(value):
    return [value] + [flip(value, 2 * t) for t in range(1, GROUP // 2)]


def gather_group(value):
    stacked = jnp.stack(gather_chips(value))
    return stacked, flip(stacked, 1)


def sum_cores(keep, send, ids, name, after):
    received = flip(send, 1)
    shape = keep.shape[1:]
    return local_call(
        split_sum,
        ids,
        [(keep, False), (received, False)],
        [(shape, FULL, False)] + [(shape, LOW, False)] * (keep.shape[0] - 1),
        [],
        1,
        keep.size,
        name,
        after=after,
    )


def exchange_chips(totals):
    return [totals[0]] + [flip(totals[t], 2 * t) for t in range(1, GROUP // 2)]


def sum_rest(value):
    for bit in range(3, lax.axis_size("rep").bit_length() - 1):
        value = (value.astype(FULL) + flip(value, 1 << bit).astype(FULL)).astype(LOW)
    return value


def dot(left, right):
    return lax.dot_general(left, right, (((1,), (0,)), ((), ())), preferred_element_type=FULL)


def dot_nt(left, right):
    return lax.dot_general(left, right, (((1,), (1,)), ((), ())), preferred_element_type=FULL)


def dot_tn(left, right):
    return lax.dot_general(left, right, (((0,), (0,)), ((), ())), preferred_element_type=FULL)


def split_low(value):
    high = value.astype(LOW)
    return high, (value - high.astype(FULL)).astype(LOW)


def dot_split(left, right, product=dot):
    return product(left[0], right[0]) + (product(left[0], right[1]) + product(left[1], right[0]))


def normalize(values):
    centered = values - jnp.mean(values, -1, keepdims=True)
    inverse_spread = lax.rsqrt(jnp.mean(centered * centered, -1, keepdims=True) + 1e-06)
    return centered * inverse_spread, inverse_spread


def normalize_back(upstream, normed, inverse_spread):
    return inverse_spread * (
        upstream
        - jnp.mean(upstream, -1, keepdims=True)
        - normed * jnp.mean(upstream * normed, -1, keepdims=True)
    )


def local_call(kernel, ids, inputs, outputs, scratch, steps, flops, name, after=()):
    def run(*refs):
        kernel(*refs[: 1 + len(inputs)], *refs[1 + len(inputs) + len(after) :])

    def spec(shape, blocked):
        zeros = (0,) * (len(shape) - 1)
        if isinstance(blocked, tuple):
            rows, place = blocked
            return pl.BlockSpec(
                (rows,) + tuple(shape[1:]), lambda i, ids: (place(ids[1]),) + zeros
            )
        if blocked:
            block = (shape[0] // steps,) + tuple(shape[1:])
            return pl.BlockSpec(block, lambda i, _: (i,) + zeros)
        return pl.BlockSpec(tuple(shape), lambda i, _: (0,) + zeros)

    moved = sum(v.size * v.dtype.itemsize for v, _ in inputs)
    moved += sum(math.prod(shape) * jnp.dtype(kind).itemsize for shape, kind, _ in outputs)
    return pl.pallas_call(
        run,
        grid_spec=pltpu.PrefetchScalarGridSpec(
            num_scalar_prefetch=1,
            grid=(steps,),
            in_specs=[spec(v.shape, blocked) for v, blocked in inputs]
            + [pl.BlockSpec(memory_space=pl.ANY) for _ in after],
            out_specs=[spec(shape, blocked) for shape, _, blocked in outputs],
            scratch_shapes=scratch,
        ),
        out_shape=[jax.ShapeDtypeStruct(shape, kind) for shape, kind, _ in outputs],
        compiler_params=pltpu.CompilerParams(
            dimension_semantics=("arbitrary",), vmem_limit_bytes=GRANTS.get(name, 16) * 1024 * 1024
        ),
        cost_estimate=pl.CostEstimate(flops=flops, bytes_accessed=moved, transcendentals=0),
        name=name,
    )(ids, *[v for v, _ in inputs], *after)


def pieces_of(ids, stacked, flipped):
    for t in range(GROUP // 2):
        for bit, blocks in enumerate((stacked, flipped)):
            yield ids[1] ^ (2 * t + bit), blocks.at[t]


def rows_at(place, rows):
    return pl.ds(pl.multiple_of(place * rows, rows), rows)


def turn(value):
    filled = value.shape[1]
    extra = -filled % 128
    if extra:
        value = jnp.concatenate([value, jnp.zeros((value.shape[0], extra), value.dtype)], axis=1)
    return value.T[:filled]


def head_masks(values):
    lane = lax.broadcasted_iota(jnp.int32, values.shape, 1) % PAIR
    zero = jnp.zeros_like(values)
    return (
        jnp.where(lane < HEAD, values, zero).astype(LOW),
        jnp.where(lane < HEAD, zero, values).astype(LOW),
    )


def split_sum(ids, keep, received, own, *others):
    own[...] = keep[0] + received[0].astype(FULL)
    for t, other in enumerate(others):
        other[...] = (keep[t + 1] + received[t + 1].astype(FULL)).astype(LOW)


def modulation_kernel(ids, *refs):
    shards = refs[-1].shape[0]
    notes, weight, answers, weight_low, stacked = (
        refs[:shards], refs[shards], refs[shards + 1 : -2], refs[-2], refs[-1],
    )
    low = weight[...].astype(LOW)
    weight_low[...] = low
    for d, (note, answer) in enumerate(zip(notes, answers)):
        answer[...] = dot_nt(note[:NOTE, :], low)[: answer.shape[0]]
        stacked[d] = note[NOTE:, :]


def total_kernel(ids, own, *refs):
    total = own[...]
    for piece in refs[:-1]:
        total = total + piece[...].astype(FULL)
    refs[-1][...] = total.astype(LOW)


def prepare(ids, condition, biases, attend, project, note, first):
    latents = condition.shape[0]
    value = condition[...].astype(FULL)
    first[...] = jnp.zeros_like(first)
    first[:latents, :] = value / (1.0 + jnp.exp(-value))
    share = biases.shape[1]
    for b in range(-(-share // D)):
        filled = min(D, share - b * D)
        first[latents + b : latents + b + 1, :filled] = biases[:, b * D : b * D + filled]
    note[:NOTE, :] = first[...].astype(LOW)

    @pl.when(ids[1] < 6)
    def _():
        note[NOTE:, :] = attend[...].astype(LOW)

    @pl.when(ids[1] >= 6)
    def _():
        note[NOTE:, :] = project[...].astype(LOW)


def pack(ids, *refs):
    start = 0
    for weight in refs[:-1]:
        width = weight.shape[1]
        refs[-1][:, start : start + width] = weight[...].astype(LOW)
        start = start + width


def stack(ids, *refs):
    for t, block in enumerate(refs[:-1]):
        refs[-1][t] = block[...]


def attention_forward(
    ids, tokens, stacked, flipped, *refs,
):
    shards = (len(refs) - 16) // 2
    answers, notes = refs[:shards], refs[shards : 2 * shards]
    (
        qkv, probs, attended, branch, wq, wo, mod_all, bias_up, bias_down,
        ordered, query_a, query_b, mod_parts, bias_parts, wq_plain, wo_plain,
    ) = refs[2 * shards :]
    rows = ordered.shape[1] // GROUP
    wide, narrow = 3 * D // shards, D // shards

    @pl.when(pl.program_id(0) == 0)
    def _():
        for place, block in pieces_of(ids, stacked, flipped):
            for d in range(shards):
                source = lax.rem(ids[0] - d + shards, shards)
                ordered[source, rows_at(place, rows), :] = block[d].astype(ordered.dtype)
        for s in range(shards):
            wq[s * wide : (s + 1) * wide, :] = ordered[s, :wide, :].astype(LOW)
            wo[s * narrow : (s + 1) * narrow, :] = ordered[s, wide:, :].astype(LOW)
        wq_plain[...] = wq[...].T
        wo_plain[...] = wo[...].T
        for d in range(shards):
            mod_parts[lax.rem(ids[0] + d, shards)] = answers[d][...]
            bias_parts[lax.rem(ids[0] - d + shards, shards)] = notes[d][:NOTE, :].astype(FULL)
        latents = mod_all.shape[0]
        share = BIAS_LEN // shards
        pieces = []
        for s in range(shards):
            for b in range(-(-share // D)):
                row = bias_parts[s, latents + b : latents + b + 1, :]
                pieces.append(row[:, : min(D, share - b * D)])
        bias = jnp.concatenate(pieces, axis=1)
        whole = jnp.concatenate([mod_parts[s] for s in range(shards)], axis=1) + bias[:, : 6 * D]
        for latent in range(latents):
            for b in range(6):
                mod_all[latent, b : b + 1, :] = whole[latent : latent + 1, b * D : (b + 1) * D]
        bias_up[...] = bias[:, 6 * D : 6 * D + FF]
        bias_down[...] = bias[:, 6 * D + FF :]

    count = tokens.shape[0]
    mod = mod_all[pl.ds(pl.program_id(0) * count, count)]
    normed, _ = normalize(tokens[...].astype(FULL))
    hidden = normed * (1.0 + mod[:, 1:2, :]) + mod[:, 0:1, :]
    hidden = hidden.reshape(count * LEN, D).astype(LOW)
    queries = dot(hidden, wq_plain[:, :D])
    masked_a, masked_b = head_masks(queries)
    query_a[...] = masked_a
    query_b[...] = masked_b
    qkv[:, :, :D] = queries.astype(LOW).reshape(count, LEN, D)
    qkv[:, :, D:] = dot(hidden, wq_plain[:, D:]).astype(LOW).reshape(count, LEN, 2 * D)
    for latent in range(count):
        span = slice(latent * LEN, (latent + 1) * LEN)
        for pair in range(HEADS // 2):
            lanes = slice(pair * PAIR, (pair + 1) * PAIR)
            keys = qkv[latent, :, D + pair * PAIR : D + (pair + 1) * PAIR]
            values = qkv[latent, :, 2 * D + pair * PAIR : 2 * D + (pair + 1) * PAIR].T
            results = []
            for member, masked in enumerate((query_a, query_b)):
                scores = dot_nt(keys, masked[span, lanes]) * (HEAD ** (-0.5) / math.log(2.0))
                top = jnp.max(scores, 0, keepdims=True)
                raised = jnp.exp2(scores - top)
                share = (raised * (1.0 / jnp.sum(raised, 0, keepdims=True))).astype(LOW)
                probs[latent, 2 * pair + member] = share
                results.append(dot(values[member * HEAD : (member + 1) * HEAD], share))
            attended[latent, :, lanes] = jnp.concatenate(results, axis=0).T.astype(LOW)
    branch[...] = dot(attended[...].reshape(count * LEN, D), wo_plain[...]).reshape(count, LEN, D)


def perceptron(
    ids, tokens, branch, mod, cotangent, attended, stacked, flipped, bias_up, bias_down, wo,
    out, grad_mixed, grad_mod, keep, send, sum_up, sum_down, grad_attended, total_project,
    ordered, wu, wd, act, slope, total_up, total_down,
):
    shards = ordered.shape[0]
    rows = D // GROUP
    width = FF // shards
    step = pl.program_id(0)

    @pl.when(step == 0)
    def _():
        for place, block in pieces_of(ids, stacked, flipped):
            for d in range(shards):
                source = lax.rem(ids[0] - d + shards, shards)
                ordered[source, rows_at(place, rows), :] = block[d]
        for i in range(GROUP):
            span = slice(i * rows, (i + 1) * rows)
            pieces = [ordered[s, span, :] for s in range(shards)]
            wu[span, :] = jnp.concatenate([p[:, :width] for p in pieces], axis=1)
            wd[span, :] = jnp.concatenate([p[:, width:] for p in pieces], axis=1)
        total_up[...] = jnp.zeros_like(total_up)
        total_down[...] = jnp.zeros_like(total_down)
        sum_up[...] = jnp.zeros_like(sum_up)
        sum_down[...] = jnp.zeros_like(sum_down)
        total_project[...] = jnp.zeros_like(total_project)

    count = tokens.shape[0]
    flat = count * LEN
    branch_out = branch[...]
    mixed = tokens[...].astype(FULL) + mod[:, 2:3, :] * branch_out
    normed, inverse_spread = normalize(mixed)
    hidden = (normed * (1.0 + mod[:, 4:5, :]) + mod[:, 3:4, :]).reshape(flat, D).astype(LOW)
    result = jnp.zeros((flat, D), FULL)
    for start in range(0, FF, CHUNK):
        span = slice(start, start + CHUNK)
        u = dot(hidden, wu[:, span]) + bias_up[:, span]
        square = u * u
        half = 0.5 + 0.5 * jnp.tanh(u * (GELU_SLOPE + (GELU_SLOPE * GELU_CUBIC) * square))
        act_low = (u * half).astype(LOW)
        act[:, span] = act_low
        steep = u * (2.0 * GELU_SLOPE + (6.0 * GELU_SLOPE * GELU_CUBIC) * square)
        slope[:, span] = half + (half - half * half) * steep
        result = result + dot_nt(act_low, wd[:, span])
    result = (result + bias_down[...]).reshape(count, LEN, D)
    gate = mod[:, 5:6, :]
    out[...] = (mixed + gate * result).astype(LOW)
    upstream = cotangent[...].astype(FULL)
    grad_mod[:, 3:4, :] = jnp.sum(upstream * result, axis=1, keepdims=True)
    grad_result = (gate * upstream).reshape(flat, D).astype(LOW)
    sum_down[...] += jnp.sum(grad_result.astype(FULL), axis=0, keepdims=True)
    grad_hidden = jnp.zeros((flat, D), FULL)
    for start in range(0, FF, CHUNK):
        span = slice(start, start + CHUNK)
        grad_u = (dot(grad_result, wd[:, span]) * slope[:, span]).astype(LOW)
        sum_up[:, span] += jnp.sum(grad_u.astype(FULL), axis=0, keepdims=True)
        total_down[:, span] += dot_tn(grad_result, act[:, span])
        total_up[:, span] += dot_tn(hidden, grad_u)
        grad_hidden = grad_hidden + dot_nt(grad_u, wu[:, span])
    grad_hidden = grad_hidden.reshape(count, LEN, D)
    grad_mod[:, 1:2, :] = jnp.sum(grad_hidden, axis=1, keepdims=True)
    grad_mod[:, 2:3, :] = jnp.sum(grad_hidden * normed, axis=1, keepdims=True)
    back = upstream + normalize_back(
        grad_hidden * (1.0 + mod[:, 4:5, :]), normed, inverse_spread
    )
    grad_mixed[...] = back
    grad_mod[:, 0:1, :] = jnp.sum(back * branch_out, axis=1, keepdims=True)
    grad_branch = (mod[:, 2:3, :] * back).reshape(flat, D).astype(LOW)
    total_project[...] += dot_tn(attended[...].reshape(flat, D), grad_branch)
    grad_attended[...] = dot(grad_branch, wo[...]).astype(LOW).reshape(count, LEN, D)

    @pl.when(step == pl.num_programs(0) - 1)
    def _():
        shard, low = ids[0], ids[1]
        for j in range(GROUP):
            span = pl.ds(pl.multiple_of((low ^ j) * rows, rows), rows)
            for s in range(shards):
                d = lax.rem(s - shard + shards, shards)
                lanes = slice(s * width, (s + 1) * width)
                piece = jnp.concatenate([total_up[span, lanes], total_down[span, lanes]], axis=1)
                if j & 1:
                    send[j // 2, d] = piece.astype(LOW)
                else:
                    keep[j // 2, d] = piece


def attention_backward(ids, qkv, probs, grad_attended, grad_qkv):
    mask = lax.broadcasted_iota(jnp.int32, (LEN, PAIR), 1) < HEAD
    scale = HEAD ** (-0.5)
    for latent in range(qkv.shape[0]):
        for pair in range(HEADS // 2):
            lanes = slice(pair * PAIR, (pair + 1) * PAIR)
            key_lanes = slice(D + pair * PAIR, D + (pair + 1) * PAIR)
            value_lanes = slice(2 * D + pair * PAIR, 2 * D + (pair + 1) * PAIR)
            queries = qkv[latent, :, lanes]
            keys = qkv[latent, :, key_lanes].T
            values = qkv[latent, :, value_lanes]
            upper = grad_attended[latent, :, lanes]
            masked = head_masks(upper.astype(FULL))
            by_query, by_key, by_value = [], [], []
            for member in range(2):
                share = probs[latent, 2 * pair + member]
                weight = share.astype(FULL)
                grad_share = dot_nt(values, masked[member])
                product = weight * grad_share
                grad_scores = (
                    product - weight * jnp.sum(product, 0, keepdims=True)
                ).astype(LOW)
                by_query.append(dot(keys[member * HEAD : (member + 1) * HEAD], grad_scores))
                by_key.append(dot(grad_scores, queries))
                by_value.append(dot(share, upper))
            merged = jnp.concatenate(by_query, axis=0).T * scale
            grad_qkv[latent, :, lanes] = merged.astype(LOW)
            merged = jnp.where(mask, by_key[0], by_key[1]) * scale
            grad_qkv[latent, :, key_lanes] = merged.astype(LOW)
            merged = jnp.where(mask, by_value[0], by_value[1])
            grad_qkv[latent, :, value_lanes] = merged.astype(LOW)


def attend_backward(
    ids, tokens, mod, grad_mixed, grad_qkv, wq, total_project, grad_mod_late, sum_up, sum_down,
    grad_tokens, keep, send, extra,
    total_attend, grad_mod, extra_rows,
):
    rows = D // GROUP
    shards = keep.shape[1]
    step = pl.program_id(0)

    @pl.when(step == 0)
    def _():
        total_attend[...] = jnp.zeros_like(total_attend)

    count = tokens.shape[0]
    flat = count * LEN
    normed, inverse_spread = normalize(tokens[...].astype(FULL))
    hidden = (normed * (1.0 + mod[:, 1:2, :]) + mod[:, 0:1, :]).reshape(flat, D).astype(LOW)
    grad_low = grad_qkv[...].reshape(flat, 3 * D)
    total_attend[...] += dot_tn(hidden, grad_low)
    grad_hidden = dot(grad_low, wq[...]).reshape(count, LEN, D)
    mine = pl.ds(step * count, count)
    grad_mod[mine, 0:1, :] = jnp.sum(grad_hidden, axis=1, keepdims=True)
    grad_mod[mine, 1:2, :] = jnp.sum(grad_hidden * normed, axis=1, keepdims=True)
    grad_tokens[...] = grad_mixed[...] + normalize_back(
        grad_hidden * (1.0 + mod[:, 1:2, :]), normed, inverse_spread
    )

    @pl.when(step == pl.num_programs(0) - 1)
    def _():
        shard, low = ids[0], ids[1]
        wide, narrow = 3 * D // shards, D // shards
        for j in range(GROUP):
            span = rows_at(low ^ j, rows)
            whole_attend, whole_project = total_attend[span, :], total_project[span, :]
            for s in range(shards):
                d = lax.rem(s - shard + shards, shards)
                piece = jnp.concatenate(
                    [
                        whole_attend[:, s * wide : (s + 1) * wide],
                        whole_project[:, s * narrow : (s + 1) * narrow],
                    ],
                    axis=1,
                )
                if j & 1:
                    send[j // 2, d] = piece.astype(LOW)
                else:
                    keep[j // 2, d] = piece
        latents = grad_mod.shape[0]
        columns = [grad_mod[:, b, :] for b in range(2)] + [grad_mod_late[:, b, :] for b in range(4)]
        whole = jnp.concatenate(columns, axis=1).astype(LOW).astype(FULL)
        sums = jnp.sum(whole, axis=0, keepdims=True)
        sums = jnp.concatenate([sums, sum_up[...], sum_down[...]], axis=1)
        mod_share, bias_share = 6 * D // shards, BIAS_LEN // shards
        blocks, lines = -(-mod_share // D), -(-bias_share // D)

        def padded(values, start, stop):
            part = values[:, start : min(start + D, stop)]
            if part.shape[1] < D:
                rest = jnp.zeros((part.shape[0], D - part.shape[1]), FULL)
                part = jnp.concatenate([part, rest], axis=1)
            return part

        extra_rows[...] = jnp.zeros_like(extra_rows)
        for s in range(shards):
            for b in range(blocks):
                extra_rows[b * latents : (b + 1) * latents, :] = padded(
                    whole, s * mod_share + b * D, (s + 1) * mod_share
                )
            for b in range(lines):
                row = padded(sums, s * bias_share + b * D, (s + 1) * bias_share)
                high = row.astype(LOW).astype(FULL)
                place = blocks * latents + b
                extra_rows[place : place + 1, :] = high
                extra_rows[place + lines : place + lines + 1, :] = row - high
            extra[lax.rem(s - shard + shards, shards)] = extra_rows[...].astype(LOW)


def late_pieces(ids, own, first, second, third, extra, *pieces):
    total = own[...]
    for received in (first, second, third):
        total = total + received[...].astype(FULL)
    for d, piece in enumerate(pieces):
        piece[:NOTE, :] = extra[d]
        if total.shape[2] < D:
            piece[NOTE:, :] = jnp.zeros((total.shape[1], D), LOW)
        piece[NOTE:, : total.shape[2]] = total[d].astype(LOW)


def combine(shards, latents, ids, *refs):
    incoming, notes, weight, payload = (
        refs[:shards], refs[shards : 2 * shards], refs[2 * shards], refs[2 * shards + 1],
    )
    answers, rows_ref = refs[2 * shards + 2 : -1], refs[-1]
    rows = D // GROUP
    mod_share, bias_share = 6 * D // shards, BIAS_LEN // shards
    blocks, lines = -(-mod_share // D), -(-bias_share // D)
    total = jnp.zeros((rows, D), FULL)
    bias = jnp.zeros((NOTE, D), FULL)
    for d in range(shards):
        total = total + incoming[d][NOTE:, :].astype(FULL)
        extra = incoming[d][:NOTE, :].astype(FULL)
        bias = bias + extra
        for b in range(blocks):
            start = (b * shards + d) * latents
            rows_ref[start : start + latents, :] = extra[b * latents : (b + 1) * latents]
        start = (blocks * shards + d) * latents
        rows_ref[start : start + latents, :] = notes[d][:NOTE, :].astype(FULL)[:latents]
    payload[:rows, :] = total.astype(LOW)
    count = (blocks + 1) * shards * latents
    start = blocks * latents
    bias = bias[start : start + lines] + bias[start + lines : start + 2 * lines]
    high = bias.astype(LOW).astype(FULL)
    rows_ref[count:, :] = jnp.zeros((16, D), FULL)
    rows_ref[count : count + lines, :] = high
    rows_ref[count + 8 : count + 8 + lines, :] = bias - high
    payload[rows:, :] = rows_ref[...].astype(LOW)
    for d, answer in enumerate(answers):
        result = jnp.zeros((NOTE, D), FULL)
        for b in range(blocks):
            filled = min(D, mod_share - b * D)
            product = dot(incoming[d][:NOTE, :filled], weight[b * D : b * D + filled, :])
            result = result + shifted(product, b * latents)
        answer[...] = result[:latents]


def shifted(values, count):
    if count == 0:
        return values
    return jnp.concatenate([values[count:], values[:count]], axis=0)


COLUMNS = (3 * D, D, FF, FF, 6 * D)
TURNED = (True, True, False, False, True)
TRIANGLE = ((0, 0), (0, 1), (0, 2), (1, 1), (1, 2), (2, 2))


def slot_spans(widths):
    counts = [sum(1 for m, _ in SLOTS if m == number) for number in range(len(widths))]
    return [
        (part * (widths[m] // counts[m]), (part + 1) * (widths[m] // counts[m]))
        for m, part in SLOTS
    ]


def late_parts(latents, widths, late, late_flipped):
    rows = D // GROUP
    blocks = -(-widths[4] // D)
    unit = (blocks + 1) * latents + 16
    parts = [
        ref.at[t, pl.ds(start, unit), :]
        for ref in (late, late_flipped)
        for t in range(GROUP // 2)
        for start in range(rows, late.shape[1], unit)
    ]

    def rows_of(start):
        return jnp.concatenate([p[start : start + latents, :] for p in parts], axis=0)

    return parts, blocks, rows_of


def modulate_gradient(latents, widths, late, late_flipped, target):
    _, blocks, rows_of = late_parts(latents, widths, late, late_flipped)
    cond = rows_of(blocks * latents)
    for block in range(blocks):
        filled = min(D, widths[4] - block * D)
        target[block * D : block * D + filled, :] = dot_tn(rows_of(block * latents), cond)[:filled]


def late_gradient(ids, late, late_flipped, late_whole):
    rows = D // GROUP
    for place, block in pieces_of(ids, late, late_flipped):
        late_whole[rows_at(place, rows), :] = block[:rows, :].astype(FULL)
    return turn(late_whole[...])


def mix(moment, grad):
    moment = MOMENTUM * moment + grad
    return moment, grad + MOMENTUM * moment


def gram_kernel(latents, ids, late, late_flipped, early, early_flipped, *refs):
    moments, gram, columns = refs[0:5], refs[5], refs[6]
    late_whole, flat_gram, early_whole, modulate_whole = refs[7:11]
    low = ids[1]
    rows = D // GROUP
    shards = gram.shape[0]
    widths = [whole // shards for whole in COLUMNS]
    spans = slot_spans(widths)
    for number in range(5):
        owners = [k for k, (m, _) in enumerate(SLOTS) if m == number]
        condition = low == owners[0]
        for owner in owners[1:]:
            condition = condition | (low == owner)

        @pl.when(condition)
        def _(number=number, owners=owners):
            if number < 2:
                start = 0 if number == 0 else widths[0]
                grad = late_gradient(ids, late, late_flipped, late_whole)
                grad = grad[start : start + widths[number]]
            elif number < 4:
                start = 0 if number == 2 else widths[2]
                for place, block in pieces_of(ids, early, early_flipped):
                    piece = block[...].astype(FULL)[:, start : start + widths[number]]
                    early_whole[rows_at(place, rows), :] = piece
                grad = early_whole[...]
            else:
                modulate_gradient(latents, widths, late, late_flipped, modulate_whole)
                grad = modulate_whole[...]
            mixed = mix(moments[number][...], grad)[1]
            parts = split_low(mixed)
            whole = dot_split(parts, parts, dot_tn if TURNED[number] else dot_nt)
            for place, (a, b) in enumerate(TRIANGLE):
                flat_gram[place * 128 : (place + 1) * 128, :] = whole[
                    a * 128 : (a + 1) * 128, b * 128 : (b + 1) * 128
                ]
            if not TURNED[number]:
                mixed = turn(mixed)
            for owner in owners:

                @pl.when(low == owner)
                def _(owner=owner, mixed=mixed):
                    start, stop = spans[owner]
                    filled = stop - start
                    columns[:filled, :] = mixed[start:stop]
                    if filled < columns.shape[0]:
                        columns[filled:, :] = jnp.zeros((columns.shape[0] - filled, D), FULL)

    size = gram.shape[1]
    for s in range(shards):
        gram[s] = flat_gram[s * size : (s + 1) * size, :]


def momenta_kernel(latents, ids, late, late_flipped, early, early_flipped, *refs):
    moments, grads, momenta = refs[0:5], refs[5:10], refs[10:15]
    bias, late_whole = refs[15:17]
    rows = D // GROUP
    widths = [m.shape[0 if turned else 1] for m, turned in zip(moments, TURNED)]
    turned = late_gradient(ids, late, late_flipped, late_whole)
    grads[0][...] = turned[: widths[0]]
    grads[1][...] = turned[widths[0] : widths[0] + widths[1]]
    for place, block in pieces_of(ids, early, early_flipped):
        piece = block[...].astype(FULL)
        grads[2][rows_at(place, rows), :] = piece[:, : widths[2]]
        grads[3][rows_at(place, rows), :] = piece[:, widths[2] :]
    modulate_gradient(latents, widths, late, late_flipped, grads[4])
    parts, blocks, _ = late_parts(latents, widths, late, late_flipped)
    total = jnp.zeros((16, D), FULL)
    for part in parts:
        total = total + part[(blocks + 1) * latents :, :].astype(FULL)
    bias[...] = total[:8] + total[8:]
    for number in range(5):
        momenta[number][...] = mix(moments[number][...], grads[number][...])[0]


def polynomial_kernel(ids, *refs):
    pieces, columns, answer, gram_ref = refs
    flat_gram = pieces.reshape(128 * len(TRIANGLE), 128)
    for place, (a, b) in enumerate(TRIANGLE):
        block = flat_gram[place * 128 : (place + 1) * 128, :]
        gram_ref[a * 128 : (a + 1) * 128, b * 128 : (b + 1) * 128] = block
        if a != b:
            gram_ref[b * 128 : (b + 1) * 128, a * 128 : (a + 1) * 128] = block.T
    gram = gram_ref[...]
    diagonal = lax.broadcasted_iota(jnp.int32, (D, D), 0) == lax.broadcasted_iota(
        jnp.int32, (D, D), 1
    )
    trace = jnp.sum(jnp.where(diagonal, gram, 0.0))
    scale = 1.0 / (jnp.sqrt(jnp.full((1, 1), trace)) + 1e-07)
    gram = (gram * scale) * scale
    product = jnp.where(diagonal, 1.0, 0.0)
    for step in range(NS_ITERS):
        mixing = POLY_CUBIC * gram + POLY_QUINTIC * dot_deep(left_deep(gram), right_deep(gram))
        mixing_deep = left_deep(mixing)
        if step == 0:
            half = POLY_LINEAR * gram + dot_deep(mixing_deep, right_deep(gram))
            product = POLY_LINEAR * product + mixing
        elif step + 1 < NS_ITERS:
            both = jnp.concatenate([gram, product], axis=1)
            both = POLY_LINEAR * both + dot_deep(mixing_deep, right_deep(both))
            half, product = both[:, :D], both[:, D:]
        else:
            product = POLY_LINEAR * product + dot_deep(mixing_deep, right_deep(product))
        if step + 1 < NS_ITERS:
            gram = POLY_LINEAR * half + dot_deep(mixing_deep, right_deep(half))
    answer[...] = dot_deep(left_deep(columns[...] * scale), right_deep(product)).astype(LOW)


def left_deep(value):
    high, rest = split_low(value)
    return jnp.concatenate([high, rest, high], axis=1)


def right_deep(value):
    high, rest = split_low(value)
    return jnp.concatenate([high, high, rest], axis=0)


def dot_deep(left, right):
    return dot(left, right)


def update_kernel(ids, answers, answers_flipped, *refs):
    masters, updated, ordered = refs[:5], refs[5:10], refs[10]
    for place, block in pieces_of(ids, answers, answers_flipped):
        ordered[place] = block[...]
    widths = [m.shape[0 if turned else 1] for m, turned in zip(masters, TURNED)]
    spans = slot_spans(widths)
    for number in range(5):
        factor = MUON_RATE * 0.2 * math.sqrt(COLUMNS[number])
        mine = [k for k, (m, _) in enumerate(SLOTS) if m == number]
        if TURNED[number]:
            for k in mine:
                start, stop = spans[k]
                updated[number][start:stop, :] = masters[number][start:stop, :] * (
                    1.0 - MUON_RATE * WEIGHT_DECAY
                ) - factor * ordered[k, : stop - start, :].astype(FULL)
        else:
            direction = jnp.concatenate(
                [ordered[k, : spans[k][1] - spans[k][0], :].astype(FULL) for k in mine], axis=0
            )
            updated[number][...] = masters[number][...] * (
                1.0 - MUON_RATE * WEIGHT_DECAY
            ) - factor * direction.T


def per_device(
    tokens,
    condition,
    cotangent,
    attend_weight,
    project_weight,
    expand_weight,
    contract_weight,
    modulate_weight,
    biases,
    attend_moment,
    project_moment,
    expand_moment,
    contract_moment,
    modulate_moment,
    bias_first,
    bias_second,
):
    latents = tokens.shape[0]
    steps = latents // BLOCK
    shards = lax.axis_size("shard")
    shard = lax.axis_index("shard")
    low = lax.axis_index("rep") % GROUP
    ids = jnp.stack([shard, low]).astype(jnp.int32)
    rows = D // GROUP
    bias_share = biases.shape[0]
    mod_share = modulate_weight.shape[1]
    late_width = 4 * D // shards
    late_rows = late_width // GROUP

    (note,) = local_call(
        prepare,
        ids,
        [
            (condition, False),
            (biases.reshape(1, -1), False),
            (attend_weight.T, (late_rows, lambda place: jnp.minimum(place, 5))),
            (project_weight.T, (late_rows, lambda place: jnp.maximum(place - 6, 0))),
        ],
        [((NOTE + late_rows, D), LOW, False)],
        [pltpu.VMEM((NOTE, D), FULL)],
        1,
        D * D,
        "prepare",
    )
    notes = exchange([note] * shards)

    *shares, modulate_low, late_weights = local_call(
        modulation_kernel,
        ids,
        [(piece, False) for piece in notes] + [(modulate_weight.T, False)],
        [((latents, mod_share), FULL, False)] * shards
        + [((mod_share, D), LOW, False), ((shards, late_rows, D), LOW, False)],
        [],
        1,
        2 * shards * NOTE * D * mod_share,
        "modulation",
    )
    answers = [shares[0]] + [shift(shares[d], shards - d) for d in range(1, shards)]
    late_weights_chips = gather_chips(late_weights)
    (early_weights,) = local_call(
        pack,
        ids,
        [(w, (rows, lambda place: place)) for w in (expand_weight, contract_weight)],
        [((rows, 2 * FF // shards), LOW, False)],
        [],
        1,
        D * D,
        "pack",
        after=(late_weights,),
    )
    early_weights = jnp.stack(exchange([early_weights] * shards))
    early_weights_chips = gather_chips(early_weights)
    (late_stacked,) = local_call(
        stack,
        ids,
        [(v, False) for v in late_weights_chips],
        [((GROUP // 2, shards, late_rows, D), LOW, False)],
        [],
        1,
        D * D,
        "stack_late",
        after=(early_weights,),
    )
    late_flipped = flip(late_stacked, 1)

    tokens_shape = (latents, LEN, D)
    qkv, probs, attended, branch, wq, wo, mod, bias_up, bias_down = local_call(
        attention_forward,
        ids,
        [(tokens, True), (late_stacked, False), (late_flipped, False)]
        + [(v, False) for v in (*answers, *notes)],
        [
            ((latents, LEN, 3 * D), LOW, True),
            ((latents, HEADS, LEN, LEN), LOW, True),
            (tokens_shape, LOW, True),
            (tokens_shape, FULL, True),
            ((3 * D, D), LOW, False),
            ((D, D), LOW, False),
            ((latents, 6, D), FULL, False),
            ((1, FF), FULL, False),
            ((1, D), FULL, False),
        ],
        [
            pltpu.VMEM((shards, late_width, D), LOW if late_rows % 16 == 0 else FULL),
            pltpu.VMEM((BLOCK * LEN, D), LOW),
            pltpu.VMEM((BLOCK * LEN, D), LOW),
            pltpu.VMEM((shards, latents, mod_share), FULL),
            pltpu.VMEM((shards, NOTE, D), FULL),
            pltpu.VMEM((D, 3 * D), LOW),
            pltpu.VMEM((D, D), LOW),
        ],
        steps,
        latents * (2 * LEN * D * 4 * D + 4 * HEADS * LEN * LEN * PAIR) * 2,
        "attention_forward",
        after=(early_weights,),
    )
    early_shape = (GROUP // 2, shards, rows, 2 * FF // shards)
    (early_weights_stacked,) = local_call(
        stack,
        ids,
        [(v, False) for v in early_weights_chips],
        [(early_shape, LOW, False)],
        [],
        1,
        D * D,
        "stack",
        after=(branch,),
    )
    early_weights_flipped = flip(early_weights_stacked, 1)
    (
        block_output, grad_mixed, grad_mod_late, keep, send, sum_up, sum_down, grad_attended,
        total_project,
    ) = local_call(
        perceptron,
        ids,
        [
            (tokens, True),
            (branch, True),
            (mod, True),
            (cotangent, True),
            (attended, True),
            (early_weights_stacked, False),
            (early_weights_flipped, False),
            (bias_up, False),
            (bias_down, False),
            (wo, False),
        ],
        [
            (tokens_shape, LOW, True),
            (tokens_shape, FULL, True),
            ((latents, 4, D), FULL, True),
            (early_shape, FULL, False),
            (early_shape, LOW, False),
            ((1, FF), FULL, False),
            ((1, D), FULL, False),
            (tokens_shape, LOW, True),
            ((D, D), FULL, False),
        ],
        [
            pltpu.VMEM((shards, D, 2 * FF // shards), LOW),
            pltpu.VMEM((D, FF), LOW),
            pltpu.VMEM((D, FF), LOW),
            pltpu.VMEM((BLOCK * LEN, FF), LOW),
            pltpu.VMEM((BLOCK * LEN, FF), FULL),
            pltpu.VMEM((D, FF), FULL),
            pltpu.VMEM((D, FF), FULL),
        ],
        steps,
        latents * 2 * LEN * D * FF * 6 * 2,
        "perceptron",
    )

    early_totals = sum_cores(keep, send, ids, "early_sum", ())
    arrived = exchange_chips(early_totals)
    early_chips = sum(piece.astype(FULL) for piece in arrived[1:]) + arrived[0]
    (grad_qkv,) = local_call(
        attention_backward,
        ids,
        [(qkv, True), (probs, True), (grad_attended, True)],
        [((latents, LEN, 3 * D), LOW, True)],
        [],
        steps,
        latents * 10 * HEADS * LEN * LEN * PAIR,
        "attention_backward",
        after=tuple(early_totals[1:]),
    )
    early_pieces = exchange([early_chips[d].astype(LOW) for d in range(shards)])
    late_shape = (GROUP // 2, shards, rows, late_width)
    tokens_grad, keep, send, extra = local_call(
        attend_backward,
        ids,
        [
            (tokens, True),
            (mod, True),
            (grad_mixed, True),
            (grad_qkv, True),
            (wq, False),
            (total_project, False),
            (grad_mod_late, False),
            (sum_up, False),
            (sum_down, False),
        ],
        [
            (tokens_shape, FULL, True),
            (late_shape, FULL, False),
            (late_shape, LOW, False),
            ((shards, NOTE, D), LOW, False),
        ],
        [
            pltpu.VMEM((D, 3 * D), FULL),
            pltpu.VMEM((latents, 2, D), FULL),
            pltpu.VMEM((NOTE, D), FULL),
        ],
        steps,
        latents * 2 * LEN * D * 6 * D * 2,
        "attend_backward",
        after=(early_chips,),
    )

    late_totals = sum_cores(keep, send, ids, "late_sum", ())
    arrived = exchange_chips(late_totals)
    (early,) = local_call(
        total_kernel,
        ids,
        [(v, False) for v in (early_chips[0], *early_pieces[1:])],
        [(early_pieces[1].shape, LOW, False)],
        [],
        1,
        D * D,
        "early_total",
        after=tuple(late_totals[1:]),
    )
    early_stacked, early_flipped = gather_group(sum_rest(early))
    outgoing = local_call(
        late_pieces,
        ids,
        [(v, False) for v in (*arrived, extra)],
        [((NOTE + rows, D), LOW, False)] * shards,
        [],
        1,
        4 * shards * rows * late_width,
        "late_pieces",
        after=(early,),
    )
    group_latents = shards * latents
    unit = (-(-mod_share // D) + 1) * group_latents + 16
    payload, *shares = local_call(
        partial(combine, shards, latents),
        ids,
        [(v, False) for v in (*exchange(outgoing), *notes, modulate_low)],
        [((rows + unit, D), LOW, False)] + [((latents, D), FULL, False)] * shards,
        [pltpu.VMEM((unit, D), FULL)],
        1,
        2 * shards * NOTE * D * mod_share,
        "combine",
        after=(early_stacked,),
    )
    if lax.axis_size("rep") > GROUP:
        late, others = sum_rest(payload[:rows]), payload[rows:]
        for bit in range(3, lax.axis_size("rep").bit_length() - 1):
            others = jnp.concatenate([others, flip(others, 1 << bit)], axis=0)
        payload = jnp.concatenate([late, others], axis=0)
    late_stacked, late_flipped = gather_group(payload)

    grad_cond_low = shares[0]
    for d in range(1, shards):
        grad_cond_low = grad_cond_low + shift(shares[d], shards - d)
    _, silu_back = jax.vjp(jax.nn.silu, condition.astype(FULL))
    condition_grad = silu_back(grad_cond_low)[0]

    def as_held(values):
        return [v.T if turned else v for v, turned in zip(values, TURNED)]

    masters = as_held(
        [attend_weight, project_weight, expand_weight, contract_weight, modulate_weight]
    )
    moments = as_held(
        [attend_moment, project_moment, expand_moment, contract_moment, modulate_moment]
    )
    shapes = [m.shape for m in masters]
    widths = [whole // shards for whole in COLUMNS]
    slot_width = max(stop - start for start, stop in slot_spans(widths))
    piece_rows = 128 * len(TRIANGLE) // shards
    sources = [
        (v, False) for v in (late_stacked, late_flipped, early_stacked, early_flipped, *moments)
    ]
    gram, columns = local_call(
        partial(gram_kernel, group_latents),
        ids,
        sources,
        [((shards, piece_rows, 128), FULL, False), ((slot_width, D), FULL, False)],
        [
            pltpu.VMEM((D, D), FULL),
            pltpu.VMEM((128 * len(TRIANGLE), 128), FULL),
            pltpu.VMEM(shapes[2], FULL),
            pltpu.VMEM(shapes[4], FULL),
        ],
        1,
        6 * D * D * D,
        "gram",
    )
    *results, bias_block = local_call(
        partial(momenta_kernel, group_latents),
        ids,
        sources,
        [(shape, FULL, False) for shape in shapes * 2] + [((8, D), FULL, False)],
        [pltpu.VMEM((D, D), FULL)],
        1,
        D * D * D,
        "momenta",
        after=(gram,),
    )
    gradients, momenta = as_held(results[0:5]), as_held(results[5:10])
    piece = jnp.sum(lax.all_to_all(gram, "shard", 0, 0, tiled=True), axis=0)
    pieces = jnp.broadcast_to(piece[None], gram.shape)
    pieces = lax.all_to_all(pieces, "shard", 0, 0, tiled=True)
    (answer,) = local_call(
        polynomial_kernel,
        ids,
        [(pieces, False), (columns, False)],
        [((slot_width, D), LOW, False)],
        [pltpu.VMEM((D, D), FULL)],
        1,
        2 * 3 * 18 * D * D * D,
        "polynomial",
        after=(condition_grad, bias_block),
    )
    updated = local_call(
        update_kernel,
        ids,
        [(v, False) for v in (*gather_group(answer), *masters)],
        [(shape, FULL, False) for shape in shapes],
        [pltpu.VMEM((GROUP, slot_width, D), LOW)],
        1,
        2 * D * sum(widths),
        "update",
    )
    updated = as_held(updated)

    bias_gradient = bias_block.reshape(-1)[:bias_share]
    bias_momentum = BETA_ONE * bias_first + (1.0 - BETA_ONE) * bias_gradient
    bias_variance = BETA_TWO * bias_second + (1.0 - BETA_TWO) * bias_gradient * bias_gradient
    corrected_first = bias_momentum / (1.0 - BETA_ONE**STEP)
    corrected_second = bias_variance / (1.0 - BETA_TWO**STEP)
    bias_updated = biases * (1.0 - ADAM_RATE * WEIGHT_DECAY) - ADAM_RATE * corrected_first / (
        jnp.sqrt(corrected_second) + ADAM_EPSILON
    )
    return (
        block_output,
        tokens_grad,
        condition_grad,
        *gradients,
        *momenta,
        *updated,
        bias_gradient,
        bias_momentum,
        bias_variance,
        bias_updated,
    )


def solution(mesh):
    rows = P(("shard", "rep"), None, None)
    vectors = P(("shard", "rep"), None)
    columns = P(None, "shard")
    flat = P("shard")
    return jax.shard_map(
        per_device,
        mesh=mesh,
        in_specs=(rows, vectors, rows) + (columns,) * 5 + (flat,) + (columns,) * 5 + (flat,) * 2,
        out_specs=(rows, rows, vectors) + (columns,) * 15 + (flat,) * 4,
        check_vma=False,
    )
```

```python
from functools import partial
import math

import jax
import jax.numpy as jnp
from jax import lax
from jax.experimental import pallas as pl
from jax.experimental.pallas import tpu as pltpu
from jax.sharding import PartitionSpec as P

D = 384
HEADS = 6
HEAD = 64
FF = 1536
LEN = 256
NS_ITERS = 5
STEP = 10
PAIR = 2 * HEAD
CHUNK = 512
GROUP = 8
BLOCK = 2
BIAS_LEN = 6 * D + FF + D
NOTE = 16
GRANTS = {
    "attention_forward": 40,
    "perceptron": 40,
    "attention_backward": 32,
    "attend_backward": 36,
    "momenta": 32,
    "gram": 24,
    "polynomial": 20,
    "update": 24,
}

POLY_LINEAR = 3.4445
POLY_CUBIC = -4.775
POLY_QUINTIC = 2.0315
MOMENTUM = 0.95
MUON_RATE = 0.4
WEIGHT_DECAY = 0.01
ADAM_RATE = 0.1
BETA_ONE = 0.9
BETA_TWO = 0.999
ADAM_EPSILON = 1e-08
GELU_SLOPE = math.sqrt(2.0 / math.pi)
GELU_CUBIC = 0.044715

LOW = jnp.bfloat16
FULL = jnp.float32

SLOTS = ((4, 0), (4, 1), (0, 0), (2, 0), (2, 1), (3, 0), (3, 1), (1, 0))


def shift(value, distance):
    size = lax.axis_size("shard")
    return lax.ppermute(value, "shard", [(i, (i + distance) % size) for i in range(size)])


def flip(value, mask):
    size = lax.axis_size("rep")
    return lax.ppermute(value, "rep", [(i, i ^ mask) for i in range(size)])


def exchange(pieces):
    return [pieces[0]] + [shift(pieces[d], d) for d in range(1, len(pieces))]


def gather_chips(value):
    return [value] + [flip(value, 2 * t) for t in range(1, GROUP // 2)]


def gather_group(value):
    stacked = jnp.stack(gather_chips(value))
    return stacked, flip(stacked, 1)


def sum_cores(keep, send, ids, name, after):
    received = flip(send, 1)
    shape = keep.shape[1:]
    return local_call(
        split_sum,
        ids,
        [(keep, False), (received, False)],
        [(shape, FULL, False)] + [(shape, LOW, False)] * (keep.shape[0] - 1),
        [],
        1,
        keep.size,
        name,
        after=after,
    )


def exchange_chips(totals):
    return [totals[0]] + [flip(totals[t], 2 * t) for t in range(1, GROUP // 2)]


def sum_rest(value):
    for bit in range(3, lax.axis_size("rep").bit_length() - 1):
        value = (value.astype(FULL) + flip(value, 1 << bit).astype(FULL)).astype(LOW)
    return value


def dot(left, right):
    return lax.dot_general(left, right, (((1,), (0,)), ((), ())), preferred_element_type=FULL)


def dot_nt(left, right):
    return lax.dot_general(left, right, (((1,), (1,)), ((), ())), preferred_element_type=FULL)


def dot_tn(left, right):
    return lax.dot_general(left, right, (((0,), (0,)), ((), ())), preferred_element_type=FULL)


def split_low(value):
    high = value.astype(LOW)
    return high, (value - high.astype(FULL)).astype(LOW)


def dot_split(left, right, product=dot):
    return product(left[0], right[0]) + (product(left[0], right[1]) + product(left[1], right[0]))


def normalize(values):
    centered = values - jnp.mean(values, -1, keepdims=True)
    inverse_spread = lax.rsqrt(jnp.mean(centered * centered, -1, keepdims=True) + 1e-06)
    return centered * inverse_spread, inverse_spread


def normalize_back(upstream, normed, inverse_spread):
    return inverse_spread * (
        upstream
        - jnp.mean(upstream, -1, keepdims=True)
        - normed * jnp.mean(upstream * normed, -1, keepdims=True)
    )


def local_call(kernel, ids, inputs, outputs, scratch, steps, flops, name, after=()):
    def run(*refs):
        kernel(*refs[: 1 + len(inputs)], *refs[1 + len(inputs) + len(after) :])

    def spec(shape, blocked):
        zeros = (0,) * (len(shape) - 1)
        if isinstance(blocked, tuple):
            rows, place = blocked
            return pl.BlockSpec(
                (rows,) + tuple(shape[1:]), lambda i, ids: (place(ids[1]),) + zeros
            )
        if blocked:
            block = (shape[0] // steps,) + tuple(shape[1:])
            return pl.BlockSpec(block, lambda i, _: (i,) + zeros)
        return pl.BlockSpec(tuple(shape), lambda i, _: (0,) + zeros)

    moved = sum(v.size * v.dtype.itemsize for v, _ in inputs)
    moved += sum(math.prod(shape) * jnp.dtype(kind).itemsize for shape, kind, _ in outputs)
    return pl.pallas_call(
        run,
        grid_spec=pltpu.PrefetchScalarGridSpec(
            num_scalar_prefetch=1,
            grid=(steps,),
            in_specs=[spec(v.shape, blocked) for v, blocked in inputs]
            + [pl.BlockSpec(memory_space=pl.ANY) for _ in after],
            out_specs=[spec(shape, blocked) for shape, _, blocked in outputs],
            scratch_shapes=scratch,
        ),
        out_shape=[jax.ShapeDtypeStruct(shape, kind) for shape, kind, _ in outputs],
        compiler_params=pltpu.CompilerParams(
            dimension_semantics=("arbitrary",), vmem_limit_bytes=GRANTS.get(name, 16) * 1024 * 1024
        ),
        cost_estimate=pl.CostEstimate(flops=flops, bytes_accessed=moved, transcendentals=0),
        name=name,
    )(ids, *[v for v, _ in inputs], *after)


def pieces_of(ids, stacked, flipped):
    for t in range(GROUP // 2):
        for bit, blocks in enumerate((stacked, flipped)):
            yield ids[1] ^ (2 * t + bit), blocks.at[t]


def rows_at(place, rows):
    return pl.ds(pl.multiple_of(place * rows, rows), rows)


def turn(value):
    filled = value.shape[1]
    extra = -filled % 128
    if extra:
        value = jnp.concatenate([value, jnp.zeros((value.shape[0], extra), value.dtype)], axis=1)
    return value.T[:filled]


def head_masks(values):
    lane = lax.broadcasted_iota(jnp.int32, values.shape, 1) % PAIR
    zero = jnp.zeros_like(values)
    return (
        jnp.where(lane < HEAD, values, zero).astype(LOW),
        jnp.where(lane < HEAD, zero, values).astype(LOW),
    )


def split_sum(ids, keep, received, own, *others):
    own[...] = keep[0] + received[0].astype(FULL)
    for t, other in enumerate(others):
        other[...] = (keep[t + 1] + received[t + 1].astype(FULL)).astype(LOW)


def modulation_kernel(ids, *refs):
    shards = refs[-1].shape[0]
    notes, weight, answers, weight_low, stacked = (
        refs[:shards], refs[shards], refs[shards + 1 : -2], refs[-2], refs[-1],
    )
    low = weight[...].astype(LOW)
    weight_low[...] = low
    for d, (note, answer) in enumerate(zip(notes, answers)):
        answer[...] = dot_nt(note[:NOTE, :], low)[: answer.shape[0]]
        stacked[d] = note[NOTE:, :]


def total_kernel(ids, own, *refs):
    total = own[...]
    for piece in refs[:-1]:
        total = total + piece[...].astype(FULL)
    refs[-1][...] = total.astype(LOW)


def prepare(ids, condition, biases, attend, project, note, first):
    latents = condition.shape[0]
    value = condition[...].astype(FULL)
    first[...] = jnp.zeros_like(first)
    first[:latents, :] = value / (1.0 + jnp.exp(-value))
    share = biases.shape[1]
    for b in range(-(-share // D)):
        filled = min(D, share - b * D)
        first[latents + b : latents + b + 1, :filled] = biases[:, b * D : b * D + filled]
    note[:NOTE, :] = first[...].astype(LOW)

    @pl.when(ids[1] < 6)
    def _():
        note[NOTE:, :] = attend[...].astype(LOW)

    @pl.when(ids[1] >= 6)
    def _():
        note[NOTE:, :] = project[...].astype(LOW)


def pack(ids, *refs):
    start = 0
    for weight in refs[:-1]:
        width = weight.shape[1]
        refs[-1][:, start : start + width] = weight[...].astype(LOW)
        start = start + width


def stack(ids, *refs):
    for t, block in enumerate(refs[:-1]):
        refs[-1][t] = block[...]


def attention_forward(
    ids, tokens, stacked, flipped, *refs,
):
    shards = (len(refs) - 16) // 2
    answers, notes = refs[:shards], refs[shards : 2 * shards]
    (
        qkv, probs, attended, branch, wq, wo, mod_all, bias_up, bias_down,
        ordered, query_a, query_b, mod_parts, bias_parts, wq_plain, wo_plain,
    ) = refs[2 * shards :]
    rows = ordered.shape[1] // GROUP
    wide, narrow = 3 * D // shards, D // shards

    @pl.when(pl.program_id(0) == 0)
    def _():
        for place, block in pieces_of(ids, stacked, flipped):
            for d in range(shards):
                source = lax.rem(ids[0] - d + shards, shards)
                ordered[source, rows_at(place, rows), :] = block[d].astype(ordered.dtype)
        for s in range(shards):
            wq[s * wide : (s + 1) * wide, :] = ordered[s, :wide, :].astype(LOW)
            wo[s * narrow : (s + 1) * narrow, :] = ordered[s, wide:, :].astype(LOW)
        wq_plain[...] = wq[...].T
        wo_plain[...] = wo[...].T
        for d in range(shards):
            mod_parts[lax.rem(ids[0] + d, shards)] = answers[d][...]
            bias_parts[lax.rem(ids[0] - d + shards, shards)] = notes[d][:NOTE, :].astype(FULL)
        latents = mod_all.shape[0]
        share = BIAS_LEN // shards
        pieces = []
        for s in range(shards):
            for b in range(-(-share // D)):
                row = bias_parts[s, latents + b : latents + b + 1, :]
                pieces.append(row[:, : min(D, share - b * D)])
        bias = jnp.concatenate(pieces, axis=1)
        whole = jnp.concatenate([mod_parts[s] for s in range(shards)], axis=1) + bias[:, : 6 * D]
        for latent in range(latents):
            for b in range(6):
                mod_all[latent, b : b + 1, :] = whole[latent : latent + 1, b * D : (b + 1) * D]
        bias_up[...] = bias[:, 6 * D : 6 * D + FF]
        bias_down[...] = bias[:, 6 * D + FF :]

    count = tokens.shape[0]
    mod = mod_all[pl.ds(pl.program_id(0) * count, count)]
    normed, _ = normalize(tokens[...].astype(FULL))
    hidden = normed * (1.0 + mod[:, 1:2, :]) + mod[:, 0:1, :]
    hidden = hidden.reshape(count * LEN, D).astype(LOW)
    queries = dot(hidden, wq_plain[:, :D])
    masked_a, masked_b = head_masks(queries)
    query_a[...] = masked_a
    query_b[...] = masked_b
    qkv[:, :, :D] = queries.astype(LOW).reshape(count, LEN, D)
    qkv[:, :, D:] = dot(hidden, wq_plain[:, D:]).astype(LOW).reshape(count, LEN, 2 * D)

    @pl.loop(0, count)
    def _(latent):
        span = pl.ds(pl.multiple_of(latent * LEN, LEN), LEN)
        for pair in range(HEADS // 2):
            lanes = slice(pair * PAIR, (pair + 1) * PAIR)
            keys = qkv[latent, :, D + pair * PAIR : D + (pair + 1) * PAIR]
            values = qkv[latent, :, 2 * D + pair * PAIR : 2 * D + (pair + 1) * PAIR].T
            results = []
            for member, masked in enumerate((query_a, query_b)):
                scores = dot_nt(keys, masked[span, lanes]) * (HEAD ** (-0.5) / math.log(2.0))
                top = jnp.max(scores, 0, keepdims=True)
                raised = jnp.exp2(scores - top)
                share = (raised * (1.0 / jnp.sum(raised, 0, keepdims=True))).astype(LOW)
                probs[latent, 2 * pair + member] = share
                results.append(dot(values[member * HEAD : (member + 1) * HEAD], share))
            attended[latent, :, lanes] = jnp.concatenate(results, axis=0).T.astype(LOW)

    branch[...] = dot(attended[...].reshape(count * LEN, D), wo_plain[...]).reshape(count, LEN, D)


def perceptron(
    ids, tokens, branch, mod, cotangent, stacked, flipped, bias_up, bias_down,
    out, grad_mixed, grad_mod, keep, send, sum_up, sum_down,
    ordered, wu, wd, act, slope, total_up, total_down,
):
    shards = ordered.shape[0]
    rows = D // GROUP
    width = FF // shards
    step = pl.program_id(0)

    @pl.when(step == 0)
    def _():
        for place, block in pieces_of(ids, stacked, flipped):
            for d in range(shards):
                source = lax.rem(ids[0] - d + shards, shards)
                ordered[source, rows_at(place, rows), :] = block[d]
        for i in range(GROUP):
            span = slice(i * rows, (i + 1) * rows)
            pieces = [ordered[s, span, :] for s in range(shards)]
            wu[span, :] = jnp.concatenate([p[:, :width] for p in pieces], axis=1)
            wd[span, :] = jnp.concatenate([p[:, width:] for p in pieces], axis=1)
        total_up[...] = jnp.zeros_like(total_up)
        total_down[...] = jnp.zeros_like(total_down)
        sum_up[...] = jnp.zeros_like(sum_up)
        sum_down[...] = jnp.zeros_like(sum_down)

    count = tokens.shape[0]
    flat = count * LEN
    branch_out = branch[...]
    mixed = tokens[...].astype(FULL) + mod[:, 2:3, :] * branch_out
    normed, inverse_spread = normalize(mixed)
    hidden = (normed * (1.0 + mod[:, 4:5, :]) + mod[:, 3:4, :]).reshape(flat, D).astype(LOW)
    result = jnp.zeros((flat, D), FULL)
    for start in range(0, FF, CHUNK):
        span = slice(start, start + CHUNK)
        u = dot(hidden, wu[:, span]) + bias_up[:, span]
        square = u * u
        half = 0.5 + 0.5 * jnp.tanh(u * (GELU_SLOPE + (GELU_SLOPE * GELU_CUBIC) * square))
        act_low = (u * half).astype(LOW)
        act[:, span] = act_low
        steep = u * (2.0 * GELU_SLOPE + (6.0 * GELU_SLOPE * GELU_CUBIC) * square)
        slope[:, span] = half + (half - half * half) * steep
        result = result + dot_nt(act_low, wd[:, span])
    result = (result + bias_down[...]).reshape(count, LEN, D)
    gate = mod[:, 5:6, :]
    out[...] = (mixed + gate * result).astype(LOW)
    upstream = cotangent[...].astype(FULL)
    grad_mod[:, 3:4, :] = jnp.sum(upstream * result, axis=1, keepdims=True)
    grad_result = (gate * upstream).reshape(flat, D).astype(LOW)
    sum_down[...] += jnp.sum(grad_result.astype(FULL), axis=0, keepdims=True)
    grad_hidden = jnp.zeros((flat, D), FULL)
    for start in range(0, FF, CHUNK):
        span = slice(start, start + CHUNK)
        grad_u = (dot(grad_result, wd[:, span]) * slope[:, span]).astype(LOW)
        sum_up[:, span] += jnp.sum(grad_u.astype(FULL), axis=0, keepdims=True)
        total_down[:, span] += dot_tn(grad_result, act[:, span])
        total_up[:, span] += dot_tn(hidden, grad_u)
        grad_hidden = grad_hidden + dot_nt(grad_u, wu[:, span])
    grad_hidden = grad_hidden.reshape(count, LEN, D)
    grad_mod[:, 1:2, :] = jnp.sum(grad_hidden, axis=1, keepdims=True)
    grad_mod[:, 2:3, :] = jnp.sum(grad_hidden * normed, axis=1, keepdims=True)
    back = upstream + normalize_back(
        grad_hidden * (1.0 + mod[:, 4:5, :]), normed, inverse_spread
    )
    grad_mixed[...] = back
    grad_mod[:, 0:1, :] = jnp.sum(back * branch_out, axis=1, keepdims=True)

    @pl.when(step == pl.num_programs(0) - 1)
    def _():
        shard, low = ids[0], ids[1]
        for j in range(GROUP):
            span = pl.ds(pl.multiple_of((low ^ j) * rows, rows), rows)
            for s in range(shards):
                d = lax.rem(s - shard + shards, shards)
                lanes = slice(s * width, (s + 1) * width)
                piece = jnp.concatenate([total_up[span, lanes], total_down[span, lanes]], axis=1)
                if j & 1:
                    send[j // 2, d] = piece.astype(LOW)
                else:
                    keep[j // 2, d] = piece


def attention_backward(
    ids, mod, attended, grad_mixed, qkv, probs, wo,
    grad_qkv, total_project,
    grad_attended,
):
    @pl.when(pl.program_id(0) == 0)
    def _():
        total_project[...] = jnp.zeros_like(total_project)

    count = attended.shape[0]
    flat = count * LEN
    grad_branch = (mod[:, 2:3, :] * grad_mixed[...]).reshape(flat, D).astype(LOW)
    total_project[...] += dot_tn(attended[...].reshape(flat, D), grad_branch)
    grad_attended[...] = dot(grad_branch, wo[...]).astype(LOW).reshape(count, LEN, D)
    mask = lax.broadcasted_iota(jnp.int32, (LEN, PAIR), 1) < HEAD
    scale = HEAD ** (-0.5)
    for latent in range(count):
        for pair in range(HEADS // 2):
            lanes = slice(pair * PAIR, (pair + 1) * PAIR)
            key_lanes = slice(D + pair * PAIR, D + (pair + 1) * PAIR)
            value_lanes = slice(2 * D + pair * PAIR, 2 * D + (pair + 1) * PAIR)
            queries = qkv[latent, :, lanes]
            keys = qkv[latent, :, key_lanes].T
            values = qkv[latent, :, value_lanes]
            upper = grad_attended[latent, :, lanes]
            masked = head_masks(upper.astype(FULL))
            by_query, by_key, by_value = [], [], []
            for member in range(2):
                share = probs[latent, 2 * pair + member]
                weight = share.astype(FULL)
                grad_share = dot_nt(values, masked[member])
                product = weight * grad_share
                grad_scores = (
                    product - weight * jnp.sum(product, 0, keepdims=True)
                ).astype(LOW)
                by_query.append(dot(keys[member * HEAD : (member + 1) * HEAD], grad_scores))
                by_key.append(dot(grad_scores, queries))
                by_value.append(dot(share, upper))
            merged = jnp.concatenate(by_query, axis=0).T * scale
            grad_qkv[latent, :, lanes] = merged.astype(LOW)
            merged = jnp.where(mask, by_key[0], by_key[1]) * scale
            grad_qkv[latent, :, key_lanes] = merged.astype(LOW)
            merged = jnp.where(mask, by_value[0], by_value[1])
            grad_qkv[latent, :, value_lanes] = merged.astype(LOW)


def attend_backward(
    ids, tokens, mod, grad_mixed, grad_qkv, wq, total_project, grad_mod_late, sum_up, sum_down,
    grad_tokens, keep, send, extra,
    total_attend, grad_mod, extra_rows,
):
    rows = D // GROUP
    shards = keep.shape[1]
    step = pl.program_id(0)

    @pl.when(step == 0)
    def _():
        total_attend[...] = jnp.zeros_like(total_attend)

    count = tokens.shape[0]
    flat = count * LEN
    normed, inverse_spread = normalize(tokens[...].astype(FULL))
    hidden = (normed * (1.0 + mod[:, 1:2, :]) + mod[:, 0:1, :]).reshape(flat, D).astype(LOW)
    grad_low = grad_qkv[...].reshape(flat, 3 * D)
    total_attend[...] += dot_tn(hidden, grad_low)
    grad_hidden = dot(grad_low, wq[...]).reshape(count, LEN, D)
    mine = pl.ds(step * count, count)
    grad_mod[mine, 0:1, :] = jnp.sum(grad_hidden, axis=1, keepdims=True)
    grad_mod[mine, 1:2, :] = jnp.sum(grad_hidden * normed, axis=1, keepdims=True)
    grad_tokens[...] = grad_mixed[...] + normalize_back(
        grad_hidden * (1.0 + mod[:, 1:2, :]), normed, inverse_spread
    )

    @pl.when(step == pl.num_programs(0) - 1)
    def _():
        shard, low = ids[0], ids[1]
        wide, narrow = 3 * D // shards, D // shards
        for j in range(GROUP):
            span = rows_at(low ^ j, rows)
            whole_attend, whole_project = total_attend[span, :], total_project[span, :]
            for s in range(shards):
                d = lax.rem(s - shard + shards, shards)
                piece = jnp.concatenate(
                    [
                        whole_attend[:, s * wide : (s + 1) * wide],
                        whole_project[:, s * narrow : (s + 1) * narrow],
                    ],
                    axis=1,
                )
                if j & 1:
                    send[j // 2, d] = piece.astype(LOW)
                else:
                    keep[j // 2, d] = piece
        latents = grad_mod.shape[0]
        columns = [grad_mod[:, b, :] for b in range(2)] + [grad_mod_late[:, b, :] for b in range(4)]
        whole = jnp.concatenate(columns, axis=1).astype(LOW).astype(FULL)
        sums = jnp.sum(whole, axis=0, keepdims=True)
        sums = jnp.concatenate([sums, sum_up[...], sum_down[...]], axis=1)
        mod_share, bias_share = 6 * D // shards, BIAS_LEN // shards
        blocks, lines = -(-mod_share // D), -(-bias_share // D)

        def padded(values, start, stop):
            part = values[:, start : min(start + D, stop)]
            if part.shape[1] < D:
                rest = jnp.zeros((part.shape[0], D - part.shape[1]), FULL)
                part = jnp.concatenate([part, rest], axis=1)
            return part

        extra_rows[...] = jnp.zeros_like(extra_rows)
        for s in range(shards):
            for b in range(blocks):
                extra_rows[b * latents : (b + 1) * latents, :] = padded(
                    whole, s * mod_share + b * D, (s + 1) * mod_share
                )
            for b in range(lines):
                row = padded(sums, s * bias_share + b * D, (s + 1) * bias_share)
                high = row.astype(LOW).astype(FULL)
                place = blocks * latents + b
                extra_rows[place : place + 1, :] = high
                extra_rows[place + lines : place + lines + 1, :] = row - high
            extra[lax.rem(s - shard + shards, shards)] = extra_rows[...].astype(LOW)


def late_pieces(ids, own, first, second, third, extra, *pieces):
    total = own[...]
    for received in (first, second, third):
        total = total + received[...].astype(FULL)
    for d, piece in enumerate(pieces):
        piece[:NOTE, :] = extra[d]
        if total.shape[2] < D:
            piece[NOTE:, :] = jnp.zeros((total.shape[1], D), LOW)
        piece[NOTE:, : total.shape[2]] = total[d].astype(LOW)


def combine(shards, latents, ids, *refs):
    incoming, notes, weight, payload = (
        refs[:shards], refs[shards : 2 * shards], refs[2 * shards], refs[2 * shards + 1],
    )
    answers, rows_ref = refs[2 * shards + 2 : -1], refs[-1]
    rows = D // GROUP
    mod_share, bias_share = 6 * D // shards, BIAS_LEN // shards
    blocks, lines = -(-mod_share // D), -(-bias_share // D)
    total = jnp.zeros((rows, D), FULL)
    bias = jnp.zeros((NOTE, D), FULL)
    for d in range(shards):
        total = total + incoming[d][NOTE:, :].astype(FULL)
        extra = incoming[d][:NOTE, :].astype(FULL)
        bias = bias + extra
        for b in range(blocks):
            start = (b * shards + d) * latents
            rows_ref[start : start + latents, :] = extra[b * latents : (b + 1) * latents]
        start = (blocks * shards + d) * latents
        rows_ref[start : start + latents, :] = notes[d][:NOTE, :].astype(FULL)[:latents]
    payload[:rows, :] = total.astype(LOW)
    count = (blocks + 1) * shards * latents
    start = blocks * latents
    bias = bias[start : start + lines] + bias[start + lines : start + 2 * lines]
    high = bias.astype(LOW).astype(FULL)
    rows_ref[count:, :] = jnp.zeros((16, D), FULL)
    rows_ref[count : count + lines, :] = high
    rows_ref[count + 8 : count + 8 + lines, :] = bias - high
    payload[rows:, :] = rows_ref[...].astype(LOW)
    for d, answer in enumerate(answers):
        result = jnp.zeros((NOTE, D), FULL)
        for b in range(blocks):
            filled = min(D, mod_share - b * D)
            product = dot(incoming[d][:NOTE, :filled], weight[b * D : b * D + filled, :])
            result = result + shifted(product, b * latents)
        answer[...] = result[:latents]


def shifted(values, count):
    if count == 0:
        return values
    return jnp.concatenate([values[count:], values[:count]], axis=0)


COLUMNS = (3 * D, D, FF, FF, 6 * D)
TURNED = (True, True, False, False, True)
TRIANGLE = ((0, 0), (0, 1), (0, 2), (1, 1), (1, 2), (2, 2))


def slot_spans(widths):
    counts = [sum(1 for m, _ in SLOTS if m == number) for number in range(len(widths))]
    return [
        (part * (widths[m] // counts[m]), (part + 1) * (widths[m] // counts[m]))
        for m, part in SLOTS
    ]


def late_parts(latents, widths, late, late_flipped):
    rows = D // GROUP
    blocks = -(-widths[4] // D)
    unit = (blocks + 1) * latents + 16
    parts = [
        ref.at[t, pl.ds(start, unit), :]
        for ref in (late, late_flipped)
        for t in range(GROUP // 2)
        for start in range(rows, late.shape[1], unit)
    ]

    def rows_of(start):
        return jnp.concatenate([p[start : start + latents, :] for p in parts], axis=0)

    return parts, blocks, rows_of


def modulate_gradient(latents, widths, late, late_flipped, target):
    _, blocks, rows_of = late_parts(latents, widths, late, late_flipped)
    cond = rows_of(blocks * latents)
    for block in range(blocks):
        filled = min(D, widths[4] - block * D)
        target[block * D : block * D + filled, :] = dot_tn(rows_of(block * latents), cond)[:filled]


def late_gradient(ids, late, late_flipped, late_whole):
    rows = D // GROUP
    for place, block in pieces_of(ids, late, late_flipped):
        late_whole[rows_at(place, rows), :] = block[:rows, :].astype(FULL)
    return turn(late_whole[...])


def mix(moment, grad):
    moment = MOMENTUM * moment + grad
    return moment, grad + MOMENTUM * moment


def gram_kernel(latents, ids, late, late_flipped, early, early_flipped, *refs):
    moments, gram, columns = refs[0:5], refs[5], refs[6]
    late_whole, flat_gram, early_whole, modulate_whole = refs[7:11]
    low = ids[1]
    rows = D // GROUP
    shards = gram.shape[0]
    widths = [whole // shards for whole in COLUMNS]
    spans = slot_spans(widths)
    for number in range(5):
        owners = [k for k, (m, _) in enumerate(SLOTS) if m == number]
        condition = low == owners[0]
        for owner in owners[1:]:
            condition = condition | (low == owner)

        @pl.when(condition)
        def _(number=number, owners=owners):
            if number < 2:
                start = 0 if number == 0 else widths[0]
                grad = late_gradient(ids, late, late_flipped, late_whole)
                grad = grad[start : start + widths[number]]
            elif number < 4:
                start = 0 if number == 2 else widths[2]
                for place, block in pieces_of(ids, early, early_flipped):
                    piece = block[...].astype(FULL)[:, start : start + widths[number]]
                    early_whole[rows_at(place, rows), :] = piece
                grad = early_whole[...]
            else:
                modulate_gradient(latents, widths, late, late_flipped, modulate_whole)
                grad = modulate_whole[...]
            mixed = mix(moments[number][...], grad)[1]
            parts = split_low(mixed)
            whole = dot_split(parts, parts, dot_tn if TURNED[number] else dot_nt)
            for place, (a, b) in enumerate(TRIANGLE):
                flat_gram[place * 128 : (place + 1) * 128, :] = whole[
                    a * 128 : (a + 1) * 128, b * 128 : (b + 1) * 128
                ]
            if not TURNED[number]:
                mixed = turn(mixed)
            for owner in owners:

                @pl.when(low == owner)
                def _(owner=owner, mixed=mixed):
                    start, stop = spans[owner]
                    filled = stop - start
                    columns[:filled, :] = mixed[start:stop]
                    if filled < columns.shape[0]:
                        columns[filled:, :] = jnp.zeros((columns.shape[0] - filled, D), FULL)

    size = gram.shape[1]
    for s in range(shards):
        gram[lax.rem(s - ids[0] + shards, shards)] = flat_gram[s * size : (s + 1) * size, :]


def momenta_kernel(latents, ids, late, late_flipped, early, early_flipped, *refs):
    moments, grads, momenta = refs[0:5], refs[5:10], refs[10:15]
    bias, late_whole = refs[15:17]
    rows = D // GROUP
    widths = [m.shape[0 if turned else 1] for m, turned in zip(moments, TURNED)]
    turned = late_gradient(ids, late, late_flipped, late_whole)
    grads[0][...] = turned[: widths[0]]
    grads[1][...] = turned[widths[0] : widths[0] + widths[1]]
    for place, block in pieces_of(ids, early, early_flipped):
        piece = block[...].astype(FULL)
        grads[2][rows_at(place, rows), :] = piece[:, : widths[2]]
        grads[3][rows_at(place, rows), :] = piece[:, widths[2] :]
    modulate_gradient(latents, widths, late, late_flipped, grads[4])
    parts, blocks, _ = late_parts(latents, widths, late, late_flipped)
    total = jnp.zeros((16, D), FULL)
    for part in parts:
        total = total + part[(blocks + 1) * latents :, :].astype(FULL)
    bias[...] = total[:8] + total[8:]
    for number in range(5):
        momenta[number][...] = mix(moments[number][...], grads[number][...])[0]


def polynomial_kernel(ids, *refs):
    shards = len(refs) - 5
    pieces, columns, answer, flat_gram, gram_ref, product_ref = refs[:shards], *refs[shards:]
    size = pieces[0].shape[0]
    for d in range(shards):
        source = lax.rem(ids[0] - d + shards, shards)
        flat_gram[rows_at(source, size), :] = pieces[d][...]
    for place, (a, b) in enumerate(TRIANGLE):
        block = flat_gram[place * 128 : (place + 1) * 128, :]
        gram_ref[a * 128 : (a + 1) * 128, b * 128 : (b + 1) * 128] = block
        if a != b:
            gram_ref[b * 128 : (b + 1) * 128, a * 128 : (a + 1) * 128] = block.T
    gram = gram_ref[...]
    diagonal = lax.broadcasted_iota(jnp.int32, (D, D), 0) == lax.broadcasted_iota(
        jnp.int32, (D, D), 1
    )
    trace = jnp.sum(jnp.where(diagonal, gram, 0.0))
    scale = 1.0 / (jnp.sqrt(jnp.full((1, 1), trace)) + 1e-07)
    gram = (gram * scale) * scale

    def advance(gram, product):
        mixing = POLY_CUBIC * gram + POLY_QUINTIC * dot(left_deep(gram), right_deep(gram))
        mixing_deep = left_deep(mixing)
        both = jnp.concatenate([gram, product], axis=1)
        both = POLY_LINEAR * both + dot(mixing_deep, right_deep(both))
        half = both[:, :D]
        return POLY_LINEAR * half + dot(mixing_deep, right_deep(half)), both[:, D:]

    gram_ref[...] = gram
    product_ref[...] = jnp.where(diagonal, 1.0, 0.0)

    @pl.loop(0, NS_ITERS - 1)
    def _(step):
        gram, product = advance(gram_ref[...], product_ref[...])
        gram_ref[...] = gram
        product_ref[...] = product

    gram, product = gram_ref[...], product_ref[...]
    mixing = POLY_CUBIC * gram + POLY_QUINTIC * dot(left_deep(gram), right_deep(gram))
    product = POLY_LINEAR * product + dot(left_deep(mixing), right_deep(product))
    answer[...] = dot(left_deep(columns[...] * scale), right_deep(product)).astype(LOW)


def left_deep(value):
    high, rest = split_low(value)
    return jnp.concatenate([high, rest, high], axis=1)


def right_deep(value):
    high, rest = split_low(value)
    return jnp.concatenate([high, high, rest], axis=0)


def update_kernel(ids, answers, answers_flipped, *refs):
    masters, updated, ordered = refs[:5], refs[5:10], refs[10]
    for place, block in pieces_of(ids, answers, answers_flipped):
        ordered[place] = block[...]
    widths = [m.shape[0 if turned else 1] for m, turned in zip(masters, TURNED)]
    spans = slot_spans(widths)
    for number in range(5):
        factor = MUON_RATE * 0.2 * math.sqrt(COLUMNS[number])
        mine = [k for k, (m, _) in enumerate(SLOTS) if m == number]
        if TURNED[number]:
            for k in mine:
                start, stop = spans[k]
                updated[number][start:stop, :] = masters[number][start:stop, :] * (
                    1.0 - MUON_RATE * WEIGHT_DECAY
                ) - factor * ordered[k, : stop - start, :].astype(FULL)
        else:
            direction = jnp.concatenate(
                [ordered[k, : spans[k][1] - spans[k][0], :].astype(FULL) for k in mine], axis=0
            )
            updated[number][...] = masters[number][...] * (
                1.0 - MUON_RATE * WEIGHT_DECAY
            ) - factor * direction.T


def per_device(
    tokens,
    condition,
    cotangent,
    attend_weight,
    project_weight,
    expand_weight,
    contract_weight,
    modulate_weight,
    biases,
    attend_moment,
    project_moment,
    expand_moment,
    contract_moment,
    modulate_moment,
    bias_first,
    bias_second,
):
    latents = tokens.shape[0]
    steps = latents // BLOCK
    shards = lax.axis_size("shard")
    shard = lax.axis_index("shard")
    low = lax.axis_index("rep") % GROUP
    ids = jnp.stack([shard, low]).astype(jnp.int32)
    rows = D // GROUP
    bias_share = biases.shape[0]
    mod_share = modulate_weight.shape[1]
    late_width = 4 * D // shards
    late_rows = late_width // GROUP

    (note,) = local_call(
        prepare,
        ids,
        [
            (condition, False),
            (biases.reshape(1, -1), False),
            (attend_weight.T, (late_rows, lambda place: jnp.minimum(place, 5))),
            (project_weight.T, (late_rows, lambda place: jnp.maximum(place - 6, 0))),
        ],
        [((NOTE + late_rows, D), LOW, False)],
        [pltpu.VMEM((NOTE, D), FULL)],
        1,
        D * D,
        "prepare",
    )
    notes = exchange([note] * shards)

    *shares, modulate_low, late_weights = local_call(
        modulation_kernel,
        ids,
        [(piece, False) for piece in notes] + [(modulate_weight.T, False)],
        [((latents, mod_share), FULL, False)] * shards
        + [((mod_share, D), LOW, False), ((shards, late_rows, D), LOW, False)],
        [],
        1,
        2 * shards * NOTE * D * mod_share,
        "modulation",
    )
    answers = [shares[0]] + [shift(shares[d], shards - d) for d in range(1, shards)]
    late_weights_chips = gather_chips(late_weights)
    (early_weights,) = local_call(
        pack,
        ids,
        [(w, (rows, lambda place: place)) for w in (expand_weight, contract_weight)],
        [((rows, 2 * FF // shards), LOW, False)],
        [],
        1,
        D * D,
        "pack",
        after=(late_weights,),
    )
    early_weights = jnp.stack(exchange([early_weights] * shards))
    early_weights_chips = gather_chips(early_weights)
    (late_stacked,) = local_call(
        stack,
        ids,
        [(v, False) for v in late_weights_chips],
        [((GROUP // 2, shards, late_rows, D), LOW, False)],
        [],
        1,
        D * D,
        "stack_late",
        after=(early_weights,),
    )
    late_flipped = flip(late_stacked, 1)

    tokens_shape = (latents, LEN, D)
    qkv, probs, attended, branch, wq, wo, mod, bias_up, bias_down = local_call(
        attention_forward,
        ids,
        [(tokens, True), (late_stacked, False), (late_flipped, False)]
        + [(v, False) for v in (*answers, *notes)],
        [
            ((latents, LEN, 3 * D), LOW, True),
            ((latents, HEADS, LEN, LEN), LOW, True),
            (tokens_shape, LOW, True),
            (tokens_shape, FULL, True),
            ((3 * D, D), LOW, False),
            ((D, D), LOW, False),
            ((latents, 6, D), FULL, False),
            ((1, FF), FULL, False),
            ((1, D), FULL, False),
        ],
        [
            pltpu.VMEM((shards, late_width, D), LOW if late_rows % 16 == 0 else FULL),
            pltpu.VMEM((BLOCK * LEN, D), LOW),
            pltpu.VMEM((BLOCK * LEN, D), LOW),
            pltpu.VMEM((shards, latents, mod_share), FULL),
            pltpu.VMEM((shards, NOTE, D), FULL),
            pltpu.VMEM((D, 3 * D), LOW),
            pltpu.VMEM((D, D), LOW),
        ],
        steps,
        latents * (2 * LEN * D * 4 * D + 4 * HEADS * LEN * LEN * PAIR) * 2,
        "attention_forward",
        after=(early_weights,),
    )
    early_shape = (GROUP // 2, shards, rows, 2 * FF // shards)
    (early_weights_stacked,) = local_call(
        stack,
        ids,
        [(v, False) for v in early_weights_chips],
        [(early_shape, LOW, False)],
        [],
        1,
        D * D,
        "stack",
        after=(branch,),
    )
    early_weights_flipped = flip(early_weights_stacked, 1)
    block_output, grad_mixed, grad_mod_late, keep, send, sum_up, sum_down = local_call(
        perceptron,
        ids,
        [
            (tokens, True),
            (branch, True),
            (mod, True),
            (cotangent, True),
            (early_weights_stacked, False),
            (early_weights_flipped, False),
            (bias_up, False),
            (bias_down, False),
        ],
        [
            (tokens_shape, LOW, True),
            (tokens_shape, FULL, True),
            ((latents, 4, D), FULL, True),
            (early_shape, FULL, False),
            (early_shape, LOW, False),
            ((1, FF), FULL, False),
            ((1, D), FULL, False),
        ],
        [
            pltpu.VMEM((shards, D, 2 * FF // shards), LOW),
            pltpu.VMEM((D, FF), LOW),
            pltpu.VMEM((D, FF), LOW),
            pltpu.VMEM((BLOCK * LEN, FF), LOW),
            pltpu.VMEM((BLOCK * LEN, FF), FULL),
            pltpu.VMEM((D, FF), FULL),
            pltpu.VMEM((D, FF), FULL),
        ],
        steps,
        latents * 2 * LEN * D * FF * 6 * 2,
        "perceptron",
    )

    early_totals = sum_cores(keep, send, ids, "early_sum", ())
    arrived = exchange_chips(early_totals)
    early_chips = sum(piece.astype(FULL) for piece in arrived[1:]) + arrived[0]
    grad_qkv, total_project = local_call(
        attention_backward,
        ids,
        [
            (mod, True),
            (attended, True),
            (grad_mixed, True),
            (qkv, True),
            (probs, True),
            (wo, False),
        ],
        [((latents, LEN, 3 * D), LOW, True), ((D, D), FULL, False)],
        [pltpu.VMEM((1, LEN, D), LOW)],
        latents,
        latents * (10 * HEADS * LEN * LEN * PAIR + 4 * LEN * D * D),
        "attention_backward",
        after=tuple(early_totals[1:]),
    )
    early_pieces = exchange([early_chips[d].astype(LOW) for d in range(shards)])
    late_shape = (GROUP // 2, shards, rows, late_width)
    tokens_grad, keep, send, extra = local_call(
        attend_backward,
        ids,
        [
            (tokens, True),
            (mod, True),
            (grad_mixed, True),
            (grad_qkv, True),
            (wq, False),
            (total_project, False),
            (grad_mod_late, False),
            (sum_up, False),
            (sum_down, False),
        ],
        [
            (tokens_shape, FULL, True),
            (late_shape, FULL, False),
            (late_shape, LOW, False),
            ((shards, NOTE, D), LOW, False),
        ],
        [
            pltpu.VMEM((D, 3 * D), FULL),
            pltpu.VMEM((latents, 2, D), FULL),
            pltpu.VMEM((NOTE, D), FULL),
        ],
        steps,
        latents * 2 * LEN * D * 6 * D * 2,
        "attend_backward",
        after=(early_chips,),
    )

    late_totals = sum_cores(keep, send, ids, "late_sum", ())
    arrived = exchange_chips(late_totals)
    (early,) = local_call(
        total_kernel,
        ids,
        [(v, False) for v in (early_chips[0], *early_pieces[1:])],
        [(early_pieces[1].shape, LOW, False)],
        [],
        1,
        D * D,
        "early_total",
        after=tuple(late_totals[1:]),
    )
    early_stacked, early_flipped = gather_group(sum_rest(early))
    outgoing = local_call(
        late_pieces,
        ids,
        [(v, False) for v in (*arrived, extra)],
        [((NOTE + rows, D), LOW, False)] * shards,
        [],
        1,
        4 * shards * rows * late_width,
        "late_pieces",
        after=(early,),
    )
    group_latents = shards * latents
    unit = (-(-mod_share // D) + 1) * group_latents + 16
    payload, *shares = local_call(
        partial(combine, shards, latents),
        ids,
        [(v, False) for v in (*exchange(outgoing), *notes, modulate_low)],
        [((rows + unit, D), LOW, False)] + [((latents, D), FULL, False)] * shards,
        [pltpu.VMEM((unit, D), FULL)],
        1,
        2 * shards * NOTE * D * mod_share,
        "combine",
        after=(early_stacked,),
    )
    if lax.axis_size("rep") > GROUP:
        late, others = sum_rest(payload[:rows]), payload[rows:]
        for bit in range(3, lax.axis_size("rep").bit_length() - 1):
            others = jnp.concatenate([others, flip(others, 1 << bit)], axis=0)
        payload = jnp.concatenate([late, others], axis=0)
    late_stacked, late_flipped = gather_group(payload)

    grad_cond_low = shares[0]
    for d in range(1, shards):
        grad_cond_low = grad_cond_low + shift(shares[d], shards - d)
    _, silu_back = jax.vjp(jax.nn.silu, condition.astype(FULL))
    condition_grad = silu_back(grad_cond_low)[0]

    def as_held(values):
        return [v.T if turned else v for v, turned in zip(values, TURNED)]

    masters = as_held(
        [attend_weight, project_weight, expand_weight, contract_weight, modulate_weight]
    )
    moments = as_held(
        [attend_moment, project_moment, expand_moment, contract_moment, modulate_moment]
    )
    shapes = [m.shape for m in masters]
    widths = [whole // shards for whole in COLUMNS]
    slot_width = max(stop - start for start, stop in slot_spans(widths))
    piece_rows = 128 * len(TRIANGLE) // shards
    sources = [
        (v, False) for v in (late_stacked, late_flipped, early_stacked, early_flipped, *moments)
    ]
    gram, columns = local_call(
        partial(gram_kernel, group_latents),
        ids,
        sources,
        [((shards, piece_rows, 128), FULL, False), ((slot_width, D), FULL, False)],
        [
            pltpu.VMEM((D, D), FULL),
            pltpu.VMEM((128 * len(TRIANGLE), 128), FULL),
            pltpu.VMEM(shapes[2], FULL),
            pltpu.VMEM(shapes[4], FULL),
        ],
        1,
        6 * D * D * D,
        "gram",
    )
    *results, bias_block = local_call(
        partial(momenta_kernel, group_latents),
        ids,
        sources,
        [(shape, FULL, False) for shape in shapes * 2] + [((8, D), FULL, False)],
        [pltpu.VMEM((D, D), FULL)],
        1,
        D * D * D,
        "momenta",
        after=(gram,),
    )
    gradients, momenta = as_held(results[0:5]), as_held(results[5:10])
    piece = sum(exchange([gram[d] for d in range(shards)]))
    (answer,) = local_call(
        polynomial_kernel,
        ids,
        [(p, False) for p in exchange([piece] * shards)] + [(columns, False)],
        [((slot_width, D), LOW, False)],
        [
            pltpu.VMEM((128 * len(TRIANGLE), 128), FULL),
            pltpu.VMEM((D, D), FULL),
            pltpu.VMEM((D, D), FULL),
        ],
        1,
        2 * 3 * 18 * D * D * D,
        "polynomial",
        after=(condition_grad, bias_block),
    )
    updated = local_call(
        update_kernel,
        ids,
        [(v, False) for v in (*gather_group(answer), *masters)],
        [(shape, FULL, False) for shape in shapes],
        [pltpu.VMEM((GROUP, slot_width, D), LOW)],
        1,
        2 * D * sum(widths),
        "update",
    )
    updated = as_held(updated)

    bias_gradient = bias_block.reshape(-1)[:bias_share]
    bias_momentum = BETA_ONE * bias_first + (1.0 - BETA_ONE) * bias_gradient
    bias_variance = BETA_TWO * bias_second + (1.0 - BETA_TWO) * bias_gradient * bias_gradient
    corrected_first = bias_momentum / (1.0 - BETA_ONE**STEP)
    corrected_second = bias_variance / (1.0 - BETA_TWO**STEP)
    bias_updated = biases * (1.0 - ADAM_RATE * WEIGHT_DECAY) - ADAM_RATE * corrected_first / (
        jnp.sqrt(corrected_second) + ADAM_EPSILON
    )
    return (
        block_output,
        tokens_grad,
        condition_grad,
        *gradients,
        *momenta,
        *updated,
        bias_gradient,
        bias_momentum,
        bias_variance,
        bias_updated,
    )


def solution(mesh):
    rows = P(("shard", "rep"), None, None)
    vectors = P(("shard", "rep"), None)
    columns = P(None, "shard")
    flat = P("shard")
    return jax.shard_map(
        per_device,
        mesh=mesh,
        in_specs=(rows, vectors, rows) + (columns,) * 5 + (flat,) + (columns,) * 5 + (flat,) * 2,
        out_specs=(rows, rows, vectors) + (columns,) * 15 + (flat,) * 4,
        check_vma=False,
    )
```

```python
from functools import partial
import math

import jax
import jax.numpy as jnp
from jax import lax
from jax.experimental import pallas as pl
from jax.experimental.pallas import tpu as pltpu
from jax.sharding import PartitionSpec as P

D = 384
HEADS = 6
HEAD = 64
FF = 1536
LEN = 256
NS_ITERS = 5
STEP = 10
PAIR = 2 * HEAD
CHUNK = 512
GROUP = 8
BLOCK = 2
BIAS_LEN = 6 * D + FF + D
NOTE = 16
GRANTS = {
    "attention_forward": 40,
    "perceptron": 40,
    "attention_backward": 32,
    "attend_backward": 36,
    "modulation": 48,
    "pack": 48,
    "momenta": 32,
    "gram": 24,
    "polynomial": 20,
    "update": 24,
}

POLY_LINEAR = 3.4445
POLY_CUBIC = -4.775
POLY_QUINTIC = 2.0315
MOMENTUM = 0.95
MUON_RATE = 0.4
WEIGHT_DECAY = 0.01
ADAM_RATE = 0.1
BETA_ONE = 0.9
BETA_TWO = 0.999
ADAM_EPSILON = 1e-08
GELU_SLOPE = math.sqrt(2.0 / math.pi)
GELU_CUBIC = 0.044715

LOW = jnp.bfloat16
FULL = jnp.float32

SLOTS = ((4, 0), (4, 1), (0, 0), (2, 0), (2, 1), (3, 0), (3, 1), (1, 0))


def shift(value, distance):
    size = lax.axis_size("shard")
    return lax.ppermute(value, "shard", [(i, (i + distance) % size) for i in range(size)])


def flip(value, mask):
    size = lax.axis_size("rep")
    return lax.ppermute(value, "rep", [(i, i ^ mask) for i in range(size)])


def exchange(pieces):
    return [pieces[0]] + [shift(pieces[d], d) for d in range(1, len(pieces))]


def gather_chips(value):
    return [value] + [flip(value, 2 * t) for t in range(1, GROUP // 2)]


def gather_group(value):
    stacked = jnp.stack(gather_chips(value))
    return stacked, flip(stacked, 1)


def sum_cores(keep, send, ids, name, after):
    received = flip(send, 1)
    shape = keep.shape[1:]
    return local_call(
        split_sum,
        ids,
        [(keep, False), (received, False)],
        [(shape, FULL, False)] + [(shape, LOW, False)] * (keep.shape[0] - 1),
        [],
        1,
        keep.size,
        name,
        after=after,
    )


def exchange_chips(totals):
    return [totals[0]] + [flip(totals[t], 2 * t) for t in range(1, GROUP // 2)]


def sum_rest(value):
    for bit in range(3, lax.axis_size("rep").bit_length() - 1):
        value = (value.astype(FULL) + flip(value, 1 << bit).astype(FULL)).astype(LOW)
    return value


def dot(left, right):
    return lax.dot_general(left, right, (((1,), (0,)), ((), ())), preferred_element_type=FULL)


def dot_nt(left, right):
    return lax.dot_general(left, right, (((1,), (1,)), ((), ())), preferred_element_type=FULL)


def dot_tn(left, right):
    return lax.dot_general(left, right, (((0,), (0,)), ((), ())), preferred_element_type=FULL)


def split_low(value):
    high = value.astype(LOW)
    return high, (value - high.astype(FULL)).astype(LOW)


def dot_split(left, right, product=dot):
    return product(left[0], right[0]) + (product(left[0], right[1]) + product(left[1], right[0]))


def normalize(values):
    centered = values - jnp.mean(values, -1, keepdims=True)
    inverse_spread = lax.rsqrt(jnp.mean(centered * centered, -1, keepdims=True) + 1e-06)
    return centered * inverse_spread, inverse_spread


def normalize_back(upstream, normed, inverse_spread):
    return inverse_spread * (
        upstream
        - jnp.mean(upstream, -1, keepdims=True)
        - normed * jnp.mean(upstream * normed, -1, keepdims=True)
    )


def local_call(kernel, ids, inputs, outputs, scratch, steps, flops, name, after=()):
    def run(*refs):
        kernel(*refs[: 1 + len(inputs)], *refs[1 + len(inputs) + len(after) :])

    def spec(shape, blocked):
        zeros = (0,) * (len(shape) - 1)
        if isinstance(blocked, tuple):
            rows, place = blocked
            return pl.BlockSpec(
                (rows,) + tuple(shape[1:]), lambda i, ids: (place(ids[1]),) + zeros
            )
        if blocked:
            block = (shape[0] // steps,) + tuple(shape[1:])
            return pl.BlockSpec(block, lambda i, _: (i,) + zeros)
        return pl.BlockSpec(tuple(shape), lambda i, _: (0,) + zeros)

    moved = sum(v.size * v.dtype.itemsize for v, _ in inputs)
    moved += sum(math.prod(shape) * jnp.dtype(kind).itemsize for shape, kind, _ in outputs)
    return pl.pallas_call(
        run,
        grid_spec=pltpu.PrefetchScalarGridSpec(
            num_scalar_prefetch=1,
            grid=(steps,),
            in_specs=[spec(v.shape, blocked) for v, blocked in inputs]
            + [pl.BlockSpec(memory_space=pl.ANY) for _ in after],
            out_specs=[spec(shape, blocked) for shape, _, blocked in outputs],
            scratch_shapes=scratch,
        ),
        out_shape=[jax.ShapeDtypeStruct(shape, kind) for shape, kind, _ in outputs],
        compiler_params=pltpu.CompilerParams(
            dimension_semantics=("arbitrary",), vmem_limit_bytes=GRANTS.get(name, 16) * 1024 * 1024
        ),
        cost_estimate=pl.CostEstimate(flops=flops, bytes_accessed=moved, transcendentals=0),
        name=name,
    )(ids, *[v for v, _ in inputs], *after)


def pieces_of(ids, stacked, flipped):
    for t in range(GROUP // 2):
        for bit, blocks in enumerate((stacked, flipped)):
            yield ids[1] ^ (2 * t + bit), blocks.at[t]


def rows_at(place, rows):
    return pl.ds(pl.multiple_of(place * rows, rows), rows)


def turn(value):
    filled = value.shape[1]
    extra = -filled % 128
    if extra:
        value = jnp.concatenate([value, jnp.zeros((value.shape[0], extra), value.dtype)], axis=1)
    return value.T[:filled]


def head_masks(values):
    lane = lax.broadcasted_iota(jnp.int32, values.shape, 1) % PAIR
    zero = jnp.zeros_like(values)
    return (
        jnp.where(lane < HEAD, values, zero).astype(LOW),
        jnp.where(lane < HEAD, zero, values).astype(LOW),
    )


def split_sum(ids, keep, received, own, *others):
    own[...] = keep[0] + received[0].astype(FULL)
    for t, other in enumerate(others):
        other[...] = (keep[t + 1] + received[t + 1].astype(FULL)).astype(LOW)


def modulation_kernel(ids, *refs):
    shards = refs[-1].shape[0]
    notes, weight, answers, weight_low, stacked = (
        refs[:shards], refs[shards], refs[shards + 1 : -2], refs[-2], refs[-1],
    )
    low = weight[...].astype(LOW)
    weight_low[...] = low
    for d, (note, answer) in enumerate(zip(notes, answers)):
        answer[...] = dot_nt(note[:NOTE, :], low)[: answer.shape[0]]
        stacked[d] = note[NOTE:, :]


def total_kernel(ids, own, *refs):
    total = own[...]
    for piece in refs[:-1]:
        total = total + piece[...].astype(FULL)
    refs[-1][...] = total.astype(LOW)


def prepare(ids, condition, biases, attend, project, note, first):
    latents = condition.shape[0]
    value = condition[...].astype(FULL)
    first[...] = jnp.zeros_like(first)
    first[:latents, :] = value / (1.0 + jnp.exp(-value))
    share = biases.shape[1]
    for b in range(-(-share // D)):
        filled = min(D, share - b * D)
        first[latents + b : latents + b + 1, :filled] = biases[:, b * D : b * D + filled]
    note[:NOTE, :] = first[...].astype(LOW)

    @pl.when(ids[1] < 6)
    def _():
        note[NOTE:, :] = attend[...].astype(LOW)

    @pl.when(ids[1] >= 6)
    def _():
        note[NOTE:, :] = project[...].astype(LOW)


def pack(ids, *refs):
    start = 0
    for weight in refs[:-1]:
        width = weight.shape[1]
        refs[-1][:, start : start + width] = weight[...].astype(LOW)
        start = start + width


def stack(ids, *refs):
    for t, block in enumerate(refs[:-1]):
        refs[-1][t] = block[...]


def attention_forward(
    ids, tokens, stacked, flipped, *refs,
):
    shards = (len(refs) - 16) // 2
    answers, notes = refs[:shards], refs[shards : 2 * shards]
    (
        qkv, probs, attended, branch, wq, wo, mod_all, bias_up, bias_down,
        ordered, query_a, query_b, mod_parts, bias_parts, wq_plain, wo_plain,
    ) = refs[2 * shards :]
    rows = ordered.shape[1] // GROUP
    wide, narrow = 3 * D // shards, D // shards

    @pl.when(pl.program_id(0) == 0)
    def _():
        for place, block in pieces_of(ids, stacked, flipped):
            for d in range(shards):
                source = lax.rem(ids[0] - d + shards, shards)
                ordered[source, rows_at(place, rows), :] = block[d].astype(ordered.dtype)
        for s in range(shards):
            wq[s * wide : (s + 1) * wide, :] = ordered[s, :wide, :].astype(LOW)
            wo[s * narrow : (s + 1) * narrow, :] = ordered[s, wide:, :].astype(LOW)
        wq_plain[...] = wq[...].T
        wo_plain[...] = wo[...].T
        for d in range(shards):
            mod_parts[lax.rem(ids[0] + d, shards)] = answers[d][...]
            bias_parts[lax.rem(ids[0] - d + shards, shards)] = notes[d][:NOTE, :].astype(FULL)
        latents = mod_all.shape[0]
        share = BIAS_LEN // shards
        pieces = []
        for s in range(shards):
            for b in range(-(-share // D)):
                row = bias_parts[s, latents + b : latents + b + 1, :]
                pieces.append(row[:, : min(D, share - b * D)])
        bias = jnp.concatenate(pieces, axis=1)
        whole = jnp.concatenate([mod_parts[s] for s in range(shards)], axis=1) + bias[:, : 6 * D]
        for latent in range(latents):
            for b in range(6):
                mod_all[latent, b : b + 1, :] = whole[latent : latent + 1, b * D : (b + 1) * D]
        bias_up[...] = bias[:, 6 * D : 6 * D + FF]
        bias_down[...] = bias[:, 6 * D + FF :]

    count = tokens.shape[0]
    mod = mod_all[pl.ds(pl.program_id(0) * count, count)]
    normed, _ = normalize(tokens[...].astype(FULL))
    hidden = normed * (1.0 + mod[:, 1:2, :]) + mod[:, 0:1, :]
    hidden = hidden.reshape(count * LEN, D).astype(LOW)
    queries = dot(hidden, wq_plain[:, :D])
    masked_a, masked_b = head_masks(queries)
    query_a[...] = masked_a
    query_b[...] = masked_b
    qkv[:, :, :D] = queries.astype(LOW).reshape(count, LEN, D)
    qkv[:, :, D:] = dot(hidden, wq_plain[:, D:]).astype(LOW).reshape(count, LEN, 2 * D)

    @pl.loop(0, count)
    def _(latent):
        span = pl.ds(pl.multiple_of(latent * LEN, LEN), LEN)
        for pair in range(HEADS // 2):
            lanes = slice(pair * PAIR, (pair + 1) * PAIR)
            keys = qkv[latent, :, D + pair * PAIR : D + (pair + 1) * PAIR]
            values = qkv[latent, :, 2 * D + pair * PAIR : 2 * D + (pair + 1) * PAIR].T
            results = []
            for member, masked in enumerate((query_a, query_b)):
                scores = dot_nt(keys, masked[span, lanes]) * (HEAD ** (-0.5) / math.log(2.0))
                top = jnp.max(scores, 0, keepdims=True)
                raised = jnp.exp2(scores - top)
                share = (raised * (1.0 / jnp.sum(raised, 0, keepdims=True))).astype(LOW)
                probs[latent, 2 * pair + member] = share
                results.append(dot(values[member * HEAD : (member + 1) * HEAD], share))
            attended[latent, :, lanes] = jnp.concatenate(results, axis=0).T.astype(LOW)

    branch[...] = dot(attended[...].reshape(count * LEN, D), wo_plain[...]).reshape(count, LEN, D)


def perceptron(
    ids, tokens, branch, mod, cotangent, stacked, flipped, bias_up, bias_down,
    out, grad_mixed, grad_mod, keep, send, sum_up, sum_down,
    ordered, wu, wd, act, slope, total_up, total_down,
):
    shards = ordered.shape[0]
    rows = D // GROUP
    width = FF // shards
    step = pl.program_id(0)

    @pl.when(step == 0)
    def _():
        for place, block in pieces_of(ids, stacked, flipped):
            for d in range(shards):
                source = lax.rem(ids[0] - d + shards, shards)
                ordered[source, rows_at(place, rows), :] = block[d]
        for i in range(GROUP):
            span = slice(i * rows, (i + 1) * rows)
            pieces = [ordered[s, span, :] for s in range(shards)]
            wu[span, :] = jnp.concatenate([p[:, :width] for p in pieces], axis=1)
            wd[span, :] = jnp.concatenate([p[:, width:] for p in pieces], axis=1)
        total_up[...] = jnp.zeros_like(total_up)
        total_down[...] = jnp.zeros_like(total_down)
        sum_up[...] = jnp.zeros_like(sum_up)
        sum_down[...] = jnp.zeros_like(sum_down)

    count = tokens.shape[0]
    flat = count * LEN
    branch_out = branch[...]
    mixed = tokens[...].astype(FULL) + mod[:, 2:3, :] * branch_out
    normed, inverse_spread = normalize(mixed)
    hidden = (normed * (1.0 + mod[:, 4:5, :]) + mod[:, 3:4, :]).reshape(flat, D).astype(LOW)
    result = jnp.zeros((flat, D), FULL)
    for start in range(0, FF, CHUNK):
        span = slice(start, start + CHUNK)
        u = dot(hidden, wu[:, span]) + bias_up[:, span]
        square = u * u
        half = 0.5 + 0.5 * jnp.tanh(u * (GELU_SLOPE + (GELU_SLOPE * GELU_CUBIC) * square))
        act_low = (u * half).astype(LOW)
        act[:, span] = act_low
        steep = u * (2.0 * GELU_SLOPE + (6.0 * GELU_SLOPE * GELU_CUBIC) * square)
        slope[:, span] = half + (half - half * half) * steep
        result = result + dot_nt(act_low, wd[:, span])
    result = (result + bias_down[...]).reshape(count, LEN, D)
    gate = mod[:, 5:6, :]
    out[...] = (mixed + gate * result).astype(LOW)
    upstream = cotangent[...].astype(FULL)
    grad_mod[:, 3:4, :] = jnp.sum(upstream * result, axis=1, keepdims=True)
    grad_result = (gate * upstream).reshape(flat, D).astype(LOW)
    sum_down[...] += jnp.sum(grad_result.astype(FULL), axis=0, keepdims=True)
    grad_hidden = jnp.zeros((flat, D), FULL)
    for start in range(0, FF, CHUNK):
        span = slice(start, start + CHUNK)
        grad_u = (dot(grad_result, wd[:, span]) * slope[:, span]).astype(LOW)
        sum_up[:, span] += jnp.sum(grad_u.astype(FULL), axis=0, keepdims=True)
        total_down[:, span] += dot_tn(grad_result, act[:, span])
        total_up[:, span] += dot_tn(hidden, grad_u)
        grad_hidden = grad_hidden + dot_nt(grad_u, wu[:, span])
    grad_hidden = grad_hidden.reshape(count, LEN, D)
    grad_mod[:, 1:2, :] = jnp.sum(grad_hidden, axis=1, keepdims=True)
    grad_mod[:, 2:3, :] = jnp.sum(grad_hidden * normed, axis=1, keepdims=True)
    back = upstream + normalize_back(
        grad_hidden * (1.0 + mod[:, 4:5, :]), normed, inverse_spread
    )
    grad_mixed[...] = back
    grad_mod[:, 0:1, :] = jnp.sum(back * branch_out, axis=1, keepdims=True)

    @pl.when(step == pl.num_programs(0) - 1)
    def _():
        shard, low = ids[0], ids[1]

        @pl.loop(0, GROUP // 2)
        def _(t):
            for bit in range(2):
                span = rows_at(low ^ (2 * t + bit), rows)
                for s in range(shards):
                    d = lax.rem(s - shard + shards, shards)
                    lanes = slice(s * width, (s + 1) * width)
                    piece = jnp.concatenate(
                        [total_up[span, lanes], total_down[span, lanes]], axis=1
                    )
                    if bit:
                        send[t, d] = piece.astype(LOW)
                    else:
                        keep[t, d] = piece


def attention_backward(
    ids, mod, attended, grad_mixed, qkv, probs, wo,
    grad_qkv, total_project,
    grad_attended,
):
    @pl.when(pl.program_id(0) == 0)
    def _():
        total_project[...] = jnp.zeros_like(total_project)

    count = attended.shape[0]
    flat = count * LEN
    grad_branch = (mod[:, 2:3, :] * grad_mixed[...]).reshape(flat, D).astype(LOW)
    total_project[...] += dot_tn(attended[...].reshape(flat, D), grad_branch)
    grad_attended[...] = dot(grad_branch, wo[...]).astype(LOW).reshape(count, LEN, D)
    mask = lax.broadcasted_iota(jnp.int32, (LEN, PAIR), 1) < HEAD
    scale = HEAD ** (-0.5)
    for latent in range(count):
        for pair in range(HEADS // 2):
            lanes = slice(pair * PAIR, (pair + 1) * PAIR)
            key_lanes = slice(D + pair * PAIR, D + (pair + 1) * PAIR)
            value_lanes = slice(2 * D + pair * PAIR, 2 * D + (pair + 1) * PAIR)
            queries = qkv[latent, :, lanes]
            keys = qkv[latent, :, key_lanes].T
            values = qkv[latent, :, value_lanes]
            upper = grad_attended[latent, :, lanes]
            masked = head_masks(upper.astype(FULL))
            by_query, by_key, by_value = [], [], []
            for member in range(2):
                share = probs[latent, 2 * pair + member]
                weight = share.astype(FULL)
                grad_share = dot_nt(values, masked[member])
                product = weight * grad_share
                grad_scores = (
                    product - weight * jnp.sum(product, 0, keepdims=True)
                ).astype(LOW)
                by_query.append(dot(keys[member * HEAD : (member + 1) * HEAD], grad_scores))
                by_key.append(dot(grad_scores, queries))
                by_value.append(dot(share, upper))
            merged = jnp.concatenate(by_query, axis=0).T * scale
            grad_qkv[latent, :, lanes] = merged.astype(LOW)
            merged = jnp.where(mask, by_key[0], by_key[1]) * scale
            grad_qkv[latent, :, key_lanes] = merged.astype(LOW)
            merged = jnp.where(mask, by_value[0], by_value[1])
            grad_qkv[latent, :, value_lanes] = merged.astype(LOW)


def attend_backward(
    ids, tokens, mod, grad_mixed, grad_qkv, wq, total_project, grad_mod_late, sum_up, sum_down,
    grad_tokens, keep, send, extra,
    total_attend, grad_mod, extra_rows,
):
    rows = D // GROUP
    shards = keep.shape[1]
    step = pl.program_id(0)

    @pl.when(step == 0)
    def _():
        total_attend[...] = jnp.zeros_like(total_attend)

    count = tokens.shape[0]
    flat = count * LEN
    normed, inverse_spread = normalize(tokens[...].astype(FULL))
    hidden = (normed * (1.0 + mod[:, 1:2, :]) + mod[:, 0:1, :]).reshape(flat, D).astype(LOW)
    grad_low = grad_qkv[...].reshape(flat, 3 * D)
    total_attend[...] += dot_tn(hidden, grad_low)
    grad_hidden = dot(grad_low, wq[...]).reshape(count, LEN, D)
    mine = pl.ds(step * count, count)
    grad_mod[mine, 0:1, :] = jnp.sum(grad_hidden, axis=1, keepdims=True)
    grad_mod[mine, 1:2, :] = jnp.sum(grad_hidden * normed, axis=1, keepdims=True)
    grad_tokens[...] = grad_mixed[...] + normalize_back(
        grad_hidden * (1.0 + mod[:, 1:2, :]), normed, inverse_spread
    )

    @pl.when(step == pl.num_programs(0) - 1)
    def _():
        shard, low = ids[0], ids[1]
        wide, narrow = 3 * D // shards, D // shards

        @pl.loop(0, GROUP // 2)
        def _(t):
            for bit in range(2):
                span = rows_at(low ^ (2 * t + bit), rows)
                whole_attend, whole_project = total_attend[span, :], total_project[span, :]
                for s in range(shards):
                    d = lax.rem(s - shard + shards, shards)
                    piece = jnp.concatenate(
                        [
                            whole_attend[:, s * wide : (s + 1) * wide],
                            whole_project[:, s * narrow : (s + 1) * narrow],
                        ],
                        axis=1,
                    )
                    if bit:
                        send[t, d] = piece.astype(LOW)
                    else:
                        keep[t, d] = piece

        latents = grad_mod.shape[0]
        columns = [grad_mod[:, b, :] for b in range(2)] + [grad_mod_late[:, b, :] for b in range(4)]
        whole = jnp.concatenate(columns, axis=1).astype(LOW).astype(FULL)
        sums = jnp.sum(whole, axis=0, keepdims=True)
        sums = jnp.concatenate([sums, sum_up[...], sum_down[...]], axis=1)
        mod_share, bias_share = 6 * D // shards, BIAS_LEN // shards
        blocks, lines = -(-mod_share // D), -(-bias_share // D)

        def padded(values, start, stop):
            part = values[:, start : min(start + D, stop)]
            if part.shape[1] < D:
                rest = jnp.zeros((part.shape[0], D - part.shape[1]), FULL)
                part = jnp.concatenate([part, rest], axis=1)
            return part

        extra_rows[...] = jnp.zeros_like(extra_rows)
        for s in range(shards):
            for b in range(blocks):
                extra_rows[b * latents : (b + 1) * latents, :] = padded(
                    whole, s * mod_share + b * D, (s + 1) * mod_share
                )
            for b in range(lines):
                row = padded(sums, s * bias_share + b * D, (s + 1) * bias_share)
                high = row.astype(LOW).astype(FULL)
                place = blocks * latents + b
                extra_rows[place : place + 1, :] = high
                extra_rows[place + lines : place + lines + 1, :] = row - high
            extra[lax.rem(s - shard + shards, shards)] = extra_rows[...].astype(LOW)


def late_pieces(ids, own, first, second, third, extra, *pieces):
    total = own[...]
    for received in (first, second, third):
        total = total + received[...].astype(FULL)
    for d, piece in enumerate(pieces):
        piece[:NOTE, :] = extra[d]
        if total.shape[2] < D:
            piece[NOTE:, :] = jnp.zeros((total.shape[1], D), LOW)
        piece[NOTE:, : total.shape[2]] = total[d].astype(LOW)


def combine(shards, latents, ids, *refs):
    incoming, notes, weight, payload = (
        refs[:shards], refs[shards : 2 * shards], refs[2 * shards], refs[2 * shards + 1],
    )
    answers, rows_ref = refs[2 * shards + 2 : -1], refs[-1]
    rows = D // GROUP
    mod_share, bias_share = 6 * D // shards, BIAS_LEN // shards
    blocks, lines = -(-mod_share // D), -(-bias_share // D)
    total = jnp.zeros((rows, D), FULL)
    bias = jnp.zeros((NOTE, D), FULL)
    for d in range(shards):
        total = total + incoming[d][NOTE:, :].astype(FULL)
        extra = incoming[d][:NOTE, :].astype(FULL)
        bias = bias + extra
        for b in range(blocks):
            start = (b * shards + d) * latents
            rows_ref[start : start + latents, :] = extra[b * latents : (b + 1) * latents]
        start = (blocks * shards + d) * latents
        rows_ref[start : start + latents, :] = notes[d][:NOTE, :].astype(FULL)[:latents]
    payload[:rows, :] = total.astype(LOW)
    count = (blocks + 1) * shards * latents
    start = blocks * latents
    bias = bias[start : start + lines] + bias[start + lines : start + 2 * lines]
    high = bias.astype(LOW).astype(FULL)
    rows_ref[count:, :] = jnp.zeros((16, D), FULL)
    rows_ref[count : count + lines, :] = high
    rows_ref[count + 8 : count + 8 + lines, :] = bias - high
    payload[rows:, :] = rows_ref[...].astype(LOW)
    for d, answer in enumerate(answers):
        result = jnp.zeros((NOTE, D), FULL)
        for b in range(blocks):
            filled = min(D, mod_share - b * D)
            product = dot(incoming[d][:NOTE, :filled], weight[b * D : b * D + filled, :])
            result = result + shifted(product, b * latents)
        answer[...] = result[:latents]


def shifted(values, count):
    if count == 0:
        return values
    return jnp.concatenate([values[count:], values[:count]], axis=0)


COLUMNS = (3 * D, D, FF, FF, 6 * D)
TURNED = (True, True, False, False, True)
TRIANGLE = ((0, 0), (0, 1), (0, 2), (1, 1), (1, 2), (2, 2))


def slot_spans(widths):
    counts = [sum(1 for m, _ in SLOTS if m == number) for number in range(len(widths))]
    return [
        (part * (widths[m] // counts[m]), (part + 1) * (widths[m] // counts[m]))
        for m, part in SLOTS
    ]


def late_parts(latents, widths, late, late_flipped):
    rows = D // GROUP
    blocks = -(-widths[4] // D)
    unit = (blocks + 1) * latents + 16
    parts = [
        ref.at[t, pl.ds(start, unit), :]
        for ref in (late, late_flipped)
        for t in range(GROUP // 2)
        for start in range(rows, late.shape[1], unit)
    ]

    def rows_of(start):
        return jnp.concatenate([p[start : start + latents, :] for p in parts], axis=0)

    return parts, blocks, rows_of


def modulate_gradient(latents, widths, late, late_flipped, target):
    _, blocks, rows_of = late_parts(latents, widths, late, late_flipped)
    cond = rows_of(blocks * latents)
    for block in range(blocks):
        filled = min(D, widths[4] - block * D)
        target[block * D : block * D + filled, :] = dot_tn(rows_of(block * latents), cond)[:filled]


def late_gradient(ids, late, late_flipped, late_whole):
    rows = D // GROUP
    for place, block in pieces_of(ids, late, late_flipped):
        late_whole[rows_at(place, rows), :] = block[:rows, :].astype(FULL)
    return turn(late_whole[...])


def mix(moment, grad):
    moment = MOMENTUM * moment + grad
    return moment, grad + MOMENTUM * moment


def gram_kernel(latents, ids, late, late_flipped, early, early_flipped, *refs):
    moments, gram, columns = refs[0:5], refs[5], refs[6]
    late_whole, flat_gram, early_whole, modulate_whole = refs[7:11]
    low = ids[1]
    rows = D // GROUP
    shards = gram.shape[0]
    widths = [whole // shards for whole in COLUMNS]
    spans = slot_spans(widths)
    for number in range(5):
        owners = [k for k, (m, _) in enumerate(SLOTS) if m == number]
        condition = low == owners[0]
        for owner in owners[1:]:
            condition = condition | (low == owner)

        @pl.when(condition)
        def _(number=number, owners=owners):
            if number < 2:
                start = 0 if number == 0 else widths[0]
                grad = late_gradient(ids, late, late_flipped, late_whole)
                grad = grad[start : start + widths[number]]
            elif number < 4:
                start = 0 if number == 2 else widths[2]
                for place, block in pieces_of(ids, early, early_flipped):
                    piece = block[...].astype(FULL)[:, start : start + widths[number]]
                    early_whole[rows_at(place, rows), :] = piece
                grad = early_whole[...]
            else:
                modulate_gradient(latents, widths, late, late_flipped, modulate_whole)
                grad = modulate_whole[...]
            mixed = mix(moments[number][...], grad)[1]
            parts = split_low(mixed)
            whole = dot_split(parts, parts, dot_tn if TURNED[number] else dot_nt)
            for place, (a, b) in enumerate(TRIANGLE):
                flat_gram[place * 128 : (place + 1) * 128, :] = whole[
                    a * 128 : (a + 1) * 128, b * 128 : (b + 1) * 128
                ]
            if not TURNED[number]:
                mixed = turn(mixed)
            for owner in owners:

                @pl.when(low == owner)
                def _(owner=owner, mixed=mixed):
                    start, stop = spans[owner]
                    filled = stop - start
                    columns[:filled, :] = mixed[start:stop]
                    if filled < columns.shape[0]:
                        columns[filled:, :] = jnp.zeros((columns.shape[0] - filled, D), FULL)

    size = gram.shape[1]
    for s in range(shards):
        gram[lax.rem(s - ids[0] + shards, shards)] = flat_gram[s * size : (s + 1) * size, :]


def momenta_kernel(latents, ids, late, late_flipped, early, early_flipped, *refs):
    moments, grads, momenta = refs[0:5], refs[5:10], refs[10:15]
    bias, late_whole = refs[15:17]
    rows = D // GROUP
    widths = [m.shape[0 if turned else 1] for m, turned in zip(moments, TURNED)]
    turned = late_gradient(ids, late, late_flipped, late_whole)
    grads[0][...] = turned[: widths[0]]
    grads[1][...] = turned[widths[0] : widths[0] + widths[1]]
    for place, block in pieces_of(ids, early, early_flipped):
        piece = block[...].astype(FULL)
        grads[2][rows_at(place, rows), :] = piece[:, : widths[2]]
        grads[3][rows_at(place, rows), :] = piece[:, widths[2] :]
    modulate_gradient(latents, widths, late, late_flipped, grads[4])
    parts, blocks, _ = late_parts(latents, widths, late, late_flipped)
    total = jnp.zeros((16, D), FULL)
    for part in parts:
        total = total + part[(blocks + 1) * latents :, :].astype(FULL)
    bias[...] = total[:8] + total[8:]
    for number in range(5):
        momenta[number][...] = mix(moments[number][...], grads[number][...])[0]


def polynomial_kernel(ids, *refs):
    shards = len(refs) - 5
    pieces, columns, answer, flat_gram, gram_ref, product_ref = refs[:shards], *refs[shards:]
    size = pieces[0].shape[0]
    for d in range(shards):
        source = lax.rem(ids[0] - d + shards, shards)
        flat_gram[rows_at(source, size), :] = pieces[d][...]
    for place, (a, b) in enumerate(TRIANGLE):
        block = flat_gram[place * 128 : (place + 1) * 128, :]
        gram_ref[a * 128 : (a + 1) * 128, b * 128 : (b + 1) * 128] = block
        if a != b:
            gram_ref[b * 128 : (b + 1) * 128, a * 128 : (a + 1) * 128] = block.T
    gram = gram_ref[...]
    diagonal = lax.broadcasted_iota(jnp.int32, (D, D), 0) == lax.broadcasted_iota(
        jnp.int32, (D, D), 1
    )
    trace = jnp.sum(jnp.where(diagonal, gram, 0.0))
    scale = 1.0 / (jnp.sqrt(jnp.full((1, 1), trace)) + 1e-07)
    gram = (gram * scale) * scale

    def advance(gram, product):
        mixing = POLY_CUBIC * gram + POLY_QUINTIC * dot(left_deep(gram), right_deep(gram))
        mixing_deep = left_deep(mixing)
        both = jnp.concatenate([gram, product], axis=1)
        both = POLY_LINEAR * both + dot(mixing_deep, right_deep(both))
        half = both[:, :D]
        return POLY_LINEAR * half + dot(mixing_deep, right_deep(half)), both[:, D:]

    mixing = POLY_CUBIC * gram + POLY_QUINTIC * dot(left_deep(gram), right_deep(gram))
    mixing_deep = left_deep(mixing)
    half = POLY_LINEAR * gram + dot(mixing_deep, right_deep(gram))
    gram_ref[...] = POLY_LINEAR * half + dot(mixing_deep, right_deep(half))
    product_ref[...] = jnp.where(diagonal, POLY_LINEAR, 0.0) + mixing

    @pl.loop(0, NS_ITERS - 2)
    def _(step):
        gram, product = advance(gram_ref[...], product_ref[...])
        gram_ref[...] = gram
        product_ref[...] = product

    gram, product = gram_ref[...], product_ref[...]
    mixing = POLY_CUBIC * gram + POLY_QUINTIC * dot(left_deep(gram), right_deep(gram))
    product = POLY_LINEAR * product + dot(left_deep(mixing), right_deep(product))
    answer[...] = dot(left_deep(columns[...] * scale), right_deep(product)).astype(LOW)


def left_deep(value):
    high, rest = split_low(value)
    return jnp.concatenate([high, rest, high], axis=1)


def right_deep(value):
    high, rest = split_low(value)
    return jnp.concatenate([high, high, rest], axis=0)


def update_kernel(ids, answers, answers_flipped, *refs):
    masters, updated, ordered = refs[:5], refs[5:10], refs[10]
    for place, block in pieces_of(ids, answers, answers_flipped):
        ordered[place] = block[...]
    widths = [m.shape[0 if turned else 1] for m, turned in zip(masters, TURNED)]
    spans = slot_spans(widths)
    for number in range(5):
        factor = MUON_RATE * 0.2 * math.sqrt(COLUMNS[number])
        mine = [k for k, (m, _) in enumerate(SLOTS) if m == number]
        if TURNED[number]:
            for k in mine:
                start, stop = spans[k]
                updated[number][start:stop, :] = masters[number][start:stop, :] * (
                    1.0 - MUON_RATE * WEIGHT_DECAY
                ) - factor * ordered[k, : stop - start, :].astype(FULL)
        else:
            direction = jnp.concatenate(
                [ordered[k, : spans[k][1] - spans[k][0], :].astype(FULL) for k in mine], axis=0
            )
            updated[number][...] = masters[number][...] * (
                1.0 - MUON_RATE * WEIGHT_DECAY
            ) - factor * direction.T


def per_device(
    tokens,
    condition,
    cotangent,
    attend_weight,
    project_weight,
    expand_weight,
    contract_weight,
    modulate_weight,
    biases,
    attend_moment,
    project_moment,
    expand_moment,
    contract_moment,
    modulate_moment,
    bias_first,
    bias_second,
):
    latents = tokens.shape[0]
    steps = latents // BLOCK
    shards = lax.axis_size("shard")
    shard = lax.axis_index("shard")
    low = lax.axis_index("rep") % GROUP
    ids = jnp.stack([shard, low]).astype(jnp.int32)
    rows = D // GROUP
    bias_share = biases.shape[0]
    mod_share = modulate_weight.shape[1]
    late_width = 4 * D // shards
    late_rows = late_width // GROUP

    (note,) = local_call(
        prepare,
        ids,
        [
            (condition, False),
            (biases.reshape(1, -1), False),
            (attend_weight.T, (late_rows, lambda place: jnp.minimum(place, 5))),
            (project_weight.T, (late_rows, lambda place: jnp.maximum(place - 6, 0))),
        ],
        [((NOTE + late_rows, D), LOW, False)],
        [pltpu.VMEM((NOTE, D), FULL)],
        1,
        D * D,
        "prepare",
    )
    notes = exchange([note] * shards)

    *shares, modulate_low, late_weights = local_call(
        modulation_kernel,
        ids,
        [(piece, False) for piece in notes] + [(modulate_weight.T, False)],
        [((latents, mod_share), FULL, False)] * shards
        + [((mod_share, D), LOW, False), ((shards, late_rows, D), LOW, False)],
        [],
        1,
        2 * shards * NOTE * D * mod_share,
        "modulation",
    )
    answers = [shares[0]] + [shift(shares[d], shards - d) for d in range(1, shards)]
    late_weights_chips = gather_chips(late_weights)
    (early_weights,) = local_call(
        pack,
        ids,
        [(w, (rows, lambda place: place)) for w in (expand_weight, contract_weight)],
        [((rows, 2 * FF // shards), LOW, False)],
        [],
        1,
        D * D,
        "pack",
        after=(late_weights,),
    )
    early_weights = jnp.stack(exchange([early_weights] * shards))
    early_weights_chips = gather_chips(early_weights)
    (late_stacked,) = local_call(
        stack,
        ids,
        [(v, False) for v in late_weights_chips],
        [((GROUP // 2, shards, late_rows, D), LOW, False)],
        [],
        1,
        D * D,
        "stack_late",
        after=(early_weights,),
    )
    late_flipped = flip(late_stacked, 1)

    tokens_shape = (latents, LEN, D)
    qkv, probs, attended, branch, wq, wo, mod, bias_up, bias_down = local_call(
        attention_forward,
        ids,
        [(tokens, True), (late_stacked, False), (late_flipped, False)]
        + [(v, False) for v in (*answers, *notes)],
        [
            ((latents, LEN, 3 * D), LOW, True),
            ((latents, HEADS, LEN, LEN), LOW, True),
            (tokens_shape, LOW, True),
            (tokens_shape, FULL, True),
            ((3 * D, D), LOW, False),
            ((D, D), LOW, False),
            ((latents, 6, D), FULL, False),
            ((1, FF), FULL, False),
            ((1, D), FULL, False),
        ],
        [
            pltpu.VMEM((shards, late_width, D), LOW if late_rows % 16 == 0 else FULL),
            pltpu.VMEM((BLOCK * LEN, D), LOW),
            pltpu.VMEM((BLOCK * LEN, D), LOW),
            pltpu.VMEM((shards, latents, mod_share), FULL),
            pltpu.VMEM((shards, NOTE, D), FULL),
            pltpu.VMEM((D, 3 * D), LOW),
            pltpu.VMEM((D, D), LOW),
        ],
        steps,
        latents * (2 * LEN * D * 4 * D + 4 * HEADS * LEN * LEN * PAIR) * 2,
        "attention_forward",
        after=(early_weights,),
    )
    early_shape = (GROUP // 2, shards, rows, 2 * FF // shards)
    (early_weights_stacked,) = local_call(
        stack,
        ids,
        [(v, False) for v in early_weights_chips],
        [(early_shape, LOW, False)],
        [],
        1,
        D * D,
        "stack",
        after=(branch,),
    )
    early_weights_flipped = flip(early_weights_stacked, 1)
    block_output, grad_mixed, grad_mod_late, keep, send, sum_up, sum_down = local_call(
        perceptron,
        ids,
        [
            (tokens, True),
            (branch, True),
            (mod, True),
            (cotangent, True),
            (early_weights_stacked, False),
            (early_weights_flipped, False),
            (bias_up, False),
            (bias_down, False),
        ],
        [
            (tokens_shape, LOW, True),
            (tokens_shape, FULL, True),
            ((latents, 4, D), FULL, True),
            (early_shape, FULL, False),
            (early_shape, LOW, False),
            ((1, FF), FULL, False),
            ((1, D), FULL, False),
        ],
        [
            pltpu.VMEM((shards, D, 2 * FF // shards), LOW),
            pltpu.VMEM((D, FF), LOW),
            pltpu.VMEM((D, FF), LOW),
            pltpu.VMEM((BLOCK * LEN, FF), LOW),
            pltpu.VMEM((BLOCK * LEN, FF), FULL),
            pltpu.VMEM((D, FF), FULL),
            pltpu.VMEM((D, FF), FULL),
        ],
        steps,
        latents * 2 * LEN * D * FF * 6 * 2,
        "perceptron",
    )

    early_totals = sum_cores(keep, send, ids, "early_sum", ())
    arrived = exchange_chips(early_totals)
    early_chips = sum(piece.astype(FULL) for piece in arrived[1:]) + arrived[0]
    grad_qkv, total_project = local_call(
        attention_backward,
        ids,
        [
            (mod, True),
            (attended, True),
            (grad_mixed, True),
            (qkv, True),
            (probs, True),
            (wo, False),
        ],
        [((latents, LEN, 3 * D), LOW, True), ((D, D), FULL, False)],
        [pltpu.VMEM((1, LEN, D), LOW)],
        latents,
        latents * (10 * HEADS * LEN * LEN * PAIR + 4 * LEN * D * D),
        "attention_backward",
        after=tuple(early_totals[1:]),
    )
    early_pieces = exchange([early_chips[d].astype(LOW) for d in range(shards)])
    late_shape = (GROUP // 2, shards, rows, late_width)
    tokens_grad, keep, send, extra = local_call(
        attend_backward,
        ids,
        [
            (tokens, True),
            (mod, True),
            (grad_mixed, True),
            (grad_qkv, True),
            (wq, False),
            (total_project, False),
            (grad_mod_late, False),
            (sum_up, False),
            (sum_down, False),
        ],
        [
            (tokens_shape, FULL, True),
            (late_shape, FULL, False),
            (late_shape, LOW, False),
            ((shards, NOTE, D), LOW, False),
        ],
        [
            pltpu.VMEM((D, 3 * D), FULL),
            pltpu.VMEM((latents, 2, D), FULL),
            pltpu.VMEM((NOTE, D), FULL),
        ],
        steps,
        latents * 2 * LEN * D * 6 * D * 2,
        "attend_backward",
        after=(early_chips,),
    )

    late_totals = sum_cores(keep, send, ids, "late_sum", ())
    arrived = exchange_chips(late_totals)
    (early,) = local_call(
        total_kernel,
        ids,
        [(v, False) for v in (early_chips[0], *early_pieces[1:])],
        [(early_pieces[1].shape, LOW, False)],
        [],
        1,
        D * D,
        "early_total",
        after=tuple(late_totals[1:]),
    )
    early_stacked, early_flipped = gather_group(sum_rest(early))
    outgoing = local_call(
        late_pieces,
        ids,
        [(v, False) for v in (*arrived, extra)],
        [((NOTE + rows, D), LOW, False)] * shards,
        [],
        1,
        4 * shards * rows * late_width,
        "late_pieces",
        after=(early,),
    )
    group_latents = shards * latents
    unit = (-(-mod_share // D) + 1) * group_latents + 16
    payload, *shares = local_call(
        partial(combine, shards, latents),
        ids,
        [(v, False) for v in (*exchange(outgoing), *notes, modulate_low)],
        [((rows + unit, D), LOW, False)] + [((latents, D), FULL, False)] * shards,
        [pltpu.VMEM((unit, D), FULL)],
        1,
        2 * shards * NOTE * D * mod_share,
        "combine",
        after=(early_stacked,),
    )
    if lax.axis_size("rep") > GROUP:
        late, others = sum_rest(payload[:rows]), payload[rows:]
        for bit in range(3, lax.axis_size("rep").bit_length() - 1):
            others = jnp.concatenate([others, flip(others, 1 << bit)], axis=0)
        payload = jnp.concatenate([late, others], axis=0)
    late_stacked, late_flipped = gather_group(payload)

    grad_cond_low = shares[0]
    for d in range(1, shards):
        grad_cond_low = grad_cond_low + shift(shares[d], shards - d)
    _, silu_back = jax.vjp(jax.nn.silu, condition.astype(FULL))
    condition_grad = silu_back(grad_cond_low)[0]

    def as_held(values):
        return [v.T if turned else v for v, turned in zip(values, TURNED)]

    masters = as_held(
        [attend_weight, project_weight, expand_weight, contract_weight, modulate_weight]
    )
    moments = as_held(
        [attend_moment, project_moment, expand_moment, contract_moment, modulate_moment]
    )
    shapes = [m.shape for m in masters]
    widths = [whole // shards for whole in COLUMNS]
    slot_width = max(stop - start for start, stop in slot_spans(widths))
    piece_rows = 128 * len(TRIANGLE) // shards
    sources = [
        (v, False) for v in (late_stacked, late_flipped, early_stacked, early_flipped, *moments)
    ]
    gram, columns = local_call(
        partial(gram_kernel, group_latents),
        ids,
        sources,
        [((shards, piece_rows, 128), FULL, False), ((slot_width, D), FULL, False)],
        [
            pltpu.VMEM((D, D), FULL),
            pltpu.VMEM((128 * len(TRIANGLE), 128), FULL),
            pltpu.VMEM(shapes[2], FULL),
            pltpu.VMEM(shapes[4], FULL),
        ],
        1,
        6 * D * D * D,
        "gram",
    )
    *results, bias_block = local_call(
        partial(momenta_kernel, group_latents),
        ids,
        sources,
        [(shape, FULL, False) for shape in shapes * 2] + [((8, D), FULL, False)],
        [pltpu.VMEM((D, D), FULL)],
        1,
        D * D * D,
        "momenta",
        after=(gram,),
    )
    gradients, momenta = as_held(results[0:5]), as_held(results[5:10])
    piece = sum(exchange([gram[d] for d in range(shards)]))
    (answer,) = local_call(
        polynomial_kernel,
        ids,
        [(p, False) for p in exchange([piece] * shards)] + [(columns, False)],
        [((slot_width, D), LOW, False)],
        [
            pltpu.VMEM((128 * len(TRIANGLE), 128), FULL),
            pltpu.VMEM((D, D), FULL),
            pltpu.VMEM((D, D), FULL),
        ],
        1,
        2 * 3 * 18 * D * D * D,
        "polynomial",
        after=(condition_grad, bias_block),
    )
    updated = local_call(
        update_kernel,
        ids,
        [(v, False) for v in (*gather_group(answer), *masters)],
        [(shape, FULL, False) for shape in shapes],
        [pltpu.VMEM((GROUP, slot_width, D), LOW)],
        1,
        2 * D * sum(widths),
        "update",
    )
    updated = as_held(updated)

    bias_gradient = bias_block.reshape(-1)[:bias_share]
    bias_momentum = BETA_ONE * bias_first + (1.0 - BETA_ONE) * bias_gradient
    bias_variance = BETA_TWO * bias_second + (1.0 - BETA_TWO) * bias_gradient * bias_gradient
    corrected_first = bias_momentum / (1.0 - BETA_ONE**STEP)
    corrected_second = bias_variance / (1.0 - BETA_TWO**STEP)
    bias_updated = biases * (1.0 - ADAM_RATE * WEIGHT_DECAY) - ADAM_RATE * corrected_first / (
        jnp.sqrt(corrected_second) + ADAM_EPSILON
    )
    return (
        block_output,
        tokens_grad,
        condition_grad,
        *gradients,
        *momenta,
        *updated,
        bias_gradient,
        bias_momentum,
        bias_variance,
        bias_updated,
    )


def solution(mesh):
    rows = P(("shard", "rep"), None, None)
    vectors = P(("shard", "rep"), None)
    columns = P(None, "shard")
    flat = P("shard")
    return jax.shard_map(
        per_device,
        mesh=mesh,
        in_specs=(rows, vectors, rows) + (columns,) * 5 + (flat,) + (columns,) * 5 + (flat,) * 2,
        out_specs=(rows, rows, vectors) + (columns,) * 15 + (flat,) * 4,
        check_vma=False,
    )
```

```python
from functools import partial
import math

import jax
import jax.numpy as jnp
from jax import lax
from jax.experimental import pallas as pl
from jax.experimental.pallas import tpu as pltpu
from jax.sharding import PartitionSpec as P

D = 384
HEADS = 6
HEAD = 64
FF = 1536
LEN = 256
NS_ITERS = 5
STEP = 10
PAIR = 2 * HEAD
CHUNK = 512
GROUP = 8
BLOCK = 2
BIAS_LEN = 6 * D + FF + D
NOTE = 16
GRANTS = {
    "attention_forward": 40,
    "perceptron": 40,
    "attention_backward": 32,
    "attend_backward": 36,
    "modulation": 48,
    "pack": 48,
    "momenta": 32,
    "gram": 24,
    "polynomial": 20,
    "update": 24,
}

POLY_LINEAR = 3.4445
POLY_CUBIC = -4.775
POLY_QUINTIC = 2.0315
MOMENTUM = 0.95
MUON_RATE = 0.4
WEIGHT_DECAY = 0.01
ADAM_RATE = 0.1
BETA_ONE = 0.9
BETA_TWO = 0.999
ADAM_EPSILON = 1e-08
GELU_SLOPE = math.sqrt(2.0 / math.pi)
GELU_CUBIC = 0.044715

LOW = jnp.bfloat16
FULL = jnp.float32

SLOTS = ((4, 0), (4, 1), (0, 0), (2, 0), (2, 1), (3, 0), (3, 1), (1, 0))


def shift(value, distance):
    size = lax.axis_size("shard")
    return lax.ppermute(value, "shard", [(i, (i + distance) % size) for i in range(size)])


def flip(value, mask):
    size = lax.axis_size("rep")
    return lax.ppermute(value, "rep", [(i, i ^ mask) for i in range(size)])


def exchange(pieces):
    return [pieces[0]] + [shift(pieces[d], d) for d in range(1, len(pieces))]


def gather_chips(value):
    return [value] + [flip(value, 2 * t) for t in range(1, GROUP // 2)]


def gather_group(value):
    stacked = jnp.stack(gather_chips(value))
    return stacked, flip(stacked, 1)


def sum_cores(keep, send, ids, name, after):
    received = flip(send, 1)
    shape = keep.shape[1:]
    return local_call(
        split_sum,
        ids,
        [(keep, False), (received, False)],
        [(shape, FULL, False)] + [(shape, LOW, False)] * (keep.shape[0] - 1),
        [],
        1,
        keep.size,
        name,
        after=after,
    )


def exchange_chips(totals):
    return [totals[0]] + [flip(totals[t], 2 * t) for t in range(1, GROUP // 2)]


def sum_rest(value):
    for bit in range(3, lax.axis_size("rep").bit_length() - 1):
        value = (value.astype(FULL) + flip(value, 1 << bit).astype(FULL)).astype(LOW)
    return value


def dot(left, right):
    return lax.dot_general(left, right, (((1,), (0,)), ((), ())), preferred_element_type=FULL)


def dot_nt(left, right):
    return lax.dot_general(left, right, (((1,), (1,)), ((), ())), preferred_element_type=FULL)


def dot_tn(left, right):
    return lax.dot_general(left, right, (((0,), (0,)), ((), ())), preferred_element_type=FULL)


def split_low(value):
    high = value.astype(LOW)
    return high, (value - high.astype(FULL)).astype(LOW)


def dot_split(left, right, product=dot):
    return product(left[0], right[0]) + (product(left[0], right[1]) + product(left[1], right[0]))


def normalize(values):
    centered = values - jnp.mean(values, -1, keepdims=True)
    inverse_spread = lax.rsqrt(jnp.mean(centered * centered, -1, keepdims=True) + 1e-06)
    return centered * inverse_spread, inverse_spread


def normalize_back(upstream, normed, inverse_spread):
    return inverse_spread * (
        upstream
        - jnp.mean(upstream, -1, keepdims=True)
        - normed * jnp.mean(upstream * normed, -1, keepdims=True)
    )


def local_call(kernel, ids, inputs, outputs, scratch, steps, flops, name, after=()):
    def run(*refs):
        kernel(*refs[: 1 + len(inputs)], *refs[1 + len(inputs) + len(after) :])

    def spec(shape, blocked):
        zeros = (0,) * (len(shape) - 1)
        if isinstance(blocked, tuple):
            rows, place = blocked
            return pl.BlockSpec(
                (rows,) + tuple(shape[1:]), lambda i, ids: (place(ids[1]),) + zeros
            )
        if blocked:
            block = (shape[0] // steps,) + tuple(shape[1:])
            return pl.BlockSpec(block, lambda i, _: (i,) + zeros)
        return pl.BlockSpec(tuple(shape), lambda i, _: (0,) + zeros)

    moved = sum(v.size * v.dtype.itemsize for v, _ in inputs)
    moved += sum(math.prod(shape) * jnp.dtype(kind).itemsize for shape, kind, _ in outputs)
    return pl.pallas_call(
        run,
        grid_spec=pltpu.PrefetchScalarGridSpec(
            num_scalar_prefetch=1,
            grid=(steps,),
            in_specs=[spec(v.shape, blocked) for v, blocked in inputs]
            + [pl.BlockSpec(memory_space=pl.ANY) for _ in after],
            out_specs=[spec(shape, blocked) for shape, _, blocked in outputs],
            scratch_shapes=scratch,
        ),
        out_shape=[jax.ShapeDtypeStruct(shape, kind) for shape, kind, _ in outputs],
        compiler_params=pltpu.CompilerParams(
            dimension_semantics=("arbitrary",), vmem_limit_bytes=GRANTS.get(name, 16) * 1024 * 1024
        ),
        cost_estimate=pl.CostEstimate(flops=flops, bytes_accessed=moved, transcendentals=0),
        name=name,
    )(ids, *[v for v, _ in inputs], *after)


def pieces_of(ids, stacked, flipped):
    for t in range(GROUP // 2):
        for bit, blocks in enumerate((stacked, flipped)):
            yield ids[1] ^ (2 * t + bit), blocks.at[t]


def rows_at(place, rows):
    return pl.ds(pl.multiple_of(place * rows, rows), rows)


def turn(value):
    filled = value.shape[1]
    extra = -filled % 128
    if extra:
        value = jnp.concatenate([value, jnp.zeros((value.shape[0], extra), value.dtype)], axis=1)
    return value.T[:filled]


def head_masks(values):
    lane = lax.broadcasted_iota(jnp.int32, values.shape, 1) % PAIR
    zero = jnp.zeros_like(values)
    return (
        jnp.where(lane < HEAD, values, zero).astype(LOW),
        jnp.where(lane < HEAD, zero, values).astype(LOW),
    )


def split_sum(ids, keep, received, own, *others):
    own[...] = keep[0] + received[0].astype(FULL)
    for t, other in enumerate(others):
        other[...] = (keep[t + 1] + received[t + 1].astype(FULL)).astype(LOW)


def modulation_kernel(ids, *refs):
    shards = refs[-1].shape[0]
    notes, weight, answers, weight_low, stacked = (
        refs[:shards], refs[shards], refs[shards + 1 : -2], refs[-2], refs[-1],
    )
    low = weight[...].astype(LOW)
    weight_low[...] = low
    for d, (note, answer) in enumerate(zip(notes, answers)):
        answer[...] = dot_nt(note[:NOTE, :], low)[: answer.shape[0]]
        stacked[d] = note[NOTE:, :]


def total_kernel(ids, own, *refs):
    total = own[...]
    for piece in refs[:-1]:
        total = total + piece[...].astype(FULL)
    refs[-1][...] = total.astype(LOW)


def prepare(ids, condition, biases, attend, project, note, first):
    latents = condition.shape[0]
    value = condition[...].astype(FULL)
    first[...] = jnp.zeros_like(first)
    first[:latents, :] = value / (1.0 + jnp.exp(-value))
    share = biases.shape[1]
    for b in range(-(-share // D)):
        filled = min(D, share - b * D)
        first[latents + b : latents + b + 1, :filled] = biases[:, b * D : b * D + filled]
    note[:NOTE, :] = first[...].astype(LOW)

    @pl.when(ids[1] < 6)
    def _():
        note[NOTE:, :] = attend[...].astype(LOW)

    @pl.when(ids[1] >= 6)
    def _():
        note[NOTE:, :] = project[...].astype(LOW)


def pack(ids, *refs):
    start = 0
    for weight in refs[:-1]:
        width = weight.shape[1]
        refs[-1][:, start : start + width] = weight[...].astype(LOW)
        start = start + width


def stack(ids, *refs):
    for t, block in enumerate(refs[:-1]):
        refs[-1][t] = block[...]


def attention_forward(
    ids, tokens, stacked, flipped, *refs,
):
    shards = (len(refs) - 16) // 2
    answers, notes = refs[:shards], refs[shards : 2 * shards]
    (
        qkv, probs, attended, branch, wq, wo, mod_all, bias_up, bias_down,
        ordered, query_a, query_b, mod_parts, bias_parts, wq_plain, wo_plain,
    ) = refs[2 * shards :]
    rows = ordered.shape[1] // GROUP
    wide, narrow = 3 * D // shards, D // shards

    @pl.when(pl.program_id(0) == 0)
    def _():
        for place, block in pieces_of(ids, stacked, flipped):
            for d in range(shards):
                source = lax.rem(ids[0] - d + shards, shards)
                ordered[source, rows_at(place, rows), :] = block[d].astype(ordered.dtype)
        for s in range(shards):
            wq[s * wide : (s + 1) * wide, :] = ordered[s, :wide, :].astype(LOW)
            wo[s * narrow : (s + 1) * narrow, :] = ordered[s, wide:, :].astype(LOW)
        wq_plain[...] = wq[...].T
        wo_plain[...] = wo[...].T
        for d in range(shards):
            mod_parts[lax.rem(ids[0] + d, shards)] = answers[d][...]
            bias_parts[lax.rem(ids[0] - d + shards, shards)] = notes[d][:NOTE, :].astype(FULL)
        latents = mod_all.shape[0]
        share = BIAS_LEN // shards
        pieces = []
        for s in range(shards):
            for b in range(-(-share // D)):
                row = bias_parts[s, latents + b : latents + b + 1, :]
                pieces.append(row[:, : min(D, share - b * D)])
        bias = jnp.concatenate(pieces, axis=1)
        whole = jnp.concatenate([mod_parts[s] for s in range(shards)], axis=1) + bias[:, : 6 * D]
        for latent in range(latents):
            for b in range(6):
                mod_all[latent, b : b + 1, :] = whole[latent : latent + 1, b * D : (b + 1) * D]
        bias_up[...] = bias[:, 6 * D : 6 * D + FF]
        bias_down[...] = bias[:, 6 * D + FF :]

    count = tokens.shape[0]
    mod = mod_all[pl.ds(pl.program_id(0) * count, count)]
    normed, _ = normalize(tokens[...].astype(FULL))
    hidden = normed * (1.0 + mod[:, 1:2, :]) + mod[:, 0:1, :]
    hidden = hidden.reshape(count * LEN, D).astype(LOW)
    queries = dot(hidden, wq_plain[:, :D])
    masked_a, masked_b = head_masks(queries)
    query_a[...] = masked_a
    query_b[...] = masked_b
    qkv[:, :, :D] = queries.astype(LOW).reshape(count, LEN, D)
    qkv[:, :, D:] = dot(hidden, wq_plain[:, D:]).astype(LOW).reshape(count, LEN, 2 * D)

    @pl.loop(0, count)
    def _(latent):
        span = pl.ds(pl.multiple_of(latent * LEN, LEN), LEN)
        for pair in range(HEADS // 2):
            lanes = slice(pair * PAIR, (pair + 1) * PAIR)
            keys = qkv[latent, :, D + pair * PAIR : D + (pair + 1) * PAIR]
            values = qkv[latent, :, 2 * D + pair * PAIR : 2 * D + (pair + 1) * PAIR].T
            results = []
            for member, masked in enumerate((query_a, query_b)):
                scores = dot_nt(keys, masked[span, lanes]) * (HEAD ** (-0.5) / math.log(2.0))
                top = jnp.max(scores, 0, keepdims=True)
                raised = jnp.exp2(scores - top)
                share = (raised * (1.0 / jnp.sum(raised, 0, keepdims=True))).astype(LOW)
                probs[latent, 2 * pair + member] = share
                results.append(dot(values[member * HEAD : (member + 1) * HEAD], share))
            attended[latent, :, lanes] = jnp.concatenate(results, axis=0).T.astype(LOW)

    branch[...] = dot(attended[...].reshape(count * LEN, D), wo_plain[...]).reshape(count, LEN, D)


def perceptron(
    ids, tokens, branch, mod, cotangent, stacked, flipped, bias_up, bias_down,
    out, grad_mixed, grad_mod, keep, send, sum_up, sum_down,
    ordered, wu, wd, act, slope, total_up, total_down,
):
    shards = ordered.shape[0]
    rows = D // GROUP
    width = FF // shards
    step = pl.program_id(0)

    @pl.when(step == 0)
    def _():
        for place, block in pieces_of(ids, stacked, flipped):
            for d in range(shards):
                source = lax.rem(ids[0] - d + shards, shards)
                ordered[source, rows_at(place, rows), :] = block[d]
        for i in range(GROUP):
            span = slice(i * rows, (i + 1) * rows)
            pieces = [ordered[s, span, :] for s in range(shards)]
            wu[span, :] = jnp.concatenate([p[:, :width] for p in pieces], axis=1)
            wd[span, :] = jnp.concatenate([p[:, width:] for p in pieces], axis=1)
        total_up[...] = jnp.zeros_like(total_up)
        total_down[...] = jnp.zeros_like(total_down)
        sum_up[...] = jnp.zeros_like(sum_up)
        sum_down[...] = jnp.zeros_like(sum_down)

    count = tokens.shape[0]
    flat = count * LEN
    branch_out = branch[...]
    mixed = tokens[...].astype(FULL) + mod[:, 2:3, :] * branch_out
    normed, inverse_spread = normalize(mixed)
    hidden = (normed * (1.0 + mod[:, 4:5, :]) + mod[:, 3:4, :]).reshape(flat, D).astype(LOW)
    result = jnp.zeros((flat, D), FULL)
    for start in range(0, FF, CHUNK):
        span = slice(start, start + CHUNK)
        u = dot(hidden, wu[:, span]) + bias_up[:, span]
        square = u * u
        half = 0.5 + 0.5 * jnp.tanh(u * (GELU_SLOPE + (GELU_SLOPE * GELU_CUBIC) * square))
        act_low = (u * half).astype(LOW)
        act[:, span] = act_low
        steep = u * (2.0 * GELU_SLOPE + (6.0 * GELU_SLOPE * GELU_CUBIC) * square)
        slope[:, span] = half + (half - half * half) * steep
        result = result + dot_nt(act_low, wd[:, span])
    result = (result + bias_down[...]).reshape(count, LEN, D)
    gate = mod[:, 5:6, :]
    out[...] = (mixed + gate * result).astype(LOW)
    upstream = cotangent[...].astype(FULL)
    grad_mod[:, 3:4, :] = jnp.sum(upstream * result, axis=1, keepdims=True)
    grad_result = (gate * upstream).reshape(flat, D).astype(LOW)
    sum_down[...] += jnp.sum(grad_result.astype(FULL), axis=0, keepdims=True)
    grad_hidden = jnp.zeros((flat, D), FULL)
    for start in range(0, FF, CHUNK):
        span = slice(start, start + CHUNK)
        grad_u = (dot(grad_result, wd[:, span]) * slope[:, span]).astype(LOW)
        sum_up[:, span] += jnp.sum(grad_u.astype(FULL), axis=0, keepdims=True)
        total_down[:, span] += dot_tn(grad_result, act[:, span])
        total_up[:, span] += dot_tn(hidden, grad_u)
        grad_hidden = grad_hidden + dot_nt(grad_u, wu[:, span])
    grad_hidden = grad_hidden.reshape(count, LEN, D)
    grad_mod[:, 1:2, :] = jnp.sum(grad_hidden, axis=1, keepdims=True)
    grad_mod[:, 2:3, :] = jnp.sum(grad_hidden * normed, axis=1, keepdims=True)
    back = upstream + normalize_back(
        grad_hidden * (1.0 + mod[:, 4:5, :]), normed, inverse_spread
    )
    grad_mixed[...] = back
    grad_mod[:, 0:1, :] = jnp.sum(back * branch_out, axis=1, keepdims=True)

    @pl.when(step == pl.num_programs(0) - 1)
    def _():
        shard, low = ids[0], ids[1]

        @pl.loop(0, GROUP // 2)
        def _(t):
            for bit in range(2):
                span = rows_at(low ^ (2 * t + bit), rows)
                for s in range(shards):
                    d = lax.rem(s - shard + shards, shards)
                    lanes = slice(s * width, (s + 1) * width)
                    piece = jnp.concatenate(
                        [total_up[span, lanes], total_down[span, lanes]], axis=1
                    )
                    if bit:
                        send[t, d] = piece.astype(LOW)
                    else:
                        keep[t, d] = piece


def attention_backward(
    ids, mod, attended, grad_mixed, qkv, probs, wo,
    grad_qkv, total_project,
    grad_attended,
):
    @pl.when(pl.program_id(0) == 0)
    def _():
        total_project[...] = jnp.zeros_like(total_project)

    count = attended.shape[0]
    flat = count * LEN
    grad_branch = (mod[:, 2:3, :] * grad_mixed[...]).reshape(flat, D).astype(LOW)
    total_project[...] += dot_tn(attended[...].reshape(flat, D), grad_branch)
    grad_attended[...] = dot(grad_branch, wo[...]).astype(LOW).reshape(count, LEN, D)
    mask = lax.broadcasted_iota(jnp.int32, (LEN, PAIR), 1) < HEAD
    scale = HEAD ** (-0.5)
    for latent in range(count):
        for pair in range(HEADS // 2):
            lanes = slice(pair * PAIR, (pair + 1) * PAIR)
            key_lanes = slice(D + pair * PAIR, D + (pair + 1) * PAIR)
            value_lanes = slice(2 * D + pair * PAIR, 2 * D + (pair + 1) * PAIR)
            queries = qkv[latent, :, lanes]
            keys = qkv[latent, :, key_lanes].T
            values = qkv[latent, :, value_lanes]
            upper = grad_attended[latent, :, lanes]
            masked = head_masks(upper.astype(FULL))
            by_query, by_key, by_value = [], [], []
            for member in range(2):
                share = probs[latent, 2 * pair + member]
                weight = share.astype(FULL)
                grad_share = dot_nt(values, masked[member])
                product = weight * grad_share
                grad_scores = (
                    product - weight * jnp.sum(product, 0, keepdims=True)
                ).astype(LOW)
                by_query.append(dot(keys[member * HEAD : (member + 1) * HEAD], grad_scores))
                by_key.append(dot(grad_scores, queries))
                by_value.append(dot(share, upper))
            merged = jnp.concatenate(by_query, axis=0).T * scale
            grad_qkv[latent, :, lanes] = merged.astype(LOW)
            merged = jnp.where(mask, by_key[0], by_key[1]) * scale
            grad_qkv[latent, :, key_lanes] = merged.astype(LOW)
            merged = jnp.where(mask, by_value[0], by_value[1])
            grad_qkv[latent, :, value_lanes] = merged.astype(LOW)


def attend_backward(
    ids, tokens, mod, grad_mixed, grad_qkv, wq, total_project, grad_mod_late, sum_up, sum_down,
    grad_tokens, keep, send, extra,
    total_attend, grad_mod, extra_rows,
):
    rows = D // GROUP
    shards = keep.shape[1]
    step = pl.program_id(0)

    @pl.when(step == 0)
    def _():
        total_attend[...] = jnp.zeros_like(total_attend)

    count = tokens.shape[0]
    flat = count * LEN
    normed, inverse_spread = normalize(tokens[...].astype(FULL))
    hidden = (normed * (1.0 + mod[:, 1:2, :]) + mod[:, 0:1, :]).reshape(flat, D).astype(LOW)
    grad_low = grad_qkv[...].reshape(flat, 3 * D)
    total_attend[...] += dot_tn(hidden, grad_low)
    grad_hidden = dot(grad_low, wq[...]).reshape(count, LEN, D)
    mine = pl.ds(step * count, count)
    grad_mod[mine, 0:1, :] = jnp.sum(grad_hidden, axis=1, keepdims=True)
    grad_mod[mine, 1:2, :] = jnp.sum(grad_hidden * normed, axis=1, keepdims=True)
    grad_tokens[...] = grad_mixed[...] + normalize_back(
        grad_hidden * (1.0 + mod[:, 1:2, :]), normed, inverse_spread
    )

    @pl.when(step == pl.num_programs(0) - 1)
    def _():
        shard, low = ids[0], ids[1]
        wide, narrow = 3 * D // shards, D // shards

        @pl.loop(0, GROUP // 2)
        def _(t):
            for bit in range(2):
                span = rows_at(low ^ (2 * t + bit), rows)
                whole_attend, whole_project = total_attend[span, :], total_project[span, :]
                for s in range(shards):
                    d = lax.rem(s - shard + shards, shards)
                    piece = jnp.concatenate(
                        [
                            whole_attend[:, s * wide : (s + 1) * wide],
                            whole_project[:, s * narrow : (s + 1) * narrow],
                        ],
                        axis=1,
                    )
                    if bit:
                        send[t, d] = piece.astype(LOW)
                    else:
                        keep[t, d] = piece

        latents = grad_mod.shape[0]
        columns = [grad_mod[:, b, :] for b in range(2)] + [grad_mod_late[:, b, :] for b in range(4)]
        whole = jnp.concatenate(columns, axis=1).astype(LOW).astype(FULL)
        sums = jnp.sum(whole, axis=0, keepdims=True)
        sums = jnp.concatenate([sums, sum_up[...], sum_down[...]], axis=1)
        mod_share, bias_share = 6 * D // shards, BIAS_LEN // shards
        blocks, lines = -(-mod_share // D), -(-bias_share // D)

        def padded(values, start, stop):
            part = values[:, start : min(start + D, stop)]
            if part.shape[1] < D:
                rest = jnp.zeros((part.shape[0], D - part.shape[1]), FULL)
                part = jnp.concatenate([part, rest], axis=1)
            return part

        extra_rows[...] = jnp.zeros_like(extra_rows)
        for s in range(shards):
            for b in range(blocks):
                extra_rows[b * latents : (b + 1) * latents, :] = padded(
                    whole, s * mod_share + b * D, (s + 1) * mod_share
                )
            for b in range(lines):
                row = padded(sums, s * bias_share + b * D, (s + 1) * bias_share)
                high = row.astype(LOW).astype(FULL)
                place = blocks * latents + b
                extra_rows[place : place + 1, :] = high
                extra_rows[place + lines : place + lines + 1, :] = row - high
            extra[lax.rem(s - shard + shards, shards)] = extra_rows[...].astype(LOW)


def late_pieces(ids, own, first, second, third, extra, *pieces):
    total = own[...]
    for received in (first, second, third):
        total = total + received[...].astype(FULL)
    for d, piece in enumerate(pieces):
        piece[:NOTE, :] = extra[d]
        if total.shape[2] < D:
            piece[NOTE:, :] = jnp.zeros((total.shape[1], D), LOW)
        piece[NOTE:, : total.shape[2]] = total[d].astype(LOW)


def combine(shards, latents, ids, *refs):
    incoming, notes, weight, payload = (
        refs[:shards], refs[shards : 2 * shards], refs[2 * shards], refs[2 * shards + 1],
    )
    answers, rows_ref = refs[2 * shards + 2 : -1], refs[-1]
    rows = D // GROUP
    mod_share, bias_share = 6 * D // shards, BIAS_LEN // shards
    blocks, lines = -(-mod_share // D), -(-bias_share // D)
    total = jnp.zeros((rows, D), FULL)
    bias = jnp.zeros((NOTE, D), FULL)
    for d in range(shards):
        total = total + incoming[d][NOTE:, :].astype(FULL)
        extra = incoming[d][:NOTE, :].astype(FULL)
        bias = bias + extra
        for b in range(blocks):
            start = (b * shards + d) * latents
            rows_ref[start : start + latents, :] = extra[b * latents : (b + 1) * latents]
        start = (blocks * shards + d) * latents
        rows_ref[start : start + latents, :] = notes[d][:NOTE, :].astype(FULL)[:latents]
    payload[:rows, :] = total.astype(LOW)
    count = (blocks + 1) * shards * latents
    start = blocks * latents
    bias = bias[start : start + lines] + bias[start + lines : start + 2 * lines]
    high = bias.astype(LOW).astype(FULL)
    rows_ref[count:, :] = jnp.zeros((16, D), FULL)
    rows_ref[count : count + lines, :] = high
    rows_ref[count + 8 : count + 8 + lines, :] = bias - high
    payload[rows:, :] = rows_ref[...].astype(LOW)
    for d, answer in enumerate(answers):
        result = jnp.zeros((NOTE, D), FULL)
        for b in range(blocks):
            filled = min(D, mod_share - b * D)
            product = dot(incoming[d][:NOTE, :filled], weight[b * D : b * D + filled, :])
            result = result + shifted(product, b * latents)
        answer[...] = result[:latents]


def shifted(values, count):
    if count == 0:
        return values
    return jnp.concatenate([values[count:], values[:count]], axis=0)


COLUMNS = (3 * D, D, FF, FF, 6 * D)
TURNED = (True, True, False, False, True)
TRIANGLE = ((0, 0), (0, 1), (0, 2), (1, 1), (1, 2), (2, 2))


def slot_spans(widths):
    counts = [sum(1 for m, _ in SLOTS if m == number) for number in range(len(widths))]
    return [
        (part * (widths[m] // counts[m]), (part + 1) * (widths[m] // counts[m]))
        for m, part in SLOTS
    ]


def late_parts(latents, widths, late, late_flipped):
    rows = D // GROUP
    blocks = -(-widths[4] // D)
    unit = (blocks + 1) * latents + 16
    parts = [
        ref.at[t, pl.ds(start, unit), :]
        for ref in (late, late_flipped)
        for t in range(GROUP // 2)
        for start in range(rows, late.shape[1], unit)
    ]

    def rows_of(start):
        return jnp.concatenate([p[start : start + latents, :] for p in parts], axis=0)

    return parts, blocks, rows_of


def modulate_gradient(latents, widths, late, late_flipped, target):
    _, blocks, rows_of = late_parts(latents, widths, late, late_flipped)
    cond = rows_of(blocks * latents)
    for block in range(blocks):
        filled = min(D, widths[4] - block * D)
        target[block * D : block * D + filled, :] = dot_tn(rows_of(block * latents), cond)[:filled]


def late_gradient(ids, late, late_flipped, late_whole):
    rows = D // GROUP
    for place, block in pieces_of(ids, late, late_flipped):
        late_whole[rows_at(place, rows), :] = block[:rows, :].astype(FULL)
    return turn(late_whole[...])


def mix(moment, grad):
    moment = MOMENTUM * moment + grad
    return moment, grad + MOMENTUM * moment


def gram_kernel(latents, ids, late, late_flipped, early, early_flipped, *refs):
    moments, gram, columns = refs[0:5], refs[5], refs[6]
    late_whole, flat_gram, early_whole, modulate_whole = refs[7:11]
    low = ids[1]
    rows = D // GROUP
    shards = gram.shape[0]
    widths = [whole // shards for whole in COLUMNS]
    spans = slot_spans(widths)
    for number in range(5):
        owners = [k for k, (m, _) in enumerate(SLOTS) if m == number]
        condition = low == owners[0]
        for owner in owners[1:]:
            condition = condition | (low == owner)

        @pl.when(condition)
        def _(number=number, owners=owners):
            if number < 2:
                start = 0 if number == 0 else widths[0]
                grad = late_gradient(ids, late, late_flipped, late_whole)
                grad = grad[start : start + widths[number]]
            elif number < 4:
                start = 0 if number == 2 else widths[2]
                for place, block in pieces_of(ids, early, early_flipped):
                    piece = block[...].astype(FULL)[:, start : start + widths[number]]
                    early_whole[rows_at(place, rows), :] = piece
                grad = early_whole[...]
            else:
                modulate_gradient(latents, widths, late, late_flipped, modulate_whole)
                grad = modulate_whole[...]
            mixed = mix(moments[number][...], grad)[1]
            parts = split_low(mixed)
            whole = dot_split(parts, parts, dot_tn if TURNED[number] else dot_nt)
            for place, (a, b) in enumerate(TRIANGLE):
                flat_gram[place * 128 : (place + 1) * 128, :] = whole[
                    a * 128 : (a + 1) * 128, b * 128 : (b + 1) * 128
                ]
            if not TURNED[number]:
                mixed = turn(mixed)
            for owner in owners:

                @pl.when(low == owner)
                def _(owner=owner, mixed=mixed):
                    start, stop = spans[owner]
                    filled = stop - start
                    columns[:filled, :] = mixed[start:stop]
                    if filled < columns.shape[0]:
                        columns[filled:, :] = jnp.zeros((columns.shape[0] - filled, D), FULL)

    size = gram.shape[1]
    for s in range(shards):
        gram[lax.rem(s - ids[0] + shards, shards)] = flat_gram[s * size : (s + 1) * size, :]


def momenta_kernel(latents, ids, late, late_flipped, early, early_flipped, *refs):
    moments, grads, momenta = refs[0:5], refs[5:10], refs[10:15]
    bias, late_whole = refs[15:17]
    rows = D // GROUP
    widths = [m.shape[0 if turned else 1] for m, turned in zip(moments, TURNED)]
    turned = late_gradient(ids, late, late_flipped, late_whole)
    grads[0][...] = turned[: widths[0]]
    grads[1][...] = turned[widths[0] : widths[0] + widths[1]]
    for place, block in pieces_of(ids, early, early_flipped):
        piece = block[...].astype(FULL)
        grads[2][rows_at(place, rows), :] = piece[:, : widths[2]]
        grads[3][rows_at(place, rows), :] = piece[:, widths[2] :]
    modulate_gradient(latents, widths, late, late_flipped, grads[4])
    parts, blocks, _ = late_parts(latents, widths, late, late_flipped)
    total = jnp.zeros((16, D), FULL)
    for part in parts:
        total = total + part[(blocks + 1) * latents :, :].astype(FULL)
    bias[...] = total[:8] + total[8:]
    for number in range(5):
        momenta[number][...] = mix(moments[number][...], grads[number][...])[0]


def polynomial_kernel(ids, *refs):
    shards = len(refs) - 5
    pieces, columns, answer, flat_gram, gram_ref, product_ref = refs[:shards], *refs[shards:]
    size = pieces[0].shape[0]
    for d in range(shards):
        source = lax.rem(ids[0] - d + shards, shards)
        flat_gram[rows_at(source, size), :] = pieces[d][...]
    for place, (a, b) in enumerate(TRIANGLE):
        block = flat_gram[place * 128 : (place + 1) * 128, :]
        gram_ref[a * 128 : (a + 1) * 128, b * 128 : (b + 1) * 128] = block
        if a != b:
            gram_ref[b * 128 : (b + 1) * 128, a * 128 : (a + 1) * 128] = block.T
    gram = gram_ref[...]
    diagonal = lax.broadcasted_iota(jnp.int32, (D, D), 0) == lax.broadcasted_iota(
        jnp.int32, (D, D), 1
    )
    trace = jnp.sum(jnp.where(diagonal, gram, 0.0))
    scale = 1.0 / (jnp.sqrt(jnp.full((1, 1), trace)) + 1e-07)
    gram = (gram * scale) * scale

    def advance(gram, product):
        mixing = POLY_CUBIC * gram + POLY_QUINTIC * dot(left_deep(gram), right_deep(gram))
        mixing_deep = left_deep(mixing)
        both = jnp.concatenate([gram, product], axis=1)
        both = POLY_LINEAR * both + dot(mixing_deep, right_deep(both))
        half = both[:, :D]
        return POLY_LINEAR * half + dot(mixing_deep, right_deep(half)), both[:, D:]

    mixing = POLY_CUBIC * gram + POLY_QUINTIC * dot(left_deep(gram), right_deep(gram))
    mixing_deep = left_deep(mixing)
    half = POLY_LINEAR * gram + dot(mixing_deep, right_deep(gram))
    gram_ref[...] = POLY_LINEAR * half + dot(mixing_deep, right_deep(half))
    product_ref[...] = jnp.where(diagonal, POLY_LINEAR, 0.0) + mixing

    @pl.loop(0, NS_ITERS - 2)
    def _(step):
        gram, product = advance(gram_ref[...], product_ref[...])
        gram_ref[...] = gram
        product_ref[...] = product

    gram, product = gram_ref[...], product_ref[...]
    mixing = POLY_CUBIC * gram + POLY_QUINTIC * dot(left_deep(gram), right_deep(gram))
    product = POLY_LINEAR * product + dot(left_deep(mixing), right_deep(product))
    answer[...] = dot(left_deep(columns[...] * scale), right_deep(product)).astype(LOW)


def left_deep(value):
    high, rest = split_low(value)
    return jnp.concatenate([high, rest, high], axis=1)


def right_deep(value):
    high, rest = split_low(value)
    return jnp.concatenate([high, high, rest], axis=0)


def update_kernel(ids, answers, answers_flipped, *refs):
    masters, updated, ordered = refs[:5], refs[5:10], refs[10]
    for place, block in pieces_of(ids, answers, answers_flipped):
        ordered[place] = block[...]
    widths = [m.shape[0 if turned else 1] for m, turned in zip(masters, TURNED)]
    spans = slot_spans(widths)
    for number in range(5):
        factor = MUON_RATE * 0.2 * math.sqrt(COLUMNS[number])
        mine = [k for k, (m, _) in enumerate(SLOTS) if m == number]
        if TURNED[number]:
            for k in mine:
                start, stop = spans[k]
                updated[number][start:stop, :] = masters[number][start:stop, :] * (
                    1.0 - MUON_RATE * WEIGHT_DECAY
                ) - factor * ordered[k, : stop - start, :].astype(FULL)
        else:
            direction = jnp.concatenate(
                [ordered[k, : spans[k][1] - spans[k][0], :].astype(FULL) for k in mine], axis=0
            )
            updated[number][...] = masters[number][...] * (
                1.0 - MUON_RATE * WEIGHT_DECAY
            ) - factor * direction.T


def per_device(
    tokens,
    condition,
    cotangent,
    attend_weight,
    project_weight,
    expand_weight,
    contract_weight,
    modulate_weight,
    biases,
    attend_moment,
    project_moment,
    expand_moment,
    contract_moment,
    modulate_moment,
    bias_first,
    bias_second,
):
    latents = tokens.shape[0]
    steps = latents // BLOCK
    shards = lax.axis_size("shard")
    shard = lax.axis_index("shard")
    low = lax.axis_index("rep") % GROUP
    ids = jnp.stack([shard, low]).astype(jnp.int32)
    rows = D // GROUP
    bias_share = biases.shape[0]
    mod_share = modulate_weight.shape[1]
    late_width = 4 * D // shards
    late_rows = late_width // GROUP

    (note,) = local_call(
        prepare,
        ids,
        [
            (condition, False),
            (biases.reshape(1, -1), False),
            (attend_weight.T, (late_rows, lambda place: jnp.minimum(place, 5))),
            (project_weight.T, (late_rows, lambda place: jnp.maximum(place - 6, 0))),
        ],
        [((NOTE + late_rows, D), LOW, False)],
        [pltpu.VMEM((NOTE, D), FULL)],
        1,
        D * D,
        "prepare",
    )
    notes = exchange([note] * shards)

    (early_weights,) = local_call(
        pack,
        ids,
        [(w, (rows, lambda place: place)) for w in (expand_weight, contract_weight)],
        [((rows, 2 * FF // shards), LOW, False)],
        [],
        1,
        D * D,
        "pack",
    )
    early_weights = exchange([early_weights] * shards)

    *shares, modulate_low, late_weights = local_call(
        modulation_kernel,
        ids,
        [(piece, False) for piece in notes] + [(modulate_weight.T, False)],
        [((latents, mod_share), FULL, False)] * shards
        + [((mod_share, D), LOW, False), ((shards, late_rows, D), LOW, False)],
        [],
        1,
        2 * shards * NOTE * D * mod_share,
        "modulation",
        after=tuple(early_weights[1:]),
    )
    answers = [shares[0]] + [shift(shares[d], shards - d) for d in range(1, shards)]
    late_weights_chips = gather_chips(late_weights)
    (late_stacked,) = local_call(
        stack,
        ids,
        [(v, False) for v in late_weights_chips],
        [((GROUP // 2, shards, late_rows, D), LOW, False)],
        [],
        1,
        D * D,
        "stack_late",
        after=tuple(answers[1:]),
    )
    late_flipped = flip(late_stacked, 1)
    (early_weights,) = local_call(
        stack,
        ids,
        [(v, False) for v in early_weights],
        [((shards, rows, 2 * FF // shards), LOW, False)],
        [],
        1,
        D * D,
        "stack_early",
        after=(late_stacked,),
    )
    early_weights_chips = gather_chips(early_weights)

    tokens_shape = (latents, LEN, D)
    qkv, probs, attended, branch, wq, wo, mod, bias_up, bias_down = local_call(
        attention_forward,
        ids,
        [(tokens, True), (late_stacked, False), (late_flipped, False)]
        + [(v, False) for v in (*answers, *notes)],
        [
            ((latents, LEN, 3 * D), LOW, True),
            ((latents, HEADS, LEN, LEN), LOW, True),
            (tokens_shape, LOW, True),
            (tokens_shape, FULL, True),
            ((3 * D, D), LOW, False),
            ((D, D), LOW, False),
            ((latents, 6, D), FULL, False),
            ((1, FF), FULL, False),
            ((1, D), FULL, False),
        ],
        [
            pltpu.VMEM((shards, late_width, D), LOW if late_rows % 16 == 0 else FULL),
            pltpu.VMEM((BLOCK * LEN, D), LOW),
            pltpu.VMEM((BLOCK * LEN, D), LOW),
            pltpu.VMEM((shards, latents, mod_share), FULL),
            pltpu.VMEM((shards, NOTE, D), FULL),
            pltpu.VMEM((D, 3 * D), LOW),
            pltpu.VMEM((D, D), LOW),
        ],
        steps,
        latents * (2 * LEN * D * 4 * D + 4 * HEADS * LEN * LEN * PAIR) * 2,
        "attention_forward",
        after=(early_weights,),
    )
    early_shape = (GROUP // 2, shards, rows, 2 * FF // shards)
    (early_weights_stacked,) = local_call(
        stack,
        ids,
        [(v, False) for v in early_weights_chips],
        [(early_shape, LOW, False)],
        [],
        1,
        D * D,
        "stack",
        after=(branch,),
    )
    early_weights_flipped = flip(early_weights_stacked, 1)
    block_output, grad_mixed, grad_mod_late, keep, send, sum_up, sum_down = local_call(
        perceptron,
        ids,
        [
            (tokens, True),
            (branch, True),
            (mod, True),
            (cotangent, True),
            (early_weights_stacked, False),
            (early_weights_flipped, False),
            (bias_up, False),
            (bias_down, False),
        ],
        [
            (tokens_shape, LOW, True),
            (tokens_shape, FULL, True),
            ((latents, 4, D), FULL, True),
            (early_shape, FULL, False),
            (early_shape, LOW, False),
            ((1, FF), FULL, False),
            ((1, D), FULL, False),
        ],
        [
            pltpu.VMEM((shards, D, 2 * FF // shards), LOW),
            pltpu.VMEM((D, FF), LOW),
            pltpu.VMEM((D, FF), LOW),
            pltpu.VMEM((BLOCK * LEN, FF), LOW),
            pltpu.VMEM((BLOCK * LEN, FF), FULL),
            pltpu.VMEM((D, FF), FULL),
            pltpu.VMEM((D, FF), FULL),
        ],
        steps,
        latents * 2 * LEN * D * FF * 6 * 2,
        "perceptron",
    )

    early_totals = sum_cores(keep, send, ids, "early_sum", ())
    arrived = exchange_chips(early_totals)
    early_chips = sum(piece.astype(FULL) for piece in arrived[1:]) + arrived[0]
    grad_qkv, total_project = local_call(
        attention_backward,
        ids,
        [
            (mod, True),
            (attended, True),
            (grad_mixed, True),
            (qkv, True),
            (probs, True),
            (wo, False),
        ],
        [((latents, LEN, 3 * D), LOW, True), ((D, D), FULL, False)],
        [pltpu.VMEM((1, LEN, D), LOW)],
        latents,
        latents * (10 * HEADS * LEN * LEN * PAIR + 4 * LEN * D * D),
        "attention_backward",
        after=tuple(early_totals[1:]),
    )
    early_pieces = exchange([early_chips[d].astype(LOW) for d in range(shards)])
    late_shape = (GROUP // 2, shards, rows, late_width)
    tokens_grad, keep, send, extra = local_call(
        attend_backward,
        ids,
        [
            (tokens, True),
            (mod, True),
            (grad_mixed, True),
            (grad_qkv, True),
            (wq, False),
            (total_project, False),
            (grad_mod_late, False),
            (sum_up, False),
            (sum_down, False),
        ],
        [
            (tokens_shape, FULL, True),
            (late_shape, FULL, False),
            (late_shape, LOW, False),
            ((shards, NOTE, D), LOW, False),
        ],
        [
            pltpu.VMEM((D, 3 * D), FULL),
            pltpu.VMEM((latents, 2, D), FULL),
            pltpu.VMEM((NOTE, D), FULL),
        ],
        steps,
        latents * 2 * LEN * D * 6 * D * 2,
        "attend_backward",
        after=(early_chips,),
    )

    late_totals = sum_cores(keep, send, ids, "late_sum", ())
    arrived = exchange_chips(late_totals)
    (early,) = local_call(
        total_kernel,
        ids,
        [(v, False) for v in (early_chips[0], *early_pieces[1:])],
        [(early_pieces[1].shape, LOW, False)],
        [],
        1,
        D * D,
        "early_total",
        after=tuple(late_totals[1:]),
    )
    early_stacked, early_flipped = gather_group(sum_rest(early))
    outgoing = local_call(
        late_pieces,
        ids,
        [(v, False) for v in (*arrived, extra)],
        [((NOTE + rows, D), LOW, False)] * shards,
        [],
        1,
        4 * shards * rows * late_width,
        "late_pieces",
        after=(early,),
    )
    group_latents = shards * latents
    unit = (-(-mod_share // D) + 1) * group_latents + 16
    payload, *shares = local_call(
        partial(combine, shards, latents),
        ids,
        [(v, False) for v in (*exchange(outgoing), *notes, modulate_low)],
        [((rows + unit, D), LOW, False)] + [((latents, D), FULL, False)] * shards,
        [pltpu.VMEM((unit, D), FULL)],
        1,
        2 * shards * NOTE * D * mod_share,
        "combine",
        after=(early_stacked,),
    )
    if lax.axis_size("rep") > GROUP:
        late, others = sum_rest(payload[:rows]), payload[rows:]
        for bit in range(3, lax.axis_size("rep").bit_length() - 1):
            others = jnp.concatenate([others, flip(others, 1 << bit)], axis=0)
        payload = jnp.concatenate([late, others], axis=0)
    late_stacked, late_flipped = gather_group(payload)

    grad_cond_low = shares[0]
    for d in range(1, shards):
        grad_cond_low = grad_cond_low + shift(shares[d], shards - d)
    _, silu_back = jax.vjp(jax.nn.silu, condition.astype(FULL))
    condition_grad = silu_back(grad_cond_low)[0]

    def as_held(values):
        return [v.T if turned else v for v, turned in zip(values, TURNED)]

    masters = as_held(
        [attend_weight, project_weight, expand_weight, contract_weight, modulate_weight]
    )
    moments = as_held(
        [attend_moment, project_moment, expand_moment, contract_moment, modulate_moment]
    )
    shapes = [m.shape for m in masters]
    widths = [whole // shards for whole in COLUMNS]
    slot_width = max(stop - start for start, stop in slot_spans(widths))
    piece_rows = 128 * len(TRIANGLE) // shards
    sources = [
        (v, False) for v in (late_stacked, late_flipped, early_stacked, early_flipped, *moments)
    ]
    gram, columns = local_call(
        partial(gram_kernel, group_latents),
        ids,
        sources,
        [((shards, piece_rows, 128), FULL, False), ((slot_width, D), FULL, False)],
        [
            pltpu.VMEM((D, D), FULL),
            pltpu.VMEM((128 * len(TRIANGLE), 128), FULL),
            pltpu.VMEM(shapes[2], FULL),
            pltpu.VMEM(shapes[4], FULL),
        ],
        1,
        6 * D * D * D,
        "gram",
    )
    *results, bias_block = local_call(
        partial(momenta_kernel, group_latents),
        ids,
        sources,
        [(shape, FULL, False) for shape in shapes * 2] + [((8, D), FULL, False)],
        [pltpu.VMEM((D, D), FULL)],
        1,
        D * D * D,
        "momenta",
        after=(gram,),
    )
    gradients, momenta = as_held(results[0:5]), as_held(results[5:10])
    piece = sum(exchange([gram[d] for d in range(shards)]))
    (answer,) = local_call(
        polynomial_kernel,
        ids,
        [(p, False) for p in exchange([piece] * shards)] + [(columns, False)],
        [((slot_width, D), LOW, False)],
        [
            pltpu.VMEM((128 * len(TRIANGLE), 128), FULL),
            pltpu.VMEM((D, D), FULL),
            pltpu.VMEM((D, D), FULL),
        ],
        1,
        2 * 3 * 18 * D * D * D,
        "polynomial",
        after=(condition_grad, bias_block),
    )
    updated = local_call(
        update_kernel,
        ids,
        [(v, False) for v in (*gather_group(answer), *masters)],
        [(shape, FULL, False) for shape in shapes],
        [pltpu.VMEM((GROUP, slot_width, D), LOW)],
        1,
        2 * D * sum(widths),
        "update",
    )
    updated = as_held(updated)

    bias_gradient = bias_block.reshape(-1)[:bias_share]
    bias_momentum = BETA_ONE * bias_first + (1.0 - BETA_ONE) * bias_gradient
    bias_variance = BETA_TWO * bias_second + (1.0 - BETA_TWO) * bias_gradient * bias_gradient
    corrected_first = bias_momentum / (1.0 - BETA_ONE**STEP)
    corrected_second = bias_variance / (1.0 - BETA_TWO**STEP)
    bias_updated = biases * (1.0 - ADAM_RATE * WEIGHT_DECAY) - ADAM_RATE * corrected_first / (
        jnp.sqrt(corrected_second) + ADAM_EPSILON
    )
    return (
        block_output,
        tokens_grad,
        condition_grad,
        *gradients,
        *momenta,
        *updated,
        bias_gradient,
        bias_momentum,
        bias_variance,
        bias_updated,
    )


def solution(mesh):
    rows = P(("shard", "rep"), None, None)
    vectors = P(("shard", "rep"), None)
    columns = P(None, "shard")
    flat = P("shard")
    return jax.shard_map(
        per_device,
        mesh=mesh,
        in_specs=(rows, vectors, rows) + (columns,) * 5 + (flat,) + (columns,) * 5 + (flat,) * 2,
        out_specs=(rows, rows, vectors) + (columns,) * 15 + (flat,) * 4,
        check_vma=False,
    )
```
